32 devices in a mesh: dp: 16 (over z, x, core), tensor: 2 (over y).
Axes of the slice: x: 2, y: 2, z: 4, core: 2. Of those that a mesh axis runs over, the one named last changes fastest.
Arguments:
- tokens: bfloat16 [16384, 1024], P('dp'), may hold values from -6 to 6
- segment: int32 [16384], P('dp'), may hold values from 0 to 39, never falling along the last dimension, each value on 1 to 800 neighbouring positions
- norm1_gain: bfloat16 [1024], replicated, may hold values from 0.5 to 1.5
- w_query: bfloat16 [1024, 1024], P(None, 'tensor'), may hold values from -0.1875 to 0.1875
- w_key: bfloat16 [1024, 1024], P(None, 'tensor'), may hold values from -0.1875 to 0.1875
- w_value: bfloat16 [1024, 1728], P(None, 'tensor'), may hold values from -0.1875 to 0.1875
- w_gate: bfloat16 [1024, 1728], P(None, 'tensor'), may hold values from -0.1875 to 0.1875
- group_gain: bfloat16 [1728], P('tensor'), may hold values from 0.5 to 1.5
- group_bias: bfloat16 [1728], P('tensor'), may hold values from -1.5 to 1.5
- w_out: bfloat16 [1728, 1024], P('tensor'), may hold values from -0.15625 to 0.15625
- norm2_gain: bfloat16 [1024], replicated, may hold values from 0.5 to 1.5
- w_mlp_gate: bfloat16 [1024, 1728], P(None, 'tensor'), may hold values from -0.1875 to 0.1875
- w_mlp_up: bfloat16 [1024, 1728], P(None, 'tensor'), may hold values from -0.1875 to 0.1875
- w_mlp_down: bfloat16 [1728, 1024], P('tensor'), may hold values from -0.15625 to 0.15625
- cotangent: bfloat16 [16384, 1024], P('dp'), may hold values from -6 to 6
Outputs:
- output: bfloat16 [16384, 1024], P(('dp', 'tensor'))
- grad_tokens: bfloat16 [16384, 1024], P('dp')
- grad_norm1_gain: float32 [1024], replicated
- grad_w_query: float32 [1024, 1024], P(None, 'tensor')
- grad_w_key: float32 [1024, 1024], P(None, 'tensor')
- grad_w_value: float32 [1024, 1728], P(None, 'tensor')
- grad_w_gate: float32 [1024, 1728], P(None, 'tensor')
- grad_group_gain: float32 [1728], P('tensor')
- grad_group_bias: float32 [1728], P('tensor')
- grad_w_out: float32 [1728, 1024], P('tensor')
- grad_norm2_gain: float32 [1024], replicated
- grad_w_mlp_gate: float32 [1024, 1728], P(None, 'tensor')
- grad_w_mlp_up: float32 [1024, 1728], P(None, 'tensor')
- grad_w_mlp_down: float32 [1728, 1024], P('tensor')
The draws below stay inside these ranges and needn't reach their ends.
Inputs may be any that keep to these rules, and one draw needn't show every extreme that they name: `segment`: document numbers never fall along the tokens; each document spans 1 to 800 tokens and one spans exactly 800.
All inputs are finite; a program needn't handle non-finite values.
Results may differ from the reference program's by a relative error of at most 0.015.
Values sent between devices are 32-bit elements; how exact they have to be, the bound alone decides.
A program may use at most 256 MiB of HBM per device.

```python
import math
import jax
import jax.numpy as jnp
import numpy as np
from jax import lax

D = 1024
HEADS = 4
KD = 256
VD = 432
FF = 1728
TOK_DEV = 1024
TOKENS = 16384
DOC_MOST = 800
DOCS = 40


def shard_levels(stream_key, shape, shards, smallest, high):
    level, own = 1.0, jax.random.fold_in(stream_key, 6)
    for dim, parts in shards:
        heights = jnp.exp(jax.random.uniform(jax.random.fold_in(own, dim), (parts,), jnp.float32, smallest / len(shards), high / len(shards)))
        level = level * jnp.repeat(heights, shape[dim] // parts).reshape([-1 if axis == dim else 1 for axis in range(len(shape))])
    return level


def split_up(amount, total, limit, skew):
    portions = [(1 << 20) // math.isqrt(rank ** skew) + 1 for rank in range(2, amount + 1)]
    surplus, given = total - limit - (amount - 1), [1] * (amount - 1)
    while surplus > 0:
        candidates = [i for i in range(amount - 1) if given[i] < limit]
        mass, remaining = sum([portions[i] for i in candidates]), surplus
        for i in candidates:
            addition = min(limit - given[i], max(1, remaining * portions[i] // mass), surplus)
            given[i] = given[i] + addition
            surplus = surplus - addition
    return np.array([limit] + given)


def uneven(key, amount, total, most, skew):
    if amount == 2:
        one = jax.random.randint(key, (), max(1, total - most), min(most, total - 1) + 1)
        return jnp.stack([one, total - one])
    lengths = jnp.asarray(split_up(amount, total, most, skew), jnp.int32)
    twos = (amount - 1) // 2
    giver, taker = lengths[1:1 + 2 * twos:2], lengths[2:2 + 2 * twos:2]
    slack = jnp.minimum(giver - 1, most - taker)
    shifted = jax.random.randint(jax.random.fold_in(key, 1), (twos,), 0, 1 << 20) % (slack + 1)
    lengths = lengths.at[1:1 + 2 * twos:2].set(giver - shifted).at[2:2 + 2 * twos:2].set(taker + shifted)
    return lengths[jax.random.permutation(jax.random.fold_in(key, 2), amount)]


def gaussian(key, dims, scale, limit, pieces=(), kind=jnp.bfloat16):
    result = scale * jax.random.normal(key, dims, jnp.float32)
    if pieces:
        result = result * shard_levels(key, dims, pieces, -0.22, 0.18)
    return jnp.clip(result, -limit, limit).astype(kind)


def setup_inputs(seed: int = 0) -> dict:
    splits = jax.random.split(jax.random.key(seed), 16)
    tokens = gaussian(splits[0], (TOKENS, D), 1.0, 6.0, ((0, 16),))
    segment = jnp.searchsorted(jnp.cumsum(uneven(splits[1], DOCS, TOKENS, DOC_MOST, 1)), jnp.arange(TOKENS), side="right").astype(jnp.int32)
    norm1_gain = jnp.clip(1.0 + 0.1 * jax.random.normal(splits[2], (D,), jnp.float32), 0.5, 1.5).astype(jnp.bfloat16)
    w_query = gaussian(splits[3], (D, HEADS * KD), D ** -0.5, 0.1875, ((1, 2),))
    w_key = gaussian(splits[4], (D, HEADS * KD), D ** -0.5, 0.1875, ((1, 2),))
    w_value = gaussian(splits[5], (D, HEADS * VD), D ** -0.5, 0.1875, ((1, 2),))
    w_gate = gaussian(splits[6], (D, HEADS * VD), D ** -0.5, 0.1875, ((1, 2),))
    group_gain = jnp.clip(1.0 + 0.1 * jax.random.normal(splits[7], (HEADS * VD,), jnp.float32), 0.5, 1.5).astype(jnp.bfloat16)
    group_bias = gaussian(splits[8], (HEADS * VD,), 0.3, 1.5, ((0, 2),))
    w_out = gaussian(splits[9], (HEADS * VD, D), (HEADS * VD) ** -0.5, 0.15625, ((0, 2),))
    norm2_gain = jnp.clip(1.0 + 0.1 * jax.random.normal(splits[10], (D,), jnp.float32), 0.5, 1.5).astype(jnp.bfloat16)
    w_mlp_gate = gaussian(splits[11], (D, FF), D ** -0.5, 0.1875, ((1, 2),))
    w_mlp_up = gaussian(splits[12], (D, FF), D ** -0.5, 0.1875, ((1, 2),))
    w_mlp_down = gaussian(splits[13], (FF, D), FF ** -0.5, 0.15625, ((0, 2),))
    cotangent = gaussian(splits[14], (TOKENS, D), 1.0, 6.0, ((0, 16),))
    return {"tokens": tokens, "segment": segment, "norm1_gain": norm1_gain, "w_query": w_query, "w_key": w_key, "w_value": w_value, "w_gate": w_gate, "group_gain": group_gain, "group_bias": group_bias, "w_out": w_out, "norm2_gain": norm2_gain, "w_mlp_gate": w_mlp_gate, "w_mlp_up": w_mlp_up, "w_mlp_down": w_mlp_down, "cotangent": cotangent}


@jax.custom_vjp
def low(v):
    return lax.optimization_barrier(v.astype(jnp.bfloat16)).astype(jnp.float32)

@jax.custom_vjp
def low_back(v):
    return v

def low_keep(v):
    return (low(v), None)

def low_pass(kept, grad):
    return (grad,)

def back_keep(v):
    return (v, None)

def back_low(kept, grad):
    return (low(grad),)
low.defvjp(low_keep, low_pass)
low_back.defvjp(back_keep, back_low)
EPSILON = 1e-06
GROUP_EPSILON = 0.25
HIGHEST = lax.Precision.HIGHEST

def matmul_high(left, right):
    return jnp.matmul(left, right, precision=HIGHEST)

def rms_norm(vectors, scales):
    return vectors * lax.rsqrt(lax.optimization_barrier(jnp.mean(vectors * vectors, axis=-1, keepdims=True)) + EPSILON) * scales

def rotate(vectors, direction):
    half_dim = vectors.shape[-1] // 2
    length = vectors.shape[-3]
    frequency = jnp.exp(-jnp.log(10000.0) * jnp.arange(half_dim, dtype=jnp.float32) / half_dim)
    angles = jnp.arange(length, dtype=jnp.float32)[:, None] * frequency[None, :]
    cosine = jnp.cos(angles)[:, None, :]
    sine_part = direction * jnp.sin(angles)[:, None, :]
    lower_half = vectors[..., :half_dim]
    upper_half = vectors[..., half_dim:]
    return jnp.concatenate([lower_half * cosine - upper_half * sine_part, upper_half * cosine + lower_half * sine_part], axis=-1)

def decay_table(segments, head_count):
    length = segments.shape[-1]
    positions = jnp.arange(length, dtype=jnp.int32)
    offsets = positions[:, None] - positions[None, :]
    visible = (offsets >= 0)[None] & (segments[:, :, None] == segments[:, None, :])
    log_rates = jnp.log1p(-jnp.exp2(-5.0 - jnp.arange(head_count, dtype=jnp.float32)))
    decays = jnp.exp(jnp.maximum(offsets, 0).astype(jnp.float32)[None] * log_rates[:, None, None])
    return jnp.where(visible[:, None], decays[None], jnp.zeros((), jnp.float32))

def block_layer(inputs, segments, params):
    gain_first, proj_query, proj_key, proj_value, proj_gate, group_scale, group_shift, proj_out, gain_second, proj_mlp_gate, proj_mlp_up, proj_mlp_down = params
    groups = inputs.shape[0]
    length = inputs.shape[1]
    normed_in = low(rms_norm(inputs, gain_first))
    queries = low(rotate(low_back(matmul_high(normed_in, proj_query)).reshape(groups, length, HEADS, KD), 1.0))
    keys_rot = low(rotate(low_back(matmul_high(normed_in, proj_key)).reshape(groups, length, HEADS, KD), 1.0) * KD ** (-0.5))
    values_low = low(low_back(matmul_high(normed_in, proj_value))).reshape(groups, length, HEADS, VD)
    gate_raw = low_back(matmul_high(normed_in, proj_gate))
    raw_scores = low_back(jnp.einsum('gnhk,gmhk->ghnm', queries, keys_rot, precision=HIGHEST))
    scores = low(raw_scores * decay_table(segments, HEADS))
    retained = low_back(jnp.einsum('ghnm,gmhv->gnhv', scores, values_low, precision=HIGHEST))
    centred = retained - lax.optimization_barrier(jnp.mean(retained, axis=-1, keepdims=True))
    normed = centred * lax.rsqrt(lax.optimization_barrier(jnp.mean(centred * centred, axis=-1, keepdims=True)) + GROUP_EPSILON)
    normed = normed.reshape(groups, length, HEADS * VD) * group_scale + group_shift
    gated_out = low(jax.nn.silu(gate_raw) * normed)
    middle = inputs + low_back(matmul_high(gated_out, proj_out))
    normed_mid = low(rms_norm(middle, gain_second))
    gate_proj = low_back(matmul_high(normed_mid, proj_mlp_gate))
    up_proj = low_back(matmul_high(normed_mid, proj_mlp_up))
    hidden = low(jax.nn.gelu(gate_proj) * up_proj)
    return middle + low_back(matmul_high(hidden, proj_mlp_down))

def reference(tokens, segment, norm1_gain, w_query, w_key, w_value, w_gate, group_gain, group_bias, w_out, norm2_gain, w_mlp_gate, w_mlp_up, w_mlp_down, cotangent):
    params = tuple((weight.astype(jnp.float32) for weight in (norm1_gain, w_query, w_key, w_value, w_gate, group_gain, group_bias, w_out, norm2_gain, w_mlp_gate, w_mlp_up, w_mlp_down)))
    inputs = tokens.astype(jnp.float32)
    segments = segment.reshape(-1, 4, TOK_DEV)
    step_layer = jax.checkpoint(block_layer)

    def forward(whole_inputs, weights):
        grouped = whole_inputs.reshape(-1, 4, TOK_DEV, D)

        def scan_step(carried, packed):
            return (carried, step_layer(packed[0], packed[1], weights))
        _, results = lax.scan(scan_step, jnp.zeros((), jnp.float32), (grouped, segments))
        return results.reshape(TOKENS, D)
    output, pull_back = jax.vjp(forward, inputs, params)
    grad_inputs, grad_params = pull_back(cotangent.astype(jnp.float32))
    grad_norm1, grad_query, grad_key, grad_value, grad_gate, grad_gscale, grad_gshift, grad_out, grad_norm2, grad_mgate, grad_mup, grad_mdown = grad_params
    return (output.astype(jnp.bfloat16), grad_inputs.astype(jnp.bfloat16), grad_norm1, grad_query, grad_key, grad_value, grad_gate, grad_gscale, grad_gshift, grad_out, grad_norm2, grad_mgate, grad_mup, grad_mdown)
```

```python
import functools

import jax
import jax.numpy as jnp
from jax import lax
from jax.experimental import pallas as pl
from jax.experimental.pallas import tpu as pltpu
from jax.sharding import PartitionSpec as P

KD = 256
VD = 432
LANE = 128
MESH = pl.DeviceIdType.MESH


EPSILON = 1e-06
GROUP_EPSILON = 0.25


def project(left, right):
    return jnp.dot(left, right, preferred_element_type=jnp.float32)


def inner_rows(left, right):
    return lax.dot_general(
        left, right, (((0,), (0,)), ((), ())), preferred_element_type=jnp.float32
    )


def outer_cols(left, right):
    return lax.dot_general(
        left, right, (((1,), (1,)), ((), ())), preferred_element_type=jnp.float32
    )


def rms_norm(vectors, scales):
    return (
        vectors * lax.rsqrt(jnp.mean(vectors * vectors, axis=-1, keepdims=True) + EPSILON) * scales
    )


def rotate(vectors, direction):
    half_dim = vectors.shape[-1] // 2
    length = vectors.shape[-3]
    frequency = jnp.exp(-jnp.log(10000.0) * jnp.arange(half_dim, dtype=jnp.float32) / half_dim)
    angles = jnp.arange(length, dtype=jnp.float32)[:, None] * frequency[None, :]
    cosine = jnp.cos(angles)[:, None, :]
    sine_part = direction * jnp.sin(angles)[:, None, :]
    lower_half = vectors[..., :half_dim]
    upper_half = vectors[..., half_dim:]
    return jnp.concatenate(
        [
            lower_half * cosine - upper_half * sine_part,
            upper_half * cosine + lower_half * sine_part,
        ],
        axis=-1,
    )


def decay_rows(segments, first_head, head_count):
    length = segments.shape[0]
    positions = jnp.arange(length, dtype=jnp.int32)
    offsets = positions[:, None] - positions[None, :]
    visible = (offsets >= 0) & (segments[:, None] == segments[None, :])
    orders = (first_head + jnp.arange(head_count, dtype=jnp.int32)).astype(jnp.float32)
    log_rates = jnp.log1p(-jnp.exp2(-5.0 - orders))
    decays = jnp.exp(jnp.maximum(offsets, 0).astype(jnp.float32)[None] * log_rates[:, None, None])
    return jnp.where(visible[None], decays, jnp.zeros((), jnp.float32))


def gate_norm(retained, gate_raw, group_scale, group_shift):
    centred = retained - jnp.mean(retained, axis=-1, keepdims=True)
    normed = centred * lax.rsqrt(
        jnp.mean(centred * centred, axis=-1, keepdims=True) + GROUP_EPSILON
    )
    normed = normed.reshape(retained.shape[0], -1) * group_scale + group_shift
    return jax.nn.silu(gate_raw) * normed


def gelu_glu(gate_proj, up_proj):
    return jax.nn.gelu(gate_proj) * up_proj


def ring_place(chip, chips):
    line = chips // 2
    x = chip % 2
    z = chip // 2
    return z + x * (chips - 1 - 2 * z), line


def ring_chip(place, chips):
    line = chips // 2
    x = place // line
    z = place + x * (chips - 1 - 2 * place)
    return z * 2 + x


def bit_partner(index, bit):
    step = 1 << bit
    return index + (1 - 2 * ((index // step) % 2)) * step


def reduce_kernel(chips, subs, widths, *refs):
    count = len(widths)
    grads = refs[:count]
    (h_ref, s_ref, r_ref, hr_ref, so_ref, own, sib, rcv, sacc, sbuf) = refs[count : count + 10]
    (own_sem, sbs_sem, sbr_sem, rss_sem, rsr_sem, ags_sem, agr_sem, cgs_sem, cgr_sem, loc_sem, hs_sem, hr_sem, ss_sem, sr_sem) = refs[
        count + 10 :
    ]
    index = lax.axis_index("dp")
    tensor = lax.axis_index("tensor")
    core = index % 2
    place, _ = ring_place(index // 2, chips)
    bits = (2 * chips).bit_length() - 1
    nexts = [
        ring_chip((place + 1) % chips, chips) * 2 + core,
        ring_chip((place + chips - 1) % chips, chips) * 2 + core,
    ]
    virtual = [place, (chips - place) % chips]
    sibling = index + 1 - 2 * core
    rows = own.shape[2]
    sub_rows = rows // subs
    quarter = rows * chips
    half = 2 * quarter

    def at_dp(device):
        return {"dp": device}

    barrier = pltpu.get_barrier_semaphore()
    greeted = [at_dp(nexts[0]), at_dp(nexts[1]), {"tensor": 1 - tensor}]
    greeted += [at_dp(bit_partner(index, bit)) for bit in range(bits)]
    for device in greeted:
        pl.semaphore_signal(barrier, inc=1, device_id=device, device_id_type=MESH)
    pl.semaphore_wait(barrier, len(greeted))

    def row_slice(which, d, chunk, sub):
        return pl.ds(
            pl.multiple_of(which * half + d * quarter + chunk * rows + sub * sub_rows, 8), sub_rows
        )

    def chunk_at(d, order):
        return (virtual[d] + 2 * chips - 1 - order) % chips

    def sub_slice(sub):
        return pl.ds(sub * sub_rows, sub_rows)

    def own_copy(d, order, sub):
        where = row_slice(core, d, chunk_at(d, order), sub)
        start = 0
        out = []
        for g, width in zip(grads, widths):
            out.append(
                pltpu.make_async_copy(
                    g.at[where, :],
                    own.at[d, order, sub_slice(sub), pl.ds(start, width)],
                    own_sem.at[d, order, sub],
                )
            )
            start += width
        return out

    def sib_copy(d, order, sub):
        where = row_slice(1 - core, d, chunk_at(d, order), sub)
        start = 0
        out = []
        for g, width in zip(grads, widths):
            out.append(
                pltpu.make_async_remote_copy(
                    g.at[where, :],
                    sib.at[d, order, sub_slice(sub), pl.ds(start, width)],
                    sbs_sem.at[d, order, sub],
                    sbr_sem.at[d, order, sub],
                    device_id=at_dp(sibling),
                    device_id_type=MESH,
                )
            )
            start += width
        return out

    def own_wait(d, order, sub):
        whole = own.at[d, order, sub_slice(sub), :]
        pltpu.make_async_copy(whole, whole, own_sem.at[d, order, sub]).wait()

    def sib_wait(d, order, sub, sems):
        whole = sib.at[d, order, sub_slice(sub), :]
        pltpu.make_async_copy(whole, whole, sems.at[d, order, sub]).wait()

    def rs_copy(d, step, sub):
        return pltpu.make_async_remote_copy(
            own.at[d, step, sub_slice(sub), :],
            rcv.at[d, step, sub_slice(sub), :],
            rss_sem.at[d, step, sub],
            rsr_sem.at[d, step, sub],
            device_id=at_dp(nexts[d]),
            device_id_type=MESH,
        )

    def ag_copy(d, step, sub, source=None):
        where = row_slice(core, d, (virtual[d] + chips - step) % chips, sub)
        return pltpu.make_async_remote_copy(
            r_ref.at[where, :] if source is None else source,
            r_ref.at[where, :],
            ags_sem.at[d, step, sub],
            agr_sem.at[d, step, sub],
            device_id=at_dp(nexts[d]),
            device_id_type=MESH,
        )

    def ag_wait(d, step, sub):
        where = row_slice(core, d, (virtual[d] + 2 * chips - step - 1) % chips, sub)
        part = r_ref.at[where, :]
        pltpu.make_async_copy(part, part, agr_sem.at[d, step, sub]).wait()

    def cg_copy(d, step, sub, source=None):
        where = row_slice(core, d, (virtual[d] + chips - step) % chips, sub)
        return pltpu.make_async_remote_copy(
            r_ref.at[where, :] if source is None else source,
            r_ref.at[where, :],
            cgs_sem.at[d, step, sub],
            cgr_sem.at[d, step, sub],
            device_id=at_dp(sibling),
            device_id_type=MESH,
        )

    def cg_wait(d, step, sub):
        where = row_slice(1 - core, d, (virtual[d] + chips - step) % chips, sub)
        part = r_ref.at[where, :]
        pltpu.make_async_copy(part, part, cgr_sem.at[d, step, sub]).wait()

    pieces = [(d, sub) for sub in range(subs) for d in range(2)]

    def load_step(order, carry):
        for d, sub in pieces:
            for copy in own_copy(d, order, sub):
                copy.start()
            for copy in sib_copy(d, order, sub):
                copy.start()
        return carry

    load_step(0, 0)
    exchange = h_ref.shape[0] // 4

    def h_copy(part):
        where = pl.ds(pl.multiple_of(part * exchange, 8), exchange)
        return pltpu.make_async_remote_copy(
            h_ref.at[where, :],
            hr_ref.at[where, :],
            hs_sem.at[part],
            hr_sem.at[part],
            device_id={"tensor": 1 - tensor},
            device_id_type=MESH,
        )

    for part in range(4):
        h_copy(part).start()
    lax.fori_loop(1, chips, load_step, 0)

    def s_copy(level):
        target = {"tensor": 1 - tensor} if level == 0 else at_dp(bit_partner(index, level - 1))
        return pltpu.make_async_remote_copy(
            sacc.at[level],
            sbuf.at[level],
            ss_sem.at[level],
            sr_sem.at[level],
            device_id=target,
            device_id_type=MESH,
        )

    def s_finish(level):
        s_copy(level).wait()
        got = sbuf[level]
        if level == 0:
            first = lax.broadcasted_iota(jnp.int32, got.shape, 0) == 0
            got = jnp.where(first, got, 0.0)
        sacc[level + 1] = sacc[level] + got

    sacc[0] = s_ref[...]

    def small_step(step):
        for level in range(bits + 2):

            @pl.when(step == level)
            def _():
                if level > 0:
                    s_finish(level - 1)
                if level <= bits:
                    s_copy(level).start()

    for d, sub in pieces:
        own_wait(d, 0, sub)
        sib_wait(d, 0, sub, sbr_sem)
        part = sub_slice(sub)
        own[d, 0, part, :] = own[d, 0, part, :] + sib[d, 0, part, :]
        rs_copy(d, 0, sub).start()
    small_step(0)

    def total(d, step, sub):
        own_wait(d, step, sub)
        sib_wait(d, step, sub, sbr_sem)
        rs_copy(d, step - 1, sub).wait_recv()
        part = sub_slice(sub)
        own[d, step, part, :] = (
            own[d, step, part, :] + sib[d, step, part, :] + rcv[d, step - 1, part, :]
        )

    def rs_step(step, carry):
        for d, sub in pieces:
            total(d, step, sub)
            rs_copy(d, step, sub).start()
        small_step(step)
        return carry

    lax.fori_loop(1, chips - 1, rs_step, 0)
    for d, sub in pieces:
        total(d, chips - 1, sub)
        source = own.at[d, chips - 1, sub_slice(sub), :]
        ag_copy(d, 0, sub, source).start()
        cg_copy(d, 0, sub, source).start()
        where = row_slice(core, d, virtual[d], sub)
        pltpu.make_async_copy(source, r_ref.at[where, :], loc_sem.at[d, sub]).start()

    def ag_step(step, carry):
        for d, sub in pieces:
            ag_wait(d, step, sub)
            ag_copy(d, step + 1, sub).start()
            cg_copy(d, step + 1, sub).start()
        return carry

    lax.fori_loop(0, chips - 2, ag_step, 0)
    for d, sub in pieces:
        ag_wait(d, chips - 2, sub)
        cg_copy(d, chips - 1, sub).start()

    so_ref[...] = sacc[bits + 1]

    def drain(step, carry):
        for d, sub in pieces:
            sib_wait(d, step, sub, sbs_sem)
            cg_copy(d, step, sub).wait_send()
            cg_wait(d, step, sub)
        return carry

    lax.fori_loop(0, chips, drain, 0)

    def drain_ring(step, carry):
        for d, sub in pieces:
            rs_copy(d, step, sub).wait_send()
            ag_copy(d, step, sub).wait_send()
        return carry

    lax.fori_loop(0, chips - 1, drain_ring, 0)
    for d, sub in pieces:
        source = own.at[d, chips - 1, sub_slice(sub), :]
        where = row_slice(core, d, virtual[d], sub)
        pltpu.make_async_copy(source, r_ref.at[where, :], loc_sem.at[d, sub]).wait()
    for part in range(4):
        h_copy(part).wait()


def reduce_all(grads, exchanged, small):
    chips = lax.axis_size("dp") // 2
    widths = tuple(g.shape[1] for g in grads)
    width = sum(widths)
    total_rows = grads[0].shape[0]
    rows = total_rows // (4 * chips)
    subs = 2 if rows % 16 == 0 else 1
    bits = (2 * chips).bit_length() - 1
    dma = lambda *shape: pltpu.SemaphoreType.DMA(shape)
    hbm = pl.BlockSpec(memory_space=pl.ANY)
    vmem = pl.BlockSpec(memory_space=pltpu.VMEM)
    f32 = jnp.float32
    return pl.pallas_call(
        functools.partial(reduce_kernel, chips, subs, widths),
        out_shape=(
            jax.ShapeDtypeStruct((total_rows, width), f32),
            jax.ShapeDtypeStruct(exchanged.shape, f32),
            jax.ShapeDtypeStruct(small.shape, f32),
        ),
        in_specs=[hbm] * (len(grads) + 1) + [vmem],
        out_specs=(hbm, hbm, vmem),
        scratch_shapes=[
            pltpu.VMEM((2, chips, rows, width), f32),
            pltpu.VMEM((2, chips, rows, width), f32),
            pltpu.VMEM((2, chips - 1, rows, width), f32),
            pltpu.VMEM((bits + 2, *small.shape), f32),
            pltpu.VMEM((bits + 1, *small.shape), f32),
            dma(2, chips, subs),
            dma(2, chips, subs),
            dma(2, chips, subs),
            dma(2, chips - 1, subs),
            dma(2, chips - 1, subs),
            dma(2, chips - 1, subs),
            dma(2, chips - 1, subs),
            dma(2, chips, subs),
            dma(2, chips, subs),
            dma(2, subs),
            dma(4),
            dma(4),
            dma(bits + 1),
            dma(bits + 1),
        ],
        compiler_params=pltpu.CompilerParams(
            collective_id=0, has_side_effects=True, vmem_limit_bytes=50 * 1024 * 1024
        ),
        cost_estimate=pl.CostEstimate(
            flops=3 * total_rows * width, bytes_accessed=16 * total_rows * width, transcendentals=0
        ),
    )(*grads, exchanged, small)


def body(
    tokens,
    segment,
    norm1_gain,
    w_query,
    w_key,
    w_value,
    w_gate,
    group_gain,
    group_bias,
    w_out,
    norm2_gain,
    w_mlp_gate,
    w_mlp_up,
    w_mlp_down,
    cotangent,
):
    length = tokens.shape[0]
    local_heads = w_query.shape[1] // KD
    inputs = tokens.astype(jnp.float32)
    normed_in_f, norm_first_pull = jax.vjp(rms_norm, inputs, norm1_gain.astype(jnp.float32))
    normed_in = normed_in_f.astype(jnp.bfloat16)
    queries = rotate(project(normed_in, w_query).reshape(length, local_heads, KD), 1.0).astype(
        jnp.bfloat16
    )
    keys_rot = (
        rotate(project(normed_in, w_key).reshape(length, local_heads, KD), 1.0) * KD ** (-0.5)
    ).astype(jnp.bfloat16)
    values_low = project(normed_in, w_value).astype(jnp.bfloat16).reshape(length, local_heads, VD)
    gate_raw = project(normed_in, w_gate)
    decays = decay_rows(segment, lax.axis_index("tensor") * local_heads, local_heads)
    raw_scores = jnp.einsum("nhk,mhk->hnm", queries, keys_rot, preferred_element_type=jnp.float32)
    scores = (raw_scores * decays).astype(jnp.bfloat16)
    retained = jnp.einsum("hnm,mhv->nhv", scores, values_low, preferred_element_type=jnp.float32)
    gated_f, gate_pull = jax.vjp(
        gate_norm,
        retained,
        gate_raw,
        group_gain.astype(jnp.float32),
        group_bias.astype(jnp.float32),
    )
    gated_out = gated_f.astype(jnp.bfloat16)
    middle = inputs + lax.psum(project(gated_out, w_out), "tensor")
    normed_mid_f, norm_second_pull = jax.vjp(rms_norm, middle, norm2_gain.astype(jnp.float32))
    normed_mid = normed_mid_f.astype(jnp.bfloat16)
    gate_proj = project(normed_mid, w_mlp_gate)
    up_proj = project(normed_mid, w_mlp_up)
    hidden_f, glu_pull = jax.vjp(gelu_glu, gate_proj, up_proj)
    hidden = hidden_f.astype(jnp.bfloat16)
    own_rows = length // lax.axis_size("tensor")
    mlp_rows = lax.psum_scatter(
        project(hidden, w_mlp_down), "tensor", scatter_dimension=0, tiled=True
    )
    middle_rows = lax.dynamic_slice_in_dim(middle, lax.axis_index("tensor") * own_rows, own_rows, 0)
    output = (middle_rows + mlp_rows).astype(jnp.bfloat16)
    grad_gate_proj, grad_up_proj = glu_pull(outer_cols(cotangent, w_mlp_down))
    grad_gate_low = grad_gate_proj.astype(jnp.bfloat16)
    grad_up_low = grad_up_proj.astype(jnp.bfloat16)
    grad_normed_mid = lax.psum(
        outer_cols(grad_gate_low, w_mlp_gate) + outer_cols(grad_up_low, w_mlp_up), "tensor"
    )
    grad_middle_part, grad_norm2_gain = norm_second_pull(grad_normed_mid)
    grad_middle = cotangent.astype(jnp.float32) + grad_middle_part
    grad_branch = grad_middle.astype(jnp.bfloat16)
    grad_retained, grad_gate_raw, grad_group_gain, grad_group_bias = gate_pull(
        outer_cols(grad_branch, w_out)
    )
    grad_gate_bf = grad_gate_raw.astype(jnp.bfloat16)
    grad_ret_low = grad_retained.astype(jnp.bfloat16)
    grad_scores = jnp.einsum(
        "nhv,mhv->hnm", grad_ret_low, values_low, preferred_element_type=jnp.float32
    )
    grad_values = jnp.einsum(
        "hnm,nhv->mhv", scores, grad_ret_low, preferred_element_type=jnp.float32
    )
    grad_raw = (grad_scores * decays).astype(jnp.bfloat16)
    grad_queries = jnp.einsum(
        "hnm,mhk->nhk", grad_raw, keys_rot, preferred_element_type=jnp.float32
    )
    grad_keys = jnp.einsum("hnm,nhk->mhk", grad_raw, queries, preferred_element_type=jnp.float32)
    grad_query_low = rotate(grad_queries, -1.0).astype(jnp.bfloat16).reshape(length, -1)
    grad_key_low = (rotate(grad_keys, -1.0) * KD ** (-0.5)).astype(jnp.bfloat16).reshape(length, -1)
    grad_value_low = grad_values.astype(jnp.bfloat16).reshape(length, -1)
    partial_in = (
        outer_cols(grad_query_low, w_query)
        + outer_cols(grad_key_low, w_key)
        + outer_cols(grad_value_low, w_value)
        + outer_cols(grad_gate_bf, w_gate)
    )
    _, grad_norm1_gain = norm_first_pull(partial_in)

    units = w_value.shape[1]
    padded = -(-units // LANE) * LANE

    def widen(array):
        return jnp.pad(array, ((0, 0), (0, padded - units)))

    key_width = w_query.shape[1]
    grads = (
        inner_rows(
            normed_in,
            jnp.concatenate(
                [grad_query_low, grad_key_low, widen(grad_value_low), widen(grad_gate_bf)], axis=1
            ),
        ),
        inner_rows(grad_branch, widen(gated_out)),
        inner_rows(
            normed_mid, jnp.concatenate([widen(grad_gate_low), widen(grad_up_low)], axis=1)
        ),
        inner_rows(cotangent, widen(hidden)),
    )
    depth = tokens.shape[1]
    small = jnp.stack(
        [
            grad_norm1_gain,
            grad_norm2_gain,
            jnp.pad(grad_group_gain, (0, depth - units)),
            jnp.pad(grad_group_bias, (0, depth - units)),
        ]
    )
    small = jnp.pad(small, ((0, 4), (0, 0)))
    reduced, received, small = reduce_all(grads, partial_in, small)
    grad_input_part, _ = norm_first_pull(partial_in + received)
    grad_tokens = (grad_middle + grad_input_part).astype(jnp.bfloat16)
    starts = [0, key_width]
    for _ in range(6):
        starts.append((2 * key_width if len(starts) == 2 else starts[-1] + padded))
    parts = []
    for position, start in enumerate(starts):
        parts.append(reduced[:, start : start + (key_width if position < 2 else units)])
    (
        grad_w_query,
        grad_w_key,
        grad_w_value,
        grad_w_gate,
        grad_w_out,
        grad_w_mlp_gate,
        grad_w_mlp_up,
        grad_w_mlp_down,
    ) = parts
    return (
        output,
        grad_tokens,
        small[0],
        grad_w_query,
        grad_w_key,
        grad_w_value,
        grad_w_gate,
        small[2, :units],
        small[3, :units],
        grad_w_out.T,
        small[1],
        grad_w_mlp_gate,
        grad_w_mlp_up,
        grad_w_mlp_down.T,
    )


def solution(mesh):
    placed = (
        P("dp", None),
        P("dp"),
        P(),
        P(None, "tensor"),
        P(None, "tensor"),
        P(None, "tensor"),
        P(None, "tensor"),
        P("tensor"),
        P("tensor"),
        P("tensor", None),
        P(),
        P(None, "tensor"),
        P(None, "tensor"),
        P("tensor", None),
        P("dp", None),
    )
    return jax.shard_map(
        body,
        mesh=mesh,
        in_specs=placed,
        out_specs=(
            P(("dp", "tensor"), None),
            P("dp", None),
            P(),
            P(None, "tensor"),
            P(None, "tensor"),
            P(None, "tensor"),
            P(None, "tensor"),
            P("tensor"),
            P("tensor"),
            P("tensor", None),
            P(),
            P(None, "tensor"),
            P(None, "tensor"),
            P("tensor", None),
        ),
        check_vma=False,
    )
```

```python
import functools

import jax
import jax.numpy as jnp
from jax import lax
from jax.experimental import pallas as pl
from jax.experimental.pallas import tpu as pltpu
from jax.sharding import PartitionSpec as P

KD = 256
VD = 432
LANE = 128
MESH = pl.DeviceIdType.MESH


EPSILON = 1e-06
GROUP_EPSILON = 0.25


def ring_place(chip, chips):
    line = chips // 2
    x = chip % 2
    z = chip // 2
    return z + x * (chips - 1 - 2 * z), line


def ring_chip(place, chips):
    line = chips // 2
    x = place // line
    z = place + x * (chips - 1 - 2 * place)
    return z * 2 + x


def bit_partner(index, bit):
    step = 1 << bit
    return index + (1 - 2 * ((index // step) % 2)) * step


def reduce_kernel(chips, quarters, groups, *refs):
    count = len(quarters)
    grads = refs[:count]
    h_ref, s_ref = refs[count : count + 2]
    outs = refs[count + 2 : 2 * count + 2]
    (hr_ref, so_ref, own, sib, rcv, sacc, sbuf) = refs[2 * count + 2 : 2 * count + 9]
    (own_sem, sbs_sem, sbr_sem, rss_sem, rsr_sem, ags_sem, agr_sem, cgs_sem, cgr_sem, loc_sem, hs_sem, hr_sem, ss_sem, sr_sem) = refs[
        2 * count + 9 :
    ]
    index = lax.axis_index("dp")
    tensor = lax.axis_index("tensor")
    core = index % 2
    place, _ = ring_place(index // 2, chips)
    bits = (2 * chips).bit_length() - 1
    nexts = [
        ring_chip((place + 1) % chips, chips) * 2 + core,
        ring_chip((place + chips - 1) % chips, chips) * 2 + core,
    ]
    virtual = [place, (chips - place) % chips]
    sibling = index + 1 - 2 * core
    offsets = [sum(quarters[:i]) for i in range(count)]
    columns = own.shape[3]

    def at_dp(device):
        return {"dp": device}

    barrier = pltpu.get_barrier_semaphore()
    greeted = [at_dp(nexts[0]), at_dp(nexts[1]), {"tensor": 1 - tensor}]
    greeted += [at_dp(bit_partner(index, bit)) for bit in range(bits)]
    for device in greeted:
        pl.semaphore_signal(barrier, inc=1, device_id=device, device_id_type=MESH)
    pl.semaphore_wait(barrier, len(greeted))

    def window(which, d, chunk, i):
        rows = quarters[i]
        return (
            pl.ds(pl.multiple_of((which * 2 + d) * rows, 8), rows),
            pl.ds(pl.multiple_of(chunk * columns, LANE), columns),
        )

    def packed(i):
        return pl.ds(offsets[i], quarters[i])

    def span(group):
        first, last = groups[group][0], groups[group][-1]
        return pl.ds(offsets[first], offsets[last] + quarters[last] - offsets[first])

    def chunk_at(d, order):
        return (virtual[d] + 2 * chips - 1 - order) % chips

    def remote(source, target, send, recv, device):
        return pltpu.make_async_remote_copy(
            source, target, send, recv, device_id=device, device_id_type=MESH
        )

    def wait_bytes(sem, group):
        whole = own.at[0, 0, span(group), :]
        pltpu.make_async_copy(whole, whole, sem).wait()

    def load(d, order, group):
        chunk = chunk_at(d, order)
        for i in groups[group]:
            pltpu.make_async_copy(
                grads[i].at[window(core, d, chunk, i)],
                own.at[d, order, packed(i), :],
                own_sem.at[d, order, group],
            ).start()
            remote(
                grads[i].at[window(1 - core, d, chunk, i)],
                sib.at[d, order, packed(i), :],
                sbs_sem.at[d, order, group],
                sbr_sem.at[d, order, group],
                at_dp(sibling),
            ).start()

    def rs_copy(d, step, group):
        return remote(
            own.at[d, step, span(group), :],
            rcv.at[d, step, span(group), :],
            rss_sem.at[d, step, group],
            rsr_sem.at[d, step, group],
            at_dp(nexts[d]),
        )

    def spread(d, step, group, first=False, ring=True):
        chunk = (virtual[d] + chips - step) % chips
        for i in groups[group]:
            part = outs[i].at[window(core, d, chunk, i)]
            source = own.at[d, chips - 1, packed(i), :] if first else part
            if ring:
                remote(
                    source, part, ags_sem.at[d, step, group], agr_sem.at[d, step, group], at_dp(nexts[d])
                ).start()
            remote(
                source, part, cgs_sem.at[d, step, group], cgr_sem.at[d, step, group], at_dp(sibling)
            ).start()
            if first:
                pltpu.make_async_copy(source, part, loc_sem.at[d, group]).start()

    pieces = [(d, group) for group in range(len(groups)) for d in range(2)]

    def load_step(order, carry):
        for d, group in pieces:
            load(d, order, group)
        return carry

    load_step(0, 0)
    exchange = h_ref.shape[0] // 4

    def h_copy(part):
        where = pl.ds(pl.multiple_of(part * exchange, 8), exchange)
        return remote(
            h_ref.at[where, :], hr_ref.at[where, :], hs_sem.at[part], hr_sem.at[part], {"tensor": 1 - tensor}
        )

    for part in range(4):
        h_copy(part).start()
    lax.fori_loop(1, chips, load_step, 0)

    def s_copy(level):
        target = {"tensor": 1 - tensor} if level == 0 else at_dp(bit_partner(index, level - 1))
        return remote(sacc.at[level], sbuf.at[level], ss_sem.at[level], sr_sem.at[level], target)

    def s_finish(level):
        s_copy(level).wait()
        got = sbuf[level]
        if level == 0:
            first = lax.broadcasted_iota(jnp.int32, got.shape, 0) == 0
            got = jnp.where(first, got, 0.0)
        sacc[level + 1] = sacc[level] + got

    sacc[0] = s_ref[...]

    def small_step(step):
        for level in range(bits + 2):

            @pl.when(step == level)
            def _():
                if level > 0:
                    s_finish(level - 1)
                if level <= bits:
                    s_copy(level).start()

    def total(d, step, group, first=False):
        wait_bytes(own_sem.at[d, step, group], group)
        wait_bytes(sbr_sem.at[d, step, group], group)
        part = span(group)
        value = own[d, step, part, :] + sib[d, step, part, :]
        if not first:
            rs_copy(d, step - 1, group).wait_recv()
            value = value + rcv[d, step - 1, part, :]
        own[d, step, part, :] = value

    for d, group in pieces:
        total(d, 0, group, True)
        rs_copy(d, 0, group).start()
    small_step(0)

    def rs_step(step, carry):
        for d, group in pieces:
            total(d, step, group)
            rs_copy(d, step, group).start()
        small_step(step)
        return carry

    lax.fori_loop(1, chips - 1, rs_step, 0)
    for d, group in pieces:
        total(d, chips - 1, group)
        spread(d, 0, group, first=True)

    def ag_step(step, carry):
        for d, group in pieces:
            wait_bytes(agr_sem.at[d, step, group], group)
            spread(d, step + 1, group)
        return carry

    lax.fori_loop(0, chips - 2, ag_step, 0)
    for d, group in pieces:
        wait_bytes(agr_sem.at[d, chips - 2, group], group)
        spread(d, chips - 1, group, ring=False)

    so_ref[...] = sacc[bits + 1]

    def drain(step, carry):
        for d, group in pieces:
            wait_bytes(sbs_sem.at[d, step, group], group)
            wait_bytes(cgs_sem.at[d, step, group], group)
            wait_bytes(cgr_sem.at[d, step, group], group)
        return carry

    lax.fori_loop(0, chips, drain, 0)

    def drain_ring(step, carry):
        for d, group in pieces:
            rs_copy(d, step, group).wait_send()
            wait_bytes(ags_sem.at[d, step, group], group)
        return carry

    lax.fori_loop(0, chips - 1, drain_ring, 0)
    for d, group in pieces:
        wait_bytes(loc_sem.at[d, group], group)
    for part in range(4):
        h_copy(part).wait()


def reduce_all(grads, groups, exchanged, small):
    chips = lax.axis_size("dp") // 2
    columns = grads[0].shape[1] // chips
    if columns % LANE:
        return (
            lax.psum(tuple(grads), "dp"),
            lax.ppermute(exchanged, "tensor", [(0, 1), (1, 0)]),
            lax.psum(small.at[0].set(lax.psum(small[0], "tensor")), "dp"),
        )
    quarters = tuple(g.shape[0] // 4 for g in grads)
    rows = sum(quarters)
    bits = (2 * chips).bit_length() - 1
    parts = len(groups)
    dma = lambda *shape: pltpu.SemaphoreType.DMA(shape)
    hbm = pl.BlockSpec(memory_space=pl.ANY)
    vmem = pl.BlockSpec(memory_space=pltpu.VMEM)
    f32 = jnp.float32
    size = 4 * rows * grads[0].shape[1]
    results = pl.pallas_call(
        functools.partial(reduce_kernel, chips, quarters, groups),
        out_shape=tuple(jax.ShapeDtypeStruct(g.shape, f32) for g in grads)
        + (
            jax.ShapeDtypeStruct(exchanged.shape, f32),
            jax.ShapeDtypeStruct(small.shape, f32),
        ),
        in_specs=[hbm] * (len(grads) + 1) + [vmem],
        out_specs=(hbm,) * (len(grads) + 1) + (vmem,),
        scratch_shapes=[
            pltpu.VMEM((2, chips, rows, columns), f32),
            pltpu.VMEM((2, chips, rows, columns), f32),
            pltpu.VMEM((2, chips - 1, rows, columns), f32),
            pltpu.VMEM((bits + 2, *small.shape), f32),
            pltpu.VMEM((bits + 1, *small.shape), f32),
            dma(2, chips, parts),
            dma(2, chips, parts),
            dma(2, chips, parts),
            dma(2, chips - 1, parts),
            dma(2, chips - 1, parts),
            dma(2, chips - 1, parts),
            dma(2, chips - 1, parts),
            dma(2, chips, parts),
            dma(2, chips, parts),
            dma(2, parts),
            dma(4),
            dma(4),
            dma(bits + 1),
            dma(bits + 1),
        ],
        compiler_params=pltpu.CompilerParams(
            collective_id=0, has_side_effects=True, vmem_limit_bytes=50 * 1024 * 1024
        ),
        cost_estimate=pl.CostEstimate(flops=size, bytes_accessed=4 * size, transcendentals=0),
    )(*grads, exchanged, small)
    return results[: len(grads)], results[-2], results[-1]


BLOCKS = 4


def dot(left, right, left_dim, right_dim):
    return lax.dot_general(
        left, right, (((left_dim,), (right_dim,)), ((), ())), preferred_element_type=jnp.float32
    )


def low(array):
    return array.astype(jnp.bfloat16)


def turn(vectors, cosine, sine):
    half = vectors.shape[1] // 2
    lower, upper = vectors[:, :half], vectors[:, half:]
    return jnp.concatenate([lower * cosine - upper * sine, upper * cosine + lower * sine], axis=1)


def swap(array):
    return lax.ppermute(array, "tensor", [(0, 1), (1, 0)])


def other_half(arrays, zero):
    dp, index = lax.axis_size("dp"), lax.axis_index("dp")
    rows = arrays[0].shape[0]
    count = len(arrays)
    if dp % count == 0 and rows % (8 * (dp // count)) == 0:
        share = rows * count // dp
        each = dp // count
        inside = (index % each) * share
        own = [lax.dynamic_slice_in_dim(a, inside, share, 0) for a in arrays]
        part = own[0]
        for number in range(1, count):
            part = jnp.where(index // each == number, own[number], part)
    else:
        share = -(-rows * count // (8 * dp)) * 8
        whole = jnp.concatenate(arrays, axis=0)
        whole = jnp.pad(whole, ((0, share * dp - rows * count), (0, 0)))
        part = lax.dynamic_slice_in_dim(whole, index * share, share, 0)
    got = lax.all_gather(swap(part.astype(jnp.float32)), "dp", axis=0, tiled=True)
    got = low(got + zero)
    return [got[number * rows : (number + 1) * rows] for number in range(count)]


def body(
    tokens,
    segment,
    norm1_gain,
    w_query,
    w_key,
    w_value,
    w_gate,
    group_gain,
    group_bias,
    w_out,
    norm2_gain,
    w_mlp_gate,
    w_mlp_up,
    w_mlp_down,
    cotangent,
):
    length, depth = tokens.shape
    heads = w_query.shape[1] // KD
    block = length // BLOCKS
    tensor = lax.axis_index("tensor")
    f32 = jnp.float32
    zero = jnp.minimum(segment[0], 0).astype(f32)
    value_t, gate_t, mg_t, mu_t = w_value.T, w_gate.T, w_mlp_gate.T, w_mlp_up.T
    mg_o, mu_o, md_o, wo_o = other_half([mg_t, mu_t, w_mlp_down, w_out], zero)
    x = tokens.astype(f32)
    gain1 = norm1_gain.astype(f32)
    gain2 = norm2_gain.astype(f32)
    ggain = group_gain.astype(f32)[:, None]
    gbias = group_bias.astype(f32)[:, None]
    r1 = lax.rsqrt(jnp.mean(x * x, axis=1, keepdims=True) + EPSILON)
    h1 = low(x * r1 * gain1)
    half = KD // 2
    frequency = jnp.exp(-jnp.log(10000.0) * jnp.arange(half, dtype=f32) / half)
    angles = jnp.arange(length, dtype=f32)[:, None] * frequency[None, :]
    cosine, sine = jnp.cos(angles), jnp.sin(angles)
    positions = jnp.arange(length, dtype=jnp.int32)
    visible = (positions[:, None] >= positions[None, :]) & (segment[:, None] == segment[None, :])
    offsets = jnp.maximum(positions[:, None] - positions[None, :], 0).astype(f32)

    def decay(head, rows, columns):
        order = (tensor * heads + head).astype(f32)
        rate = jnp.log1p(-jnp.exp2(-5.0 - order))
        return jnp.where(visible[rows, columns], jnp.exp(offsets[rows, columns] * rate), 0.0)

    queries = [[] for _ in range(heads)]
    keys = [[] for _ in range(heads)]
    values = [[] for _ in range(heads)]
    gates = [[] for _ in range(heads)]
    nhats = [[] for _ in range(heads)]
    spreads = [[] for _ in range(heads)]
    gated_blocks, received = [], []
    for number in range(BLOCKS):
        rows = slice(number * block, (number + 1) * block)
        seen = slice(0, (number + 1) * block)
        own = []
        for head in range(heads):
            wide = slice(head * KD, (head + 1) * KD)
            tall = slice(head * VD, (head + 1) * VD)
            q = low(turn(dot(h1[rows], w_query[:, wide], 1, 0), cosine[rows], sine[rows]))
            k = turn(dot(h1[rows], w_key[:, wide], 1, 0), cosine[rows], sine[rows])
            queries[head].append(q)
            keys[head].append(low(k * KD ** (-0.5)))
            values[head].append(low(dot(value_t[tall], h1[rows], 1, 1)))
            g = dot(gate_t[tall], h1[rows], 1, 1)
            gates[head].append(g)
            scores = dot(q, jnp.concatenate(keys[head], axis=0), 1, 1)
            scores = low(scores * decay(head, rows, seen))
            ret = dot(jnp.concatenate(values[head], axis=1), scores, 1, 1)
            centred = ret - jnp.mean(ret, axis=0, keepdims=True)
            scale = lax.rsqrt(jnp.mean(centred * centred, axis=0, keepdims=True) + GROUP_EPSILON)
            nhat = centred * scale
            nhats[head].append(nhat)
            spreads[head].append(scale)
            own.append(low(jax.nn.silu(g) * (nhat * ggain[tall] + gbias[tall])))
        gated_blocks.append(jnp.concatenate(own, axis=0))
        received.append(low(swap(gated_blocks[-1].astype(f32)) + zero))

    mids, h2s, r2s, hidden_own, hidden_oth, das, dbs, dmids = [], [], [], [], [], [], [], []
    norm2_rows = []
    for number in range(BLOCKS):
        rows = slice(number * block, (number + 1) * block)
        mid = x[rows] + (dot(gated_blocks[number], w_out, 0, 0) + dot(received[number], wo_o, 0, 0))
        r2 = lax.rsqrt(jnp.mean(mid * mid, axis=1, keepdims=True) + EPSILON)
        h2 = low(mid * r2 * gain2)
        cot = cotangent[rows]

        def mlp(gate_w, up_w, down_w):
            a, b = dot(gate_w, h2, 1, 1), dot(up_w, h2, 1, 1)
            hidden, pull = jax.vjp(lambda s, t: jax.nn.gelu(s) * t, a, b)
            da, db = pull(dot(down_w, cot, 1, 1))
            da, db = low(da), low(db)
            return low(hidden), da, db, dot(da, gate_w, 0, 0) + dot(db, up_w, 0, 0)

        own_hidden, da, db, part = mlp(mg_t, mu_t, w_mlp_down)
        oth_hidden, _, _, more = mlp(mg_o, mu_o, md_o)
        dh2 = part + more
        e = dh2 * gain2
        dmid = cot.astype(f32) + r2 * e - mid * (r2 * r2 * r2) * jnp.mean(e * mid, axis=1, keepdims=True)
        norm2_rows.append(jnp.sum(dh2 * mid * r2, axis=0))
        for where, value in zip(
            (mids, h2s, hidden_own, hidden_oth, das, dbs, dmids),
            (mid, h2, own_hidden, oth_hidden, da, db, dmid),
        ):
            where.append(value)
    grad_norm2 = sum(norm2_rows)
    mid = jnp.concatenate(mids, axis=0)
    h2 = jnp.concatenate(h2s, axis=0)
    hidden = jnp.concatenate(hidden_own, axis=1)
    hidden_o = jnp.concatenate(hidden_oth, axis=1)
    dmid = jnp.concatenate(dmids, axis=0)
    own_rows = length // lax.axis_size("tensor")
    place = tensor * own_rows
    output = low(
        lax.dynamic_slice_in_dim(mid, place, own_rows, 0)
        + dot(lax.dynamic_slice_in_dim(hidden, place, own_rows, 1), w_mlp_down, 0, 0)
        + dot(lax.dynamic_slice_in_dim(hidden_o, place, own_rows, 1), md_o, 0, 0)
    )
    grad_mg = dot(jnp.concatenate(das, axis=1), h2, 1, 0)
    grad_mu = dot(jnp.concatenate(dbs, axis=1), h2, 1, 0)
    grad_md = dot(hidden, cotangent, 1, 0)

    branch = low(dmid)
    gated = jnp.concatenate(gated_blocks, axis=1)
    grad_out = dot(gated, branch, 1, 0)
    dgated = dot(w_out, branch, 1, 1)
    dqs, dks, dvs, dgs, ggains, gbiases = [], [], [], [], [], []
    everything = slice(0, length)
    for head in range(heads):
        tall = slice(head * VD, (head + 1) * VD)
        g = jnp.concatenate(gates[head], axis=1)
        nhat = jnp.concatenate(nhats[head], axis=1)
        spread = jnp.concatenate(spreads[head], axis=1)
        q = jnp.concatenate(queries[head], axis=0)
        k = jnp.concatenate(keys[head], axis=0)
        v = jnp.concatenate(values[head], axis=1)
        sigmoid = jax.nn.sigmoid(g)
        silu = g * sigmoid
        up = dgated[tall]
        dgn = up * silu
        ggains.append(jnp.sum(dgn * nhat, axis=1))
        gbiases.append(jnp.sum(dgn, axis=1))
        f = dgn * ggain[tall]
        dret = (
            f - jnp.mean(f, axis=0, keepdims=True) - nhat * jnp.mean(f * nhat, axis=0, keepdims=True)
        ) * spread
        dret = low(dret)
        gn = nhat * ggain[tall] + gbias[tall]
        dgs.append(low(up * gn * (sigmoid + silu * (1.0 - sigmoid))))
        table = decay(head, everything, everything)
        scores = low(dot(q, k, 1, 1) * table)
        draw = low(dot(dret, v, 0, 0) * table)
        dvs.append(low(dot(dret, scores, 1, 0)))
        dqs.append(low(turn(dot(draw, k, 1, 0), cosine, -sine)))
        dks.append(low(turn(dot(draw, q, 0, 0), cosine, -sine) * KD ** (-0.5)))
    dv = jnp.concatenate(dvs, axis=0)
    dg = jnp.concatenate(dgs, axis=0)
    dq = jnp.concatenate(dqs, axis=1)
    dk = jnp.concatenate(dks, axis=1)
    partial_in = dot(dq, w_query, 1, 1) + dot(dk, w_key, 1, 1) + dot(dv, value_t, 0, 0) + dot(dg, gate_t, 0, 0)
    grad_norm1 = jnp.sum(partial_in * x * r1, axis=0)
    grad_qk = dot(h1, jnp.concatenate([dq, dk], axis=1), 0, 0)
    grad_v = dot(dv, h1, 1, 0)
    grad_g = dot(dg, h1, 1, 0)

    units = w_value.shape[1]
    small = jnp.stack(
        [
            grad_norm1,
            grad_norm2,
            jnp.pad(jnp.concatenate(ggains), (0, depth - units)),
            jnp.pad(jnp.concatenate(gbiases), (0, depth - units)),
        ]
    )
    small = jnp.pad(small, ((0, 4), (0, 0)))
    grads, peer, small = reduce_all(
        (grad_qk, grad_v, grad_g, grad_out, grad_mg, grad_mu, grad_md),
        ((0, 1, 2), (3, 4, 5, 6)),
        partial_in,
        small,
    )
    grad_qk, grad_v, grad_g, grad_out, grad_mg, grad_mu, grad_md = grads
    e1 = (partial_in + peer) * gain1
    grad_tokens = low(dmid + r1 * e1 - x * (r1 * r1 * r1) * jnp.mean(e1 * x, axis=1, keepdims=True))
    key_width = w_query.shape[1]
    return (
        output,
        grad_tokens,
        small[0],
        grad_qk[:, :key_width],
        grad_qk[:, key_width:],
        grad_v.T,
        grad_g.T,
        small[2, :units],
        small[3, :units],
        grad_out,
        small[1],
        grad_mg.T,
        grad_mu.T,
        grad_md,
    )


def solution(mesh):
    placed = (
        P("dp", None),
        P("dp"),
        P(),
        P(None, "tensor"),
        P(None, "tensor"),
        P(None, "tensor"),
        P(None, "tensor"),
        P("tensor"),
        P("tensor"),
        P("tensor", None),
        P(),
        P(None, "tensor"),
        P(None, "tensor"),
        P("tensor", None),
        P("dp", None),
    )
    return jax.shard_map(
        body,
        mesh=mesh,
        in_specs=placed,
        out_specs=(
            P(("dp", "tensor"), None),
            P("dp", None),
            P(),
            P(None, "tensor"),
            P(None, "tensor"),
            P(None, "tensor"),
            P(None, "tensor"),
            P("tensor"),
            P("tensor"),
            P("tensor", None),
            P(),
            P(None, "tensor"),
            P(None, "tensor"),
            P("tensor", None),
        ),
        check_vma=False,
    )
```

```python
import functools
import math

import jax
import jax.numpy as jnp
from jax import lax
from jax.experimental import pallas as pl
from jax.experimental.pallas import tpu as pltpu
from jax.sharding import PartitionSpec as P

KD = 256
VD = 432
LANE = 128
MESH = pl.DeviceIdType.MESH
VMEM_LIMIT = 63 * 1024 * 1024


EPSILON = 1e-06
GROUP_EPSILON = 0.25


def ring_place(chip, chips):
    line = chips // 2
    x = chip % 2
    z = chip // 2
    return z + x * (chips - 1 - 2 * z), line


def ring_chip(place, chips):
    line = chips // 2
    x = place // line
    z = place + x * (chips - 1 - 2 * place)
    return z * 2 + x


def bit_partner(index, bit):
    step = 1 << bit
    return index + (1 - 2 * ((index // step) % 2)) * step


def reduce_kernel(chips, quarters, groups, *refs):
    count = len(quarters)
    grads = refs[:count]
    h_ref, s_ref = refs[count : count + 2]
    outs = refs[count + 2 : 2 * count + 2]
    (hr_ref, so_ref, own, sib, rcv, sacc, sbuf) = refs[2 * count + 2 : 2 * count + 9]
    (own_sem, sbs_sem, sbr_sem, rss_sem, rsr_sem, ags_sem, agr_sem, cgs_sem, cgr_sem, loc_sem, hs_sem, hr_sem, ss_sem, sr_sem) = refs[
        2 * count + 9 :
    ]
    index = lax.axis_index("dp")
    tensor = lax.axis_index("tensor")
    core = index % 2
    place, _ = ring_place(index // 2, chips)
    bits = (2 * chips).bit_length() - 1
    nexts = [
        ring_chip((place + 1) % chips, chips) * 2 + core,
        ring_chip((place + chips - 1) % chips, chips) * 2 + core,
    ]
    virtual = [place, (chips - place) % chips]
    sibling = index + 1 - 2 * core
    offsets = [sum(quarters[:i]) for i in range(count)]
    columns = own.shape[3]

    def at_dp(device):
        return {"dp": device}

    barrier = pltpu.get_barrier_semaphore()
    greeted = [at_dp(nexts[0]), at_dp(nexts[1]), {"tensor": 1 - tensor}]
    greeted += [at_dp(bit_partner(index, bit)) for bit in range(bits)]
    for device in greeted:
        pl.semaphore_signal(barrier, inc=1, device_id=device, device_id_type=MESH)
    pl.semaphore_wait(barrier, len(greeted))

    def window(which, d, chunk, i):
        rows = quarters[i]
        return (
            pl.ds(pl.multiple_of((which * 2 + d) * rows, 8), rows),
            pl.ds(pl.multiple_of(chunk * columns, LANE), columns),
        )

    def packed(i):
        return pl.ds(offsets[i], quarters[i])

    def span(group):
        first, last = groups[group][0], groups[group][-1]
        return pl.ds(offsets[first], offsets[last] + quarters[last] - offsets[first])

    def chunk_at(d, order):
        return (virtual[d] + 2 * chips - 1 - order) % chips

    def remote(source, target, send, recv, device):
        return pltpu.make_async_remote_copy(
            source, target, send, recv, device_id=device, device_id_type=MESH
        )

    def wait_bytes(sem, group):
        whole = own.at[0, 0, span(group), :]
        pltpu.make_async_copy(whole, whole, sem).wait()

    def load(d, order, group):
        chunk = chunk_at(d, order)
        for i in groups[group]:
            pltpu.make_async_copy(
                grads[i].at[window(core, d, chunk, i)],
                own.at[d, order, packed(i), :],
                own_sem.at[d, order, group],
            ).start()
            remote(
                grads[i].at[window(1 - core, d, chunk, i)],
                sib.at[d, order, packed(i), :],
                sbs_sem.at[d, order, group],
                sbr_sem.at[d, order, group],
                at_dp(sibling),
            ).start()

    def rs_copy(d, step, group):
        return remote(
            own.at[d, step, span(group), :],
            rcv.at[d, step, span(group), :],
            rss_sem.at[d, step, group],
            rsr_sem.at[d, step, group],
            at_dp(nexts[d]),
        )

    def spread(d, step, group, first=False, ring=True):
        chunk = (virtual[d] + chips - step) % chips
        for i in groups[group]:
            part = outs[i].at[window(core, d, chunk, i)]
            source = own.at[d, chips - 1, packed(i), :] if first else part
            if ring:
                remote(
                    source, part, ags_sem.at[d, step, group], agr_sem.at[d, step, group], at_dp(nexts[d])
                ).start()
            remote(
                source, part, cgs_sem.at[d, step, group], cgr_sem.at[d, step, group], at_dp(sibling)
            ).start()
            if first:
                pltpu.make_async_copy(source, part, loc_sem.at[d, group]).start()

    pieces = [(d, group) for group in range(len(groups)) for d in range(2)]

    def load_step(order, carry):
        for d, group in pieces:
            load(d, order, group)
        return carry

    load_step(0, 0)
    exchange = h_ref.shape[0] // 4

    def h_copy(part):
        where = pl.ds(pl.multiple_of(part * exchange, 8), exchange)
        return remote(
            h_ref.at[where, :], hr_ref.at[where, :], hs_sem.at[part], hr_sem.at[part], {"tensor": 1 - tensor}
        )

    for part in range(4):
        h_copy(part).start()
    lax.fori_loop(1, chips, load_step, 0)

    def s_copy(level):
        target = {"tensor": 1 - tensor} if level == 0 else at_dp(bit_partner(index, level - 1))
        return remote(sacc.at[level], sbuf.at[level], ss_sem.at[level], sr_sem.at[level], target)

    def s_finish(level):
        s_copy(level).wait()
        got = sbuf[level]
        if level == 0:
            first = lax.broadcasted_iota(jnp.int32, got.shape, 0) == 0
            got = jnp.where(first, got, 0.0)
        sacc[level + 1] = sacc[level] + got

    sacc[0] = s_ref[...]

    def small_step(step):
        for level in range(bits + 2):

            @pl.when(step == level)
            def _():
                if level > 0:
                    s_finish(level - 1)
                if level <= bits:
                    s_copy(level).start()

    def total(d, step, group, first=False):
        wait_bytes(own_sem.at[d, step, group], group)
        wait_bytes(sbr_sem.at[d, step, group], group)
        part = span(group)
        value = own[d, step, part, :] + sib[d, step, part, :]
        if not first:
            rs_copy(d, step - 1, group).wait_recv()
            value = value + rcv[d, step - 1, part, :]
        own[d, step, part, :] = value

    for d, group in pieces:
        total(d, 0, group, True)
        rs_copy(d, 0, group).start()
    small_step(0)

    def rs_step(step, carry):
        for d, group in pieces:
            total(d, step, group)
            rs_copy(d, step, group).start()
        small_step(step)
        return carry

    lax.fori_loop(1, chips - 1, rs_step, 0)
    for d, group in pieces:
        total(d, chips - 1, group)
        spread(d, 0, group, first=True)

    def ag_step(step, carry):
        for d, group in pieces:
            wait_bytes(agr_sem.at[d, step, group], group)
            spread(d, step + 1, group)
        return carry

    lax.fori_loop(0, chips - 2, ag_step, 0)
    for d, group in pieces:
        wait_bytes(agr_sem.at[d, chips - 2, group], group)
        spread(d, chips - 1, group, ring=False)

    so_ref[...] = sacc[bits + 1]

    def drain(step, carry):
        for d, group in pieces:
            wait_bytes(sbs_sem.at[d, step, group], group)
            wait_bytes(cgs_sem.at[d, step, group], group)
            wait_bytes(cgr_sem.at[d, step, group], group)
        return carry

    lax.fori_loop(0, chips, drain, 0)

    def drain_ring(step, carry):
        for d, group in pieces:
            rs_copy(d, step, group).wait_send()
            wait_bytes(ags_sem.at[d, step, group], group)
        return carry

    lax.fori_loop(0, chips - 1, drain_ring, 0)
    for d, group in pieces:
        wait_bytes(loc_sem.at[d, group], group)
    for part in range(4):
        h_copy(part).wait()


def reduce_all(grads, groups, exchanged, small):
    chips = lax.axis_size("dp") // 2
    columns = grads[0].shape[1] // chips
    if columns % LANE:
        return (
            lax.psum(tuple(grads), "dp"),
            lax.ppermute(exchanged, "tensor", [(0, 1), (1, 0)]),
            lax.psum(small.at[0].set(lax.psum(small[0], "tensor")), "dp"),
        )
    quarters = tuple(g.shape[0] // 4 for g in grads)
    rows = sum(quarters)
    bits = (2 * chips).bit_length() - 1
    parts = len(groups)
    dma = lambda *shape: pltpu.SemaphoreType.DMA(shape)
    hbm = pl.BlockSpec(memory_space=pl.ANY)
    vmem = pl.BlockSpec(memory_space=pltpu.VMEM)
    f32 = jnp.float32
    size = 4 * rows * grads[0].shape[1]
    results = pl.pallas_call(
        functools.partial(reduce_kernel, chips, quarters, groups),
        out_shape=tuple(jax.ShapeDtypeStruct(g.shape, f32) for g in grads)
        + (
            jax.ShapeDtypeStruct(exchanged.shape, f32),
            jax.ShapeDtypeStruct(small.shape, f32),
        ),
        in_specs=[hbm] * (len(grads) + 1) + [vmem],
        out_specs=(hbm,) * (len(grads) + 1) + (vmem,),
        scratch_shapes=[
            pltpu.VMEM((2, chips, rows, columns), f32),
            pltpu.VMEM((2, chips, rows, columns), f32),
            pltpu.VMEM((2, chips - 1, rows, columns), f32),
            pltpu.VMEM((bits + 2, *small.shape), f32),
            pltpu.VMEM((bits + 1, *small.shape), f32),
            dma(2, chips, parts),
            dma(2, chips, parts),
            dma(2, chips, parts),
            dma(2, chips - 1, parts),
            dma(2, chips - 1, parts),
            dma(2, chips - 1, parts),
            dma(2, chips - 1, parts),
            dma(2, chips, parts),
            dma(2, chips, parts),
            dma(2, parts),
            dma(4),
            dma(4),
            dma(bits + 1),
            dma(bits + 1),
        ],
        compiler_params=pltpu.CompilerParams(
            collective_id=0, has_side_effects=True, vmem_limit_bytes=50 * 1024 * 1024
        ),
        cost_estimate=pl.CostEstimate(flops=size, bytes_accessed=4 * size, transcendentals=0),
    )(*grads, exchanged, small)
    return results[: len(grads)], results[-2], results[-1]


BLOCKS = 4
GELU_A = math.sqrt(2.0 / math.pi)
GELU_B = 0.044715


def dot(left, right, left_dim, right_dim):
    return lax.dot_general(
        left, right, (((left_dim,), (right_dim,)), ((), ())), preferred_element_type=jnp.float32
    )


def low(array):
    return array.astype(jnp.bfloat16)


def turn(vectors, cosine, sine):
    half = vectors.shape[1] // 2
    lower, upper = vectors[:, :half], vectors[:, half:]
    return jnp.concatenate([lower * cosine - upper * sine, upper * cosine + lower * sine], axis=1)


def remote(source, target, send, recv, device):
    return pltpu.make_async_remote_copy(
        source, target, send, recv, device_id=device, device_id_type=MESH
    )


def greet(devices):
    barrier = pltpu.get_barrier_semaphore()
    for device in devices:
        pl.semaphore_signal(barrier, inc=1, device_id=device, device_id_type=MESH)
    pl.semaphore_wait(barrier, len(devices))


def forward_kernel(
    chips,
    x_ref,
    segc_ref,
    segr_ref,
    gain1_ref,
    gain2_ref,
    ggain_ref,
    gbias_ref,
    cos_ref,
    sin_ref,
    table_ref,
    power_ref,
    wq_hbm,
    wk_hbm,
    wv_hbm,
    wg_hbm,
    wo_ref,
    mg_ref,
    mu_ref,
    md_ref,
    cot_ref,
    h1_out,
    q_out,
    k_out,
    v_out,
    g_out,
    nh_out,
    rstd_out,
    gated_out,
    dmid_out,
    branch_out,
    grad_mg_out,
    grad_mu_out,
    grad_md_out,
    norm2_out,
    output_out,
    gath_out,
    weights,
    others,
    cot,
    h1,
    q,
    k,
    v,
    g,
    nh,
    rstd,
    gated,
    acc,
    gsend,
    grecv,
    h2,
    hid,
    da,
    db,
    stage,
    mid,
    dh_own,
    dh_oth,
    out_sum,
    branch,
    in_sem,
    out_sem,
    stage_sem,
    block_sem,
    xs_sem,
    xr_sem,
    ys_sem,
    yr_sem,
    gs_sem,
    gr_sem,
    cs_sem,
    cr_sem,
):
    index, tensor = lax.axis_index("dp"), lax.axis_index("tensor")
    core = index % 2
    place, _ = ring_place(index // 2, chips)
    nexts = [
        {"dp": ring_chip((place + 1) % chips, chips) * 2 + core},
        {"dp": ring_chip((place + chips - 1) % chips, chips) * 2 + core},
    ]
    sibling, peer = {"dp": index + 1 - 2 * core}, {"tensor": 1 - tensor}
    heads = q.shape[0]
    units = h1.shape[1] and v.shape[0]
    block = h1.shape[0] // BLOCKS
    f32 = jnp.float32

    wv_ref, wg_ref = hid, da
    key_width = wq_hbm.shape[1]
    early = [
        pltpu.make_async_copy(wq_hbm, h2.at[:, pl.ds(0, key_width)], in_sem.at[5]),
        pltpu.make_async_copy(wk_hbm, h2.at[:, pl.ds(key_width, key_width)], in_sem.at[6]),
        pltpu.make_async_copy(wv_hbm, wv_ref, in_sem.at[7]),
        pltpu.make_async_copy(wg_hbm, wg_ref, in_sem.at[8]),
    ]
    for copy in early:
        copy.start()
    for number, source in enumerate((wo_ref, mg_ref, mu_ref, md_ref)):
        pltpu.make_async_copy(source, weights.at[number], in_sem.at[number]).start()
    pltpu.make_async_copy(cot_ref, cot, in_sem.at[4]).start()
    greet([*nexts, sibling, peer])

    rows_slice = units // 2
    half_slice = rows_slice // 2

    def area(w, where, which, half=None):
        start = which * rows_slice + (0 if half is None else half * half_slice)
        size = rows_slice if half is None else half_slice
        return gath_out.at[
            w,
            pl.ds(pl.multiple_of(start, 8), size),
            pl.ds(pl.multiple_of(where * LANE, LANE), LANE),
        ]

    def slice_spot(w):
        return gsend.at[
            BLOCKS - 1,
            pl.ds((w % 2) * rows_slice, rows_slice),
            pl.ds((w // 2) * LANE, LANE),
        ]

    def y_copy(w):
        return remote(slice_spot(w), area(w, place, core), ys_sem.at[w], yr_sem.at[w], peer)

    def hop(w, d, t):
        where = (place - t + chips) % chips if d == 0 else (place + t) % chips
        part = area(w, where, core, d if t == chips // 2 - 1 else None)
        return remote(part, part, gs_sem.at[w, d, t], gr_sem.at[w, d, t], nexts[d])

    def arrived(w, d, t):
        where = (place - t - 1 + chips) % chips if d == 0 else (place + t + 1) % chips
        part = area(w, where, core, d if t == chips // 2 - 1 else None)
        pltpu.make_async_copy(part, part, gr_sem.at[w, d, t]).wait()
        return where

    def share(w, slot, where, half=None):
        part = area(w, where, core, half)
        remote(part, part, cs_sem.at[w, slot], cr_sem.at[w, slot], sibling).start()

    steps = chips // 2

    def begin(w):
        y_copy(w).wait_recv()
        for d in range(2):
            hop(w, d, 0).start()
        share(w, 0, place)

    def pump(w, t):
        for d in range(2):
            where = arrived(w, d, t)
            if t < steps - 1:
                hop(w, d, t + 1).start()
            share(w, 1 + 2 * t + d, where, d if t == steps - 1 else None)

    for number in range(4):
        pltpu.make_async_copy(wo_ref, weights.at[number], in_sem.at[number]).wait()
        slice_spot(number)[...] = weights[
            number,
            pl.ds(pl.multiple_of(core * rows_slice, 16), rows_slice),
            pl.ds(pl.multiple_of(place * LANE, LANE), LANE),
        ].astype(f32)
        y_copy(number).start()

    def exchange(i):
        return remote(gsend.at[i], grecv.at[i], xs_sem.at[i], xr_sem.at[i], peer)

    ahead = lax.broadcasted_iota(jnp.int32, (block, block), 0) - lax.broadcasted_iota(
        jnp.int32, (block, block), 1
    )

    def attention(i, carry):
        rows = pl.ds(pl.multiple_of(i * block, block), block)
        xb = x_ref[rows, :].astype(f32)
        r1 = lax.rsqrt(jnp.mean(xb * xb, axis=1, keepdims=True) + EPSILON)
        h1[rows, :] = low(xb * r1 * gain1_ref[...])
        cosine, sine = cos_ref[rows, :], sin_ref[rows, :]
        for head in range(heads):
            wide = slice(head * KD, (head + 1) * KD)
            q[head, rows, :] = low(turn(dot(h1[rows, :], h2[:, wide], 1, 0), cosine, sine))
            k[head, rows, :] = low(
                turn(dot(h1[rows, :], h2[:, key_width + head * KD : key_width + (head + 1) * KD], 1, 0), cosine, sine) * KD ** (-0.5)
            )
        v[:, rows] = low(dot(wv_ref[...], h1[rows, :], 1, 1))

        @pl.when(i == BLOCKS - 1)
        def _():
            for w in range(4):
                y_copy(w).wait_send()

        segc = segc_ref[rows, :]
        for head in range(heads):
            tall = slice(head * VD, (head + 1) * VD)
            acc[...] = jnp.zeros_like(acc)

            def tile(m, carry):
                cols = pl.ds(pl.multiple_of(m * block, block), block)
                s = dot(q[head, rows, :], k[head, cols, :], 1, 1)
                seen = (segc == segr_ref[:, cols]) & (ahead + (i - m) * block >= 0)
                s = jnp.where(seen, s * (table_ref[head] * power_ref[head, i - m]), 0.0)
                acc[...] += dot(v[tall, cols], low(s), 1, 1)
                return carry

            lax.fori_loop(0, i + 1, tile, 0)
            ret = acc[...]
            centred = ret - jnp.mean(ret, axis=0, keepdims=True)
            scale = lax.rsqrt(jnp.mean(centred * centred, axis=0, keepdims=True) + GROUP_EPSILON)
            nhat = centred * scale
            nh[tall, rows] = low(nhat)
            rstd[head : head + 1, rows] = scale
            gate = dot(wg_ref[tall, :], h1[rows, :], 1, 1)
            g[tall, rows] = low(gate)
            gn = nhat * ggain_ref[tall, :] + gbias_ref[tall, :]
            out = low(gate / (1.0 + jnp.exp(-gate)) * gn)
            gated[tall, rows] = out
            gsend[i, tall, :] = out.astype(f32)
        exchange(i).start()

        @pl.when(i == 0)
        def _():
            begin(0)

        @pl.when(i == 1)
        def _():
            pump(0, 0)
            for w in range(1, 4):
                begin(w)

        @pl.when(i == 2)
        def _():
            pump(0, 1)

        return carry

    rstd[...] = jnp.zeros_like(rstd)
    for copy in early:
        copy.wait()
    lax.fori_loop(0, BLOCKS, attention, 0)
    saved = [(h1, h1_out), (q, q_out), (k, k_out), (v, v_out), (g, g_out), (nh, nh_out), (rstd, rstd_out), (gated, gated_out)]
    for number, (source, target) in enumerate(saved):
        pltpu.make_async_copy(source, target, out_sem.at[number]).start()
    pump(0, 2)
    for t in range(3):
        for w in range(1, 4):
            pump(w, t)
    for w in range(4):
        pump(w, 3)

    def cast_in(w):
        for slot in range(1 + 2 * steps):
            t = (slot - 1) // 2
            d = (slot - 1) % 2
            if slot == 0:
                where = place
            else:
                where = (place - t - 1 + chips) % chips if d == 0 else (place + t + 1) % chips
            part = area(w, where, 1 - core, d if slot > 0 and t == steps - 1 else None)
            pltpu.make_async_copy(part, part, cr_sem.at[w, slot]).wait()

        def piece(n):
            where = pl.ds(n * third, third)
            return pltpu.make_async_copy(
                gath_out.at[w, where, :], stage.at[n % 2], stage_sem.at[n % 2]
            )

        piece(0).start()
        for n in range(3):
            if n < 2:
                piece(n + 1).start()
            piece(n).wait()
            others[w, n * third : (n + 1) * third, :] = low(stage[n % 2])

    third = units // 3
    for w in range(4):
        cast_in(w)

    pltpu.make_async_copy(cot_ref, cot, in_sem.at[4]).wait()
    norm2_out[...] = jnp.zeros_like(norm2_out)
    part = units // 2

    def mlp(i, carry):
        rows = pl.ds(pl.multiple_of(i * block, block), block)

        @pl.when(i > 0)
        def _():
            block_wait()

        exchange(i).wait_recv()
        mid[...] = x_ref[rows, :].astype(f32) + (
            dot(gated[:, rows], weights[0], 0, 0) + dot(low(grecv[i]), others[0], 0, 0)
        )
        r2 = lax.rsqrt(jnp.mean(mid[...] * mid[...], axis=1, keepdims=True) + EPSILON)
        h2[rows, :] = low(mid[...] * r2 * gain2_ref[...])
        mine = i // (BLOCKS // 2) == tensor

        for source, total in ((weights, dh_own), (others, dh_oth)):
            for f in range(2):
                tall = slice(f * part, (f + 1) * part)
                a = dot(source[1, tall, :], h2[rows, :], 1, 1)
                b = dot(source[2, tall, :], h2[rows, :], 1, 1)
                dhidden = dot(source[3, tall, :], cot[rows, :], 1, 1)
                square = a * a
                t = jnp.tanh(GELU_A * a * (1.0 + GELU_B * square))
                gelu = 0.5 * a * (1.0 + t)
                slope = 0.5 * (1.0 + t) + 0.5 * a * (1.0 - t * t) * (
                    GELU_A * (1.0 + 3.0 * GELU_B * square)
                )
                hidden = low(gelu * b)
                dga = low(dhidden * b * slope)
                dup = low(dhidden * gelu)
                if source is weights:
                    hid[tall, rows] = hidden
                    da[tall, rows] = dga
                    db[tall, rows] = dup
                more = dot(dga, source[1, tall, :], 0, 0) + dot(dup, source[2, tall, :], 0, 0)
                total[...] = more if f == 0 else total[...] + more

                @pl.when(mine)
                def _():
                    lift = dot(hidden, source[3, tall, :], 0, 0)
                    first = source is weights and f == 0
                    out_sum[...] = lift if first else out_sum[...] + lift

        @pl.when(mine)
        def _():
            spot = pl.ds(pl.multiple_of((i % (BLOCKS // 2)) * block, block), block)
            output_out[spot, :] = low(mid[...] + out_sum[...])

        dh2 = dh_own[...] + dh_oth[...]
        e = dh2 * gain2_ref[...]
        inner = jnp.mean(e * mid[...], axis=1, keepdims=True)
        norm2_out[0:1, :] += jnp.sum(dh2 * mid[...] * r2, axis=0, keepdims=True)
        result = cot[rows, :].astype(f32) + r2 * e - mid[...] * (r2 * r2 * r2 * inner)
        dh_own[...] = result
        branch[...] = low(result)
        pltpu.make_async_copy(dh_own, dmid_out.at[rows, :], block_sem.at[0]).start()
        pltpu.make_async_copy(branch, branch_out.at[rows, :], block_sem.at[1]).start()
        return carry

    def block_wait():
        pltpu.make_async_copy(dh_own, dh_own, block_sem.at[0]).wait()
        pltpu.make_async_copy(branch, branch, block_sem.at[1]).wait()

    lax.fori_loop(0, BLOCKS, mlp, 0)

    count = 0
    for source, right, target in ((da, h2, grad_mg_out), (db, h2, grad_mu_out), (hid, cot, grad_md_out)):
        for n in range(3):
            where = pl.ds(n * third, third)
            slot = count % 2
            if count >= 2:
                pltpu.make_async_copy(stage.at[slot], stage.at[slot], stage_sem.at[slot]).wait()
            stage[slot] = dot(source[where, :], right[...], 1, 0)
            pltpu.make_async_copy(stage.at[slot], target.at[where, :], stage_sem.at[slot]).start()
            count += 1

    for slot in range(2):
        pltpu.make_async_copy(stage.at[slot], stage.at[slot], stage_sem.at[slot]).wait()
    block_wait()
    for number, (source, target) in enumerate(saved):
        pltpu.make_async_copy(source, target, out_sem.at[number]).wait()
    for w in range(4):
        for t in range(steps):
            for d in range(2):
                hop(w, d, t).wait_send()
        for slot in range(1 + 2 * steps):
            last = slot > 0 and (slot - 1) // 2 == steps - 1
            part_ref = area(w, place, core, 0 if last else None)
            pltpu.make_async_copy(part_ref, part_ref, cs_sem.at[w, slot]).wait()
    for i in range(BLOCKS):
        exchange(i).wait_send()


def forward(tokens, segment, tables, gains, ws, cotangent):
    chips = lax.axis_size("dp") // 2
    length, depth = tokens.shape
    wq, wk, wv, wg, wo, mg, mu, md = ws
    units = wv.shape[0]
    heads = wq.shape[1] // KD
    block = length // BLOCKS
    f32, bf16 = jnp.float32, jnp.bfloat16
    vmem = pl.BlockSpec(memory_space=pltpu.VMEM)
    hbm = pl.BlockSpec(memory_space=pl.ANY)
    smem = pl.BlockSpec(memory_space=pltpu.SMEM)
    dma = lambda *shape: pltpu.SemaphoreType.DMA(shape)
    shape = jax.ShapeDtypeStruct
    tall = (units, length)
    steps = chips // 2
    outs = [
        (shape((length, depth), bf16), hbm),
        (shape((heads, length, KD), bf16), hbm),
        (shape((heads, length, KD), bf16), hbm),
        (shape(tall, bf16), hbm),
        (shape(tall, bf16), hbm),
        (shape(tall, bf16), hbm),
        (shape((8, length), f32), hbm),
        (shape(tall, bf16), hbm),
        (shape((length, depth), f32), hbm),
        (shape((length, depth), bf16), hbm),
        (shape((units, depth), f32), hbm),
        (shape((units, depth), f32), hbm),
        (shape((units, depth), f32), hbm),
        (shape((8, depth), f32), vmem),
        (shape((length // 2, depth), bf16), vmem),
        (shape((4, units, depth), f32), hbm),
    ]
    scratch = [
        pltpu.VMEM((4, units, depth), bf16),
        pltpu.VMEM((4, units, depth), bf16),
        pltpu.VMEM((length, depth), bf16),
        pltpu.VMEM((length, depth), bf16),
        pltpu.VMEM((heads, length, KD), bf16),
        pltpu.VMEM((heads, length, KD), bf16),
        pltpu.VMEM(tall, bf16),
        pltpu.VMEM(tall, bf16),
        pltpu.VMEM(tall, bf16),
        pltpu.VMEM((8, length), f32),
        pltpu.VMEM(tall, bf16),
        pltpu.VMEM((VD, block), f32),
        pltpu.VMEM((BLOCKS, units, block), f32),
        pltpu.VMEM((BLOCKS, units, block), f32),
        pltpu.VMEM((length, depth), bf16),
        pltpu.VMEM(tall, bf16),
        pltpu.VMEM(tall, bf16),
        pltpu.VMEM(tall, bf16),
        pltpu.VMEM((2, units // 3, depth), f32),
        pltpu.VMEM((block, depth), f32),
        pltpu.VMEM((block, depth), f32),
        pltpu.VMEM((block, depth), f32),
        pltpu.VMEM((block, depth), f32),
        pltpu.VMEM((block, depth), bf16),
        dma(9),
        dma(8),
        dma(2),
        dma(2),
        dma(BLOCKS),
        dma(BLOCKS),
        dma(4),
        dma(4),
        dma(4, 2, steps),
        dma(4, 2, steps),
        dma(4, 1 + 2 * steps),
        dma(4, 1 + 2 * steps),
    ]
    results = pl.pallas_call(
        functools.partial(forward_kernel, chips),
        out_shape=tuple(o for o, _ in outs),
        in_specs=[vmem] * 10 + [smem] + [hbm] * 9,
        out_specs=tuple(s for _, s in outs),
        scratch_shapes=scratch,
        compiler_params=pltpu.CompilerParams(
            collective_id=1, has_side_effects=True, vmem_limit_bytes=VMEM_LIMIT
        ),
        cost_estimate=pl.CostEstimate(
            flops=40 * length * depth * units, bytes_accessed=80 * length * depth, transcendentals=0
        ),
    )(
        tokens,
        segment[:, None],
        segment[None, :],
        gains[0],
        gains[1],
        gains[2],
        gains[3],
        tables[0],
        tables[1],
        tables[2],
        tables[3],
        wq,
        wk,
        wv,
        wg,
        wo,
        mg,
        mu,
        md,
        cotangent,
    )
    return results


def make_tables(length, heads):
    block = length // BLOCKS
    half = KD // 2
    f32 = jnp.float32
    frequency = jnp.exp(-jnp.log(10000.0) * jnp.arange(half, dtype=f32) / half)
    angles = jnp.arange(length, dtype=f32)[:, None] * frequency[None, :]
    orders = (lax.axis_index("tensor") * heads + jnp.arange(heads, dtype=jnp.int32)).astype(f32)
    rates = jnp.log1p(-jnp.exp2(-5.0 - orders))
    inside = jnp.arange(block, dtype=f32)
    table = jnp.exp((inside[:, None] - inside[None, :])[None] * rates[:, None, None])
    power = jnp.exp(jnp.arange(BLOCKS, dtype=f32)[None, :] * block * rates[:, None])
    return jnp.cos(angles), jnp.sin(angles), table, power

def swap(array):
    return lax.ppermute(array, "tensor", [(0, 1), (1, 0)])


def other_half(arrays, zero):
    dp, index = lax.axis_size("dp"), lax.axis_index("dp")
    rows = arrays[0].shape[0]
    count = len(arrays)
    if dp % count == 0 and rows % (8 * (dp // count)) == 0:
        share = rows * count // dp
        each = dp // count
        inside = (index % each) * share
        own = [lax.dynamic_slice_in_dim(a, inside, share, 0) for a in arrays]
        part = own[0]
        for number in range(1, count):
            part = jnp.where(index // each == number, own[number], part)
    else:
        share = -(-rows * count // (8 * dp)) * 8
        whole = jnp.concatenate(arrays, axis=0)
        whole = jnp.pad(whole, ((0, share * dp - rows * count), (0, 0)))
        part = lax.dynamic_slice_in_dim(whole, index * share, share, 0)
    got = lax.all_gather(swap(part.astype(jnp.float32)), "dp", axis=0, tiled=True)
    got = low(got + zero)
    return [got[number * rows : (number + 1) * rows] for number in range(count)]


def plain_body(
    tokens,
    segment,
    norm1_gain,
    w_query,
    w_key,
    w_value,
    w_gate,
    group_gain,
    group_bias,
    w_out,
    norm2_gain,
    w_mlp_gate,
    w_mlp_up,
    w_mlp_down,
    cotangent,
):
    length, depth = tokens.shape
    heads = w_query.shape[1] // KD
    block = length // BLOCKS
    tensor = lax.axis_index("tensor")
    f32 = jnp.float32
    zero = jnp.minimum(segment[0], 0).astype(f32)
    value_t, gate_t, mg_t, mu_t = w_value.T, w_gate.T, w_mlp_gate.T, w_mlp_up.T
    mg_o, mu_o, md_o, wo_o = other_half([mg_t, mu_t, w_mlp_down, w_out], zero)
    x = tokens.astype(f32)
    gain1 = norm1_gain.astype(f32)
    gain2 = norm2_gain.astype(f32)
    ggain = group_gain.astype(f32)[:, None]
    gbias = group_bias.astype(f32)[:, None]
    r1 = lax.rsqrt(jnp.mean(x * x, axis=1, keepdims=True) + EPSILON)
    h1 = low(x * r1 * gain1)
    half = KD // 2
    frequency = jnp.exp(-jnp.log(10000.0) * jnp.arange(half, dtype=f32) / half)
    angles = jnp.arange(length, dtype=f32)[:, None] * frequency[None, :]
    cosine, sine = jnp.cos(angles), jnp.sin(angles)
    positions = jnp.arange(length, dtype=jnp.int32)
    visible = (positions[:, None] >= positions[None, :]) & (segment[:, None] == segment[None, :])
    offsets = jnp.maximum(positions[:, None] - positions[None, :], 0).astype(f32)

    def decay(head, rows, columns):
        order = (tensor * heads + head).astype(f32)
        rate = jnp.log1p(-jnp.exp2(-5.0 - order))
        return jnp.where(visible[rows, columns], jnp.exp(offsets[rows, columns] * rate), 0.0)

    queries = [[] for _ in range(heads)]
    keys = [[] for _ in range(heads)]
    values = [[] for _ in range(heads)]
    gates = [[] for _ in range(heads)]
    nhats = [[] for _ in range(heads)]
    spreads = [[] for _ in range(heads)]
    gated_blocks, received = [], []
    for number in range(BLOCKS):
        rows = slice(number * block, (number + 1) * block)
        seen = slice(0, (number + 1) * block)
        own = []
        for head in range(heads):
            wide = slice(head * KD, (head + 1) * KD)
            tall = slice(head * VD, (head + 1) * VD)
            q = low(turn(dot(h1[rows], w_query[:, wide], 1, 0), cosine[rows], sine[rows]))
            k = turn(dot(h1[rows], w_key[:, wide], 1, 0), cosine[rows], sine[rows])
            queries[head].append(q)
            keys[head].append(low(k * KD ** (-0.5)))
            values[head].append(low(dot(value_t[tall], h1[rows], 1, 1)))
            g = dot(gate_t[tall], h1[rows], 1, 1)
            gates[head].append(g)
            scores = dot(q, jnp.concatenate(keys[head], axis=0), 1, 1)
            scores = low(scores * decay(head, rows, seen))
            ret = dot(jnp.concatenate(values[head], axis=1), scores, 1, 1)
            centred = ret - jnp.mean(ret, axis=0, keepdims=True)
            scale = lax.rsqrt(jnp.mean(centred * centred, axis=0, keepdims=True) + GROUP_EPSILON)
            nhat = centred * scale
            nhats[head].append(nhat)
            spreads[head].append(scale)
            own.append(low(jax.nn.silu(g) * (nhat * ggain[tall] + gbias[tall])))
        gated_blocks.append(jnp.concatenate(own, axis=0))
        received.append(low(swap(gated_blocks[-1].astype(f32)) + zero))

    mids, h2s, r2s, hidden_own, hidden_oth, das, dbs, dmids = [], [], [], [], [], [], [], []
    norm2_rows = []
    for number in range(BLOCKS):
        rows = slice(number * block, (number + 1) * block)
        mid = x[rows] + (dot(gated_blocks[number], w_out, 0, 0) + dot(received[number], wo_o, 0, 0))
        r2 = lax.rsqrt(jnp.mean(mid * mid, axis=1, keepdims=True) + EPSILON)
        h2 = low(mid * r2 * gain2)
        cot = cotangent[rows]

        def mlp(gate_w, up_w, down_w):
            a, b = dot(gate_w, h2, 1, 1), dot(up_w, h2, 1, 1)
            hidden, pull = jax.vjp(lambda s, t: jax.nn.gelu(s) * t, a, b)
            da, db = pull(dot(down_w, cot, 1, 1))
            da, db = low(da), low(db)
            return low(hidden), da, db, dot(da, gate_w, 0, 0) + dot(db, up_w, 0, 0)

        own_hidden, da, db, part = mlp(mg_t, mu_t, w_mlp_down)
        oth_hidden, _, _, more = mlp(mg_o, mu_o, md_o)
        dh2 = part + more
        e = dh2 * gain2
        dmid = cot.astype(f32) + r2 * e - mid * (r2 * r2 * r2) * jnp.mean(e * mid, axis=1, keepdims=True)
        norm2_rows.append(jnp.sum(dh2 * mid * r2, axis=0))
        for where, value in zip(
            (mids, h2s, hidden_own, hidden_oth, das, dbs, dmids),
            (mid, h2, own_hidden, oth_hidden, da, db, dmid),
        ):
            where.append(value)
    grad_norm2 = sum(norm2_rows)
    mid = jnp.concatenate(mids, axis=0)
    h2 = jnp.concatenate(h2s, axis=0)
    hidden = jnp.concatenate(hidden_own, axis=1)
    hidden_o = jnp.concatenate(hidden_oth, axis=1)
    dmid = jnp.concatenate(dmids, axis=0)
    own_rows = length // lax.axis_size("tensor")
    place = tensor * own_rows
    output = low(
        lax.dynamic_slice_in_dim(mid, place, own_rows, 0)
        + dot(lax.dynamic_slice_in_dim(hidden, place, own_rows, 1), w_mlp_down, 0, 0)
        + dot(lax.dynamic_slice_in_dim(hidden_o, place, own_rows, 1), md_o, 0, 0)
    )
    grad_mg = dot(jnp.concatenate(das, axis=1), h2, 1, 0)
    grad_mu = dot(jnp.concatenate(dbs, axis=1), h2, 1, 0)
    grad_md = dot(hidden, cotangent, 1, 0)

    branch = low(dmid)
    gated = jnp.concatenate(gated_blocks, axis=1)
    grad_out = dot(gated, branch, 1, 0)
    dgated = dot(w_out, branch, 1, 1)
    dqs, dks, dvs, dgs, ggains, gbiases = [], [], [], [], [], []
    everything = slice(0, length)
    for head in range(heads):
        tall = slice(head * VD, (head + 1) * VD)
        g = jnp.concatenate(gates[head], axis=1)
        nhat = jnp.concatenate(nhats[head], axis=1)
        spread = jnp.concatenate(spreads[head], axis=1)
        q = jnp.concatenate(queries[head], axis=0)
        k = jnp.concatenate(keys[head], axis=0)
        v = jnp.concatenate(values[head], axis=1)
        sigmoid = jax.nn.sigmoid(g)
        silu = g * sigmoid
        up = dgated[tall]
        dgn = up * silu
        ggains.append(jnp.sum(dgn * nhat, axis=1))
        gbiases.append(jnp.sum(dgn, axis=1))
        f = dgn * ggain[tall]
        dret = (
            f - jnp.mean(f, axis=0, keepdims=True) - nhat * jnp.mean(f * nhat, axis=0, keepdims=True)
        ) * spread
        dret = low(dret)
        gn = nhat * ggain[tall] + gbias[tall]
        dgs.append(low(up * gn * (sigmoid + silu * (1.0 - sigmoid))))
        table = decay(head, everything, everything)
        scores = low(dot(q, k, 1, 1) * table)
        draw = low(dot(dret, v, 0, 0) * table)
        dvs.append(low(dot(dret, scores, 1, 0)))
        dqs.append(low(turn(dot(draw, k, 1, 0), cosine, -sine)))
        dks.append(low(turn(dot(draw, q, 0, 0), cosine, -sine) * KD ** (-0.5)))
    dv = jnp.concatenate(dvs, axis=0)
    dg = jnp.concatenate(dgs, axis=0)
    dq = jnp.concatenate(dqs, axis=1)
    dk = jnp.concatenate(dks, axis=1)
    partial_in = dot(dq, w_query, 1, 1) + dot(dk, w_key, 1, 1) + dot(dv, value_t, 0, 0) + dot(dg, gate_t, 0, 0)
    grad_norm1 = jnp.sum(partial_in * x * r1, axis=0)
    grad_qk = dot(h1, jnp.concatenate([dq, dk], axis=1), 0, 0)
    grad_v = dot(dv, h1, 1, 0)
    grad_g = dot(dg, h1, 1, 0)

    units = w_value.shape[1]
    small = jnp.stack(
        [
            grad_norm1,
            grad_norm2,
            jnp.pad(jnp.concatenate(ggains), (0, depth - units)),
            jnp.pad(jnp.concatenate(gbiases), (0, depth - units)),
        ]
    )
    small = jnp.pad(small, ((0, 4), (0, 0)))
    grads, peer, small = reduce_all(
        (grad_qk, grad_v, grad_g, grad_out, grad_mg, grad_mu, grad_md),
        ((0, 1, 2), (3, 4, 5, 6)),
        partial_in,
        small,
    )
    grad_qk, grad_v, grad_g, grad_out, grad_mg, grad_mu, grad_md = grads
    e1 = (partial_in + peer) * gain1
    grad_tokens = low(dmid + r1 * e1 - x * (r1 * r1 * r1) * jnp.mean(e1 * x, axis=1, keepdims=True))
    key_width = w_query.shape[1]
    return (
        output,
        grad_tokens,
        small[0],
        grad_qk[:, :key_width],
        grad_qk[:, key_width:],
        grad_v.T,
        grad_g.T,
        small[2, :units],
        small[3, :units],
        grad_out,
        small[1],
        grad_mg.T,
        grad_mu.T,
        grad_md,
    )


def body(
    tokens,
    segment,
    norm1_gain,
    w_query,
    w_key,
    w_value,
    w_gate,
    group_gain,
    group_bias,
    w_out,
    norm2_gain,
    w_mlp_gate,
    w_mlp_up,
    w_mlp_down,
    cotangent,
):
    length, depth = tokens.shape
    if depth % (LANE * (lax.axis_size("dp") // 2)):
        return plain_body(
            tokens, segment, norm1_gain, w_query, w_key, w_value, w_gate, group_gain, group_bias, w_out,
            norm2_gain, w_mlp_gate, w_mlp_up, w_mlp_down, cotangent,
        )
    heads = w_query.shape[1] // KD
    f32 = jnp.float32
    value_t, gate_t, mg_t, mu_t = w_value.T, w_gate.T, w_mlp_gate.T, w_mlp_up.T
    gain1 = norm1_gain.astype(f32)
    ggain = group_gain.astype(f32)[:, None]
    gbias = group_bias.astype(f32)[:, None]
    tables = make_tables(length, heads)
    (h1, qs, ks, vs, g, nhat, rstd, gated, dmid, branch, grad_mg, grad_mu, grad_md, norm2, output, _) = forward(
        tokens,
        segment,
        tables,
        (gain1[None, :], norm2_gain.astype(f32)[None, :], ggain, gbias),
        (w_query, w_key, value_t, gate_t, w_out, mg_t, mu_t, w_mlp_down),
        cotangent,
    )
    cosine, sine = tables[:2]
    positions = jnp.arange(length, dtype=jnp.int32)
    visible = (positions[:, None] >= positions[None, :]) & (segment[:, None] == segment[None, :])
    offsets = jnp.maximum(positions[:, None] - positions[None, :], 0).astype(f32)
    x = tokens.astype(f32)
    r1 = lax.rsqrt(jnp.mean(x * x, axis=1, keepdims=True) + EPSILON)
    g = g.astype(f32)
    nhat = nhat.astype(f32)
    grad_out = dot(gated, branch, 1, 0)
    dgated = dot(w_out, branch, 1, 1)
    dqs, dks, dvs, dgs, ggains, gbiases = [], [], [], [], [], []
    for head in range(heads):
        tall = slice(head * VD, (head + 1) * VD)
        order = (lax.axis_index("tensor") * heads + head).astype(f32)
        rate = jnp.log1p(-jnp.exp2(-5.0 - order))
        table = jnp.where(visible, jnp.exp(offsets * rate), 0.0)
        sigmoid = jax.nn.sigmoid(g[tall])
        silu = g[tall] * sigmoid
        up = dgated[tall]
        dgn = up * silu
        ggains.append(jnp.sum(dgn * nhat[tall], axis=1))
        gbiases.append(jnp.sum(dgn, axis=1))
        f = dgn * ggain[tall]
        dret = low(
            (f - jnp.mean(f, axis=0, keepdims=True) - nhat[tall] * jnp.mean(f * nhat[tall], axis=0, keepdims=True))
            * rstd[head : head + 1]
        )
        gn = nhat[tall] * ggain[tall] + gbias[tall]
        dgs.append(low(up * gn * (sigmoid + silu * (1.0 - sigmoid))))
        scores = low(dot(qs[head], ks[head], 1, 1) * table)
        draw = low(dot(dret, vs[tall], 0, 0) * table)
        dvs.append(low(dot(dret, scores, 1, 0)))
        dqs.append(low(turn(dot(draw, ks[head], 1, 0), cosine, -sine)))
        dks.append(low(turn(dot(draw, qs[head], 0, 0), cosine, -sine) * KD ** (-0.5)))
    dv = jnp.concatenate(dvs, axis=0)
    dg = jnp.concatenate(dgs, axis=0)
    dq = jnp.concatenate(dqs, axis=1)
    dk = jnp.concatenate(dks, axis=1)
    partial_in = dot(dq, w_query, 1, 1) + dot(dk, w_key, 1, 1) + dot(dv, value_t, 0, 0) + dot(dg, gate_t, 0, 0)
    grad_norm1 = jnp.sum(partial_in * x * r1, axis=0)
    grad_qk = dot(h1, jnp.concatenate([dq, dk], axis=1), 0, 0)
    grad_v = dot(dv, h1, 1, 0)
    grad_g = dot(dg, h1, 1, 0)

    units = w_value.shape[1]
    small = jnp.stack(
        [
            grad_norm1,
            norm2[0],
            jnp.pad(jnp.concatenate(ggains), (0, depth - units)),
            jnp.pad(jnp.concatenate(gbiases), (0, depth - units)),
        ]
    )
    small = jnp.pad(small, ((0, 4), (0, 0)))
    grads, peer, small = reduce_all(
        (grad_qk, grad_v, grad_g, grad_out, grad_mg, grad_mu, grad_md),
        ((0, 1, 2), (3, 4, 5, 6)),
        partial_in,
        small,
    )
    grad_qk, grad_v, grad_g, grad_out, grad_mg, grad_mu, grad_md = grads
    e1 = (partial_in + peer) * gain1
    grad_tokens = low(dmid + r1 * e1 - x * (r1 * r1 * r1) * jnp.mean(e1 * x, axis=1, keepdims=True))
    key_width = w_query.shape[1]
    return (
        output,
        grad_tokens,
        small[0],
        grad_qk[:, :key_width],
        grad_qk[:, key_width:],
        grad_v.T,
        grad_g.T,
        small[2, :units],
        small[3, :units],
        grad_out,
        small[1],
        grad_mg.T,
        grad_mu.T,
        grad_md,
    )


def solution(mesh):
    placed = (
        P("dp", None),
        P("dp"),
        P(),
        P(None, "tensor"),
        P(None, "tensor"),
        P(None, "tensor"),
        P(None, "tensor"),
        P("tensor"),
        P("tensor"),
        P("tensor", None),
        P(),
        P(None, "tensor"),
        P(None, "tensor"),
        P("tensor", None),
        P("dp", None),
    )
    return jax.shard_map(
        body,
        mesh=mesh,
        in_specs=placed,
        out_specs=(
            P(("dp", "tensor"), None),
            P("dp", None),
            P(),
            P(None, "tensor"),
            P(None, "tensor"),
            P(None, "tensor"),
            P(None, "tensor"),
            P("tensor"),
            P("tensor"),
            P("tensor", None),
            P(),
            P(None, "tensor"),
            P(None, "tensor"),
            P("tensor", None),
        ),
        check_vma=False,
    )
```

```python
import functools
import math

import jax
import jax.numpy as jnp
from jax import lax
from jax.experimental import pallas as pl
from jax.experimental.pallas import tpu as pltpu
from jax.sharding import PartitionSpec as P

KD = 256
VD = 432
LANE = 128
MESH = pl.DeviceIdType.MESH
VMEM_LIMIT = 63 * 1024 * 1024


EPSILON = 1e-06
GROUP_EPSILON = 0.25


def ring_place(chip, chips):
    line = chips // 2
    x = chip % 2
    z = chip // 2
    return z + x * (chips - 1 - 2 * z), line


def ring_chip(place, chips):
    line = chips // 2
    x = place // line
    z = place + x * (chips - 1 - 2 * place)
    return z * 2 + x


def bit_partner(index, bit):
    step = 1 << bit
    return index + (1 - 2 * ((index // step) % 2)) * step


BLOCKS = 4
GELU_A = math.sqrt(2.0 / math.pi)
GELU_B = 0.044715


def dot(left, right, left_dim, right_dim):
    return lax.dot_general(
        left, right, (((left_dim,), (right_dim,)), ((), ())), preferred_element_type=jnp.float32
    )


def low(array):
    return array.astype(jnp.bfloat16)


def turn(vectors, cosine, sine):
    half = vectors.shape[1] // 2
    lower, upper = vectors[:, :half], vectors[:, half:]
    return jnp.concatenate([lower * cosine - upper * sine, upper * cosine + lower * sine], axis=1)


def remote(source, target, send, recv, device):
    return pltpu.make_async_remote_copy(
        source, target, send, recv, device_id=device, device_id_type=MESH
    )


def greet(devices):
    barrier = pltpu.get_barrier_semaphore()
    for device in devices:
        pl.semaphore_signal(barrier, inc=1, device_id=device, device_id_type=MESH)
    pl.semaphore_wait(barrier, len(devices))


def forward_kernel(
    chips,
    x_ref,
    segc_ref,
    segr_ref,
    gain1_ref,
    gain2_ref,
    ggain_ref,
    gbias_ref,
    cos_ref,
    sin_ref,
    table_ref,
    power_ref,
    wq_hbm,
    wk_hbm,
    wv_hbm,
    wg_hbm,
    wo_ref,
    mg_ref,
    mu_ref,
    md_ref,
    cot_ref,
    h1_out,
    q_out,
    k_out,
    v_out,
    g_out,
    nh_out,
    rstd_out,
    gated_out,
    dmid_out,
    branch_out,
    grad_mg_out,
    grad_mu_out,
    grad_md_out,
    norm2_out,
    output_out,
    gath_out,
    weights,
    others,
    cot,
    h1,
    q,
    k,
    v,
    g,
    nh,
    rstd,
    gated,
    acc,
    gsend,
    grecv,
    h2,
    hid,
    da,
    db,
    stage,
    mid,
    dh_own,
    dh_oth,
    out_sum,
    branch,
    in_sem,
    out_sem,
    stage_sem,
    block_sem,
    xs_sem,
    xr_sem,
    ys_sem,
    yr_sem,
    gs_sem,
    gr_sem,
    cs_sem,
    cr_sem,
):
    index, tensor = lax.axis_index("dp"), lax.axis_index("tensor")
    core = index % 2
    place, _ = ring_place(index // 2, chips)
    nexts = [
        {"dp": ring_chip((place + 1) % chips, chips) * 2 + core},
        {"dp": ring_chip((place + chips - 1) % chips, chips) * 2 + core},
    ]
    sibling, peer = {"dp": index + 1 - 2 * core}, {"tensor": 1 - tensor}
    heads = q.shape[0]
    units = h1.shape[1] and v.shape[0]
    block = h1.shape[0] // BLOCKS
    f32 = jnp.float32

    wv_ref, wg_ref = hid, da
    key_width = wq_hbm.shape[1]
    early = [
        pltpu.make_async_copy(wq_hbm, h2.at[:, pl.ds(0, key_width)], in_sem.at[5]),
        pltpu.make_async_copy(wk_hbm, h2.at[:, pl.ds(key_width, key_width)], in_sem.at[6]),
        pltpu.make_async_copy(wv_hbm, wv_ref, in_sem.at[7]),
        pltpu.make_async_copy(wg_hbm, wg_ref, in_sem.at[8]),
    ]
    for copy in early:
        copy.start()
    for number, source in enumerate((wo_ref, mg_ref, mu_ref, md_ref)):
        pltpu.make_async_copy(source, weights.at[number], in_sem.at[number]).start()
    pltpu.make_async_copy(cot_ref, cot, in_sem.at[4]).start()
    greet([*nexts, sibling, peer])

    rows_slice = units // 2
    half_slice = rows_slice // 2

    def area(w, where, which, half=None):
        start = which * rows_slice + (0 if half is None else half * half_slice)
        size = rows_slice if half is None else half_slice
        return gath_out.at[
            w,
            pl.ds(pl.multiple_of(start, 8), size),
            pl.ds(pl.multiple_of(where * LANE, LANE), LANE),
        ]

    def slice_spot(w):
        return gsend.at[
            BLOCKS - 1,
            pl.ds((w % 2) * rows_slice, rows_slice),
            pl.ds((w // 2) * LANE, LANE),
        ]

    def y_copy(w):
        return remote(slice_spot(w), area(w, place, core), ys_sem.at[w], yr_sem.at[w], peer)

    def hop(w, d, t):
        where = (place - t + chips) % chips if d == 0 else (place + t) % chips
        part = area(w, where, core, d if t == chips // 2 - 1 else None)
        return remote(part, part, gs_sem.at[w, d, t], gr_sem.at[w, d, t], nexts[d])

    def arrived(w, d, t):
        where = (place - t - 1 + chips) % chips if d == 0 else (place + t + 1) % chips
        part = area(w, where, core, d if t == chips // 2 - 1 else None)
        pltpu.make_async_copy(part, part, gr_sem.at[w, d, t]).wait()
        return where

    def share(w, slot, where, half=None):
        part = area(w, where, core, half)
        remote(part, part, cs_sem.at[w, slot], cr_sem.at[w, slot], sibling).start()

    steps = chips // 2

    def begin(w):
        y_copy(w).wait_recv()
        for d in range(2):
            hop(w, d, 0).start()
        share(w, 0, place)

    def pump(w, t):
        for d in range(2):
            where = arrived(w, d, t)
            if t < steps - 1:
                hop(w, d, t + 1).start()
            share(w, 1 + 2 * t + d, where, d if t == steps - 1 else None)

    for number in range(4):
        pltpu.make_async_copy(wo_ref, weights.at[number], in_sem.at[number]).wait()
        slice_spot(number)[...] = weights[
            number,
            pl.ds(pl.multiple_of(core * rows_slice, 16), rows_slice),
            pl.ds(pl.multiple_of(place * LANE, LANE), LANE),
        ].astype(f32)
        y_copy(number).start()

    def exchange(i):
        return remote(gsend.at[i], grecv.at[i], xs_sem.at[i], xr_sem.at[i], peer)

    ahead = lax.broadcasted_iota(jnp.int32, (block, block), 0) - lax.broadcasted_iota(
        jnp.int32, (block, block), 1
    )

    def attention(i, carry):
        rows = pl.ds(pl.multiple_of(i * block, block), block)
        xb = x_ref[rows, :].astype(f32)
        r1 = lax.rsqrt(jnp.mean(xb * xb, axis=1, keepdims=True) + EPSILON)
        h1[rows, :] = low(xb * r1 * gain1_ref[...])
        cosine, sine = cos_ref[rows, :], sin_ref[rows, :]
        for head in range(heads):
            wide = slice(head * KD, (head + 1) * KD)
            q[head, rows, :] = low(turn(dot(h1[rows, :], h2[:, wide], 1, 0), cosine, sine))
            k[head, rows, :] = low(
                turn(dot(h1[rows, :], h2[:, key_width + head * KD : key_width + (head + 1) * KD], 1, 0), cosine, sine) * KD ** (-0.5)
            )
        v[:, rows] = low(dot(wv_ref[...], h1[rows, :], 1, 1))

        @pl.when(i == BLOCKS - 1)
        def _():
            for w in range(4):
                y_copy(w).wait_send()

        segc = segc_ref[rows, :]
        for head in range(heads):
            tall = slice(head * VD, (head + 1) * VD)
            acc[...] = jnp.zeros_like(acc)

            def tile(m, carry):
                cols = pl.ds(pl.multiple_of(m * block, block), block)
                s = dot(q[head, rows, :], k[head, cols, :], 1, 1)
                seen = (segc == segr_ref[:, cols]) & (ahead + (i - m) * block >= 0)
                s = jnp.where(seen, s * (table_ref[head] * power_ref[head, i - m]), 0.0)
                acc[...] += dot(v[tall, cols], low(s), 1, 1)
                return carry

            lax.fori_loop(0, i + 1, tile, 0)
            ret = acc[...]
            centred = ret - jnp.mean(ret, axis=0, keepdims=True)
            scale = lax.rsqrt(jnp.mean(centred * centred, axis=0, keepdims=True) + GROUP_EPSILON)
            nhat = centred * scale
            nh[tall, rows] = low(nhat)
            rstd[head : head + 1, rows] = scale
            gate = dot(wg_ref[tall, :], h1[rows, :], 1, 1)
            g[tall, rows] = low(gate)
            gn = nhat * ggain_ref[tall, :] + gbias_ref[tall, :]
            out = low(gate / (1.0 + jnp.exp(-gate)) * gn)
            gated[tall, rows] = out
            gsend[i, tall, :] = out.astype(f32)
        exchange(i).start()

        @pl.when(i == 0)
        def _():
            begin(0)

        @pl.when(i == 1)
        def _():
            pump(0, 0)
            for w in range(1, 4):
                begin(w)

        @pl.when(i == 2)
        def _():
            pump(0, 1)

        return carry

    rstd[...] = jnp.zeros_like(rstd)
    for copy in early:
        copy.wait()
    lax.fori_loop(0, BLOCKS, attention, 0)
    saved = [(h1, h1_out), (q, q_out), (k, k_out), (v, v_out), (g, g_out), (nh, nh_out), (rstd, rstd_out), (gated, gated_out)]
    for number, (source, target) in enumerate(saved):
        pltpu.make_async_copy(source, target, out_sem.at[number]).start()
    pump(0, 2)
    for t in range(3):
        for w in range(1, 4):
            pump(w, t)
    for w in range(4):
        pump(w, 3)

    def cast_in(w):
        for slot in range(1 + 2 * steps):
            t = (slot - 1) // 2
            d = (slot - 1) % 2
            if slot == 0:
                where = place
            else:
                where = (place - t - 1 + chips) % chips if d == 0 else (place + t + 1) % chips
            part = area(w, where, 1 - core, d if slot > 0 and t == steps - 1 else None)
            pltpu.make_async_copy(part, part, cr_sem.at[w, slot]).wait()

        def piece(n):
            where = pl.ds(n * third, third)
            return pltpu.make_async_copy(
                gath_out.at[w, where, :], stage.at[n % 2], stage_sem.at[n % 2]
            )

        piece(0).start()
        for n in range(3):
            if n < 2:
                piece(n + 1).start()
            piece(n).wait()
            others[w, n * third : (n + 1) * third, :] = low(stage[n % 2])

    third = units // 3
    for w in range(4):
        cast_in(w)

    pltpu.make_async_copy(cot_ref, cot, in_sem.at[4]).wait()
    norm2_out[...] = jnp.zeros_like(norm2_out)
    part = units // 2

    def mlp(i, carry):
        rows = pl.ds(pl.multiple_of(i * block, block), block)

        @pl.when(i > 0)
        def _():
            block_wait()

        exchange(i).wait_recv()
        mid[...] = x_ref[rows, :].astype(f32) + (
            dot(gated[:, rows], weights[0], 0, 0) + dot(low(grecv[i]), others[0], 0, 0)
        )
        r2 = lax.rsqrt(jnp.mean(mid[...] * mid[...], axis=1, keepdims=True) + EPSILON)
        h2[rows, :] = low(mid[...] * r2 * gain2_ref[...])
        mine = i // (BLOCKS // 2) == tensor

        for source, total in ((weights, dh_own), (others, dh_oth)):
            for f in range(2):
                tall = slice(f * part, (f + 1) * part)
                a = dot(source[1, tall, :], h2[rows, :], 1, 1)
                b = dot(source[2, tall, :], h2[rows, :], 1, 1)
                dhidden = dot(source[3, tall, :], cot[rows, :], 1, 1)
                square = a * a
                t = jnp.tanh(GELU_A * a * (1.0 + GELU_B * square))
                gelu = 0.5 * a * (1.0 + t)
                slope = 0.5 * (1.0 + t) + 0.5 * a * (1.0 - t * t) * (
                    GELU_A * (1.0 + 3.0 * GELU_B * square)
                )
                hidden = low(gelu * b)
                dga = low(dhidden * b * slope)
                dup = low(dhidden * gelu)
                if source is weights:
                    hid[tall, rows] = hidden
                    da[tall, rows] = dga
                    db[tall, rows] = dup
                more = dot(dga, source[1, tall, :], 0, 0) + dot(dup, source[2, tall, :], 0, 0)
                total[...] = more if f == 0 else total[...] + more

                @pl.when(mine)
                def _():
                    lift = dot(hidden, source[3, tall, :], 0, 0)
                    first = source is weights and f == 0
                    out_sum[...] = lift if first else out_sum[...] + lift

        @pl.when(mine)
        def _():
            spot = pl.ds(pl.multiple_of((i % (BLOCKS // 2)) * block, block), block)
            output_out[spot, :] = low(mid[...] + out_sum[...])

        dh2 = dh_own[...] + dh_oth[...]
        e = dh2 * gain2_ref[...]
        inner = jnp.mean(e * mid[...], axis=1, keepdims=True)
        norm2_out[0:1, :] += jnp.sum(dh2 * mid[...] * r2, axis=0, keepdims=True)
        result = cot[rows, :].astype(f32) + r2 * e - mid[...] * (r2 * r2 * r2 * inner)
        dh_own[...] = result
        branch[...] = low(result)
        pltpu.make_async_copy(dh_own, dmid_out.at[rows, :], block_sem.at[0]).start()
        pltpu.make_async_copy(branch, branch_out.at[rows, :], block_sem.at[1]).start()
        return carry

    def block_wait():
        pltpu.make_async_copy(dh_own, dh_own, block_sem.at[0]).wait()
        pltpu.make_async_copy(branch, branch, block_sem.at[1]).wait()

    lax.fori_loop(0, BLOCKS, mlp, 0)

    count = 0
    for source, right, target in ((da, h2, grad_mg_out), (db, h2, grad_mu_out), (hid, cot, grad_md_out)):
        for n in range(3):
            where = pl.ds(n * third, third)
            slot = count % 2
            if count >= 2:
                pltpu.make_async_copy(stage.at[slot], stage.at[slot], stage_sem.at[slot]).wait()
            stage[slot] = dot(source[where, :], right[...], 1, 0)
            pltpu.make_async_copy(stage.at[slot], target.at[where, :], stage_sem.at[slot]).start()
            count += 1

    for slot in range(2):
        pltpu.make_async_copy(stage.at[slot], stage.at[slot], stage_sem.at[slot]).wait()
    block_wait()
    for number, (source, target) in enumerate(saved):
        pltpu.make_async_copy(source, target, out_sem.at[number]).wait()
    for w in range(4):
        for t in range(steps):
            for d in range(2):
                hop(w, d, t).wait_send()
        for slot in range(1 + 2 * steps):
            last = slot > 0 and (slot - 1) // 2 == steps - 1
            part_ref = area(w, place, core, 0 if last else None)
            pltpu.make_async_copy(part_ref, part_ref, cs_sem.at[w, slot]).wait()
    for i in range(BLOCKS):
        exchange(i).wait_send()


def forward(tokens, segment, tables, gains, ws, cotangent):
    chips = lax.axis_size("dp") // 2
    length, depth = tokens.shape
    wq, wk, wv, wg, wo, mg, mu, md = ws
    units = wv.shape[0]
    heads = wq.shape[1] // KD
    block = length // BLOCKS
    f32, bf16 = jnp.float32, jnp.bfloat16
    vmem = pl.BlockSpec(memory_space=pltpu.VMEM)
    hbm = pl.BlockSpec(memory_space=pl.ANY)
    smem = pl.BlockSpec(memory_space=pltpu.SMEM)
    dma = lambda *shape: pltpu.SemaphoreType.DMA(shape)
    shape = jax.ShapeDtypeStruct
    tall = (units, length)
    steps = chips // 2
    outs = [
        (shape((length, depth), bf16), hbm),
        (shape((heads, length, KD), bf16), hbm),
        (shape((heads, length, KD), bf16), hbm),
        (shape(tall, bf16), hbm),
        (shape(tall, bf16), hbm),
        (shape(tall, bf16), hbm),
        (shape((8, length), f32), hbm),
        (shape(tall, bf16), hbm),
        (shape((length, depth), f32), hbm),
        (shape((length, depth), bf16), hbm),
        (shape((units, depth), f32), hbm),
        (shape((units, depth), f32), hbm),
        (shape((units, depth), f32), hbm),
        (shape((8, depth), f32), vmem),
        (shape((length // 2, depth), bf16), vmem),
        (shape((4, units, depth), f32), hbm),
    ]
    scratch = [
        pltpu.VMEM((4, units, depth), bf16),
        pltpu.VMEM((4, units, depth), bf16),
        pltpu.VMEM((length, depth), bf16),
        pltpu.VMEM((length, depth), bf16),
        pltpu.VMEM((heads, length, KD), bf16),
        pltpu.VMEM((heads, length, KD), bf16),
        pltpu.VMEM(tall, bf16),
        pltpu.VMEM(tall, bf16),
        pltpu.VMEM(tall, bf16),
        pltpu.VMEM((8, length), f32),
        pltpu.VMEM(tall, bf16),
        pltpu.VMEM((VD, block), f32),
        pltpu.VMEM((BLOCKS, units, block), f32),
        pltpu.VMEM((BLOCKS, units, block), f32),
        pltpu.VMEM((length, depth), bf16),
        pltpu.VMEM(tall, bf16),
        pltpu.VMEM(tall, bf16),
        pltpu.VMEM(tall, bf16),
        pltpu.VMEM((2, units // 3, depth), f32),
        pltpu.VMEM((block, depth), f32),
        pltpu.VMEM((block, depth), f32),
        pltpu.VMEM((block, depth), f32),
        pltpu.VMEM((block, depth), f32),
        pltpu.VMEM((block, depth), bf16),
        dma(9),
        dma(8),
        dma(2),
        dma(2),
        dma(BLOCKS),
        dma(BLOCKS),
        dma(4),
        dma(4),
        dma(4, 2, steps),
        dma(4, 2, steps),
        dma(4, 1 + 2 * steps),
        dma(4, 1 + 2 * steps),
    ]
    results = pl.pallas_call(
        functools.partial(forward_kernel, chips),
        out_shape=tuple(o for o, _ in outs),
        in_specs=[vmem] * 10 + [smem] + [hbm] * 9,
        out_specs=tuple(s for _, s in outs),
        scratch_shapes=scratch,
        compiler_params=pltpu.CompilerParams(
            collective_id=1, has_side_effects=True, vmem_limit_bytes=VMEM_LIMIT
        ),
        cost_estimate=pl.CostEstimate(
            flops=40 * length * depth * units, bytes_accessed=80 * length * depth, transcendentals=0
        ),
    )(
        tokens,
        segment[:, None],
        segment[None, :],
        gains[0],
        gains[1],
        gains[2],
        gains[3],
        tables[0],
        tables[1],
        tables[2],
        tables[3],
        wq,
        wk,
        wv,
        wg,
        wo,
        mg,
        mu,
        md,
        cotangent,
    )
    return results


def make_tables(length, heads):
    block = length // BLOCKS
    half = KD // 2
    f32 = jnp.float32
    frequency = jnp.exp(-jnp.log(10000.0) * jnp.arange(half, dtype=f32) / half)
    angles = jnp.arange(length, dtype=f32)[:, None] * frequency[None, :]
    orders = (lax.axis_index("tensor") * heads + jnp.arange(heads, dtype=jnp.int32)).astype(f32)
    rates = jnp.log1p(-jnp.exp2(-5.0 - orders))
    inside = jnp.arange(block, dtype=f32)
    table = jnp.exp((inside[:, None] - inside[None, :])[None] * rates[:, None, None])
    power = jnp.exp(jnp.arange(BLOCKS, dtype=f32)[None, :] * block * rates[:, None])
    return jnp.cos(angles), jnp.sin(angles), table, power


class Ring:
    def __init__(self, chips, quarters, own, sib, rcv, own_sem, sbs_sem, sbr_sem, rss_sem, rsr_sem):
        self.chips, self.quarters = chips, quarters
        self.index, self.tensor = lax.axis_index("dp"), lax.axis_index("tensor")
        self.core = self.index % 2
        place, _ = ring_place(self.index // 2, chips)
        self.place = place
        self.nexts = [
            {"dp": ring_chip((place + 1) % chips, chips) * 2 + self.core},
            {"dp": ring_chip((place + chips - 1) % chips, chips) * 2 + self.core},
        ]
        self.virtual = [place, (chips - place) % chips]
        self.sibling = {"dp": self.index + 1 - 2 * self.core}
        self.peer = {"tensor": 1 - self.tensor}
        self.offsets = [sum(quarters[:i]) for i in range(len(quarters))]
        self.own, self.sib, self.rcv = own, sib, rcv
        self.own_sem, self.sbs_sem, self.sbr_sem = own_sem, sbs_sem, sbr_sem
        self.rss_sem, self.rsr_sem = rss_sem, rsr_sem
        self.tokens = [(d, a) for a in range(len(quarters)) for d in range(2)]

    def window(self, which, d, chunk, rows):
        return (
            pl.ds(pl.multiple_of((which * 2 + d) * rows, 8), rows),
            pl.ds(pl.multiple_of(chunk * LANE, LANE), LANE),
        )

    def packed(self, a):
        return pl.ds(self.offsets[a], self.quarters[a])

    def chunk_at(self, d, order):
        return (self.virtual[d] + 2 * self.chips - 1 - order) % self.chips

    def own_copy(self, grads, d, a, order):
        return pltpu.make_async_copy(
            grads[a].at[self.window(self.core, d, self.chunk_at(d, order), self.quarters[a])],
            self.own.at[d, order, self.packed(a), :],
            self.own_sem.at[d, a, order],
        )

    def sib_copy(self, grads, d, a, order):
        return remote(
            grads[a].at[self.window(1 - self.core, d, self.chunk_at(d, order), self.quarters[a])],
            self.sib.at[d, order, self.packed(a), :],
            self.sbs_sem.at[d, a, order],
            self.sbr_sem.at[d, a, order],
            self.sibling,
        )

    def load(self, grads, order):
        for d, a in self.tokens:
            self.own_copy(grads, d, a, order).start()
            self.sib_copy(grads, d, a, order).start()

    def rs_copy(self, d, a, step):
        return remote(
            self.own.at[d, step, self.packed(a), :],
            self.rcv.at[d, step, self.packed(a), :],
            self.rss_sem.at[d, a, step],
            self.rsr_sem.at[d, a, step],
            self.nexts[d],
        )

    def total(self, grads, d, a, step, first=False):
        self.own_copy(grads, d, a, step).wait()
        self.sib_copy(grads, d, a, step).wait_recv()
        part = self.packed(a)
        value = self.own[d, step, part, :] + self.sib[d, step, part, :]
        if not first:
            self.rs_copy(d, a, step - 1).wait_recv()
            value = value + self.rcv[d, step - 1, part, :]
        self.own[d, step, part, :] = value

    def pump(self, grads, step, first=False):
        for d, a in self.tokens:
            self.total(grads, d, a, step, first)
            self.rs_copy(d, a, step).start()

    def drain(self, grads):
        def ring_step(step, carry):
            for d, a in self.tokens:
                self.rs_copy(d, a, step).wait_send()
            return carry

        def pair_step(order, carry):
            for d, a in self.tokens:
                self.sib_copy(grads, d, a, order).wait_send()
            return carry

        lax.fori_loop(0, self.chips - 1, ring_step, 0)
        lax.fori_loop(0, self.chips, pair_step, 0)


class Spread:
    def __init__(self, ring, quarters, outs, ags_sem, agr_sem, cgs_sem, cgr_sem, loc_sem):
        self.ring, self.quarters, self.outs = ring, quarters, outs
        self.ags_sem, self.agr_sem, self.cgs_sem, self.cgr_sem, self.loc_sem = (
            ags_sem, agr_sem, cgs_sem, cgr_sem, loc_sem,
        )
        self.tokens = [(d, a) for a in range(len(quarters)) for d in range(2)]

    def part(self, which, d, a, step):
        ring = self.ring
        chunk = (ring.virtual[d] + 2 * ring.chips - step) % ring.chips
        return self.outs[a].at[ring.window(which, d, chunk, self.quarters[a])]

    def ring_copy(self, d, a, step, source=None):
        part = self.part(self.ring.core, d, a, step)
        return remote(
            part if source is None else source,
            part,
            self.ags_sem.at[d, a, step],
            self.agr_sem.at[d, a, step],
            self.ring.nexts[d],
        )

    def pair_copy(self, d, a, step, source=None):
        part = self.part(self.ring.core, d, a, step)
        return remote(
            part if source is None else source,
            part,
            self.cgs_sem.at[d, a, step],
            self.cgr_sem.at[d, a, step],
            self.ring.sibling,
        )

    def begin(self, d, a, source):
        self.ring_copy(d, a, 0, source).start()
        self.pair_copy(d, a, 0, source).start()
        pltpu.make_async_copy(source, self.part(self.ring.core, d, a, 0), self.loc_sem.at[d, a]).start()

    def arrived(self, d, a, step):
        part = self.part(self.ring.core, d, a, step + 1)
        pltpu.make_async_copy(part, part, self.agr_sem.at[d, a, step]).wait()

    def pump(self, step, last=False):
        for d, a in self.tokens:
            self.arrived(d, a, step)
            if not last:
                self.ring_copy(d, a, step + 1).start()
            self.pair_copy(d, a, step + 1).start()

    def drain(self):
        chips = self.ring.chips

        def ring_step(step, carry):
            for d, a in self.tokens:
                self.ring_copy(d, a, step).wait_send()
            return carry

        def pair_step(step, carry):
            for d, a in self.tokens:
                self.pair_copy(d, a, step).wait()
            return carry

        lax.fori_loop(0, chips - 1, ring_step, 0)
        lax.fori_loop(0, chips, pair_step, 0)
        for d, a in self.tokens:
            part = self.part(self.ring.core, d, a, 0)
            pltpu.make_async_copy(part, part, self.loc_sem.at[d, a]).wait()


def backward_kernel(
    chips,
    quarters,
    x_hbm,
    segc_ref,
    segr_ref,
    ggain_ref,
    gbias_ref,
    cos_ref,
    sin_ref,
    table_ref,
    power_ref,
    norm2_ref,
    branch_hbm,
    wo_hbm,
    g_hbm,
    nh_hbm,
    rstd_hbm,
    q_hbm,
    k_hbm,
    v_hbm,
    wq_hbm,
    wk_hbm,
    wv_hbm,
    wg_hbm,
    h1_hbm,
    gated_hbm,
    grad_mg,
    grad_mu,
    grad_md,
    part_out,
    grad_qk_out,
    grad_v_out,
    grad_g_out,
    grad_out_out,
    small_out,
    reduced_out,
    x,
    branch,
    wo,
    g,
    nh,
    rstd,
    q,
    k,
    v,
    wq,
    wk,
    wv,
    wg,
    h1,
    gated,
    acc_gain,
    acc_bias,
    dk,
    dv,
    dq,
    stage,
    column,
    own,
    sib,
    rcv,
    in_sem,
    stage_sem,
    column_sem,
    red_sem,
    own_sem,
    sbs_sem,
    sbr_sem,
    rss_sem,
    rsr_sem,
):
    ring = Ring(chips, quarters, own, sib, rcv, own_sem, sbs_sem, sbr_sem, rss_sem, rsr_sem)
    grads = (grad_mg, grad_mu, grad_md)
    f32 = jnp.float32
    heads = q.shape[0]
    length = h1.shape[0]
    units = v.shape[0]
    block = length // BLOCKS
    third = units // 3
    pairs = [
        (wo_hbm, wo), (branch_hbm, branch), (g_hbm, g), (nh_hbm, nh), (rstd_hbm, rstd),
        (q_hbm, q), (k_hbm, k), (v_hbm, v),
        (wq_hbm, wq), (wk_hbm, wk), (wv_hbm, wv), (wg_hbm, wg), (x_hbm, x), (h1_hbm, h1), (gated_hbm, gated),
    ]
    copies = [pltpu.make_async_copy(a, b, in_sem.at[n]) for n, (a, b) in enumerate(pairs)]
    for copy in copies[:5]:
        copy.start()
    greet([*ring.nexts, ring.sibling])
    ring.load(grads, 0)
    for copy in copies[5:8]:
        copy.start()
    ring.load(grads, 1)
    for copy in copies[8:]:
        copy.start()
    acc_gain[...] = jnp.zeros_like(acc_gain)
    acc_bias[...] = jnp.zeros_like(acc_bias)
    small_out[...] = jnp.zeros_like(small_out)
    for copy in copies[:5]:
        copy.wait()

    def fold(values):
        return values[:, :LANE] + values[:, LANE:]

    def gate_block(i):
        rows = pl.ds(i * block, block)
        for head in range(heads):
            tall = slice(head * VD, (head + 1) * VD)
            up = dot(wo[tall, :], branch[rows, :], 1, 1)
            gate = g[tall, rows].astype(f32)
            nhat = nh[tall, rows].astype(f32)
            sigmoid = 1.0 / (1.0 + jnp.exp(-gate))
            silu = gate * sigmoid
            dgn = up * silu
            acc_gain[tall, :] += fold(dgn * nhat)
            acc_bias[tall, :] += fold(dgn)
            gain = ggain_ref[tall, :]
            f = dgn * gain
            mean = jnp.mean(f, axis=0, keepdims=True)
            inner = jnp.mean(f * nhat, axis=0, keepdims=True)
            nh[tall, rows] = low((f - mean - nhat * inner) * rstd[head : head + 1, rows])
            gn = nhat * gain + gbias_ref[tall, :]
            g[tall, rows] = low(up * gn * (sigmoid + silu * (1.0 - sigmoid)))

    gate_block(0)
    ring.pump(grads, 0, True)
    ring.load(grads, 2)
    gate_block(1)
    gate_block(2)
    ring.pump(grads, 1)
    ring.load(grads, 3)
    gate_block(3)
    for copy in copies[5:8]:
        copy.wait()

    ahead = lax.broadcasted_iota(jnp.int32, (block, block), 0) - lax.broadcasted_iota(
        jnp.int32, (block, block), 1
    )

    def key_block(head, m):
        tall = slice(head * VD, (head + 1) * VD)
        cols = pl.ds(m * block, block)
        dk[...] = jnp.zeros_like(dk)
        dv[...] = jnp.zeros_like(dv)

        def tile(i, carry):
            rows = pl.ds(pl.multiple_of(i * block, block), block)
            seen = (segc_ref[rows, :] == segr_ref[:, cols]) & (ahead + (i - m) * block >= 0)
            decay = jnp.where(seen, table_ref[head] * power_ref[head, i - m], 0.0)
            scores = low(dot(q[head, rows, :], k[head, cols, :], 1, 1) * decay)
            draw = low(dot(nh[tall, rows], v[tall, cols], 0, 0) * decay)
            dv[...] += dot(nh[tall, rows], scores, 1, 0)
            dk[...] += dot(draw, q[head, rows, :], 0, 0)
            more = dot(draw, k[head, cols, :], 1, 0)
            if m == 0:
                dq[rows, :] = more
            else:
                dq[rows, :] += more
            return carry

        lax.fori_loop(m, BLOCKS, tile, 0)
        v[tall, cols] = low(dv[...])
        k[head, cols, :] = low(turn(dk[...], cos_ref[cols, :], -sin_ref[cols, :]) * KD ** (-0.5))

    step = 2
    for head in range(heads):
        for m in range(BLOCKS):
            key_block(head, m)
            if m in (0, BLOCKS - 1):
                if m:
                    q[head] = low(turn(dq[...], cos_ref[...], -sin_ref[...]))
                ring.pump(grads, step)
                if step + 2 < chips:
                    ring.load(grads, step + 2)
                step += 1

    for copy in copies[8:]:
        copy.wait()

    def stage_wait(slot):
        pltpu.make_async_copy(stage.at[slot], stage.at[slot], stage_sem.at[slot]).wait()

    key_parts = [(q, wq), (k, wk)]
    for i in range(BLOCKS):
        slot = i % 2
        rows = pl.ds(i * block, block)
        if i >= 2:
            stage_wait(slot)
        total = None
        for values, weights in key_parts:
            for head in range(heads):
                wide = slice(head * KD, (head + 1) * KD)
                more = dot(values[head, rows, :], weights[:, wide], 1, 1)
                total = more if total is None else total + more
        stage[slot, 0:block, :] = total
        stage[slot, 0:block, :] += dot(v[:, rows], wv[...], 0, 0)
        stage[slot, 0:block, :] += dot(g[:, rows], wg[...], 0, 0)
        xb = x[rows, :].astype(f32)
        r1 = lax.rsqrt(jnp.mean(xb * xb, axis=1, keepdims=True) + EPSILON)
        small_out[0:1, :] += jnp.sum(stage[slot, 0:block, :] * (xb * r1), axis=0, keepdims=True)
        pltpu.make_async_copy(stage.at[slot], part_out.at[i], stage_sem.at[slot]).start()
        if i == BLOCKS - 1:
            ring.pump(grads, step)
            step += 1

    count = BLOCKS
    for source, right, target in ((v, h1, grad_v_out), (g, h1, grad_g_out), (gated, branch, grad_out_out)):
        for n in range(3):
            where = pl.ds(n * third, third)
            slot = count % 2
            stage_wait(slot)
            stage[slot] = dot(source[where, :], right[...], 1, 0)
            pltpu.make_async_copy(stage.at[slot], target.at[where, :], stage_sem.at[slot]).start()
            count += 1

    for number, (values, head) in enumerate([(q, 0), (q, 1), (k, 0), (k, 1)][: 2 * heads]):
        if number:
            pltpu.make_async_copy(column, column, column_sem).wait()
        column[...] = dot(h1[...], values[head], 0, 0)
        pltpu.make_async_copy(column, grad_qk_out.at[:, pl.ds(number * KD, KD)], column_sem).start()

    ones = jnp.ones((8, LANE), jnp.bfloat16)

    def row_of(acc):
        whole = acc[...]
        high = low(whole)
        return dot(ones, high, 1, 1) + dot(ones, low(whole - high.astype(f32)), 1, 1)

    small_out[1:2, :] = norm2_ref[0:1, :]
    small_out[2:3, 0:units] = row_of(acc_gain)[0:1, :]
    small_out[3:4, 0:units] = row_of(acc_bias)[0:1, :]

    last = chips - 1
    for d, a in ring.tokens:
        ring.total(grads, d, a, last)
    reduced = pltpu.make_async_copy(own.at[:, last], reduced_out, red_sem)
    reduced.start()
    ring.drain(grads)
    reduced.wait()
    for slot in range(2):
        stage_wait(slot)
    pltpu.make_async_copy(column, column, column_sem).wait()


def backward(tokens, segment, tables, gains, norm2, saved, ws, mlp_grads):
    chips = lax.axis_size("dp") // 2
    length, depth = tokens.shape
    wq, wk, wv, wg, wo = ws
    h1, q, k, v, g, nh, rstd, gated, branch = saved
    units = wv.shape[0]
    heads = q.shape[0]
    block = length // BLOCKS
    quarters = tuple(a.shape[0] // 4 for a in mlp_grads)
    rows = sum(quarters)
    count = len(quarters)
    f32, bf16 = jnp.float32, jnp.bfloat16
    vmem = pl.BlockSpec(memory_space=pltpu.VMEM)
    hbm = pl.BlockSpec(memory_space=pl.ANY)
    smem = pl.BlockSpec(memory_space=pltpu.SMEM)
    dma = lambda *shape: pltpu.SemaphoreType.DMA(shape)
    shape = jax.ShapeDtypeStruct
    tall = (units, length)
    stage_rows = max(block, units // 3)
    outs = [
        (shape((BLOCKS, stage_rows, depth), f32), hbm),
        (shape((depth, 2 * heads * KD), f32), hbm),
        (shape((units, depth), f32), hbm),
        (shape((units, depth), f32), hbm),
        (shape((units, depth), f32), hbm),
        (shape((8, depth), f32), vmem),
        (shape((2, rows, LANE), f32), hbm),
    ]
    scratch = [
        pltpu.VMEM((length, depth), bf16),
        pltpu.VMEM((length, depth), bf16),
        pltpu.VMEM((units, depth), bf16),
        pltpu.VMEM(tall, bf16),
        pltpu.VMEM(tall, bf16),
        pltpu.VMEM((8, length), f32),
        pltpu.VMEM((heads, length, KD), bf16),
        pltpu.VMEM((heads, length, KD), bf16),
        pltpu.VMEM(tall, bf16),
        pltpu.VMEM((depth, heads * KD), bf16),
        pltpu.VMEM((depth, heads * KD), bf16),
        pltpu.VMEM((units, depth), bf16),
        pltpu.VMEM((units, depth), bf16),
        pltpu.VMEM((length, depth), bf16),
        pltpu.VMEM(tall, bf16),
        pltpu.VMEM((units, LANE), f32),
        pltpu.VMEM((units, LANE), f32),
        pltpu.VMEM((block, KD), f32),
        pltpu.VMEM((VD, block), f32),
        pltpu.VMEM((length, KD), f32),
        pltpu.VMEM((2, stage_rows, depth), f32),
        pltpu.VMEM((depth, KD), f32),
        pltpu.VMEM((2, chips, rows, LANE), f32),
        pltpu.VMEM((2, chips, rows, LANE), f32),
        pltpu.VMEM((2, chips - 1, rows, LANE), f32),
        dma(15),
        dma(2),
        pltpu.SemaphoreType.DMA,
        pltpu.SemaphoreType.DMA,
        dma(2, count, chips),
        dma(2, count, chips),
        dma(2, count, chips),
        dma(2, count, chips - 1),
        dma(2, count, chips - 1),
    ]
    return pl.pallas_call(
        functools.partial(backward_kernel, chips, quarters),
        out_shape=tuple(o for o, _ in outs),
        in_specs=[hbm] + [vmem] * 7 + [smem] + [vmem] + [hbm] * 17,
        out_specs=tuple(s for _, s in outs),
        scratch_shapes=scratch,
        compiler_params=pltpu.CompilerParams(
            collective_id=2, has_side_effects=True, vmem_limit_bytes=VMEM_LIMIT
        ),
        cost_estimate=pl.CostEstimate(
            flops=20 * length * depth * units, bytes_accessed=80 * length * depth, transcendentals=0
        ),
    )(
        tokens, segment[:, None], segment[None, :], gains[0], gains[1], *tables, norm2,
        branch, wo, g, nh, rstd, q, k, v, wq, wk, wv, wg, h1, gated, *mlp_grads,
    )


def finish_kernel(
    chips,
    quarters,
    early_quarters,
    *refs,
):
    count, early_count = len(quarters), len(early_quarters)
    grads = refs[:count]
    part_hbm, small_ref, reduced_hbm, x_hbm, dmid_hbm, gain1_ref = refs[count : count + 6]
    refs = refs[count + 6 :]
    outs, early_outs = refs[:count], refs[count : count + early_count]
    tokens_out, small_out, peer_hbm = refs[count + early_count : count + early_count + 3]
    (own, sib, rcv, sacc, sbuf, part, peer, x, dmid, result, in_sem, res_sem, hs_sem, hr_sem, ss_sem, sr_sem) = refs[
        count + early_count + 3 : count + early_count + 19
    ]
    sems = refs[count + early_count + 19 :]
    ring = Ring(chips, quarters, own, sib, rcv, *sems[:5])
    late = Spread(ring, quarters, outs, *sems[5:10])
    early = Spread(ring, early_quarters, early_outs, *sems[10:15])
    bits = (2 * chips).bit_length() - 1
    f32 = jnp.float32
    block = part.shape[0]
    greet(
        [*ring.nexts, ring.peer] + [{"dp": bit_partner(ring.index, bit)} for bit in range(bits)]
    )

    start = 0
    for a in range(early_count):
        for d in range(2):
            early.begin(d, a, reduced_hbm.at[d, pl.ds(start, early_quarters[a]), :])
        start += early_quarters[a]
    ring.load(grads, 0)

    def h_copy(i):
        here = part_hbm.at[i, pl.ds(0, block), :]
        return remote(here, peer_hbm.at[i], hs_sem.at[i], hr_sem.at[i], ring.peer)

    for i in range(BLOCKS):
        h_copy(i).start()
    ring.load(grads, 1)

    def s_copy(level):
        target = ring.peer if level == 0 else {"dp": bit_partner(ring.index, level - 1)}
        return remote(sacc.at[level], sbuf.at[level], ss_sem.at[level], sr_sem.at[level], target)

    def s_finish(level):
        s_copy(level).wait()
        got = sbuf[level]
        if level == 0:
            first = lax.broadcasted_iota(jnp.int32, got.shape, 0) == 0
            got = jnp.where(first, got, 0.0)
        sacc[level + 1] = sacc[level] + got

    sacc[0] = small_ref[...]

    def small_step(step):
        for level in range(bits + 2):

            @pl.when(step == level)
            def _():
                if level > 0:
                    s_finish(level - 1)
                if level <= bits:
                    s_copy(level).start()

    def rs_step(step, carry):
        ring.pump(grads, step)

        @pl.when(step + 2 < chips)
        def _():
            ring.load(grads, step + 2)

        early.pump(step - 1)
        small_step(step)
        return carry

    ring.pump(grads, 0, True)
    ring.load(grads, 2)
    small_step(0)
    lax.fori_loop(1, chips - 1, rs_step, 0)
    for d, a in ring.tokens:
        ring.total(grads, d, a, chips - 1)
        late.begin(d, a, own.at[d, chips - 1, ring.packed(a), :])
    early.pump(chips - 2, True)

    def token_block(i):
        rows = pl.ds(pl.multiple_of(i * block, block), block)
        h_copy(i).wait_recv()
        mine = part_hbm.at[i, pl.ds(0, block), :]
        loads = [
            pltpu.make_async_copy(mine, part, in_sem.at[0]),
            pltpu.make_async_copy(peer_hbm.at[i], peer, in_sem.at[1]),
            pltpu.make_async_copy(x_hbm.at[rows, :], x, in_sem.at[2]),
            pltpu.make_async_copy(dmid_hbm.at[rows, :], dmid, in_sem.at[3]),
        ]
        for copy in loads:
            copy.start()
        for copy in loads:
            copy.wait()
        xb = x[...].astype(f32)
        r1 = lax.rsqrt(jnp.mean(xb * xb, axis=1, keepdims=True) + EPSILON)
        e = (part[...] + peer[...]) * gain1_ref[...]
        inner = jnp.mean(e * xb, axis=1, keepdims=True)
        result[rows, :] = low(dmid[...] + r1 * e - xb * (r1 * r1 * r1 * inner))
        pltpu.make_async_copy(result.at[rows, :], tokens_out.at[rows, :], res_sem.at[i]).start()

    def ag_step(step, carry):
        late.pump(step)

        @pl.when(step < BLOCKS)
        def _():
            token_block(step)

        return carry

    lax.fori_loop(0, chips - 2, ag_step, 0)
    late.pump(chips - 2, True)
    small_out[...] = sacc[bits + 1]
    ring.drain(grads)
    early.drain()
    late.drain()
    for i in range(BLOCKS):
        h_copy(i).wait_send()
        pltpu.make_async_copy(result.at[pl.ds(0, block), :], result.at[pl.ds(0, block), :], res_sem.at[i]).wait()


def finish(grads, part, small, reduced, mlp_shapes, tokens, dmid, gain1):
    chips = lax.axis_size("dp") // 2
    length, depth = tokens.shape
    block = length // BLOCKS
    quarters = tuple(g.shape[0] // 4 for g in grads)
    early_quarters = tuple(g.shape[0] // 4 for g in mlp_shapes)
    rows = sum(quarters)
    count, early = len(quarters), len(early_quarters)
    bits = (2 * chips).bit_length() - 1
    f32, bf16 = jnp.float32, jnp.bfloat16
    vmem = pl.BlockSpec(memory_space=pltpu.VMEM)
    hbm = pl.BlockSpec(memory_space=pl.ANY)
    dma = lambda *shape: pltpu.SemaphoreType.DMA(shape)
    shape = jax.ShapeDtypeStruct
    outs = [(shape(g.shape, f32), hbm) for g in (*grads, *mlp_shapes)]
    outs += [
        (shape((length, depth), bf16), hbm),
        (shape(small.shape, f32), vmem),
        (shape((BLOCKS, block, depth), f32), hbm),
    ]
    scratch = [
        pltpu.VMEM((2, chips, rows, LANE), f32),
        pltpu.VMEM((2, chips, rows, LANE), f32),
        pltpu.VMEM((2, chips - 1, rows, LANE), f32),
        pltpu.VMEM((bits + 2, *small.shape), f32),
        pltpu.VMEM((bits + 1, *small.shape), f32),
        pltpu.VMEM((block, depth), f32),
        pltpu.VMEM((block, depth), f32),
        pltpu.VMEM((block, depth), bf16),
        pltpu.VMEM((block, depth), f32),
        pltpu.VMEM((length, depth), bf16),
        dma(4),
        dma(BLOCKS),
        dma(BLOCKS),
        dma(BLOCKS),
        dma(bits + 1),
        dma(bits + 1),
        dma(2, count, chips),
        dma(2, count, chips),
        dma(2, count, chips),
        dma(2, count, chips - 1),
        dma(2, count, chips - 1),
    ]
    for number in (count, early):
        scratch += [
            dma(2, number, chips - 1),
            dma(2, number, chips - 1),
            dma(2, number, chips),
            dma(2, number, chips),
            dma(2, number),
        ]
    return pl.pallas_call(
        functools.partial(finish_kernel, chips, quarters, early_quarters),
        out_shape=tuple(o for o, _ in outs),
        in_specs=[hbm] * (count + 1) + [vmem] + [hbm] * 3 + [vmem],
        out_specs=tuple(s for _, s in outs),
        scratch_shapes=scratch,
        compiler_params=pltpu.CompilerParams(
            collective_id=3, has_side_effects=True, vmem_limit_bytes=50 * 1024 * 1024
        ),
        cost_estimate=pl.CostEstimate(
            flops=20 * rows * depth, bytes_accessed=80 * rows * depth, transcendentals=0
        ),
    )(*grads, part, small, reduced, tokens, dmid, gain1)

def swap(array):
    return lax.ppermute(array, "tensor", [(0, 1), (1, 0)])


def other_half(arrays, zero):
    dp, index = lax.axis_size("dp"), lax.axis_index("dp")
    rows = arrays[0].shape[0]
    count = len(arrays)
    if dp % count == 0 and rows % (8 * (dp // count)) == 0:
        share = rows * count // dp
        each = dp // count
        inside = (index % each) * share
        own = [lax.dynamic_slice_in_dim(a, inside, share, 0) for a in arrays]
        part = own[0]
        for number in range(1, count):
            part = jnp.where(index // each == number, own[number], part)
    else:
        share = -(-rows * count // (8 * dp)) * 8
        whole = jnp.concatenate(arrays, axis=0)
        whole = jnp.pad(whole, ((0, share * dp - rows * count), (0, 0)))
        part = lax.dynamic_slice_in_dim(whole, index * share, share, 0)
    got = lax.all_gather(swap(part.astype(jnp.float32)), "dp", axis=0, tiled=True)
    got = low(got + zero)
    return [got[number * rows : (number + 1) * rows] for number in range(count)]


def plain_body(
    tokens,
    segment,
    norm1_gain,
    w_query,
    w_key,
    w_value,
    w_gate,
    group_gain,
    group_bias,
    w_out,
    norm2_gain,
    w_mlp_gate,
    w_mlp_up,
    w_mlp_down,
    cotangent,
):
    length, depth = tokens.shape
    heads = w_query.shape[1] // KD
    block = length // BLOCKS
    tensor = lax.axis_index("tensor")
    f32 = jnp.float32
    zero = jnp.minimum(segment[0], 0).astype(f32)
    value_t, gate_t, mg_t, mu_t = w_value.T, w_gate.T, w_mlp_gate.T, w_mlp_up.T
    mg_o, mu_o, md_o, wo_o = other_half([mg_t, mu_t, w_mlp_down, w_out], zero)
    x = tokens.astype(f32)
    gain1 = norm1_gain.astype(f32)
    gain2 = norm2_gain.astype(f32)
    ggain = group_gain.astype(f32)[:, None]
    gbias = group_bias.astype(f32)[:, None]
    r1 = lax.rsqrt(jnp.mean(x * x, axis=1, keepdims=True) + EPSILON)
    h1 = low(x * r1 * gain1)
    half = KD // 2
    frequency = jnp.exp(-jnp.log(10000.0) * jnp.arange(half, dtype=f32) / half)
    angles = jnp.arange(length, dtype=f32)[:, None] * frequency[None, :]
    cosine, sine = jnp.cos(angles), jnp.sin(angles)
    positions = jnp.arange(length, dtype=jnp.int32)
    visible = (positions[:, None] >= positions[None, :]) & (segment[:, None] == segment[None, :])
    offsets = jnp.maximum(positions[:, None] - positions[None, :], 0).astype(f32)

    def decay(head, rows, columns):
        order = (tensor * heads + head).astype(f32)
        rate = jnp.log1p(-jnp.exp2(-5.0 - order))
        return jnp.where(visible[rows, columns], jnp.exp(offsets[rows, columns] * rate), 0.0)

    queries = [[] for _ in range(heads)]
    keys = [[] for _ in range(heads)]
    values = [[] for _ in range(heads)]
    gates = [[] for _ in range(heads)]
    nhats = [[] for _ in range(heads)]
    spreads = [[] for _ in range(heads)]
    gated_blocks, received = [], []
    for number in range(BLOCKS):
        rows = slice(number * block, (number + 1) * block)
        seen = slice(0, (number + 1) * block)
        own = []
        for head in range(heads):
            wide = slice(head * KD, (head + 1) * KD)
            tall = slice(head * VD, (head + 1) * VD)
            q = low(turn(dot(h1[rows], w_query[:, wide], 1, 0), cosine[rows], sine[rows]))
            k = turn(dot(h1[rows], w_key[:, wide], 1, 0), cosine[rows], sine[rows])
            queries[head].append(q)
            keys[head].append(low(k * KD ** (-0.5)))
            values[head].append(low(dot(value_t[tall], h1[rows], 1, 1)))
            g = dot(gate_t[tall], h1[rows], 1, 1)
            gates[head].append(g)
            scores = dot(q, jnp.concatenate(keys[head], axis=0), 1, 1)
            scores = low(scores * decay(head, rows, seen))
            ret = dot(jnp.concatenate(values[head], axis=1), scores, 1, 1)
            centred = ret - jnp.mean(ret, axis=0, keepdims=True)
            scale = lax.rsqrt(jnp.mean(centred * centred, axis=0, keepdims=True) + GROUP_EPSILON)
            nhat = centred * scale
            nhats[head].append(nhat)
            spreads[head].append(scale)
            own.append(low(jax.nn.silu(g) * (nhat * ggain[tall] + gbias[tall])))
        gated_blocks.append(jnp.concatenate(own, axis=0))
        received.append(low(swap(gated_blocks[-1].astype(f32)) + zero))

    mids, h2s, r2s, hidden_own, hidden_oth, das, dbs, dmids = [], [], [], [], [], [], [], []
    norm2_rows = []
    for number in range(BLOCKS):
        rows = slice(number * block, (number + 1) * block)
        mid = x[rows] + (dot(gated_blocks[number], w_out, 0, 0) + dot(received[number], wo_o, 0, 0))
        r2 = lax.rsqrt(jnp.mean(mid * mid, axis=1, keepdims=True) + EPSILON)
        h2 = low(mid * r2 * gain2)
        cot = cotangent[rows]

        def mlp(gate_w, up_w, down_w):
            a, b = dot(gate_w, h2, 1, 1), dot(up_w, h2, 1, 1)
            hidden, pull = jax.vjp(lambda s, t: jax.nn.gelu(s) * t, a, b)
            da, db = pull(dot(down_w, cot, 1, 1))
            da, db = low(da), low(db)
            return low(hidden), da, db, dot(da, gate_w, 0, 0) + dot(db, up_w, 0, 0)

        own_hidden, da, db, part = mlp(mg_t, mu_t, w_mlp_down)
        oth_hidden, _, _, more = mlp(mg_o, mu_o, md_o)
        dh2 = part + more
        e = dh2 * gain2
        dmid = cot.astype(f32) + r2 * e - mid * (r2 * r2 * r2) * jnp.mean(e * mid, axis=1, keepdims=True)
        norm2_rows.append(jnp.sum(dh2 * mid * r2, axis=0))
        for where, value in zip(
            (mids, h2s, hidden_own, hidden_oth, das, dbs, dmids),
            (mid, h2, own_hidden, oth_hidden, da, db, dmid),
        ):
            where.append(value)
    grad_norm2 = sum(norm2_rows)
    mid = jnp.concatenate(mids, axis=0)
    h2 = jnp.concatenate(h2s, axis=0)
    hidden = jnp.concatenate(hidden_own, axis=1)
    hidden_o = jnp.concatenate(hidden_oth, axis=1)
    dmid = jnp.concatenate(dmids, axis=0)
    own_rows = length // lax.axis_size("tensor")
    place = tensor * own_rows
    output = low(
        lax.dynamic_slice_in_dim(mid, place, own_rows, 0)
        + dot(lax.dynamic_slice_in_dim(hidden, place, own_rows, 1), w_mlp_down, 0, 0)
        + dot(lax.dynamic_slice_in_dim(hidden_o, place, own_rows, 1), md_o, 0, 0)
    )
    grad_mg = dot(jnp.concatenate(das, axis=1), h2, 1, 0)
    grad_mu = dot(jnp.concatenate(dbs, axis=1), h2, 1, 0)
    grad_md = dot(hidden, cotangent, 1, 0)

    branch = low(dmid)
    gated = jnp.concatenate(gated_blocks, axis=1)
    grad_out = dot(gated, branch, 1, 0)
    dgated = dot(w_out, branch, 1, 1)
    dqs, dks, dvs, dgs, ggains, gbiases = [], [], [], [], [], []
    everything = slice(0, length)
    for head in range(heads):
        tall = slice(head * VD, (head + 1) * VD)
        g = jnp.concatenate(gates[head], axis=1)
        nhat = jnp.concatenate(nhats[head], axis=1)
        spread = jnp.concatenate(spreads[head], axis=1)
        q = jnp.concatenate(queries[head], axis=0)
        k = jnp.concatenate(keys[head], axis=0)
        v = jnp.concatenate(values[head], axis=1)
        sigmoid = jax.nn.sigmoid(g)
        silu = g * sigmoid
        up = dgated[tall]
        dgn = up * silu
        ggains.append(jnp.sum(dgn * nhat, axis=1))
        gbiases.append(jnp.sum(dgn, axis=1))
        f = dgn * ggain[tall]
        dret = (
            f - jnp.mean(f, axis=0, keepdims=True) - nhat * jnp.mean(f * nhat, axis=0, keepdims=True)
        ) * spread
        dret = low(dret)
        gn = nhat * ggain[tall] + gbias[tall]
        dgs.append(low(up * gn * (sigmoid + silu * (1.0 - sigmoid))))
        table = decay(head, everything, everything)
        scores = low(dot(q, k, 1, 1) * table)
        draw = low(dot(dret, v, 0, 0) * table)
        dvs.append(low(dot(dret, scores, 1, 0)))
        dqs.append(low(turn(dot(draw, k, 1, 0), cosine, -sine)))
        dks.append(low(turn(dot(draw, q, 0, 0), cosine, -sine) * KD ** (-0.5)))
    dv = jnp.concatenate(dvs, axis=0)
    dg = jnp.concatenate(dgs, axis=0)
    dq = jnp.concatenate(dqs, axis=1)
    dk = jnp.concatenate(dks, axis=1)
    partial_in = dot(dq, w_query, 1, 1) + dot(dk, w_key, 1, 1) + dot(dv, value_t, 0, 0) + dot(dg, gate_t, 0, 0)
    grad_norm1 = jnp.sum(partial_in * x * r1, axis=0)
    grad_qk = dot(h1, jnp.concatenate([dq, dk], axis=1), 0, 0)
    grad_v = dot(dv, h1, 1, 0)
    grad_g = dot(dg, h1, 1, 0)

    units = w_value.shape[1]
    small = jnp.stack(
        [
            grad_norm1,
            grad_norm2,
            jnp.pad(jnp.concatenate(ggains), (0, depth - units)),
            jnp.pad(jnp.concatenate(gbiases), (0, depth - units)),
        ]
    )
    small = jnp.pad(small, ((0, 4), (0, 0)))
    grads = lax.psum((grad_qk, grad_v, grad_g, grad_out, grad_mg, grad_mu, grad_md), "dp")
    peer = swap(partial_in)
    small = lax.psum(small.at[0].set(lax.psum(small[0], "tensor")), "dp")
    grad_qk, grad_v, grad_g, grad_out, grad_mg, grad_mu, grad_md = grads
    e1 = (partial_in + peer) * gain1
    grad_tokens = low(dmid + r1 * e1 - x * (r1 * r1 * r1) * jnp.mean(e1 * x, axis=1, keepdims=True))
    key_width = w_query.shape[1]
    return (
        output,
        grad_tokens,
        small[0],
        grad_qk[:, :key_width],
        grad_qk[:, key_width:],
        grad_v.T,
        grad_g.T,
        small[2, :units],
        small[3, :units],
        grad_out,
        small[1],
        grad_mg.T,
        grad_mu.T,
        grad_md,
    )


def body(
    tokens,
    segment,
    norm1_gain,
    w_query,
    w_key,
    w_value,
    w_gate,
    group_gain,
    group_bias,
    w_out,
    norm2_gain,
    w_mlp_gate,
    w_mlp_up,
    w_mlp_down,
    cotangent,
):
    length, depth = tokens.shape
    if depth % (LANE * (lax.axis_size("dp") // 2)):
        return plain_body(
            tokens, segment, norm1_gain, w_query, w_key, w_value, w_gate, group_gain, group_bias, w_out,
            norm2_gain, w_mlp_gate, w_mlp_up, w_mlp_down, cotangent,
        )
    heads = w_query.shape[1] // KD
    f32 = jnp.float32
    value_t, gate_t, mg_t, mu_t = w_value.T, w_gate.T, w_mlp_gate.T, w_mlp_up.T
    gain1 = norm1_gain.astype(f32)
    ggain = group_gain.astype(f32)[:, None]
    gbias = group_bias.astype(f32)[:, None]
    tables = make_tables(length, heads)
    (h1, qs, ks, vs, g, nhat, rstd, gated, dmid, branch, grad_mg, grad_mu, grad_md, norm2, output, _) = forward(
        tokens,
        segment,
        tables,
        (gain1[None, :], norm2_gain.astype(f32)[None, :], ggain, gbias),
        (w_query, w_key, value_t, gate_t, w_out, mg_t, mu_t, w_mlp_down),
        cotangent,
    )
    results = backward(
        tokens,
        segment,
        tables,
        (ggain, gbias),
        norm2,
        (h1, qs, ks, vs, g, nhat, rstd, gated, branch),
        (w_query, w_key, value_t, gate_t, w_out),
        (grad_mg, grad_mu, grad_md),
    )
    part, grad_qk, grad_v, grad_g, grad_out, small, reduced = results
    (grad_qk, grad_v, grad_g, grad_out, grad_mg, grad_mu, grad_md, grad_tokens, small, _) = finish(
        (grad_qk, grad_v, grad_g, grad_out),
        part,
        small,
        reduced,
        (grad_mg, grad_mu, grad_md),
        tokens,
        dmid,
        gain1[None, :],
    )
    units = w_value.shape[1]
    key_width = w_query.shape[1]
    return (
        output,
        grad_tokens,
        small[0],
        grad_qk[:, :key_width],
        grad_qk[:, key_width:],
        grad_v.T,
        grad_g.T,
        small[2, :units],
        small[3, :units],
        grad_out,
        small[1],
        grad_mg.T,
        grad_mu.T,
        grad_md,
    )


def solution(mesh):
    placed = (
        P("dp", None),
        P("dp"),
        P(),
        P(None, "tensor"),
        P(None, "tensor"),
        P(None, "tensor"),
        P(None, "tensor"),
        P("tensor"),
        P("tensor"),
        P("tensor", None),
        P(),
        P(None, "tensor"),
        P(None, "tensor"),
        P("tensor", None),
        P("dp", None),
    )
    return jax.shard_map(
        body,
        mesh=mesh,
        in_specs=placed,
        out_specs=(
            P(("dp", "tensor"), None),
            P("dp", None),
            P(),
            P(None, "tensor"),
            P(None, "tensor"),
            P(None, "tensor"),
            P(None, "tensor"),
            P("tensor"),
            P("tensor"),
            P("tensor", None),
            P(),
            P(None, "tensor"),
            P(None, "tensor"),
            P("tensor", None),
        ),
        check_vma=False,
    )
```

```python
import functools
import math

import jax
import jax.numpy as jnp
import numpy as np
from jax import lax
from jax.experimental import pallas as pl
from jax.experimental.pallas import tpu as pltpu
from jax.sharding import PartitionSpec as P

KD = 256
VD = 432
LANE = 128
MESH = pl.DeviceIdType.MESH
WINDOW = 2
VMEM_LIMIT = 63 * 1024 * 1024


EPSILON = 1e-06
GROUP_EPSILON = 0.25


def ring_place(chip, chips):
    line = chips // 2
    x = chip % 2
    z = chip // 2
    return z + x * (chips - 1 - 2 * z), line


def ring_chip(place, chips):
    line = chips // 2
    x = place // line
    z = place + x * (chips - 1 - 2 * place)
    return z * 2 + x


def bit_partner(index, bit):
    step = 1 << bit
    return index + (1 - 2 * ((index // step) % 2)) * step


BLOCKS = 4
GELU_A = math.sqrt(2.0 / math.pi)
GELU_B = 0.044715


def dot(left, right, left_dim, right_dim):
    return lax.dot_general(
        left, right, (((left_dim,), (right_dim,)), ((), ())), preferred_element_type=jnp.float32
    )


def low(array):
    return array.astype(jnp.bfloat16)


def turn(vectors, cosine, sine):
    half = vectors.shape[1] // 2
    lower, upper = vectors[:, :half], vectors[:, half:]
    return jnp.concatenate([lower * cosine - upper * sine, upper * cosine + lower * sine], axis=1)


def remote(source, target, send, recv, device):
    return pltpu.make_async_remote_copy(
        source, target, send, recv, device_id=device, device_id_type=MESH
    )


def rate_of(head, heads, tensor):
    rates = [math.log1p(-(2.0 ** (-5 - order))) for order in range(2 * heads)]
    return jnp.where(tensor == 0, rates[head], rates[heads + head]).astype(jnp.float32)


def upright(row, size):
    diagonal = lax.broadcasted_iota(jnp.int32, (size, size), 0) == lax.broadcasted_iota(
        jnp.int32, (size, size), 1
    )
    return jnp.sum(jnp.where(diagonal, row, 0.0), axis=1, keepdims=True)


def upright_part(row, start, size):
    shape = (size, row.shape[1])
    chosen = lax.broadcasted_iota(jnp.int32, shape, 0) + start == lax.broadcasted_iota(jnp.int32, shape, 1)
    return jnp.sum(jnp.where(chosen, row, 0.0), axis=1, keepdims=True)


GAIN1, GAIN2, GROUP_GAIN, GROUP_BIAS, SEGMENT = range(5)


def greet(devices):
    barrier = pltpu.get_barrier_semaphore()
    for device in devices:
        pl.semaphore_signal(barrier, inc=1, device_id=device, device_id_type=MESH)
    pl.semaphore_wait(barrier, len(devices))


def forward_kernel(
    chips,
    x_ref,
    rows_ref,
    cos_ref,
    sin_ref,
    wq_hbm,
    wk_hbm,
    wv_hbm,
    wg_hbm,
    wo_ref,
    mg_ref,
    mu_ref,
    md_ref,
    cot_ref,
    h1_out,
    q_out,
    k_out,
    v_out,
    g_out,
    nh_out,
    rstd_out,
    gated_out,
    dmid_out,
    branch_out,
    grad_mg_out,
    grad_mu_out,
    grad_md_out,
    norm2_out,
    output_out,
    gath_out,
    weights,
    others,
    cot,
    h1,
    q,
    k,
    v,
    g,
    nh,
    rstd,
    gated,
    acc,
    gsend,
    grecv,
    h2,
    hid,
    da,
    db,
    stage,
    mid,
    dh_own,
    dh_oth,
    out_sum,
    branch,
    ggain_ref,
    gbias_ref,
    in_sem,
    save_sem,
    out_sem,
    stage_sem,
    dmid_sem,
    branch_sem,
    xs_sem,
    xr_sem,
    ys_sem,
    yr_sem,
    gs_sem,
    gr_sem,
    cs_sem,
    cr_sem,
):
    index, tensor = lax.axis_index("dp"), lax.axis_index("tensor")
    core = index % 2
    place, _ = ring_place(index // 2, chips)
    nexts = [
        {"dp": ring_chip((place + 1) % chips, chips) * 2 + core},
        {"dp": ring_chip((place + chips - 1) % chips, chips) * 2 + core},
    ]
    sibling, peer = {"dp": index + 1 - 2 * core}, {"tensor": 1 - tensor}
    heads = q.shape[1]
    units, length = v.shape
    block = length // BLOCKS
    third = units // 3
    f32 = jnp.float32

    for number, source in enumerate((wo_ref, mg_ref, mu_ref, md_ref)):
        pltpu.make_async_copy(source, weights.at[number], in_sem.at[number]).start()
    wv_ref, wg_ref = hid, da
    key_width = wq_hbm.shape[1]
    early = [
        pltpu.make_async_copy(wq_hbm, h2.at[:, pl.ds(0, key_width)], in_sem.at[5]),
        pltpu.make_async_copy(wk_hbm, h2.at[:, pl.ds(key_width, key_width)], in_sem.at[6]),
        pltpu.make_async_copy(wv_hbm, wv_ref, in_sem.at[7]),
        pltpu.make_async_copy(wg_hbm, wg_ref, in_sem.at[8]),
    ]
    for copy in early:
        copy.start()
    pltpu.make_async_copy(cot_ref, cot, in_sem.at[4]).start()
    greet([*nexts, sibling, peer])

    rows_slice = units // 2
    half_slice = rows_slice // 2

    def area(w, where, which, half=None):
        start = which * rows_slice + (0 if half is None else half * half_slice)
        size = rows_slice if half is None else half_slice
        return gath_out.at[
            w,
            pl.ds(pl.multiple_of(start, 8), size),
            pl.ds(pl.multiple_of(where * LANE, LANE), LANE),
        ]

    def slice_spot(w):
        return gsend.at[
            BLOCKS - 1,
            pl.ds((w % 2) * rows_slice, rows_slice),
            pl.ds((w // 2) * LANE, LANE),
        ]

    def y_copy(w):
        return remote(slice_spot(w), area(w, place, core), ys_sem.at[w], yr_sem.at[w], peer)

    def hop(w, d, t):
        where = (place - t + chips) % chips if d == 0 else (place + t) % chips
        part = area(w, where, core, d if t == chips // 2 - 1 else None)
        return remote(part, part, gs_sem.at[w, d, t], gr_sem.at[w, d, t], nexts[d])

    def arrived(w, d, t):
        where = (place - t - 1 + chips) % chips if d == 0 else (place + t + 1) % chips
        part = area(w, where, core, d if t == chips // 2 - 1 else None)
        pltpu.make_async_copy(part, part, gr_sem.at[w, d, t]).wait()
        return where

    def share(w, slot, where, half=None):
        part = area(w, where, core, half)
        remote(part, part, cs_sem.at[w, slot], cr_sem.at[w, slot], sibling).start()

    steps = chips // 2

    def begin(w):
        y_copy(w).wait_recv()
        for d in range(2):
            hop(w, d, 0).start()
        share(w, 0, place)

    def pump(w, t):
        for d in range(2):
            where = arrived(w, d, t)
            if t < steps - 1:
                hop(w, d, t + 1).start()
            share(w, 1 + 2 * t + d, where, d if t == steps - 1 else None)

    for number in range(4):
        pltpu.make_async_copy(wo_ref, weights.at[number], in_sem.at[number]).wait()
        slice_spot(number)[...] = weights[
            number,
            pl.ds(pl.multiple_of(core * rows_slice, 16), rows_slice),
            pl.ds(pl.multiple_of(place * LANE, LANE), LANE),
        ].astype(f32)
        y_copy(number).start()

    def exchange(i):
        return remote(gsend.at[i], grecv.at[i], xs_sem.at[i], xr_sem.at[i], peer)

    ahead = lax.broadcasted_iota(jnp.int32, (block, block), 0) - lax.broadcasted_iota(
        jnp.int32, (block, block), 1
    )

    def saves(i):
        slot = i % 2
        rows = pl.ds(pl.multiple_of(i * block, block), block)
        pairs = (
            (h1.at[slot], h1_out.at[rows, :]),
            (q.at[slot], q_out.at[:, rows, :]),
            (g.at[slot], g_out.at[:, rows]),
            (nh.at[slot], nh_out.at[:, rows]),
        )
        return [
            pltpu.make_async_copy(source, target, save_sem.at[number, slot])
            for number, (source, target) in enumerate(pairs)
        ]

    def attention(i, carry):
        rows = pl.ds(pl.multiple_of(i * block, block), block)
        slot = i % 2

        @pl.when(i >= 2)
        def _():
            for copy in saves(i - 2):
                copy.wait()

        xb = x_ref[rows, :].astype(f32)
        r1 = lax.rsqrt(jnp.mean(xb * xb, axis=1, keepdims=True) + EPSILON)
        h1[slot] = low(xb * r1 * rows_ref[GAIN1 : GAIN1 + 1, :])
        cosine, sine = cos_ref[rows, :], sin_ref[rows, :]
        for head in range(heads):
            wide = slice(head * KD, (head + 1) * KD)
            q[slot, head] = low(turn(dot(h1[slot], h2[:, wide], 1, 0), cosine, sine))
            wide = slice(key_width + head * KD, key_width + (head + 1) * KD)
            k[head, rows, :] = low(turn(dot(h1[slot], h2[:, wide], 1, 0), cosine, sine) * KD ** (-0.5))
        v[:, rows] = low(dot(wv_ref[...], h1[slot], 1, 1))

        @pl.when(i == BLOCKS - 1)
        def _():
            for w in range(4):
                y_copy(w).wait_send()

        segc = upright(rows_ref[SEGMENT : SEGMENT + 1, rows], block)
        for head in range(heads):
            tall = slice(head * VD, (head + 1) * VD)
            rate = rate_of(head, heads, tensor)
            acc[...] = jnp.zeros_like(acc)

            def tile(m, carry):
                cols = pl.ds(pl.multiple_of(m * block, block), block)
                s = dot(q[slot, head], k[head, cols, :], 1, 1)
                gap = ahead + (i - m) * block
                seen = (segc == rows_ref[SEGMENT : SEGMENT + 1, cols]) & (gap >= 0)
                s = jnp.where(seen, s * jnp.exp(gap.astype(f32) * rate), 0.0)
                acc[...] += dot(v[tall, cols], low(s), 1, 1)
                return carry

            lax.fori_loop(0, i + 1, tile, 0)
            ret = acc[...]
            centred = ret - jnp.mean(ret, axis=0, keepdims=True)
            scale = lax.rsqrt(jnp.mean(centred * centred, axis=0, keepdims=True) + GROUP_EPSILON)
            nhat = centred * scale
            nh[slot, tall, :] = low(nhat)
            rstd[head : head + 1, rows] = scale
            gate = dot(wg_ref[tall, :], h1[slot], 1, 1)
            g[slot, tall, :] = low(gate)
            gn = nhat * ggain_ref[tall, :] + gbias_ref[tall, :]
            out = low(gate / (1.0 + jnp.exp(-gate)) * gn)
            gated[tall, rows] = out
            gsend[i, tall, :] = out.astype(f32)
        exchange(i).start()
        for copy in saves(i):
            copy.start()

        @pl.when(i == 0)
        def _():
            begin(0)

        @pl.when(i == 1)
        def _():
            pump(0, 0)
            for w in range(1, 4):
                begin(w)

        @pl.when(i == 2)
        def _():
            pump(0, 1)

        return carry

    rstd[...] = jnp.zeros_like(rstd)
    for n in range(3):
        where = slice(n * third, (n + 1) * third)
        ggain_ref[where, :] = upright_part(rows_ref[GROUP_GAIN : GROUP_GAIN + 1, :], n * third, third)
        gbias_ref[where, :] = upright_part(rows_ref[GROUP_BIAS : GROUP_BIAS + 1, :], n * third, third)
    for copy in early:
        copy.wait()
    lax.fori_loop(0, BLOCKS, attention, 0)
    saved = [(k, k_out), (v, v_out), (rstd, rstd_out), (gated, gated_out)]
    for number, (source, target) in enumerate(saved):
        pltpu.make_async_copy(source, target, out_sem.at[number]).start()

    def cast_in(w):
        for slot in range(1 + 2 * steps):
            t = (slot - 1) // 2
            d = (slot - 1) % 2
            if slot == 0:
                where = place
            else:
                where = (place - t - 1 + chips) % chips if d == 0 else (place + t + 1) % chips
            part = area(w, where, 1 - core, d if slot > 0 and t == steps - 1 else None)
            pltpu.make_async_copy(part, part, cr_sem.at[w, slot]).wait()

        def piece(n):
            where = pl.ds(n * third, third)
            return pltpu.make_async_copy(
                gath_out.at[w, where, :], stage.at[n % 2], stage_sem.at[n % 2]
            )

        piece(0).start()
        for n in range(3):
            if n < 2:
                piece(n + 1).start()
            piece(n).wait()
            others[w, n * third : (n + 1) * third, :] = low(stage[n % 2])

    pump(0, 2)
    pump(0, 3)
    cast_in(0)
    pltpu.make_async_copy(cot_ref, cot, in_sem.at[4]).wait()
    norm2_out[...] = jnp.zeros_like(norm2_out)
    part = units // 2

    def middle(i, rows):
        mid[...] = x_ref[rows, :].astype(f32) + (
            dot(gated[:, rows], weights[0], 0, 0) + dot(low(grecv[i]), others[0], 0, 0)
        )
        return lax.rsqrt(jnp.mean(mid[...] * mid[...], axis=1, keepdims=True) + EPSILON)

    def mlp_part(source, tall, rows):
        a = dot(source[1, tall, :], h2[rows, :], 1, 1)
        b = dot(source[2, tall, :], h2[rows, :], 1, 1)
        dhidden = dot(source[3, tall, :], cot[rows, :], 1, 1)
        square = a * a
        t = jnp.tanh(GELU_A * a * (1.0 + GELU_B * square))
        gelu = 0.5 * a * (1.0 + t)
        slope = 0.5 * (1.0 + t) + 0.5 * a * (1.0 - t * t) * (
            GELU_A * (1.0 + 3.0 * GELU_B * square)
        )
        dga = low(dhidden * b * slope)
        dup = low(dhidden * gelu)
        more = dot(dga, source[1, tall, :], 0, 0) + dot(dup, source[2, tall, :], 0, 0)
        return low(gelu * b), dga, dup, more

    def own_half(i):
        rows = pl.ds(pl.multiple_of(i * block, block), block)
        exchange(i).wait_recv()
        r2 = middle(i, rows)
        h2[rows, :] = low(mid[...] * r2 * rows_ref[GAIN2 : GAIN2 + 1, :])
        for f in range(2):
            tall = slice(f * part, (f + 1) * part)
            hid[tall, rows], da[tall, rows], db[tall, rows], more = mlp_part(weights, tall, rows)
            dh_own[i] = more if f == 0 else dh_own[i] + more

    def branch_wait():
        pltpu.make_async_copy(branch, branch, branch_sem).wait()

    def other_half(i, first=False):
        rows = pl.ds(pl.multiple_of(i * block, block), block)
        mine = i // (BLOCKS // 2) == tensor
        r2 = middle(i, rows)
        for f in range(2):
            tall = slice(f * part, (f + 1) * part)
            hidden, _, _, more = mlp_part(others, tall, rows)
            dh_oth[...] = more if f == 0 else dh_oth[...] + more

            @pl.when(mine)
            def _():
                lift = dot(hidden, others[3, tall, :], 0, 0) + dot(hid[tall, rows], weights[3, tall, :], 0, 0)
                out_sum[...] = lift if f == 0 else out_sum[...] + lift

        @pl.when(mine)
        def _():
            spot = pl.ds(pl.multiple_of((i % (BLOCKS // 2)) * block, block), block)
            output_out[spot, :] = low(mid[...] + out_sum[...])

        dh2 = dh_own[i] + dh_oth[...]
        e = dh2 * rows_ref[GAIN2 : GAIN2 + 1, :]
        inner = jnp.mean(e * mid[...], axis=1, keepdims=True)
        norm2_out[0:1, :] += jnp.sum(dh2 * mid[...] * r2, axis=0, keepdims=True)
        result = cot[rows, :].astype(f32) + r2 * e - mid[...] * (r2 * r2 * r2 * inner)
        dh_own[i] = result
        pltpu.make_async_copy(dh_own.at[i], dmid_out.at[rows, :], dmid_sem.at[i]).start()
        if not first:
            branch_wait()
        branch[...] = low(result)
        pltpu.make_async_copy(branch, branch_out.at[rows, :], branch_sem).start()

    def first_pass(i, carry):
        for t in range(3):

            @pl.when(i == t)
            def _():
                for w in range(1, 4):
                    pump(w, t)

        own_half(i)
        return carry

    def second_pass(i, carry):
        other_half(i)
        return carry

    lax.fori_loop(0, BLOCKS - 1, first_pass, 0)
    for w in range(1, 4):
        pump(w, 3)
    for w in range(1, 4):
        cast_in(w)
    other_half(0, True)
    own_half(BLOCKS - 1)
    lax.fori_loop(1, BLOCKS, second_pass, 0)

    count = 0
    for source, right, target in ((da, h2, grad_mg_out), (db, h2, grad_mu_out), (hid, cot, grad_md_out)):
        for n in range(3):
            where = pl.ds(n * third, third)
            slot = count % 2
            if count >= 2:
                pltpu.make_async_copy(stage.at[slot], stage.at[slot], stage_sem.at[slot]).wait()
            stage[slot] = dot(source[where, :], right[...], 1, 0)
            pltpu.make_async_copy(stage.at[slot], target.at[where, :], stage_sem.at[slot]).start()
            count += 1

    for slot in range(2):
        pltpu.make_async_copy(stage.at[slot], stage.at[slot], stage_sem.at[slot]).wait()
    branch_wait()
    for i in range(BLOCKS):
        pltpu.make_async_copy(dh_own.at[i], dh_own.at[i], dmid_sem.at[i]).wait()
    for i in range(BLOCKS - 2, BLOCKS):
        for copy in saves(i):
            copy.wait()
    for number, (source, target) in enumerate(saved):
        pltpu.make_async_copy(source, target, out_sem.at[number]).wait()
    for w in range(4):
        for t in range(steps):
            for d in range(2):
                hop(w, d, t).wait_send()
        for slot in range(1 + 2 * steps):
            last = slot > 0 and (slot - 1) // 2 == steps - 1
            part_ref = area(w, place, core, 0 if last else None)
            pltpu.make_async_copy(part_ref, part_ref, cs_sem.at[w, slot]).wait()
    for i in range(BLOCKS):
        exchange(i).wait_send()


def forward(tokens, vectors, tables, ws, cotangent):
    chips = lax.axis_size("dp") // 2
    length, depth = tokens.shape
    wq, wk, wv, wg, wo, mg, mu, md = ws
    units = wv.shape[0]
    heads = wq.shape[1] // KD
    block = length // BLOCKS
    f32, bf16 = jnp.float32, jnp.bfloat16
    vmem = pl.BlockSpec(memory_space=pltpu.VMEM)
    hbm = pl.BlockSpec(memory_space=pl.ANY)
    dma = lambda *shape: pltpu.SemaphoreType.DMA(shape)
    shape = jax.ShapeDtypeStruct
    tall = (units, length)
    steps = chips // 2
    outs = [
        (shape((length, depth), bf16), hbm),
        (shape((heads, length, KD), bf16), hbm),
        (shape((heads, length, KD), bf16), hbm),
        (shape(tall, bf16), hbm),
        (shape(tall, bf16), hbm),
        (shape(tall, bf16), hbm),
        (shape((8, length), f32), hbm),
        (shape(tall, bf16), hbm),
        (shape((length, depth), f32), hbm),
        (shape((length, depth), bf16), hbm),
        (shape((units, depth), f32), hbm),
        (shape((units, depth), f32), hbm),
        (shape((units, depth), f32), hbm),
        (shape((8, depth), f32), vmem),
        (shape((length // 2, depth), bf16), vmem),
        (shape((4, units, depth), f32), hbm),
    ]
    scratch = [
        pltpu.VMEM((4, units, depth), bf16),
        pltpu.VMEM((4, units, depth), bf16),
        pltpu.VMEM((length, depth), bf16),
        pltpu.VMEM((2, block, depth), bf16),
        pltpu.VMEM((2, heads, block, KD), bf16),
        pltpu.VMEM((heads, length, KD), bf16),
        pltpu.VMEM(tall, bf16),
        pltpu.VMEM((2, units, block), bf16),
        pltpu.VMEM((2, units, block), bf16),
        pltpu.VMEM((8, length), f32),
        pltpu.VMEM(tall, bf16),
        pltpu.VMEM((VD, block), f32),
        pltpu.VMEM((BLOCKS, units, block), f32),
        pltpu.VMEM((BLOCKS, units, block), f32),
        pltpu.VMEM((length, depth), bf16),
        pltpu.VMEM(tall, bf16),
        pltpu.VMEM(tall, bf16),
        pltpu.VMEM(tall, bf16),
        pltpu.VMEM((2, units // 3, depth), f32),
        pltpu.VMEM((block, depth), f32),
        pltpu.VMEM((BLOCKS, block, depth), f32),
        pltpu.VMEM((block, depth), f32),
        pltpu.VMEM((block, depth), f32),
        pltpu.VMEM((block, depth), bf16),
        pltpu.VMEM((units, 1), f32),
        pltpu.VMEM((units, 1), f32),
        dma(9),
        dma(4, 2),
        dma(4),
        dma(2),
        dma(BLOCKS),
        pltpu.SemaphoreType.DMA,
        dma(BLOCKS),
        dma(BLOCKS),
        dma(4),
        dma(4),
        dma(4, 2, steps),
        dma(4, 2, steps),
        dma(4, 1 + 2 * steps),
        dma(4, 1 + 2 * steps),
    ]
    return pl.pallas_call(
        functools.partial(forward_kernel, chips),
        out_shape=tuple(o for o, _ in outs),
        in_specs=[vmem] * 4 + [hbm] * 9,
        out_specs=tuple(s for _, s in outs),
        scratch_shapes=scratch,
        compiler_params=pltpu.CompilerParams(
            collective_id=1, has_side_effects=True, vmem_limit_bytes=VMEM_LIMIT
        ),
        cost_estimate=pl.CostEstimate(
            flops=40 * length * depth * units, bytes_accessed=80 * length * depth, transcendentals=0
        ),
    )(tokens, vectors, *tables, wq, wk, wv, wg, wo, mg, mu, md, cotangent)


def make_tables(length):
    half = KD // 2
    frequency = np.exp(-np.log(10000.0) * np.arange(half) / half)
    angles = np.arange(length)[:, None] * frequency[None, :]
    return jnp.asarray(np.cos(angles), jnp.float32), jnp.asarray(np.sin(angles), jnp.float32)


def pack_rows(arrays, width):
    rows = [jnp.pad(a.astype(jnp.float32), (0, width - a.shape[0])) for a in arrays]
    return jnp.pad(jnp.stack(rows), ((0, 8 - len(rows)), (0, 0)))


class Ring:
    def __init__(self, chips, quarters, own, sib, rcv, own_sem, sbs_sem, sbr_sem, rss_sem, rsr_sem):
        self.chips, self.quarters = chips, quarters
        self.index, self.tensor = lax.axis_index("dp"), lax.axis_index("tensor")
        self.core = self.index % 2
        place, _ = ring_place(self.index // 2, chips)
        self.place = place
        self.nexts = [
            {"dp": ring_chip((place + 1) % chips, chips) * 2 + self.core},
            {"dp": ring_chip((place + chips - 1) % chips, chips) * 2 + self.core},
        ]
        self.virtual = [place, (chips - place) % chips]
        self.sibling = {"dp": self.index + 1 - 2 * self.core}
        self.peer = {"tensor": 1 - self.tensor}
        self.offsets = [sum(quarters[:i]) for i in range(len(quarters))]
        self.own, self.sib, self.rcv = own, sib, rcv
        self.own_sem, self.sbs_sem, self.sbr_sem = own_sem, sbs_sem, sbr_sem
        self.rss_sem, self.rsr_sem = rss_sem, rsr_sem
        self.tokens = [(d, a) for a in range(len(quarters)) for d in range(2)]

    def window(self, which, d, chunk, rows):
        return (
            pl.ds(pl.multiple_of((which * 2 + d) * rows, 8), rows),
            pl.ds(pl.multiple_of(chunk * LANE, LANE), LANE),
        )

    def packed(self, a):
        return pl.ds(self.offsets[a], self.quarters[a])

    def chunk_at(self, d, order):
        return (self.virtual[d] + 2 * self.chips - 1 - order) % self.chips

    def own_copy(self, grads, d, a, order):
        return pltpu.make_async_copy(
            grads[a].at[self.window(self.core, d, self.chunk_at(d, order), self.quarters[a])],
            self.own.at[d, order, self.packed(a), :],
            self.own_sem.at[d, a, order],
        )

    def sib_copy(self, grads, d, a, order):
        return remote(
            grads[a].at[self.window(1 - self.core, d, self.chunk_at(d, order), self.quarters[a])],
            self.sib.at[d, order, self.packed(a), :],
            self.sbs_sem.at[d, a, order],
            self.sbr_sem.at[d, a, order],
            self.sibling,
        )

    def load(self, grads, order):
        for d, a in self.tokens:
            self.own_copy(grads, d, a, order).start()
            self.sib_copy(grads, d, a, order).start()

    def rs_copy(self, d, a, step):
        return remote(
            self.own.at[d, step, self.packed(a), :],
            self.rcv.at[d, step, self.packed(a), :],
            self.rss_sem.at[d, a, step],
            self.rsr_sem.at[d, a, step],
            self.nexts[d],
        )

    def total(self, grads, d, a, step, first=False):
        self.own_copy(grads, d, a, step).wait()
        self.sib_copy(grads, d, a, step).wait_recv()
        part = self.packed(a)
        value = self.own[d, step, part, :] + self.sib[d, step, part, :]
        if not first:
            self.rs_copy(d, a, step - 1).wait_recv()
            value = value + self.rcv[d, step - 1, part, :]
        self.own[d, step, part, :] = value

    def drain_ring(self):
        def ring_step(step, carry):
            for d, a in self.tokens:
                self.rs_copy(d, a, step).wait_send()
            return carry

        lax.fori_loop(0, self.chips - 1, ring_step, 0)

    def drain_pair(self, grads):
        def pair_step(order, carry):
            for d, a in self.tokens:
                self.sib_copy(grads, d, a, order).wait_send()
            return carry

        lax.fori_loop(0, self.chips, pair_step, 0)


class Spread:
    def __init__(self, ring, quarters, outs, ags_sem, agr_sem, cgs_sem, cgr_sem, loc_sem):
        self.ring, self.quarters, self.outs = ring, quarters, outs
        self.ags_sem, self.agr_sem, self.cgs_sem, self.cgr_sem, self.loc_sem = (
            ags_sem, agr_sem, cgs_sem, cgr_sem, loc_sem,
        )
        self.tokens = [(d, a) for a in range(len(quarters)) for d in range(2)]

    def part(self, which, d, a, step):
        ring = self.ring
        chunk = (ring.virtual[d] + 2 * ring.chips - step) % ring.chips
        return self.outs[a].at[ring.window(which, d, chunk, self.quarters[a])]

    def ring_copy(self, d, a, step, source=None):
        part = self.part(self.ring.core, d, a, step)
        return remote(
            part if source is None else source,
            part,
            self.ags_sem.at[d, a, step],
            self.agr_sem.at[d, a, step],
            self.ring.nexts[d],
        )

    def pair_copy(self, d, a, step, source=None):
        part = self.part(self.ring.core, d, a, step)
        return remote(
            part if source is None else source,
            part,
            self.cgs_sem.at[d, a, step],
            self.cgr_sem.at[d, a, step],
            self.ring.sibling,
        )

    def begin(self, d, a, source):
        self.ring_copy(d, a, 0, source).start()
        self.begin_pair(d, a, source)

    def begin_pair(self, d, a, source):
        self.pair_copy(d, a, 0, source).start()
        pltpu.make_async_copy(source, self.part(self.ring.core, d, a, 0), self.loc_sem.at[d, a]).start()

    def arrived(self, d, a, step):
        part = self.part(self.ring.core, d, a, step + 1)
        pltpu.make_async_copy(part, part, self.agr_sem.at[d, a, step]).wait()

    def finish_pair(self, step):
        for d, a in self.tokens:
            self.arrived(d, a, step)
            self.pair_copy(d, a, step + 1).start()

    def drain_pair(self):
        def pair_step(step, carry):
            for d, a in self.tokens:
                self.pair_copy(d, a, step).wait()
            return carry

        lax.fori_loop(0, self.ring.chips, pair_step, 0)
        for d, a in self.tokens:
            part = self.part(self.ring.core, d, a, 0)
            pltpu.make_async_copy(part, part, self.loc_sem.at[d, a]).wait()


def backward_kernel(
    chips,
    quarters,
    x_hbm,
    rows_ref,
    cos_ref,
    sin_ref,
    norm2_ref,
    branch_hbm,
    wo_hbm,
    g_hbm,
    nh_hbm,
    rstd_hbm,
    q_hbm,
    k_hbm,
    v_hbm,
    wq_hbm,
    wk_hbm,
    wv_hbm,
    wg_hbm,
    h1_hbm,
    gated_hbm,
    grad_mg,
    grad_mu,
    grad_md,
    part_out,
    grad_qk_out,
    grad_v_out,
    grad_g_out,
    grad_out_out,
    small_out,
    reduced_out,
    x,
    branch,
    wo,
    g,
    nh,
    rstd,
    q,
    k,
    v,
    wq,
    wk,
    wv,
    wg,
    h1,
    gated,
    acc_gain,
    acc_bias,
    dk,
    dv,
    dq,
    stage,
    column,
    own,
    sib,
    rcv,
    ggain_ref,
    gbias_ref,
    segc_ref,
    in_sem,
    stage_sem,
    column_sem,
    red_sem,
    own_sem,
    sbs_sem,
    sbr_sem,
    rss_sem,
    rsr_sem,
):
    ring = Ring(chips, quarters, own, sib, rcv, own_sem, sbs_sem, sbr_sem, rss_sem, rsr_sem)
    grads = (grad_mg, grad_mu, grad_md)
    f32 = jnp.float32
    heads = q.shape[0]
    length = h1.shape[0]
    units = v.shape[0]
    block = length // BLOCKS
    third = units // 3
    pairs = [
        (wo_hbm, wo), (branch_hbm, branch), (g_hbm, g), (nh_hbm, nh), (rstd_hbm, rstd),
        (q_hbm, q), (k_hbm, k), (v_hbm, v),
        (wq_hbm, wq), (wk_hbm, wk), (wv_hbm, wv), (wg_hbm, wg), (x_hbm, x), (h1_hbm, h1), (gated_hbm, gated),
    ]
    copies = [pltpu.make_async_copy(a, b, in_sem.at[n]) for n, (a, b) in enumerate(pairs)]
    for copy in copies[:5]:
        copy.start()
    greet([*ring.nexts, ring.sibling])
    ring.load(grads, 0)
    for copy in copies[5:8]:
        copy.start()
    ring.load(grads, 1)
    for copy in copies[8:]:
        copy.start()
    acc_gain[...] = jnp.zeros_like(acc_gain)
    acc_bias[...] = jnp.zeros_like(acc_bias)
    small_out[...] = jnp.zeros_like(small_out)
    for n in range(3):
        where = slice(n * third, (n + 1) * third)
        ggain_ref[where, :] = upright_part(rows_ref[GROUP_GAIN : GROUP_GAIN + 1, :], n * third, third)
        gbias_ref[where, :] = upright_part(rows_ref[GROUP_BIAS : GROUP_BIAS + 1, :], n * third, third)
    for n in range(BLOCKS):
        where = slice(n * block, (n + 1) * block)
        segc_ref[where, :] = upright(rows_ref[SEGMENT : SEGMENT + 1, where], block)
    for copy in copies[:5]:
        copy.wait()
    plan = [(step, a) for step in range(chips - 1) for a in range(len(quarters))]

    def pump(count=1):
        for _ in range(count):
            if plan:
                step, a = plan.pop(0)
                for d in range(2):
                    ring.total(grads, d, a, step, step == 0)
                    ring.rs_copy(d, a, step).start()
                if a == len(quarters) - 1 and step + 2 < chips:
                    ring.load(grads, step + 2)

    def fold(values):
        return values[:, :LANE] + values[:, LANE:]

    def gate_block(i):
        rows = pl.ds(i * block, block)
        for head in range(heads):
            tall = slice(head * VD, (head + 1) * VD)
            up = dot(wo[tall, :], branch[rows, :], 1, 1)
            gate = g[tall, rows].astype(f32)
            nhat = nh[tall, rows].astype(f32)
            sigmoid = 1.0 / (1.0 + jnp.exp(-gate))
            silu = gate * sigmoid
            dgn = up * silu
            acc_gain[tall, :] += fold(dgn * nhat)
            acc_bias[tall, :] += fold(dgn)
            gain = ggain_ref[tall, :]
            f = dgn * gain
            mean = jnp.mean(f, axis=0, keepdims=True)
            inner = jnp.mean(f * nhat, axis=0, keepdims=True)
            nh[tall, rows] = low((f - mean - nhat * inner) * rstd[head : head + 1, rows])
            gn = nhat * gain + gbias_ref[tall, :]
            g[tall, rows] = low(up * gn * (sigmoid + silu * (1.0 - sigmoid)))

    for i in range(BLOCKS):
        gate_block(i)
        pump()
    for copy in copies[5:8]:
        copy.wait()

    ahead = lax.broadcasted_iota(jnp.int32, (block, block), 0) - lax.broadcasted_iota(
        jnp.int32, (block, block), 1
    )

    def key_block(head, m):
        tall = slice(head * VD, (head + 1) * VD)
        cols = pl.ds(m * block, block)
        rate = rate_of(head, heads, ring.tensor)
        dk[...] = jnp.zeros_like(dk)
        dv[...] = jnp.zeros_like(dv)

        def tile(i, carry):
            rows = pl.ds(pl.multiple_of(i * block, block), block)
            gap = ahead + (i - m) * block
            seen = (segc_ref[rows, :] == rows_ref[SEGMENT : SEGMENT + 1, cols]) & (gap >= 0)
            decay = jnp.where(seen, jnp.exp(gap.astype(f32) * rate), 0.0)
            scores = low(dot(q[head, rows, :], k[head, cols, :], 1, 1) * decay)
            draw = low(dot(nh[tall, rows], v[tall, cols], 0, 0) * decay)
            dv[...] += dot(nh[tall, rows], scores, 1, 0)
            dk[...] += dot(draw, q[head, rows, :], 0, 0)
            more = dot(draw, k[head, cols, :], 1, 0)
            if m == 0:
                dq[rows, :] = more
            else:
                dq[rows, :] += more
            return carry

        if m == 0:
            lax.fori_loop(0, BLOCKS // 2, tile, 0)
            pump()
            lax.fori_loop(BLOCKS // 2, BLOCKS, tile, 0)
        else:
            lax.fori_loop(m, BLOCKS, tile, 0)
        v[tall, cols] = low(dv[...])
        k[head, cols, :] = low(turn(dk[...], cos_ref[cols, :], -sin_ref[cols, :]) * KD ** (-0.5))

    for head in range(heads):
        for m in range(BLOCKS):
            key_block(head, m)
            if m == BLOCKS - 1:
                q[head] = low(turn(dq[...], cos_ref[...], -sin_ref[...]))
            pump()

    for copy in copies[8:]:
        copy.wait()

    def stage_wait(slot):
        pltpu.make_async_copy(stage.at[slot], stage.at[slot], stage_sem.at[slot]).wait()

    key_parts = [(q, wq), (k, wk)]
    for i in range(BLOCKS):
        slot = i % 2
        rows = pl.ds(i * block, block)
        if i >= 2:
            stage_wait(slot)
        total = None
        for values, weights in key_parts:
            for head in range(heads):
                wide = slice(head * KD, (head + 1) * KD)
                more = dot(values[head, rows, :], weights[:, wide], 1, 1)
                total = more if total is None else total + more
        stage[slot, 0:block, :] = total
        stage[slot, 0:block, :] += dot(v[:, rows], wv[...], 0, 0)
        stage[slot, 0:block, :] += dot(g[:, rows], wg[...], 0, 0)
        xb = x[rows, :].astype(f32)
        r1 = lax.rsqrt(jnp.mean(xb * xb, axis=1, keepdims=True) + EPSILON)
        small_out[0:1, :] += jnp.sum(stage[slot, 0:block, :] * (xb * r1), axis=0, keepdims=True)
        pltpu.make_async_copy(stage.at[slot], part_out.at[i], stage_sem.at[slot]).start()
        pump()

    count = BLOCKS
    for source, right, target in ((v, h1, grad_v_out), (g, h1, grad_g_out), (gated, branch, grad_out_out)):
        for n in range(3):
            where = pl.ds(n * third, third)
            slot = count % 2
            stage_wait(slot)
            stage[slot] = dot(source[where, :], right[...], 1, 0)
            pltpu.make_async_copy(stage.at[slot], target.at[where, :], stage_sem.at[slot]).start()
            count += 1
            if n != 1:
                pump()

    for number, (values, head) in enumerate([(q, 0), (q, 1), (k, 0), (k, 1)][: 2 * heads]):
        if number:
            pltpu.make_async_copy(column, column, column_sem).wait()
        column[...] = dot(h1[...], values[head], 0, 0)
        pltpu.make_async_copy(column, grad_qk_out.at[:, pl.ds(number * KD, KD)], column_sem).start()
    pump(len(plan))

    ones = jnp.ones((8, LANE), jnp.bfloat16)

    def row_of(acc):
        whole = acc[...]
        high = low(whole)
        return dot(ones, high, 1, 1) + dot(ones, low(whole - high.astype(f32)), 1, 1)

    small_out[1:2, :] = norm2_ref[0:1, :]
    small_out[2:3, 0:units] = row_of(acc_gain)[0:1, :]
    small_out[3:4, 0:units] = row_of(acc_bias)[0:1, :]

    last = chips - 1
    for d, a in ring.tokens:
        ring.total(grads, d, a, last)
    reduced = pltpu.make_async_copy(own.at[:, last], reduced_out, red_sem)
    reduced.start()
    ring.drain_ring()
    ring.drain_pair(grads)
    reduced.wait()
    for slot in range(2):
        stage_wait(slot)
    pltpu.make_async_copy(column, column, column_sem).wait()


def backward(tokens, vectors, tables, norm2, saved, ws, mlp_grads):
    chips = lax.axis_size("dp") // 2
    length, depth = tokens.shape
    wq, wk, wv, wg, wo = ws
    h1, q, k, v, g, nh, rstd, gated, branch = saved
    units = wv.shape[0]
    heads = q.shape[0]
    block = length // BLOCKS
    quarters = tuple(a.shape[0] // 4 for a in mlp_grads)
    rows = sum(quarters)
    count = len(quarters)
    f32, bf16 = jnp.float32, jnp.bfloat16
    vmem = pl.BlockSpec(memory_space=pltpu.VMEM)
    hbm = pl.BlockSpec(memory_space=pl.ANY)
    dma = lambda *shape: pltpu.SemaphoreType.DMA(shape)
    shape = jax.ShapeDtypeStruct
    tall = (units, length)
    stage_rows = max(block, units // 3)
    outs = [
        (shape((BLOCKS, stage_rows, depth), f32), hbm),
        (shape((depth, 2 * heads * KD), f32), hbm),
        (shape((units, depth), f32), hbm),
        (shape((units, depth), f32), hbm),
        (shape((units, depth), f32), hbm),
        (shape((8, depth), f32), vmem),
        (shape((2, rows, LANE), f32), hbm),
    ]
    scratch = [
        pltpu.VMEM((length, depth), bf16),
        pltpu.VMEM((length, depth), bf16),
        pltpu.VMEM((units, depth), bf16),
        pltpu.VMEM(tall, bf16),
        pltpu.VMEM(tall, bf16),
        pltpu.VMEM((8, length), f32),
        pltpu.VMEM((heads, length, KD), bf16),
        pltpu.VMEM((heads, length, KD), bf16),
        pltpu.VMEM(tall, bf16),
        pltpu.VMEM((depth, heads * KD), bf16),
        pltpu.VMEM((depth, heads * KD), bf16),
        pltpu.VMEM((units, depth), bf16),
        pltpu.VMEM((units, depth), bf16),
        pltpu.VMEM((length, depth), bf16),
        pltpu.VMEM(tall, bf16),
        pltpu.VMEM((units, LANE), f32),
        pltpu.VMEM((units, LANE), f32),
        pltpu.VMEM((block, KD), f32),
        pltpu.VMEM((VD, block), f32),
        pltpu.VMEM((length, KD), f32),
        pltpu.VMEM((2, stage_rows, depth), f32),
        pltpu.VMEM((depth, KD), f32),
        pltpu.VMEM((2, chips, rows, LANE), f32),
        pltpu.VMEM((2, chips, rows, LANE), f32),
        pltpu.VMEM((2, chips - 1, rows, LANE), f32),
        pltpu.VMEM((units, 1), f32),
        pltpu.VMEM((units, 1), f32),
        pltpu.VMEM((length, 1), f32),
        dma(15),
        dma(2),
        pltpu.SemaphoreType.DMA,
        pltpu.SemaphoreType.DMA,
        dma(2, count, chips),
        dma(2, count, chips),
        dma(2, count, chips),
        dma(2, count, chips - 1),
        dma(2, count, chips - 1),
    ]
    return pl.pallas_call(
        functools.partial(backward_kernel, chips, quarters),
        out_shape=tuple(o for o, _ in outs),
        in_specs=[hbm] + [vmem] * 4 + [hbm] * 17,
        out_specs=tuple(s for _, s in outs),
        scratch_shapes=scratch,
        compiler_params=pltpu.CompilerParams(
            collective_id=2, has_side_effects=True, vmem_limit_bytes=VMEM_LIMIT
        ),
        cost_estimate=pl.CostEstimate(
            flops=20 * length * depth * units, bytes_accessed=80 * length * depth, transcendentals=0
        ),
    )(
        tokens, vectors, *tables, norm2,
        branch, wo, g, nh, rstd, q, k, v, wq, wk, wv, wg, h1, gated, *mlp_grads,
    )


def finish_kernel(
    chips,
    quarters,
    early_quarters,
    *refs,
):
    count, early_count = len(quarters), len(early_quarters)
    grads = refs[:count]
    part_hbm, small_ref, reduced_hbm, x_hbm, dmid_hbm, rows_ref = refs[count : count + 6]
    refs = refs[count + 6 :]
    outs, early_outs = refs[:count], refs[count : count + early_count]
    tokens_out, small_out, peer_hbm = refs[count + early_count : count + early_count + 3]
    (own, sib, rcv, sacc, sbuf, part, peer, x, dmid, result, in_sem, res_sem, hs_sem, hr_sem, ss_sem, sr_sem) = refs[
        count + early_count + 3 : count + early_count + 19
    ]
    sems = refs[count + early_count + 19 :]
    ring = Ring(chips, quarters, own, sib, rcv, *sems[:5])
    late = Spread(ring, quarters, outs, *sems[5:10])
    early = Spread(ring, early_quarters, early_outs, *sems[10:15])
    bits = (2 * chips).bit_length() - 1
    f32 = jnp.float32
    block = part.shape[0]
    greet(
        [*ring.nexts, ring.peer] + [{"dp": bit_partner(ring.index, bit)} for bit in range(bits)]
    )

    ring.load(grads, 0)

    def h_copy(i):
        here = part_hbm.at[i, pl.ds(0, block), :]
        return remote(here, peer_hbm.at[i], hs_sem.at[i], hr_sem.at[i], ring.peer)

    for i in range(BLOCKS):
        h_copy(i).start()
    ring.load(grads, 1)

    def s_copy(level):
        target = ring.peer if level == 0 else {"dp": bit_partner(ring.index, level - 1)}
        return remote(sacc.at[level], sbuf.at[level], ss_sem.at[level], sr_sem.at[level], target)

    def s_finish(level):
        s_copy(level).wait()
        got = sbuf[level]
        if level == 0:
            first = lax.broadcasted_iota(jnp.int32, got.shape, 0) == 0
            got = jnp.where(first, got, 0.0)
        sacc[level + 1] = sacc[level] + got

    sacc[0] = small_ref[...]

    def small_step(step):
        for level in range(bits + 2):

            @pl.when(step == level)
            def _():
                if level > 0:
                    s_finish(level - 1)
                if level <= bits:
                    s_copy(level).start()

    first_order = []
    for a in range(max(count, early_count)):
        first_order += [(ring, a)] * (a < count) + [(early, a)] * (a < early_count)
    second_order = [(late, a) for a in range(count)]

    def sent(entry, d, step):
        who, a = entry
        (who.rs_copy(d, a, step) if who is ring else who.ring_copy(d, a, step)).wait_send()

    def hold(order, before, position, d, step):
        if position >= WINDOW:
            sent(order[position - WINDOW], d, step)
        elif before is not None:
            last_order, last_step = before
            sent(last_order[len(last_order) - WINDOW + position], d, last_step)

    starts = [sum(early_quarters[:a]) for a in range(early_count)]

    def first_step(step, before):
        for position, (who, a) in enumerate(first_order):
            for d in range(2):
                if who is ring:
                    ring.total(grads, d, a, step, before is None)
                    hold(first_order, before, position, d, step)
                    ring.rs_copy(d, a, step).start()
                elif before is None:
                    source = reduced_hbm.at[d, pl.ds(starts[a], early_quarters[a]), :]
                    early.begin_pair(d, a, source)
                    hold(first_order, before, position, d, step)
                    early.ring_copy(d, a, 0, source).start()
                else:
                    early.arrived(d, a, step - 1)
                    early.pair_copy(d, a, step).start()
                    hold(first_order, before, position, d, step)
                    early.ring_copy(d, a, step).start()

    def rs_step(step, carry):
        first_step(step, (first_order, step - 1))

        @pl.when(step + 2 < chips)
        def _():
            ring.load(grads, step + 2)

        small_step(step)
        return carry

    first_step(0, None)
    ring.load(grads, 2)
    small_step(0)
    lax.fori_loop(1, chips - 1, rs_step, 0)
    for position, (_, a) in enumerate(second_order):
        for d in range(2):
            ring.total(grads, d, a, chips - 1)
            source = own.at[d, chips - 1, ring.packed(a), :]
            late.begin_pair(d, a, source)
            hold(second_order, (first_order, chips - 2), position, d, 0)
            late.ring_copy(d, a, 0, source).start()
    early.finish_pair(chips - 2)

    def token_block(i):
        rows = pl.ds(pl.multiple_of(i * block, block), block)
        h_copy(i).wait_recv()
        mine = part_hbm.at[i, pl.ds(0, block), :]
        loads = [
            pltpu.make_async_copy(mine, part, in_sem.at[0]),
            pltpu.make_async_copy(peer_hbm.at[i], peer, in_sem.at[1]),
            pltpu.make_async_copy(x_hbm.at[rows, :], x, in_sem.at[2]),
            pltpu.make_async_copy(dmid_hbm.at[rows, :], dmid, in_sem.at[3]),
        ]
        for copy in loads:
            copy.start()
        for copy in loads:
            copy.wait()
        xb = x[...].astype(f32)
        r1 = lax.rsqrt(jnp.mean(xb * xb, axis=1, keepdims=True) + EPSILON)
        e = (part[...] + peer[...]) * rows_ref[GAIN1 : GAIN1 + 1, :]
        inner = jnp.mean(e * xb, axis=1, keepdims=True)
        result[rows, :] = low(dmid[...] + r1 * e - xb * (r1 * r1 * r1 * inner))
        pltpu.make_async_copy(result.at[rows, :], tokens_out.at[rows, :], res_sem.at[i]).start()

    def ag_step(step, carry):
        for position, (_, a) in enumerate(second_order):
            for d in range(2):
                late.arrived(d, a, step - 1)
                late.pair_copy(d, a, step).start()
                hold(second_order, (second_order, step - 1), position, d, step)
                late.ring_copy(d, a, step).start()

        @pl.when(step <= BLOCKS)
        def _():
            token_block(step - 1)

        return carry

    lax.fori_loop(1, chips - 1, ag_step, 0)
    late.finish_pair(chips - 2)
    small_out[...] = sacc[bits + 1]
    for d in range(2):
        for entry in second_order[len(second_order) - WINDOW :]:
            sent(entry, d, chips - 2)
    ring.drain_pair(grads)
    early.drain_pair()
    late.drain_pair()
    for i in range(BLOCKS):
        h_copy(i).wait_send()
        pltpu.make_async_copy(result.at[pl.ds(0, block), :], result.at[pl.ds(0, block), :], res_sem.at[i]).wait()


def finish(grads, part, small, reduced, mlp_shapes, tokens, dmid, vectors):
    chips = lax.axis_size("dp") // 2
    length, depth = tokens.shape
    block = length // BLOCKS
    quarters = tuple(g.shape[0] // 4 for g in grads)
    early_quarters = tuple(g.shape[0] // 4 for g in mlp_shapes)
    rows = sum(quarters)
    count, early = len(quarters), len(early_quarters)
    bits = (2 * chips).bit_length() - 1
    f32, bf16 = jnp.float32, jnp.bfloat16
    vmem = pl.BlockSpec(memory_space=pltpu.VMEM)
    hbm = pl.BlockSpec(memory_space=pl.ANY)
    dma = lambda *shape: pltpu.SemaphoreType.DMA(shape)
    shape = jax.ShapeDtypeStruct
    outs = [(shape(g.shape, f32), hbm) for g in (*grads, *mlp_shapes)]
    outs += [
        (shape((length, depth), bf16), hbm),
        (shape(small.shape, f32), vmem),
        (shape((BLOCKS, block, depth), f32), hbm),
    ]
    scratch = [
        pltpu.VMEM((2, chips, rows, LANE), f32),
        pltpu.VMEM((2, chips, rows, LANE), f32),
        pltpu.VMEM((2, chips - 1, rows, LANE), f32),
        pltpu.VMEM((bits + 2, *small.shape), f32),
        pltpu.VMEM((bits + 1, *small.shape), f32),
        pltpu.VMEM((block, depth), f32),
        pltpu.VMEM((block, depth), f32),
        pltpu.VMEM((block, depth), bf16),
        pltpu.VMEM((block, depth), f32),
        pltpu.VMEM((length, depth), bf16),
        dma(4),
        dma(BLOCKS),
        dma(BLOCKS),
        dma(BLOCKS),
        dma(bits + 1),
        dma(bits + 1),
        dma(2, count, chips),
        dma(2, count, chips),
        dma(2, count, chips),
        dma(2, count, chips - 1),
        dma(2, count, chips - 1),
    ]
    for number in (count, early):
        scratch += [
            dma(2, number, chips - 1),
            dma(2, number, chips - 1),
            dma(2, number, chips),
            dma(2, number, chips),
            dma(2, number),
        ]
    return pl.pallas_call(
        functools.partial(finish_kernel, chips, quarters, early_quarters),
        out_shape=tuple(o for o, _ in outs),
        in_specs=[hbm] * (count + 1) + [vmem] + [hbm] * 3 + [vmem],
        out_specs=tuple(s for _, s in outs),
        scratch_shapes=scratch,
        compiler_params=pltpu.CompilerParams(
            collective_id=3, has_side_effects=True, vmem_limit_bytes=50 * 1024 * 1024
        ),
        cost_estimate=pl.CostEstimate(
            flops=20 * rows * depth, bytes_accessed=80 * rows * depth, transcendentals=0
        ),
    )(*grads, part, small, reduced, tokens, dmid, vectors)

def swap(array):
    return lax.ppermute(array, "tensor", [(0, 1), (1, 0)])


def other_half(arrays, zero):
    dp, index = lax.axis_size("dp"), lax.axis_index("dp")
    rows = arrays[0].shape[0]
    count = len(arrays)
    if dp % count == 0 and rows % (8 * (dp // count)) == 0:
        share = rows * count // dp
        each = dp // count
        inside = (index % each) * share
        own = [lax.dynamic_slice_in_dim(a, inside, share, 0) for a in arrays]
        part = own[0]
        for number in range(1, count):
            part = jnp.where(index // each == number, own[number], part)
    else:
        share = -(-rows * count // (8 * dp)) * 8
        whole = jnp.concatenate(arrays, axis=0)
        whole = jnp.pad(whole, ((0, share * dp - rows * count), (0, 0)))
        part = lax.dynamic_slice_in_dim(whole, index * share, share, 0)
    got = lax.all_gather(swap(part.astype(jnp.float32)), "dp", axis=0, tiled=True)
    got = low(got + zero)
    return [got[number * rows : (number + 1) * rows] for number in range(count)]


def plain_body(
    tokens,
    segment,
    norm1_gain,
    w_query,
    w_key,
    w_value,
    w_gate,
    group_gain,
    group_bias,
    w_out,
    norm2_gain,
    w_mlp_gate,
    w_mlp_up,
    w_mlp_down,
    cotangent,
):
    length, depth = tokens.shape
    heads = w_query.shape[1] // KD
    block = length // BLOCKS
    tensor = lax.axis_index("tensor")
    f32 = jnp.float32
    zero = jnp.minimum(segment[0], 0).astype(f32)
    value_t, gate_t, mg_t, mu_t = w_value.T, w_gate.T, w_mlp_gate.T, w_mlp_up.T
    mg_o, mu_o, md_o, wo_o = other_half([mg_t, mu_t, w_mlp_down, w_out], zero)
    x = tokens.astype(f32)
    gain1 = norm1_gain.astype(f32)
    gain2 = norm2_gain.astype(f32)
    ggain = group_gain.astype(f32)[:, None]
    gbias = group_bias.astype(f32)[:, None]
    r1 = lax.rsqrt(jnp.mean(x * x, axis=1, keepdims=True) + EPSILON)
    h1 = low(x * r1 * gain1)
    half = KD // 2
    frequency = jnp.exp(-jnp.log(10000.0) * jnp.arange(half, dtype=f32) / half)
    angles = jnp.arange(length, dtype=f32)[:, None] * frequency[None, :]
    cosine, sine = jnp.cos(angles), jnp.sin(angles)
    positions = jnp.arange(length, dtype=jnp.int32)
    visible = (positions[:, None] >= positions[None, :]) & (segment[:, None] == segment[None, :])
    offsets = jnp.maximum(positions[:, None] - positions[None, :], 0).astype(f32)

    def decay(head, rows, columns):
        order = (tensor * heads + head).astype(f32)
        rate = jnp.log1p(-jnp.exp2(-5.0 - order))
        return jnp.where(visible[rows, columns], jnp.exp(offsets[rows, columns] * rate), 0.0)

    queries = [[] for _ in range(heads)]
    keys = [[] for _ in range(heads)]
    values = [[] for _ in range(heads)]
    gates = [[] for _ in range(heads)]
    nhats = [[] for _ in range(heads)]
    spreads = [[] for _ in range(heads)]
    gated_blocks, received = [], []
    for number in range(BLOCKS):
        rows = slice(number * block, (number + 1) * block)
        seen = slice(0, (number + 1) * block)
        own = []
        for head in range(heads):
            wide = slice(head * KD, (head + 1) * KD)
            tall = slice(head * VD, (head + 1) * VD)
            q = low(turn(dot(h1[rows], w_query[:, wide], 1, 0), cosine[rows], sine[rows]))
            k = turn(dot(h1[rows], w_key[:, wide], 1, 0), cosine[rows], sine[rows])
            queries[head].append(q)
            keys[head].append(low(k * KD ** (-0.5)))
            values[head].append(low(dot(value_t[tall], h1[rows], 1, 1)))
            g = dot(gate_t[tall], h1[rows], 1, 1)
            gates[head].append(g)
            scores = dot(q, jnp.concatenate(keys[head], axis=0), 1, 1)
            scores = low(scores * decay(head, rows, seen))
            ret = dot(jnp.concatenate(values[head], axis=1), scores, 1, 1)
            centred = ret - jnp.mean(ret, axis=0, keepdims=True)
            scale = lax.rsqrt(jnp.mean(centred * centred, axis=0, keepdims=True) + GROUP_EPSILON)
            nhat = centred * scale
            nhats[head].append(nhat)
            spreads[head].append(scale)
            own.append(low(jax.nn.silu(g) * (nhat * ggain[tall] + gbias[tall])))
        gated_blocks.append(jnp.concatenate(own, axis=0))
        received.append(low(swap(gated_blocks[-1].astype(f32)) + zero))

    mids, h2s, r2s, hidden_own, hidden_oth, das, dbs, dmids = [], [], [], [], [], [], [], []
    norm2_rows = []
    for number in range(BLOCKS):
        rows = slice(number * block, (number + 1) * block)
        mid = x[rows] + (dot(gated_blocks[number], w_out, 0, 0) + dot(received[number], wo_o, 0, 0))
        r2 = lax.rsqrt(jnp.mean(mid * mid, axis=1, keepdims=True) + EPSILON)
        h2 = low(mid * r2 * gain2)
        cot = cotangent[rows]

        def mlp(gate_w, up_w, down_w):
            a, b = dot(gate_w, h2, 1, 1), dot(up_w, h2, 1, 1)
            hidden, pull = jax.vjp(lambda s, t: jax.nn.gelu(s) * t, a, b)
            da, db = pull(dot(down_w, cot, 1, 1))
            da, db = low(da), low(db)
            return low(hidden), da, db, dot(da, gate_w, 0, 0) + dot(db, up_w, 0, 0)

        own_hidden, da, db, part = mlp(mg_t, mu_t, w_mlp_down)
        oth_hidden, _, _, more = mlp(mg_o, mu_o, md_o)
        dh2 = part + more
        e = dh2 * gain2
        dmid = cot.astype(f32) + r2 * e - mid * (r2 * r2 * r2) * jnp.mean(e * mid, axis=1, keepdims=True)
        norm2_rows.append(jnp.sum(dh2 * mid * r2, axis=0))
        for where, value in zip(
            (mids, h2s, hidden_own, hidden_oth, das, dbs, dmids),
            (mid, h2, own_hidden, oth_hidden, da, db, dmid),
        ):
            where.append(value)
    grad_norm2 = sum(norm2_rows)
    mid = jnp.concatenate(mids, axis=0)
    h2 = jnp.concatenate(h2s, axis=0)
    hidden = jnp.concatenate(hidden_own, axis=1)
    hidden_o = jnp.concatenate(hidden_oth, axis=1)
    dmid = jnp.concatenate(dmids, axis=0)
    own_rows = length // lax.axis_size("tensor")
    place = tensor * own_rows
    output = low(
        lax.dynamic_slice_in_dim(mid, place, own_rows, 0)
        + dot(lax.dynamic_slice_in_dim(hidden, place, own_rows, 1), w_mlp_down, 0, 0)
        + dot(lax.dynamic_slice_in_dim(hidden_o, place, own_rows, 1), md_o, 0, 0)
    )
    grad_mg = dot(jnp.concatenate(das, axis=1), h2, 1, 0)
    grad_mu = dot(jnp.concatenate(dbs, axis=1), h2, 1, 0)
    grad_md = dot(hidden, cotangent, 1, 0)

    branch = low(dmid)
    gated = jnp.concatenate(gated_blocks, axis=1)
    grad_out = dot(gated, branch, 1, 0)
    dgated = dot(w_out, branch, 1, 1)
    dqs, dks, dvs, dgs, ggains, gbiases = [], [], [], [], [], []
    everything = slice(0, length)
    for head in range(heads):
        tall = slice(head * VD, (head + 1) * VD)
        g = jnp.concatenate(gates[head], axis=1)
        nhat = jnp.concatenate(nhats[head], axis=1)
        spread = jnp.concatenate(spreads[head], axis=1)
        q = jnp.concatenate(queries[head], axis=0)
        k = jnp.concatenate(keys[head], axis=0)
        v = jnp.concatenate(values[head], axis=1)
        sigmoid = jax.nn.sigmoid(g)
        silu = g * sigmoid
        up = dgated[tall]
        dgn = up * silu
        ggains.append(jnp.sum(dgn * nhat, axis=1))
        gbiases.append(jnp.sum(dgn, axis=1))
        f = dgn * ggain[tall]
        dret = (
            f - jnp.mean(f, axis=0, keepdims=True) - nhat * jnp.mean(f * nhat, axis=0, keepdims=True)
        ) * spread
        dret = low(dret)
        gn = nhat * ggain[tall] + gbias[tall]
        dgs.append(low(up * gn * (sigmoid + silu * (1.0 - sigmoid))))
        table = decay(head, everything, everything)
        scores = low(dot(q, k, 1, 1) * table)
        draw = low(dot(dret, v, 0, 0) * table)
        dvs.append(low(dot(dret, scores, 1, 0)))
        dqs.append(low(turn(dot(draw, k, 1, 0), cosine, -sine)))
        dks.append(low(turn(dot(draw, q, 0, 0), cosine, -sine) * KD ** (-0.5)))
    dv = jnp.concatenate(dvs, axis=0)
    dg = jnp.concatenate(dgs, axis=0)
    dq = jnp.concatenate(dqs, axis=1)
    dk = jnp.concatenate(dks, axis=1)
    partial_in = dot(dq, w_query, 1, 1) + dot(dk, w_key, 1, 1) + dot(dv, value_t, 0, 0) + dot(dg, gate_t, 0, 0)
    grad_norm1 = jnp.sum(partial_in * x * r1, axis=0)
    grad_qk = dot(h1, jnp.concatenate([dq, dk], axis=1), 0, 0)
    grad_v = dot(dv, h1, 1, 0)
    grad_g = dot(dg, h1, 1, 0)

    units = w_value.shape[1]
    small = jnp.stack(
        [
            grad_norm1,
            grad_norm2,
            jnp.pad(jnp.concatenate(ggains), (0, depth - units)),
            jnp.pad(jnp.concatenate(gbiases), (0, depth - units)),
        ]
    )
    small = jnp.pad(small, ((0, 4), (0, 0)))
    grads = lax.psum((grad_qk, grad_v, grad_g, grad_out, grad_mg, grad_mu, grad_md), "dp")
    peer = swap(partial_in)
    small = lax.psum(small.at[0].set(lax.psum(small[0], "tensor")), "dp")
    grad_qk, grad_v, grad_g, grad_out, grad_mg, grad_mu, grad_md = grads
    e1 = (partial_in + peer) * gain1
    grad_tokens = low(dmid + r1 * e1 - x * (r1 * r1 * r1) * jnp.mean(e1 * x, axis=1, keepdims=True))
    key_width = w_query.shape[1]
    return (
        output,
        grad_tokens,
        small[0],
        grad_qk[:, :key_width],
        grad_qk[:, key_width:],
        grad_v.T,
        grad_g.T,
        small[2, :units],
        small[3, :units],
        grad_out,
        small[1],
        grad_mg.T,
        grad_mu.T,
        grad_md,
    )


def body(
    tokens,
    segment,
    norm1_gain,
    w_query,
    w_key,
    w_value,
    w_gate,
    group_gain,
    group_bias,
    w_out,
    norm2_gain,
    w_mlp_gate,
    w_mlp_up,
    w_mlp_down,
    cotangent,
):
    length, depth = tokens.shape
    if depth % (LANE * (lax.axis_size("dp") // 2)):
        return plain_body(
            tokens, segment, norm1_gain, w_query, w_key, w_value, w_gate, group_gain, group_bias, w_out,
            norm2_gain, w_mlp_gate, w_mlp_up, w_mlp_down, cotangent,
        )
    value_t, gate_t, mg_t, mu_t = w_value.T, w_gate.T, w_mlp_gate.T, w_mlp_up.T
    tables = make_tables(length)
    vectors = pack_rows((norm1_gain, norm2_gain, group_gain, group_bias, segment), depth)
    (h1, qs, ks, vs, g, nhat, rstd, gated, dmid, branch, grad_mg, grad_mu, grad_md, norm2, output, _) = forward(
        tokens,
        vectors,
        tables,
        (w_query, w_key, value_t, gate_t, w_out, mg_t, mu_t, w_mlp_down),
        cotangent,
    )
    part, grad_qk, grad_v, grad_g, grad_out, small, reduced = backward(
        tokens,
        vectors,
        tables,
        norm2,
        (h1, qs, ks, vs, g, nhat, rstd, gated, branch),
        (w_query, w_key, value_t, gate_t, w_out),
        (grad_mg, grad_mu, grad_md),
    )
    (grad_qk, grad_v, grad_g, grad_out, grad_mg, grad_mu, grad_md, grad_tokens, small, _) = finish(
        (grad_qk, grad_v, grad_g, grad_out),
        part,
        small,
        reduced,
        (grad_mg, grad_mu, grad_md),
        tokens,
        dmid,
        vectors,
    )
    units = w_value.shape[1]
    key_width = w_query.shape[1]
    return (
        output,
        grad_tokens,
        small[0],
        grad_qk[:, :key_width],
        grad_qk[:, key_width:],
        grad_v.T,
        grad_g.T,
        small[2, :units],
        small[3, :units],
        grad_out,
        small[1],
        grad_mg.T,
        grad_mu.T,
        grad_md,
    )


def solution(mesh):
    placed = (
        P("dp", None),
        P("dp"),
        P(),
        P(None, "tensor"),
        P(None, "tensor"),
        P(None, "tensor"),
        P(None, "tensor"),
        P("tensor"),
        P("tensor"),
        P("tensor", None),
        P(),
        P(None, "tensor"),
        P(None, "tensor"),
        P("tensor", None),
        P("dp", None),
    )
    return jax.shard_map(
        body,
        mesh=mesh,
        in_specs=placed,
        out_specs=(
            P(("dp", "tensor"), None),
            P("dp", None),
            P(),
            P(None, "tensor"),
            P(None, "tensor"),
            P(None, "tensor"),
            P(None, "tensor"),
            P("tensor"),
            P("tensor"),
            P("tensor", None),
            P(),
            P(None, "tensor"),
            P(None, "tensor"),
            P("tensor", None),
        ),
        check_vma=False,
    )
```

```python
import functools
import math

import jax
import jax.numpy as jnp
import numpy as np
from jax import lax
from jax.experimental import pallas as pl
from jax.experimental.pallas import tpu as pltpu
from jax.sharding import PartitionSpec as P

KD = 256
VD = 432
LANE = 128
MESH = pl.DeviceIdType.MESH
DELIVER = 4
PIECES = 4
VMEM_LIMIT = 63 * 1024 * 1024


EPSILON = 1e-06
GROUP_EPSILON = 0.25


def ring_place(chip, chips):
    line = chips // 2
    x = chip % 2
    z = chip // 2
    return z + x * (chips - 1 - 2 * z), line


def ring_chip(place, chips):
    line = chips // 2
    x = place // line
    z = place + x * (chips - 1 - 2 * place)
    return z * 2 + x


def bit_partner(index, bit):
    step = 1 << bit
    return index + (1 - 2 * ((index // step) % 2)) * step


BLOCKS = 4
GELU_A = math.sqrt(2.0 / math.pi)
GELU_B = 0.044715


def dot(left, right, left_dim, right_dim):
    return lax.dot_general(
        left, right, (((left_dim,), (right_dim,)), ((), ())), preferred_element_type=jnp.float32
    )


def low(array):
    return array.astype(jnp.bfloat16)


def turn(vectors, cosine, sine):
    half = vectors.shape[1] // 2
    lower, upper = vectors[:, :half], vectors[:, half:]
    return jnp.concatenate([lower * cosine - upper * sine, upper * cosine + lower * sine], axis=1)


def remote(source, target, send, recv, device):
    return pltpu.make_async_remote_copy(
        source, target, send, recv, device_id=device, device_id_type=MESH
    )


def rate_of(head, heads, tensor):
    rates = [math.log1p(-(2.0 ** (-5 - order))) for order in range(2 * heads)]
    return jnp.where(tensor == 0, rates[head], rates[heads + head]).astype(jnp.float32)


def upright(row, size):
    diagonal = lax.broadcasted_iota(jnp.int32, (size, size), 0) == lax.broadcasted_iota(
        jnp.int32, (size, size), 1
    )
    return jnp.sum(jnp.where(diagonal, row, 0.0), axis=1, keepdims=True)


def upright_part(row, start, size):
    shape = (size, row.shape[1])
    chosen = lax.broadcasted_iota(jnp.int32, shape, 0) + start == lax.broadcasted_iota(jnp.int32, shape, 1)
    return jnp.sum(jnp.where(chosen, row, 0.0), axis=1, keepdims=True)


GAIN1, GAIN2, GROUP_GAIN, GROUP_BIAS, SEGMENT = range(5)


def greet(devices):
    barrier = pltpu.get_barrier_semaphore()
    for device in devices:
        pl.semaphore_signal(barrier, inc=1, device_id=device, device_id_type=MESH)
    pl.semaphore_wait(barrier, len(devices))


def mlp_part(gate_w, up_w, down_w, h2, cot, tall, rows):
    a = dot(gate_w[tall, :], h2[rows, :], 1, 1)
    b = dot(up_w[tall, :], h2[rows, :], 1, 1)
    dhidden = dot(down_w[tall, :], cot[rows, :], 1, 1)
    square = a * a
    t = jnp.tanh(GELU_A * a * (1.0 + GELU_B * square))
    gelu = 0.5 * a * (1.0 + t)
    slope = 0.5 * (1.0 + t) + 0.5 * a * (1.0 - t * t) * (GELU_A * (1.0 + 3.0 * GELU_B * square))
    dga = low(dhidden * b * slope)
    dup = low(dhidden * gelu)
    more = dot(dga, gate_w[tall, :], 0, 0) + dot(dup, up_w[tall, :], 0, 0)
    return low(gelu * b), dga, dup, more


def forward_kernel(
    chips,
    x_ref,
    rows_ref,
    cos_ref,
    sin_ref,
    wq_hbm,
    wk_hbm,
    wv_hbm,
    wg_hbm,
    wo_ref,
    mg_ref,
    mu_ref,
    md_ref,
    cot_ref,
    h1_out,
    q_out,
    k_out,
    v_out,
    g_out,
    nh_out,
    rstd_out,
    gated_out,
    mid_out,
    dh_out,
    h2_out,
    hid_out,
    grad_mg_out,
    grad_mu_out,
    grad_md_out,
    gath_out,
    weights,
    others,
    cot,
    h1,
    q,
    k,
    v,
    g,
    nh,
    rstd,
    gated,
    acc,
    gsend,
    grecv,
    h2,
    hid,
    da,
    db,
    mid,
    dh_own,
    sums,
    ggain_ref,
    gbias_ref,
    in_sem,
    save_sem,
    out_sem,
    stage_sem,
    mid_sem,
    dh_sem,
    sum_sem,
    xs_sem,
    xr_sem,
    ys_sem,
    yr_sem,
    gs_sem,
    gr_sem,
    cs_sem,
    cr_sem,
):
    index, tensor = lax.axis_index("dp"), lax.axis_index("tensor")
    core = index % 2
    place, _ = ring_place(index // 2, chips)
    nexts = [
        {"dp": ring_chip((place + 1) % chips, chips) * 2 + core},
        {"dp": ring_chip((place + chips - 1) % chips, chips) * 2 + core},
    ]
    sibling, peer = {"dp": index + 1 - 2 * core}, {"tensor": 1 - tensor}
    heads = q.shape[1]
    units, length = v.shape
    block = length // BLOCKS
    third = units // 3
    f32 = jnp.float32

    for number, source in enumerate((wo_ref, mg_ref, mu_ref, md_ref)):
        pltpu.make_async_copy(source, weights.at[number], in_sem.at[number]).start()
    wv_ref, wg_ref = hid, da
    key_width = wq_hbm.shape[1]
    early = [
        pltpu.make_async_copy(wq_hbm, h2.at[:, pl.ds(0, key_width)], in_sem.at[5]),
        pltpu.make_async_copy(wk_hbm, h2.at[:, pl.ds(key_width, key_width)], in_sem.at[6]),
        pltpu.make_async_copy(wv_hbm, wv_ref, in_sem.at[7]),
        pltpu.make_async_copy(wg_hbm, wg_ref, in_sem.at[8]),
    ]
    for copy in early:
        copy.start()
    pltpu.make_async_copy(cot_ref, cot, in_sem.at[4]).start()
    greet([*nexts, sibling, peer])

    rows_slice = units // 2
    half_slice = rows_slice // 2

    def area(w, where, which, half=None):
        start = which * rows_slice + (0 if half is None else half * half_slice)
        size = rows_slice if half is None else half_slice
        return gath_out.at[
            w,
            pl.ds(pl.multiple_of(start, 8), size),
            pl.ds(pl.multiple_of(where * LANE, LANE), LANE),
        ]

    def slice_spot(w):
        return gsend.at[
            BLOCKS - 1,
            pl.ds((w % 2) * rows_slice, rows_slice),
            pl.ds((w // 2) * LANE, LANE),
        ]

    def y_copy(w):
        return remote(slice_spot(w), area(w, place, core), ys_sem.at[w], yr_sem.at[w], peer)

    def hop(w, d, t):
        where = (place - t + chips) % chips if d == 0 else (place + t) % chips
        part = area(w, where, core, d if t == chips // 2 - 1 else None)
        return remote(part, part, gs_sem.at[w, d, t], gr_sem.at[w, d, t], nexts[d])

    def arrived(w, d, t):
        where = (place - t - 1 + chips) % chips if d == 0 else (place + t + 1) % chips
        part = area(w, where, core, d if t == chips // 2 - 1 else None)
        pltpu.make_async_copy(part, part, gr_sem.at[w, d, t]).wait()
        return where

    def share(w, slot, where, half=None):
        part = area(w, where, core, half)
        remote(part, part, cs_sem.at[w, slot], cr_sem.at[w, slot], sibling).start()

    steps = chips // 2

    def begin(w):
        y_copy(w).wait_recv()
        for d in range(2):
            hop(w, d, 0).start()
        share(w, 0, place)

    def pump(w, t):
        for d in range(2):
            where = arrived(w, d, t)
            if t < steps - 1:
                hop(w, d, t + 1).start()
            share(w, 1 + 2 * t + d, where, d if t == steps - 1 else None)

    for number in range(4):
        pltpu.make_async_copy(wo_ref, weights.at[number], in_sem.at[number]).wait()
        slice_spot(number)[...] = weights[
            number,
            pl.ds(pl.multiple_of(core * rows_slice, 16), rows_slice),
            pl.ds(pl.multiple_of(place * LANE, LANE), LANE),
        ].astype(f32)
        y_copy(number).start()

    def exchange(i):
        return remote(gsend.at[i], grecv.at[i], xs_sem.at[i], xr_sem.at[i], peer)

    ahead = lax.broadcasted_iota(jnp.int32, (block, block), 0) - lax.broadcasted_iota(
        jnp.int32, (block, block), 1
    )

    def saves(i):
        slot = i % 2
        rows = pl.ds(pl.multiple_of(i * block, block), block)
        pairs = (
            (h1.at[slot], h1_out.at[rows, :]),
            (q.at[slot], q_out.at[:, rows, :]),
            (g.at[slot], g_out.at[:, rows]),
            (nh.at[slot], nh_out.at[:, rows]),
        )
        return [
            pltpu.make_async_copy(source, target, save_sem.at[number, slot])
            for number, (source, target) in enumerate(pairs)
        ]

    def attention(i, carry):
        rows = pl.ds(pl.multiple_of(i * block, block), block)
        slot = i % 2

        @pl.when(i >= 2)
        def _():
            for copy in saves(i - 2):
                copy.wait()

        xb = x_ref[rows, :].astype(f32)
        r1 = lax.rsqrt(jnp.mean(xb * xb, axis=1, keepdims=True) + EPSILON)
        h1[slot] = low(xb * r1 * rows_ref[GAIN1 : GAIN1 + 1, :])
        cosine, sine = cos_ref[rows, :], sin_ref[rows, :]
        for head in range(heads):
            wide = slice(head * KD, (head + 1) * KD)
            q[slot, head] = low(turn(dot(h1[slot], h2[:, wide], 1, 0), cosine, sine))
            wide = slice(key_width + head * KD, key_width + (head + 1) * KD)
            k[head, rows, :] = low(turn(dot(h1[slot], h2[:, wide], 1, 0), cosine, sine) * KD ** (-0.5))
        v[:, rows] = low(dot(wv_ref[...], h1[slot], 1, 1))

        @pl.when(i == BLOCKS - 1)
        def _():
            for w in range(4):
                y_copy(w).wait_send()

        segc = upright(rows_ref[SEGMENT : SEGMENT + 1, rows], block)
        for head in range(heads):
            tall = slice(head * VD, (head + 1) * VD)
            rate = rate_of(head, heads, tensor)
            acc[...] = jnp.zeros_like(acc)

            def tile(m, carry):
                cols = pl.ds(pl.multiple_of(m * block, block), block)
                s = dot(q[slot, head], k[head, cols, :], 1, 1)
                gap = ahead + (i - m) * block
                seen = (segc == rows_ref[SEGMENT : SEGMENT + 1, cols]) & (gap >= 0)
                s = jnp.where(seen, s * jnp.exp(gap.astype(f32) * rate), 0.0)
                acc[...] += dot(v[tall, cols], low(s), 1, 1)
                return carry

            lax.fori_loop(0, i + 1, tile, 0)
            ret = acc[...]
            centred = ret - jnp.mean(ret, axis=0, keepdims=True)
            scale = lax.rsqrt(jnp.mean(centred * centred, axis=0, keepdims=True) + GROUP_EPSILON)
            nhat = centred * scale
            nh[slot, tall, :] = low(nhat)
            rstd[head : head + 1, rows] = scale
            gate = dot(wg_ref[tall, :], h1[slot], 1, 1)
            g[slot, tall, :] = low(gate)
            gn = nhat * ggain_ref[tall, :] + gbias_ref[tall, :]
            out = low(gate / (1.0 + jnp.exp(-gate)) * gn)
            gated[tall, rows] = out
            gsend[i, tall, :] = out.astype(f32)
        exchange(i).start()
        for copy in saves(i):
            copy.start()

        @pl.when(i == 0)
        def _():
            begin(0)

        @pl.when(i == 1)
        def _():
            pump(0, 0)
            for w in range(1, 4):
                begin(w)

        @pl.when(i == 2)
        def _():
            pump(0, 1)

        return carry

    rstd[...] = jnp.zeros_like(rstd)
    for n in range(3):
        where = slice(n * third, (n + 1) * third)
        ggain_ref[where, :] = upright_part(rows_ref[GROUP_GAIN : GROUP_GAIN + 1, :], n * third, third)
        gbias_ref[where, :] = upright_part(rows_ref[GROUP_BIAS : GROUP_BIAS + 1, :], n * third, third)
    for copy in early:
        copy.wait()
    lax.fori_loop(0, BLOCKS, attention, 0)
    for i in range(BLOCKS - 2, BLOCKS):
        for copy in saves(i):
            copy.wait()
    saved = [(k, k_out), (v, v_out), (rstd, rstd_out), (gated, gated_out)]
    for number, (source, target) in enumerate(saved):
        pltpu.make_async_copy(source, target, out_sem.at[number]).start()

    def cast_ready(w):
        for slot in range(1 + 2 * steps):
            t = (slot - 1) // 2
            d = (slot - 1) % 2
            if slot == 0:
                where = place
            else:
                where = (place - t - 1 + chips) % chips if d == 0 else (place + t + 1) % chips
            part = area(w, where, 1 - core, d if slot > 0 and t == steps - 1 else None)
            pltpu.make_async_copy(part, part, cr_sem.at[w, slot]).wait()

    def stage(number):
        return sums.at[0, pl.ds((number % 2) * third, third), :]

    def cast_in(ws):
        pieces = [(w, n) for w in ws for n in range(3)]

        def piece(number):
            w, n = pieces[number]
            return pltpu.make_async_copy(
                gath_out.at[w, pl.ds(n * third, third), :], stage(number), stage_sem.at[number % 2]
            )

        cast_ready(ws[0])
        piece(0).start()
        for number, (w, n) in enumerate(pieces):
            if number + 1 < len(pieces):
                if pieces[number + 1][1] == 0:
                    cast_ready(pieces[number + 1][0])
                piece(number + 1).start()
            piece(number).wait()
            others[n * third : (n + 1) * third, :] = low(stage(number)[...])

    pump(0, 2)
    pump(0, 3)
    cast_in([0])
    pltpu.make_async_copy(cot_ref, cot, in_sem.at[4]).wait()
    part = units // 2

    def mid_copy(i):
        rows = pl.ds(pl.multiple_of(i * block, block), block)
        return pltpu.make_async_copy(mid.at[i % 2], mid_out.at[rows, :], mid_sem.at[i % 2])

    def dh_copy(i):
        rows = pl.ds(pl.multiple_of(i * block, block), block)
        return pltpu.make_async_copy(dh_own.at[i % 2], dh_out.at[rows, :], dh_sem.at[i % 2])

    def own_half(i):
        rows = pl.ds(pl.multiple_of(i * block, block), block)
        slot = i % 2

        @pl.when(i >= 2)
        def _():
            mid_copy(i - 2).wait()
            dh_copy(i - 2).wait()

        exchange(i).wait_recv()
        mid[slot] = x_ref[rows, :].astype(f32) + (
            dot(gated[:, rows], weights[0], 0, 0) + dot(low(grecv[i]), others[...], 0, 0)
        )
        mid_copy(i).start()
        r2 = lax.rsqrt(jnp.mean(mid[slot] * mid[slot], axis=1, keepdims=True) + EPSILON)
        h2[rows, :] = low(mid[slot] * r2 * rows_ref[GAIN2 : GAIN2 + 1, :])
        for f in range(2):
            tall = slice(f * part, (f + 1) * part)
            hid[tall, rows], da[tall, rows], db[tall, rows], more = mlp_part(
                weights.at[1], weights.at[2], weights.at[3], h2, cot, tall, rows
            )
            dh_own[slot] = more if f == 0 else dh_own[slot] + more
        dh_copy(i).start()

    def first_pass(i, carry):
        for t in range(3):

            @pl.when(i == t)
            def _():
                for w in range(1, 4):
                    pump(w, t)

        own_half(i)
        return carry

    products = ((da, h2, grad_mg_out), (db, h2, grad_mu_out), (hid, cot, grad_md_out))
    before = (BLOCKS - 1) * block
    lax.fori_loop(0, BLOCKS - 1, first_pass, 0)
    for w in range(1, 4):
        pump(w, 3)
    for number, (source, right, _) in enumerate(products):
        for n in range(3):
            where = slice(n * third, (n + 1) * third)
            sums[number, where, :] = dot(source[where, 0:before], right[0:before, :], 1, 0)
    own_half(BLOCKS - 1)
    late = [
        pltpu.make_async_copy(h2, h2_out, out_sem.at[4]),
        pltpu.make_async_copy(hid, hid_out, out_sem.at[5]),
    ]
    for copy in late:
        copy.start()
    for number, (source, right, target) in enumerate(products):
        for n in range(3):
            where = slice(n * third, (n + 1) * third)
            sums[number, where, :] += dot(source[where, before:length], right[before:length, :], 1, 0)
            late.append(
                pltpu.make_async_copy(
                    sums.at[number, pl.ds(n * third, third), :],
                    target.at[pl.ds(n * third, third), :],
                    sum_sem.at[number, n],
                )
            )
            late[-1].start()
    for copy in late:
        copy.wait()
    for w in range(1, 4):
        cast_ready(w)
    for i in range(BLOCKS - 2, BLOCKS):
        mid_copy(i).wait()
        dh_copy(i).wait()
    for number, (source, target) in enumerate(saved):
        pltpu.make_async_copy(source, target, out_sem.at[number]).wait()
    for w in range(4):
        for t in range(steps):
            for d in range(2):
                hop(w, d, t).wait_send()
        for slot in range(1 + 2 * steps):
            last = slot > 0 and (slot - 1) // 2 == steps - 1
            part_ref = area(w, place, core, 0 if last else None)
            pltpu.make_async_copy(part_ref, part_ref, cs_sem.at[w, slot]).wait()
    for i in range(BLOCKS):
        exchange(i).wait_send()


def forward(tokens, vectors, tables, ws, cotangent):
    chips = lax.axis_size("dp") // 2
    length, depth = tokens.shape
    wq, wk, wv, wg, wo, mg, mu, md = ws
    units = wv.shape[0]
    heads = wq.shape[1] // KD
    block = length // BLOCKS
    f32, bf16 = jnp.float32, jnp.bfloat16
    vmem = pl.BlockSpec(memory_space=pltpu.VMEM)
    hbm = pl.BlockSpec(memory_space=pl.ANY)
    dma = lambda *shape: pltpu.SemaphoreType.DMA(shape)
    shape = jax.ShapeDtypeStruct
    tall = (units, length)
    steps = chips // 2
    outs = [
        (shape((length, depth), bf16), hbm),
        (shape((heads, length, KD), bf16), hbm),
        (shape((heads, length, KD), bf16), hbm),
        (shape(tall, bf16), hbm),
        (shape(tall, bf16), hbm),
        (shape(tall, bf16), hbm),
        (shape((8, length), f32), hbm),
        (shape(tall, bf16), hbm),
        (shape((length, depth), f32), hbm),
        (shape((length, depth), f32), hbm),
        (shape((length, depth), bf16), hbm),
        (shape(tall, bf16), hbm),
        (shape((units, depth), f32), hbm),
        (shape((units, depth), f32), hbm),
        (shape((units, depth), f32), hbm),
        (shape((4, units, depth), f32), hbm),
    ]
    scratch = [
        pltpu.VMEM((4, units, depth), bf16),
        pltpu.VMEM((units, depth), bf16),
        pltpu.VMEM((length, depth), bf16),
        pltpu.VMEM((2, block, depth), bf16),
        pltpu.VMEM((2, heads, block, KD), bf16),
        pltpu.VMEM((heads, length, KD), bf16),
        pltpu.VMEM(tall, bf16),
        pltpu.VMEM((2, units, block), bf16),
        pltpu.VMEM((2, units, block), bf16),
        pltpu.VMEM((8, length), f32),
        pltpu.VMEM(tall, bf16),
        pltpu.VMEM((VD, block), f32),
        pltpu.VMEM((BLOCKS, units, block), f32),
        pltpu.VMEM((BLOCKS, units, block), f32),
        pltpu.VMEM((length, depth), bf16),
        pltpu.VMEM(tall, bf16),
        pltpu.VMEM(tall, bf16),
        pltpu.VMEM(tall, bf16),
        pltpu.VMEM((2, block, depth), f32),
        pltpu.VMEM((2, block, depth), f32),
        pltpu.VMEM((3, units, depth), f32),
        pltpu.VMEM((units, 1), f32),
        pltpu.VMEM((units, 1), f32),
        dma(9),
        dma(4, 2),
        dma(6),
        dma(2),
        dma(2),
        dma(2),
        dma(3, 3),
        dma(BLOCKS),
        dma(BLOCKS),
        dma(4),
        dma(4),
        dma(4, 2, steps),
        dma(4, 2, steps),
        dma(4, 1 + 2 * steps),
        dma(4, 1 + 2 * steps),
    ]
    return pl.pallas_call(
        functools.partial(forward_kernel, chips),
        out_shape=tuple(o for o, _ in outs),
        in_specs=[vmem] * 4 + [hbm] * 9,
        out_specs=tuple(s for _, s in outs),
        scratch_shapes=scratch,
        compiler_params=pltpu.CompilerParams(
            collective_id=1, has_side_effects=True, vmem_limit_bytes=VMEM_LIMIT
        ),
        cost_estimate=pl.CostEstimate(
            flops=40 * length * depth * units, bytes_accessed=80 * length * depth, transcendentals=0
        ),
    )(tokens, vectors, *tables, wq, wk, wv, wg, wo, mg, mu, md, cotangent)


def make_tables(length):
    half = KD // 2
    frequency = np.exp(-np.log(10000.0) * np.arange(half) / half)
    angles = np.arange(length)[:, None] * frequency[None, :]
    return jnp.asarray(np.cos(angles), jnp.float32), jnp.asarray(np.sin(angles), jnp.float32)


def pack_rows(arrays, width):
    rows = [jnp.pad(a.astype(jnp.float32), (0, width - a.shape[0])) for a in arrays]
    return jnp.pad(jnp.stack(rows), ((0, 8 - len(rows)), (0, 0)))


class Ring:
    def __init__(self, chips, quarters, own, sib, rcv, own_sem, sbs_sem, sbr_sem, rss_sem, rsr_sem):
        self.chips, self.quarters = chips, quarters
        self.index, self.tensor = lax.axis_index("dp"), lax.axis_index("tensor")
        self.core = self.index % 2
        place, _ = ring_place(self.index // 2, chips)
        self.place = place
        self.nexts = [
            {"dp": ring_chip((place + 1) % chips, chips) * 2 + self.core},
            {"dp": ring_chip((place + chips - 1) % chips, chips) * 2 + self.core},
        ]
        self.virtual = [place, (chips - place) % chips]
        self.sibling = {"dp": self.index + 1 - 2 * self.core}
        self.peer = {"tensor": 1 - self.tensor}
        self.offsets = [sum(quarters[:i]) for i in range(len(quarters))]
        self.own, self.sib, self.rcv = own, sib, rcv
        self.own_sem, self.sbs_sem, self.sbr_sem = own_sem, sbs_sem, sbr_sem
        self.rss_sem, self.rsr_sem = rss_sem, rsr_sem
        self.tokens = [(d, a) for a in range(len(quarters)) for d in range(2)]

    def window(self, which, d, chunk, rows):
        return (
            pl.ds(pl.multiple_of((which * 2 + d) * rows, 8), rows),
            pl.ds(pl.multiple_of(chunk * LANE, LANE), LANE),
        )

    def packed(self, a):
        return pl.ds(self.offsets[a], self.quarters[a])

    def chunk_at(self, d, order):
        return (self.virtual[d] + 2 * self.chips - 1 - order) % self.chips

    def quarter(self, which, d, a):
        rows = self.quarters[a]
        return pl.ds(pl.multiple_of((which * 2 + d) * rows, 8), rows)

    def own_copy(self, grads, d, a):
        return pltpu.make_async_copy(
            grads[a].at[self.quarter(self.core, d, a), :],
            self.own.at[d, self.packed(a), :],
            self.own_sem.at[d, a],
        )

    def sib_copy(self, grads, d, a):
        return remote(
            grads[a].at[self.quarter(1 - self.core, d, a), :],
            self.sib.at[d, self.packed(a), :],
            self.sbs_sem.at[d, a],
            self.sbr_sem.at[d, a],
            self.sibling,
        )

    def load(self, grads):
        for d, a in self.tokens:
            self.own_copy(grads, d, a).start()
            self.sib_copy(grads, d, a).start()

    def columns(self, d, order):
        return pl.ds(pl.multiple_of(self.chunk_at(d, order) * LANE, LANE), LANE)

    def chunk(self, d, a, order):
        return self.own.at[d, self.packed(a), self.columns(d, order)]

    def rs_copy(self, d, a, step):
        return remote(
            self.chunk(d, a, step),
            self.rcv.at[d, step, self.packed(a), :],
            self.rss_sem.at[d, a, step],
            self.rsr_sem.at[d, a, step],
            self.nexts[d],
        )

    def total(self, grads, d, a, step, first=False):
        if first:
            self.own_copy(grads, d, a).wait()
            self.sib_copy(grads, d, a).wait_recv()
        part, where = self.packed(a), self.columns(d, step)
        value = self.own[d, part, where] + self.sib[d, part, where]
        if not first:
            self.rs_copy(d, a, step - 1).wait_recv()
            value = value + self.rcv[d, step - 1, part, :]
        self.own[d, part, where] = value

    def drain_ring(self):
        def ring_step(step, carry):
            for d, a in self.tokens:
                self.rs_copy(d, a, step).wait_send()
            return carry

        lax.fori_loop(0, self.chips - 1, ring_step, 0)

    def drain_pair(self, grads):
        for d, a in self.tokens:
            self.sib_copy(grads, d, a).wait_send()


class Spread:
    def __init__(self, ring, quarters, outs, buffer, ags_sem, agr_sem, cgs_sem, cgr_sem, loc_sem):
        self.ring, self.quarters, self.outs, self.buffer = ring, quarters, outs, buffer
        self.ags_sem, self.agr_sem, self.cgs_sem, self.cgr_sem, self.loc_sem = (
            ags_sem, agr_sem, cgs_sem, cgr_sem, loc_sem,
        )
        self.offsets = [sum(quarters[:i]) for i in range(len(quarters))]
        self.tokens = [(d, a) for a in range(len(quarters)) for d in range(2)]

    def packed(self, a):
        return pl.ds(self.offsets[a], self.quarters[a])

    def part(self, which, d, a, step):
        ring = self.ring
        chunk = (ring.virtual[d] + 2 * ring.chips - step) % ring.chips
        return self.outs[a].at[ring.window(which, d, chunk, self.quarters[a])]

    def slot(self, d, a, step):
        return self.buffer.at[d, step, self.packed(a), :]

    def ring_copy(self, d, a, step, source=None):
        return remote(
            self.slot(d, a, step - 1) if source is None else source,
            self.slot(d, a, step),
            self.ags_sem.at[d, a, step],
            self.agr_sem.at[d, a, step],
            self.ring.nexts[d],
        )

    def pair_copy(self, d, a, step, source=None):
        return remote(
            self.slot(d, a, step - 1) if source is None else source,
            self.part(self.ring.core, d, a, step),
            self.cgs_sem.at[d, a, step],
            self.cgr_sem.at[d, a, step],
            self.ring.sibling,
        )

    def local_copy(self, d, a, step, source=None):
        return pltpu.make_async_copy(
            self.slot(d, a, step - 1) if source is None else source,
            self.part(self.ring.core, d, a, step),
            self.loc_sem.at[d, a, step],
        )

    def place(self, d, a, step, source=None):
        self.pair_copy(d, a, step, source).start()
        self.local_copy(d, a, step, source).start()

    def arrived(self, d, a, step):
        part = self.slot(d, a, step)
        pltpu.make_async_copy(part, part, self.agr_sem.at[d, a, step]).wait()

    def finish(self, step):
        for d, a in self.tokens:
            self.arrived(d, a, step)
            self.place(d, a, step + 1)

    def drain_ring(self):
        def ring_step(step, carry):
            for d, a in self.tokens:
                part = self.slot(d, a, step)
                pltpu.make_async_copy(part, part, self.ags_sem.at[d, a, step]).wait()
            return carry

        lax.fori_loop(0, self.ring.chips - 1, ring_step, 0)

    def drain(self):
        def pair_step(step, carry):
            for d, a in self.tokens:
                part = self.part(self.ring.core, d, a, step)
                pltpu.make_async_copy(part, part, self.cgs_sem.at[d, a, step]).wait()
                pltpu.make_async_copy(part, part, self.cgr_sem.at[d, a, step]).wait()
                pltpu.make_async_copy(part, part, self.loc_sem.at[d, a, step]).wait()
            return carry

        lax.fori_loop(0, self.ring.chips, pair_step, 0)


def backward_kernel(
    chips,
    quarters,
    x_hbm,
    rows_ref,
    cos_ref,
    sin_ref,
    cot_hbm,
    h2_hbm,
    hid_hbm,
    md_hbm,
    mid_hbm,
    dh_hbm,
    gath_hbm,
    wo_hbm,
    g_hbm,
    nh_hbm,
    rstd_hbm,
    q_hbm,
    k_hbm,
    v_hbm,
    wq_hbm,
    wk_hbm,
    wv_hbm,
    wg_hbm,
    h1_hbm,
    gated_hbm,
    grad_mg,
    grad_mu,
    grad_md,
    dmid_out,
    output_out,
    grad_mg_out,
    grad_mu_out,
    grad_md_out,
    part_out,
    grad_qk_out,
    grad_v_out,
    grad_g_out,
    grad_out_out,
    small_out,
    x,
    branch,
    wo,
    g,
    nh,
    rstd,
    q,
    k,
    v,
    wq,
    wk,
    wv,
    wg,
    h1,
    gated,
    acc_gain,
    acc_bias,
    dk,
    dv,
    dq,
    stage,
    fin,
    finished,
    own,
    sib,
    rcv,
    buffer,
    ggain_ref,
    gbias_ref,
    segc_ref,
    in_sem,
    stage_sem,
    column_sem,
    fin_sem,
    dmid_sem,
    output_sem,
    own_sem,
    sbs_sem,
    sbr_sem,
    rss_sem,
    rsr_sem,
    *spread_sems,
):
    ring = Ring(chips, quarters, own, sib, rcv, own_sem, sbs_sem, sbr_sem, rss_sem, rsr_sem)
    grads = (grad_mg, grad_mu, grad_md)
    spread = Spread(ring, quarters, (grad_mg_out, grad_mu_out, grad_md_out), buffer, *spread_sems)
    f32 = jnp.float32
    heads = q.shape[0]
    length = h1.shape[0]
    units = v.shape[0]
    block = length // BLOCKS
    third = units // 3
    cot, h2, hid, md = x, h1, gated, v
    mg_o, mu_o, md_o = wv, wg, wo
    pairs = [
        (cot_hbm, cot), (h2_hbm, h2), (hid_hbm, hid), (md_hbm, md),
        (g_hbm, g), (nh_hbm, nh), (rstd_hbm, rstd), (q_hbm, q), (k_hbm, k), (wq_hbm, wq), (wk_hbm, wk),
        (wo_hbm, wo), (v_hbm, v), (wv_hbm, wv), (wg_hbm, wg), (x_hbm, x), (h1_hbm, h1), (gated_hbm, gated),
    ]
    copies = [pltpu.make_async_copy(a, b, in_sem.at[n]) for n, (a, b) in enumerate(pairs)]
    greet([*ring.nexts, ring.sibling])
    ring.load(grads)

    cast_list = [(w, target, n) for w, target in ((1, mg_o), (2, mu_o), (3, md_o)) for n in range(3)]

    def cast_copy(number):
        w, _, n = cast_list[number]
        return pltpu.make_async_copy(
            gath_hbm.at[w, pl.ds(n * third, third), :], stage.at[number % 2], stage_sem.at[number % 2]
        )

    cast_copy(0).start()
    for copy in copies[:4]:
        copy.start()
    for copy in copies[4:11]:
        copy.start()
    acc_gain[...] = jnp.zeros_like(acc_gain)
    acc_bias[...] = jnp.zeros_like(acc_bias)
    small_out[...] = jnp.zeros_like(small_out)
    for n in range(3):
        where = slice(n * third, (n + 1) * third)
        ggain_ref[where, :] = upright_part(rows_ref[GROUP_GAIN : GROUP_GAIN + 1, :], n * third, third)
        gbias_ref[where, :] = upright_part(rows_ref[GROUP_BIAS : GROUP_BIAS + 1, :], n * third, third)
    for n in range(BLOCKS):
        where = slice(n * block, (n + 1) * block)
        segc_ref[where, :] = upright(rows_ref[SEGMENT : SEGMENT + 1, where], block)
    plan = [(step, a) for step in range(2 * chips - 1) for a in range(len(quarters))]

    def pump(count=1):
        for _ in range(min(count, len(plan))):
            step, a = plan.pop(0)
            for d in range(2):
                if step < chips:
                    ring.total(grads, d, a, step, step == 0)
                if step < chips - 1:
                    ring.rs_copy(d, a, step).start()
                    continue
                turn_step = step - (chips - 1)
                source = ring.chunk(d, a, chips - 1) if turn_step == 0 else None
                if turn_step > 0:
                    spread.arrived(d, a, turn_step - 1)
                if turn_step < chips - 1:
                    spread.ring_copy(d, a, turn_step, source).start()
                spread.place(d, a, turn_step, source)

    fin_rows = [pl.ds(i * block, block) for i in range(BLOCKS)]

    def fin_copy(i, which):
        source = (mid_hbm, dh_hbm)[which]
        return pltpu.make_async_copy(source.at[fin_rows[i], :], fin.at[which], fin_sem.at[which])

    for which in range(2):
        fin_copy(0, which).start()
    for number, (_, target, n) in enumerate(cast_list):
        if number + 1 < len(cast_list):
            cast_copy(number + 1).start()
        cast_copy(number).wait()
        target[n * third : (n + 1) * third, :] = low(stage[number % 2])
        if number % 2 == 0:
            pump()
    for copy in copies[:4]:
        copy.wait()
    dh_oth, out_sum = stage.at[0, pl.ds(0, block), :], stage.at[1, pl.ds(0, block), :]
    half_units = units // 2

    def output_copy(i):
        spot = pl.ds((i % (BLOCKS // 2)) * block, block)
        return pltpu.make_async_copy(finished, output_out.at[spot, :], output_sem)

    def dmid_copy(i):
        return pltpu.make_async_copy(fin.at[1], dmid_out.at[fin_rows[i], :], dmid_sem)

    gain2 = rows_ref[GAIN2 : GAIN2 + 1, :]
    for i in range(BLOCKS):
        rows = fin_rows[i]
        for which in range(2):
            fin_copy(i, which).wait()
        mine = ring.tensor == i // (BLOCKS // 2)
        for f in range(2):
            tall = slice(f * half_units, (f + 1) * half_units)
            hidden, _, _, more = mlp_part(mg_o, mu_o, md_o, h2, cot, tall, rows)
            dh_oth[...] = more if f == 0 else dh_oth[...] + more

            @pl.when(mine)
            def _():
                lift = dot(hidden, md_o[tall, :], 0, 0) + dot(hid[tall, rows], md[tall, :], 0, 0)
                out_sum[...] = lift if f == 0 else out_sum[...] + lift

            pump()

        @pl.when(mine)
        def _():
            if i % (BLOCKS // 2):
                output_copy(i - 1).wait()
            finished[...] = low(fin[0] + out_sum[...])
            output_copy(i).start()

        mid = fin[0]
        r2 = lax.rsqrt(jnp.mean(mid * mid, axis=1, keepdims=True) + EPSILON)
        dh2 = fin[1] + dh_oth[...]
        e = dh2 * gain2
        inner = jnp.mean(e * mid, axis=1, keepdims=True)
        small_out[1:2, :] += jnp.sum(dh2 * mid * r2, axis=0, keepdims=True)
        result = cot[rows, :].astype(f32) + r2 * e - mid * (r2 * r2 * r2 * inner)
        fin[1] = result
        branch[rows, :] = low(result)
        dmid_copy(i).start()
        if i < BLOCKS - 1:
            fin_copy(i + 1, 0).start()
            dmid_copy(i).wait()
            fin_copy(i + 1, 1).start()
        pump()
    for copy in copies[11:]:
        copy.start()
    for copy in copies[4:7]:
        copy.wait()
    copies[11].wait()

    def fold(values):
        return values[:, :LANE] + values[:, LANE:]

    def gate_block(i):
        rows = pl.ds(i * block, block)
        for head in range(heads):
            tall = slice(head * VD, (head + 1) * VD)
            up = dot(wo[tall, :], branch[rows, :], 1, 1)
            gate = g[tall, rows].astype(f32)
            nhat = nh[tall, rows].astype(f32)
            sigmoid = 1.0 / (1.0 + jnp.exp(-gate))
            silu = gate * sigmoid
            dgn = up * silu
            acc_gain[tall, :] += fold(dgn * nhat)
            acc_bias[tall, :] += fold(dgn)
            gain = ggain_ref[tall, :]
            f = dgn * gain
            mean = jnp.mean(f, axis=0, keepdims=True)
            inner = jnp.mean(f * nhat, axis=0, keepdims=True)
            nh[tall, rows] = low((f - mean - nhat * inner) * rstd[head : head + 1, rows])
            gn = nhat * gain + gbias_ref[tall, :]
            g[tall, rows] = low(up * gn * (sigmoid + silu * (1.0 - sigmoid)))

    for i in range(BLOCKS):
        gate_block(i)
        pump()
    for copy in (copies[7], copies[8], copies[12]):
        copy.wait()

    ahead = lax.broadcasted_iota(jnp.int32, (block, block), 0) - lax.broadcasted_iota(
        jnp.int32, (block, block), 1
    )

    def key_block(head, m):
        tall = slice(head * VD, (head + 1) * VD)
        cols = pl.ds(m * block, block)
        rate = rate_of(head, heads, ring.tensor)
        dk[...] = jnp.zeros_like(dk)
        dv[...] = jnp.zeros_like(dv)

        def tile(i, carry):
            rows = pl.ds(pl.multiple_of(i * block, block), block)
            gap = ahead + (i - m) * block
            seen = (segc_ref[rows, :] == rows_ref[SEGMENT : SEGMENT + 1, cols]) & (gap >= 0)
            decay = jnp.where(seen, jnp.exp(gap.astype(f32) * rate), 0.0)
            scores = low(dot(q[head, rows, :], k[head, cols, :], 1, 1) * decay)
            draw = low(dot(nh[tall, rows], v[tall, cols], 0, 0) * decay)
            dv[...] += dot(nh[tall, rows], scores, 1, 0)
            dk[...] += dot(draw, q[head, rows, :], 0, 0)
            more = dot(draw, k[head, cols, :], 1, 0)
            if m == 0:
                dq[rows, :] = more
            else:
                dq[rows, :] += more
            return carry

        if m == 0:
            lax.fori_loop(0, BLOCKS // 2, tile, 0)
            pump()
            lax.fori_loop(BLOCKS // 2, BLOCKS, tile, 0)
        else:
            lax.fori_loop(m, BLOCKS, tile, 0)
        v[tall, cols] = low(dv[...])
        k[head, cols, :] = low(turn(dk[...], cos_ref[cols, :], -sin_ref[cols, :]) * KD ** (-0.5))

    for head in range(heads):
        for m in range(BLOCKS):
            key_block(head, m)
            if m == BLOCKS - 1:
                q[head] = low(turn(dq[...], cos_ref[...], -sin_ref[...]))
            pump()

    for copy in (*copies[9:11], *copies[13:]):
        copy.wait()
    column = dq

    def stage_wait(slot):
        pltpu.make_async_copy(stage.at[slot], stage.at[slot], stage_sem.at[slot]).wait()

    key_parts = [(q, wq), (k, wk)]
    for i in range(BLOCKS):
        slot = i % 2
        rows = pl.ds(i * block, block)
        if i >= 2:
            stage_wait(slot)
        total = None
        for values, weights in key_parts:
            for head in range(heads):
                wide = slice(head * KD, (head + 1) * KD)
                more = dot(values[head, rows, :], weights[:, wide], 1, 1)
                total = more if total is None else total + more
        stage[slot, 0:block, :] = total
        stage[slot, 0:block, :] += dot(v[:, rows], wv[...], 0, 0)
        stage[slot, 0:block, :] += dot(g[:, rows], wg[...], 0, 0)
        xb = x[rows, :].astype(f32)
        r1 = lax.rsqrt(jnp.mean(xb * xb, axis=1, keepdims=True) + EPSILON)
        small_out[0:1, :] += jnp.sum(stage[slot, 0:block, :] * (xb * r1), axis=0, keepdims=True)
        pltpu.make_async_copy(stage.at[slot], part_out.at[i], stage_sem.at[slot]).start()
        pump()

    count = BLOCKS
    for source, right, target in ((v, h1, grad_v_out), (g, h1, grad_g_out), (gated, branch, grad_out_out)):
        for n in range(3):
            where = pl.ds(n * third, third)
            slot = count % 2
            stage_wait(slot)
            stage[slot] = dot(source[where, :], right[...], 1, 0)
            pltpu.make_async_copy(stage.at[slot], target.at[where, :], stage_sem.at[slot]).start()
            count += 1
            pump()

    for number, (values, head) in enumerate([(q, 0), (q, 1), (k, 0), (k, 1)][: 2 * heads]):
        if number:
            pltpu.make_async_copy(column, column, column_sem).wait()
        column[...] = dot(h1[...], values[head], 0, 0)
        pltpu.make_async_copy(column, grad_qk_out.at[:, pl.ds(number * KD, KD)], column_sem).start()
        pump()
    pump(len(plan))

    ones = jnp.ones((8, LANE), jnp.bfloat16)

    def row_of(acc):
        whole = acc[...]
        high = low(whole)
        return dot(ones, high, 1, 1) + dot(ones, low(whole - high.astype(f32)), 1, 1)

    small_out[2:3, 0:units] = row_of(acc_gain)[0:1, :]
    small_out[3:4, 0:units] = row_of(acc_bias)[0:1, :]

    ring.drain_ring()
    ring.drain_pair(grads)
    spread.drain_ring()
    spread.drain()
    dmid_copy(BLOCKS - 1).wait()
    output_copy(BLOCKS - 1).wait()
    for slot in range(2):
        stage_wait(slot)
    pltpu.make_async_copy(column, column, column_sem).wait()


def backward(tokens, vectors, tables, cotangent, mlp, saved, ws, mlp_grads):
    chips = lax.axis_size("dp") // 2
    length, depth = tokens.shape
    wq, wk, wv, wg, wo, md = ws
    h1, q, k, v, g, nh, rstd, gated = saved
    mid, dh, h2, hid, gathered = mlp
    units = wv.shape[0]
    heads = q.shape[0]
    block = length // BLOCKS
    quarters = tuple(a.shape[0] // 4 for a in mlp_grads)
    rows = sum(quarters)
    count = len(quarters)
    f32, bf16 = jnp.float32, jnp.bfloat16
    vmem = pl.BlockSpec(memory_space=pltpu.VMEM)
    hbm = pl.BlockSpec(memory_space=pl.ANY)
    dma = lambda *shape: pltpu.SemaphoreType.DMA(shape)
    shape = jax.ShapeDtypeStruct
    tall = (units, length)
    stage_rows = max(block, units // 3)
    outs = [
        (shape((length, depth), f32), hbm),
        (shape((length // 2, depth), bf16), hbm),
        (shape((units, depth), f32), hbm),
        (shape((units, depth), f32), hbm),
        (shape((units, depth), f32), hbm),
        (shape((BLOCKS, stage_rows, depth), f32), hbm),
        (shape((depth, 2 * heads * KD), f32), hbm),
        (shape((units, depth), f32), hbm),
        (shape((units, depth), f32), hbm),
        (shape((units, depth), f32), hbm),
        (shape((8, depth), f32), vmem),
    ]
    scratch = [
        pltpu.VMEM((length, depth), bf16),
        pltpu.VMEM((length, depth), bf16),
        pltpu.VMEM((units, depth), bf16),
        pltpu.VMEM(tall, bf16),
        pltpu.VMEM(tall, bf16),
        pltpu.VMEM((8, length), f32),
        pltpu.VMEM((heads, length, KD), bf16),
        pltpu.VMEM((heads, length, KD), bf16),
        pltpu.VMEM(tall, bf16),
        pltpu.VMEM((depth, heads * KD), bf16),
        pltpu.VMEM((depth, heads * KD), bf16),
        pltpu.VMEM((units, depth), bf16),
        pltpu.VMEM((units, depth), bf16),
        pltpu.VMEM((length, depth), bf16),
        pltpu.VMEM(tall, bf16),
        pltpu.VMEM((units, LANE), f32),
        pltpu.VMEM((units, LANE), f32),
        pltpu.VMEM((block, KD), f32),
        pltpu.VMEM((VD, block), f32),
        pltpu.VMEM((length, KD), f32),
        pltpu.VMEM((2, stage_rows, depth), f32),
        pltpu.VMEM((2, block, depth), f32),
        pltpu.VMEM((block, depth), bf16),
        pltpu.VMEM((2, rows, depth), f32),
        pltpu.VMEM((2, rows, depth), f32),
        pltpu.VMEM((2, chips - 1, rows, LANE), f32),
        pltpu.VMEM((2, chips - 1, rows, LANE), f32),
        pltpu.VMEM((units, 1), f32),
        pltpu.VMEM((units, 1), f32),
        pltpu.VMEM((length, 1), f32),
        dma(18),
        dma(2),
        pltpu.SemaphoreType.DMA,
        dma(2),
        pltpu.SemaphoreType.DMA,
        pltpu.SemaphoreType.DMA,
        dma(2, count),
        dma(2, count),
        dma(2, count),
        dma(2, count, chips - 1),
        dma(2, count, chips - 1),
        dma(2, count, chips - 1),
        dma(2, count, chips - 1),
        dma(2, count, chips),
        dma(2, count, chips),
        dma(2, count, chips),
    ]
    return pl.pallas_call(
        functools.partial(backward_kernel, chips, quarters),
        out_shape=tuple(o for o, _ in outs),
        in_specs=[hbm] + [vmem] * 3 + [hbm] * 23,
        out_specs=tuple(s for _, s in outs),
        scratch_shapes=scratch,
        compiler_params=pltpu.CompilerParams(
            collective_id=2, has_side_effects=True, vmem_limit_bytes=VMEM_LIMIT
        ),
        cost_estimate=pl.CostEstimate(
            flops=20 * length * depth * units, bytes_accessed=80 * length * depth, transcendentals=0
        ),
    )(
        tokens, vectors, *tables, cotangent, h2, hid, md, mid, dh, gathered,
        wo, g, nh, rstd, q, k, v, wq, wk, wv, wg, h1, gated, *mlp_grads,
    )


def finish_kernel(
    chips,
    quarters,
    *refs,
):
    count = len(quarters)
    grads = refs[:count]
    part_hbm, small_ref, x_hbm, dmid_hbm, rows_ref = refs[count : count + 5]
    refs = refs[count + 5 :]
    outs = refs[:count]
    tokens_out, small_out = refs[count : count + 2]
    (late_buffer, own, sib, rcv, sacc, sbuf, part, peer, x, dmid, result, in_sem, res_sem, hs_sem, hr_sem, ss_sem, sr_sem) = refs[
        count + 2 : count + 19
    ]
    sems = refs[count + 19 :]
    ring = Ring(chips, quarters, own, sib, rcv, *sems[:5])
    late = Spread(ring, quarters, outs, late_buffer, *sems[5:10])
    bits = (2 * chips).bit_length() - 1
    f32 = jnp.float32
    block = part.shape[1]
    greet(
        [*ring.nexts, ring.peer] + [{"dp": bit_partner(ring.index, bit)} for bit in range(bits)]
    )

    ring.load(grads)

    few = block // (2 * PIECES)
    swaps = 2 * PIECES * BLOCKS

    def h_copy(n):
        i, inside = n // (2 * PIECES), pl.ds(pl.multiple_of((n % (2 * PIECES)) * few, few), few)
        return remote(part_hbm.at[i, inside, :], peer.at[i, inside, :], hs_sem.at[n], hr_sem.at[n], ring.peer)

    def h_step(n, early=False):
        if not early:
            h_copy(n - 2).wait_send()
        h_copy(n).start()

    loads = [pltpu.make_async_copy(x_hbm, x, in_sem.at[0]), pltpu.make_async_copy(dmid_hbm, dmid, in_sem.at[1])]
    for i in range(BLOCKS):
        loads.append(pltpu.make_async_copy(part_hbm.at[i, pl.ds(0, block), :], part.at[i], in_sem.at[2 + i]))

    def s_copy(level):
        target = ring.peer if level == 0 else {"dp": bit_partner(ring.index, level - 1)}
        return remote(sacc.at[level], sbuf.at[level], ss_sem.at[level], sr_sem.at[level], target)

    def s_finish(level):
        s_copy(level).wait()
        got = sbuf[level]
        if level == 0:
            first = lax.broadcasted_iota(jnp.int32, got.shape, 0) == 0
            got = jnp.where(first, got, 0.0)
        sacc[level + 1] = sacc[level] + got

    sacc[0] = small_ref[...]

    def small_step(step):
        for level in range(bits + 2):

            @pl.when(step == level)
            def _():
                if level > 0:
                    s_finish(level - 1)
                if level <= bits:
                    s_copy(level).start()

    first_order = [(ring, a) for a in range(count)]
    second_order = [(late, a) for a in range(count)]

    def first_step(step, before):
        for position, (_, a) in enumerate(first_order):
            for d in range(2):
                ring.total(grads, d, a, step, before is None)
                ring.rs_copy(d, a, step).start()
            if before is None:
                h_step(position, position < 2)
            else:
                h_step(step * len(first_order) + position)

    def rs_step(step, carry):
        first_step(step, (first_order, step - 1))

        small_step(step)
        return carry

    first_step(0, None)
    for copy in loads:
        copy.start()
    small_step(0)
    lax.fori_loop(1, chips - 1, rs_step, 0)
    for position, (_, a) in enumerate(second_order):
        for d in range(2):
            ring.total(grads, d, a, chips - 1)
            source = ring.chunk(d, a, chips - 1)
            late.ring_copy(d, a, 0, source).start()
            late.place(d, a, 0, source)
        h_step((chips - 1) * len(second_order) + position)

    each = block // PIECES
    pieces = BLOCKS * PIECES

    def token_piece(number):
        i = number // PIECES
        for n in range(2):
            h_copy(2 * number + n).wait_recv()
        inside = pl.ds(pl.multiple_of((number % PIECES) * each, each), each)
        rows = pl.ds(pl.multiple_of(number * each, each), each)
        xb = x[rows, :].astype(f32)
        r1 = lax.rsqrt(jnp.mean(xb * xb, axis=1, keepdims=True) + EPSILON)
        e = (part[i, inside, :] + peer[i, inside, :]) * rows_ref[GAIN1 : GAIN1 + 1, :]
        inner = jnp.mean(e * xb, axis=1, keepdims=True)
        result[rows, :] = low(dmid[rows, :] + r1 * e - xb * (r1 * r1 * r1 * inner))

    def ag_step(step, carry):
        for position, (_, a) in enumerate(second_order):
            for d in range(2):
                late.arrived(d, a, step - 1)
                late.ring_copy(d, a, step).start()
                late.place(d, a, step)
            number = (step - 2) * len(second_order) + position

            @pl.when((number >= 0) & (number < pieces))
            def _():
                token_piece(number)

        return carry

    for copy in loads:
        copy.wait()
    lax.fori_loop(1, chips - 1, ag_step, 0)
    tokens_copy = pltpu.make_async_copy(result, tokens_out, res_sem)
    tokens_copy.start()
    late.finish(chips - 2)
    small_out[...] = sacc[bits + 1]
    ring.drain_ring()
    late.drain_ring()
    ring.drain_pair(grads)
    late.drain()
    for n in range(swaps - 2, swaps):
        h_copy(n).wait_send()
    tokens_copy.wait()


def finish(grads, part, small, tokens, dmid, vectors):
    chips = lax.axis_size("dp") // 2
    length, depth = tokens.shape
    block = length // BLOCKS
    quarters = tuple(g.shape[0] // 4 for g in grads)
    rows = sum(quarters)
    count = len(quarters)
    bits = (2 * chips).bit_length() - 1
    f32, bf16 = jnp.float32, jnp.bfloat16
    vmem = pl.BlockSpec(memory_space=pltpu.VMEM)
    hbm = pl.BlockSpec(memory_space=pl.ANY)
    dma = lambda *shape: pltpu.SemaphoreType.DMA(shape)
    shape = jax.ShapeDtypeStruct
    outs = [(shape(g.shape, f32), hbm) for g in grads]
    outs += [
        (shape((length, depth), bf16), hbm),
        (shape(small.shape, f32), vmem),
    ]
    scratch = [
        pltpu.VMEM((2, chips - 1, rows, LANE), f32),
        pltpu.VMEM((2, rows, depth), f32),
        pltpu.VMEM((2, rows, depth), f32),
        pltpu.VMEM((2, chips - 1, rows, LANE), f32),
        pltpu.VMEM((bits + 2, *small.shape), f32),
        pltpu.VMEM((bits + 1, *small.shape), f32),
        pltpu.VMEM((BLOCKS, block, depth), f32),
        pltpu.VMEM((BLOCKS, block, depth), f32),
        pltpu.VMEM((length, depth), bf16),
        pltpu.VMEM((length, depth), f32),
        pltpu.VMEM((length, depth), bf16),
        dma(2 + BLOCKS),
        pltpu.SemaphoreType.DMA,
        dma(2 * PIECES * BLOCKS),
        dma(2 * PIECES * BLOCKS),
        dma(bits + 1),
        dma(bits + 1),
        dma(2, count),
        dma(2, count),
        dma(2, count),
        dma(2, count, chips - 1),
        dma(2, count, chips - 1),
    ]
    scratch += [
        dma(2, count, chips - 1),
        dma(2, count, chips - 1),
        dma(2, count, chips),
        dma(2, count, chips),
        dma(2, count, chips),
    ]
    return pl.pallas_call(
        functools.partial(finish_kernel, chips, quarters),
        out_shape=tuple(o for o, _ in outs),
        in_specs=[hbm] * (count + 1) + [vmem] + [hbm] * 2 + [vmem],
        out_specs=tuple(s for _, s in outs),
        scratch_shapes=scratch,
        compiler_params=pltpu.CompilerParams(
            collective_id=3, has_side_effects=True, vmem_limit_bytes=VMEM_LIMIT
        ),
        cost_estimate=pl.CostEstimate(
            flops=20 * rows * depth, bytes_accessed=80 * rows * depth, transcendentals=0
        ),
    )(*grads, part, small, tokens, dmid, vectors)


def deliver_kernel(count, key_width, *refs):
    sources, targets = refs[:count], refs[count : 2 * count + 1]
    buffer, low_buffer, in_sem, out_sem = refs[2 * count + 1 :]
    pieces = []
    for a in range(count):
        parts = DELIVER if sources[a].dtype == jnp.float32 else 1
        rows = sources[a].shape[0] // parts
        for n in range(parts):
            pieces.append((a, pl.ds(n * rows, rows), rows))
    wide = sum(sources[a].dtype == jnp.float32 for a, _, _ in pieces)
    low_start = [sum(r for _, _, r in pieces[wide:n]) for n in range(wide, len(pieces))]

    def spot(number):
        rows = pieces[number][2]
        if number < wide:
            return buffer.at[number, pl.ds(0, rows), :]
        return low_buffer.at[pl.ds(low_start[number - wide], rows), :]

    def load(number):
        a, where, rows = pieces[number]
        return pltpu.make_async_copy(sources[a].at[where, :], spot(number), in_sem.at[number])

    def stores(number):
        a, where, rows = pieces[number]
        if a:
            spots = [(spot(number), targets[a + 1].at[where, :])]
        else:
            spots = [
                (buffer.at[number, pl.ds(0, rows), pl.ds(half * key_width, key_width)], targets[half].at[where, :])
                for half in range(2)
            ]
        return [pltpu.make_async_copy(s, t, out_sem.at[number, n]) for n, (s, t) in enumerate(spots)]

    for number in range(len(pieces)):
        load(number).start()
    for number in range(len(pieces)):
        load(number).wait()
        for copy in stores(number):
            copy.start()
    for number in range(len(pieces)):
        for copy in stores(number):
            copy.wait()


def deliver(arrays, narrow, key_width):
    hbm = pl.BlockSpec(memory_space=pl.ANY)
    every = (*arrays, *narrow)
    shapes = [((arrays[0].shape[0], key_width), jnp.float32)] * 2 + [(a.shape, a.dtype) for a in every[1:]]
    size = sum(a.size for a in arrays)
    wide = DELIVER * len(arrays)
    pieces = wide + len(narrow)
    depth = arrays[0].shape[1]
    rows = max(a.shape[0] for a in arrays) // DELIVER
    return pl.pallas_call(
        functools.partial(deliver_kernel, len(every), key_width),
        out_shape=tuple(jax.ShapeDtypeStruct(s, t) for s, t in shapes),
        in_specs=[hbm] * len(every),
        out_specs=(hbm,) * len(shapes),
        scratch_shapes=[
            pltpu.VMEM((wide, rows, depth), jnp.float32),
            pltpu.VMEM((sum(a.shape[0] for a in narrow), depth), jnp.bfloat16),
            pltpu.SemaphoreType.DMA((pieces,)),
            pltpu.SemaphoreType.DMA((pieces, 2)),
        ],
        compiler_params=pltpu.CompilerParams(vmem_limit_bytes=56 * 1024 * 1024),
        cost_estimate=pl.CostEstimate(flops=0, bytes_accessed=8 * size, transcendentals=0),
    )(*every)

def swap(array):
    return lax.ppermute(array, "tensor", [(0, 1), (1, 0)])


def other_half(arrays, zero):
    dp, index = lax.axis_size("dp"), lax.axis_index("dp")
    rows = arrays[0].shape[0]
    count = len(arrays)
    if dp % count == 0 and rows % (8 * (dp // count)) == 0:
        share = rows * count // dp
        each = dp // count
        inside = (index % each) * share
        own = [lax.dynamic_slice_in_dim(a, inside, share, 0) for a in arrays]
        part = own[0]
        for number in range(1, count):
            part = jnp.where(index // each == number, own[number], part)
    else:
        share = -(-rows * count // (8 * dp)) * 8
        whole = jnp.concatenate(arrays, axis=0)
        whole = jnp.pad(whole, ((0, share * dp - rows * count), (0, 0)))
        part = lax.dynamic_slice_in_dim(whole, index * share, share, 0)
    got = lax.all_gather(swap(part.astype(jnp.float32)), "dp", axis=0, tiled=True)
    got = low(got + zero)
    return [got[number * rows : (number + 1) * rows] for number in range(count)]


def plain_body(
    tokens,
    segment,
    norm1_gain,
    w_query,
    w_key,
    w_value,
    w_gate,
    group_gain,
    group_bias,
    w_out,
    norm2_gain,
    w_mlp_gate,
    w_mlp_up,
    w_mlp_down,
    cotangent,
):
    length, depth = tokens.shape
    heads = w_query.shape[1] // KD
    block = length // BLOCKS
    tensor = lax.axis_index("tensor")
    f32 = jnp.float32
    zero = jnp.minimum(segment[0], 0).astype(f32)
    value_t, gate_t, mg_t, mu_t = w_value.T, w_gate.T, w_mlp_gate.T, w_mlp_up.T
    mg_o, mu_o, md_o, wo_o = other_half([mg_t, mu_t, w_mlp_down, w_out], zero)
    x = tokens.astype(f32)
    gain1 = norm1_gain.astype(f32)
    gain2 = norm2_gain.astype(f32)
    ggain = group_gain.astype(f32)[:, None]
    gbias = group_bias.astype(f32)[:, None]
    r1 = lax.rsqrt(jnp.mean(x * x, axis=1, keepdims=True) + EPSILON)
    h1 = low(x * r1 * gain1)
    half = KD // 2
    frequency = jnp.exp(-jnp.log(10000.0) * jnp.arange(half, dtype=f32) / half)
    angles = jnp.arange(length, dtype=f32)[:, None] * frequency[None, :]
    cosine, sine = jnp.cos(angles), jnp.sin(angles)
    positions = jnp.arange(length, dtype=jnp.int32)
    visible = (positions[:, None] >= positions[None, :]) & (segment[:, None] == segment[None, :])
    offsets = jnp.maximum(positions[:, None] - positions[None, :], 0).astype(f32)

    def decay(head, rows, columns):
        order = (tensor * heads + head).astype(f32)
        rate = jnp.log1p(-jnp.exp2(-5.0 - order))
        return jnp.where(visible[rows, columns], jnp.exp(offsets[rows, columns] * rate), 0.0)

    queries = [[] for _ in range(heads)]
    keys = [[] for _ in range(heads)]
    values = [[] for _ in range(heads)]
    gates = [[] for _ in range(heads)]
    nhats = [[] for _ in range(heads)]
    spreads = [[] for _ in range(heads)]
    gated_blocks, received = [], []
    for number in range(BLOCKS):
        rows = slice(number * block, (number + 1) * block)
        seen = slice(0, (number + 1) * block)
        own = []
        for head in range(heads):
            wide = slice(head * KD, (head + 1) * KD)
            tall = slice(head * VD, (head + 1) * VD)
            q = low(turn(dot(h1[rows], w_query[:, wide], 1, 0), cosine[rows], sine[rows]))
            k = turn(dot(h1[rows], w_key[:, wide], 1, 0), cosine[rows], sine[rows])
            queries[head].append(q)
            keys[head].append(low(k * KD ** (-0.5)))
            values[head].append(low(dot(value_t[tall], h1[rows], 1, 1)))
            g = dot(gate_t[tall], h1[rows], 1, 1)
            gates[head].append(g)
            scores = dot(q, jnp.concatenate(keys[head], axis=0), 1, 1)
            scores = low(scores * decay(head, rows, seen))
            ret = dot(jnp.concatenate(values[head], axis=1), scores, 1, 1)
            centred = ret - jnp.mean(ret, axis=0, keepdims=True)
            scale = lax.rsqrt(jnp.mean(centred * centred, axis=0, keepdims=True) + GROUP_EPSILON)
            nhat = centred * scale
            nhats[head].append(nhat)
            spreads[head].append(scale)
            own.append(low(jax.nn.silu(g) * (nhat * ggain[tall] + gbias[tall])))
        gated_blocks.append(jnp.concatenate(own, axis=0))
        received.append(low(swap(gated_blocks[-1].astype(f32)) + zero))

    mids, h2s, r2s, hidden_own, hidden_oth, das, dbs, dmids = [], [], [], [], [], [], [], []
    norm2_rows = []
    for number in range(BLOCKS):
        rows = slice(number * block, (number + 1) * block)
        mid = x[rows] + (dot(gated_blocks[number], w_out, 0, 0) + dot(received[number], wo_o, 0, 0))
        r2 = lax.rsqrt(jnp.mean(mid * mid, axis=1, keepdims=True) + EPSILON)
        h2 = low(mid * r2 * gain2)
        cot = cotangent[rows]

        def mlp(gate_w, up_w, down_w):
            a, b = dot(gate_w, h2, 1, 1), dot(up_w, h2, 1, 1)
            hidden, pull = jax.vjp(lambda s, t: jax.nn.gelu(s) * t, a, b)
            da, db = pull(dot(down_w, cot, 1, 1))
            da, db = low(da), low(db)
            return low(hidden), da, db, dot(da, gate_w, 0, 0) + dot(db, up_w, 0, 0)

        own_hidden, da, db, part = mlp(mg_t, mu_t, w_mlp_down)
        oth_hidden, _, _, more = mlp(mg_o, mu_o, md_o)
        dh2 = part + more
        e = dh2 * gain2
        dmid = cot.astype(f32) + r2 * e - mid * (r2 * r2 * r2) * jnp.mean(e * mid, axis=1, keepdims=True)
        norm2_rows.append(jnp.sum(dh2 * mid * r2, axis=0))
        for where, value in zip(
            (mids, h2s, hidden_own, hidden_oth, das, dbs, dmids),
            (mid, h2, own_hidden, oth_hidden, da, db, dmid),
        ):
            where.append(value)
    grad_norm2 = sum(norm2_rows)
    mid = jnp.concatenate(mids, axis=0)
    h2 = jnp.concatenate(h2s, axis=0)
    hidden = jnp.concatenate(hidden_own, axis=1)
    hidden_o = jnp.concatenate(hidden_oth, axis=1)
    dmid = jnp.concatenate(dmids, axis=0)
    own_rows = length // lax.axis_size("tensor")
    place = tensor * own_rows
    output = low(
        lax.dynamic_slice_in_dim(mid, place, own_rows, 0)
        + dot(lax.dynamic_slice_in_dim(hidden, place, own_rows, 1), w_mlp_down, 0, 0)
        + dot(lax.dynamic_slice_in_dim(hidden_o, place, own_rows, 1), md_o, 0, 0)
    )
    grad_mg = dot(jnp.concatenate(das, axis=1), h2, 1, 0)
    grad_mu = dot(jnp.concatenate(dbs, axis=1), h2, 1, 0)
    grad_md = dot(hidden, cotangent, 1, 0)

    branch = low(dmid)
    gated = jnp.concatenate(gated_blocks, axis=1)
    grad_out = dot(gated, branch, 1, 0)
    dgated = dot(w_out, branch, 1, 1)
    dqs, dks, dvs, dgs, ggains, gbiases = [], [], [], [], [], []
    everything = slice(0, length)
    for head in range(heads):
        tall = slice(head * VD, (head + 1) * VD)
        g = jnp.concatenate(gates[head], axis=1)
        nhat = jnp.concatenate(nhats[head], axis=1)
        spread = jnp.concatenate(spreads[head], axis=1)
        q = jnp.concatenate(queries[head], axis=0)
        k = jnp.concatenate(keys[head], axis=0)
        v = jnp.concatenate(values[head], axis=1)
        sigmoid = jax.nn.sigmoid(g)
        silu = g * sigmoid
        up = dgated[tall]
        dgn = up * silu
        ggains.append(jnp.sum(dgn * nhat, axis=1))
        gbiases.append(jnp.sum(dgn, axis=1))
        f = dgn * ggain[tall]
        dret = (
            f - jnp.mean(f, axis=0, keepdims=True) - nhat * jnp.mean(f * nhat, axis=0, keepdims=True)
        ) * spread
        dret = low(dret)
        gn = nhat * ggain[tall] + gbias[tall]
        dgs.append(low(up * gn * (sigmoid + silu * (1.0 - sigmoid))))
        table = decay(head, everything, everything)
        scores = low(dot(q, k, 1, 1) * table)
        draw = low(dot(dret, v, 0, 0) * table)
        dvs.append(low(dot(dret, scores, 1, 0)))
        dqs.append(low(turn(dot(draw, k, 1, 0), cosine, -sine)))
        dks.append(low(turn(dot(draw, q, 0, 0), cosine, -sine) * KD ** (-0.5)))
    dv = jnp.concatenate(dvs, axis=0)
    dg = jnp.concatenate(dgs, axis=0)
    dq = jnp.concatenate(dqs, axis=1)
    dk = jnp.concatenate(dks, axis=1)
    partial_in = dot(dq, w_query, 1, 1) + dot(dk, w_key, 1, 1) + dot(dv, value_t, 0, 0) + dot(dg, gate_t, 0, 0)
    grad_norm1 = jnp.sum(partial_in * x * r1, axis=0)
    grad_qk = dot(h1, jnp.concatenate([dq, dk], axis=1), 0, 0)
    grad_v = dot(dv, h1, 1, 0)
    grad_g = dot(dg, h1, 1, 0)

    units = w_value.shape[1]
    small = jnp.stack(
        [
            grad_norm1,
            grad_norm2,
            jnp.pad(jnp.concatenate(ggains), (0, depth - units)),
            jnp.pad(jnp.concatenate(gbiases), (0, depth - units)),
        ]
    )
    small = jnp.pad(small, ((0, 4), (0, 0)))
    grads = lax.psum((grad_qk, grad_v, grad_g, grad_out, grad_mg, grad_mu, grad_md), "dp")
    peer = swap(partial_in)
    small = lax.psum(small.at[0].set(lax.psum(small[0], "tensor")), "dp")
    grad_qk, grad_v, grad_g, grad_out, grad_mg, grad_mu, grad_md = grads
    e1 = (partial_in + peer) * gain1
    grad_tokens = low(dmid + r1 * e1 - x * (r1 * r1 * r1) * jnp.mean(e1 * x, axis=1, keepdims=True))
    key_width = w_query.shape[1]
    return (
        output,
        grad_tokens,
        small[0],
        grad_qk[:, :key_width],
        grad_qk[:, key_width:],
        grad_v.T,
        grad_g.T,
        small[2, :units],
        small[3, :units],
        grad_out,
        small[1],
        grad_mg.T,
        grad_mu.T,
        grad_md,
    )


def body(
    tokens,
    segment,
    norm1_gain,
    w_query,
    w_key,
    w_value,
    w_gate,
    group_gain,
    group_bias,
    w_out,
    norm2_gain,
    w_mlp_gate,
    w_mlp_up,
    w_mlp_down,
    cotangent,
):
    length, depth = tokens.shape
    if depth % (LANE * (lax.axis_size("dp") // 2)):
        return plain_body(
            tokens, segment, norm1_gain, w_query, w_key, w_value, w_gate, group_gain, group_bias, w_out,
            norm2_gain, w_mlp_gate, w_mlp_up, w_mlp_down, cotangent,
        )
    value_t, gate_t, mg_t, mu_t = w_value.T, w_gate.T, w_mlp_gate.T, w_mlp_up.T
    tables = make_tables(length)
    vectors = pack_rows((norm1_gain, norm2_gain, group_gain, group_bias, segment), depth)
    (h1, qs, ks, vs, g, nhat, rstd, gated, mid, dh, h2, hid, grad_mg, grad_mu, grad_md, gathered) = forward(
        tokens,
        vectors,
        tables,
        (w_query, w_key, value_t, gate_t, w_out, mg_t, mu_t, w_mlp_down),
        cotangent,
    )
    (dmid, output, grad_mg, grad_mu, grad_md, part, grad_qk, grad_v, grad_g, grad_out, small) = backward(
        tokens,
        vectors,
        tables,
        cotangent,
        (mid, dh, h2, hid, gathered),
        (h1, qs, ks, vs, g, nhat, rstd, gated),
        (w_query, w_key, value_t, gate_t, w_out, w_mlp_down),
        (grad_mg, grad_mu, grad_md),
    )
    (grad_qk, grad_v, grad_g, grad_out, grad_tokens, small) = finish(
        (grad_qk, grad_v, grad_g, grad_out), part, small, tokens, dmid, vectors
    )
    units = w_value.shape[1]
    grad_q, grad_k, grad_v, grad_g, grad_out, grad_mg, grad_mu, grad_md, output, grad_tokens = deliver(
        (grad_qk, grad_v, grad_g, grad_out, grad_mg, grad_mu, grad_md), (output, grad_tokens), w_query.shape[1]
    )
    return (
        output,
        grad_tokens,
        small[0],
        grad_q,
        grad_k,
        grad_v.T,
        grad_g.T,
        small[2, :units],
        small[3, :units],
        grad_out,
        small[1],
        grad_mg.T,
        grad_mu.T,
        grad_md,
    )


def solution(mesh):
    placed = (
        P("dp", None),
        P("dp"),
        P(),
        P(None, "tensor"),
        P(None, "tensor"),
        P(None, "tensor"),
        P(None, "tensor"),
        P("tensor"),
        P("tensor"),
        P("tensor", None),
        P(),
        P(None, "tensor"),
        P(None, "tensor"),
        P("tensor", None),
        P("dp", None),
    )
    return jax.shard_map(
        body,
        mesh=mesh,
        in_specs=placed,
        out_specs=(
            P(("dp", "tensor"), None),
            P("dp", None),
            P(),
            P(None, "tensor"),
            P(None, "tensor"),
            P(None, "tensor"),
            P(None, "tensor"),
            P("tensor"),
            P("tensor"),
            P("tensor", None),
            P(),
            P(None, "tensor"),
            P(None, "tensor"),
            P("tensor", None),
        ),
        check_vma=False,
    )
```

```python
import functools
import math

import jax
import jax.numpy as jnp
import numpy as np
from jax import lax
from jax.experimental import pallas as pl
from jax.experimental.pallas import tpu as pltpu
from jax.sharding import PartitionSpec as P

KD = 256
VD = 432
LANE = 128
MESH = pl.DeviceIdType.MESH
DELIVER = 4
PIECES = 4
LAG = 8
VMEM_LIMIT = 63 * 1024 * 1024


EPSILON = 1e-06
GROUP_EPSILON = 0.25


def ring_place(chip, chips):
    line = chips // 2
    x = chip % 2
    z = chip // 2
    return z + x * (chips - 1 - 2 * z), line


def ring_chip(place, chips):
    line = chips // 2
    x = place // line
    z = place + x * (chips - 1 - 2 * place)
    return z * 2 + x


def bit_partner(index, bit):
    step = 1 << bit
    return index + (1 - 2 * ((index // step) % 2)) * step


BLOCKS = 4
GELU_A = math.sqrt(2.0 / math.pi)
GELU_B = 0.044715


def dot(left, right, left_dim, right_dim):
    return lax.dot_general(
        left, right, (((left_dim,), (right_dim,)), ((), ())), preferred_element_type=jnp.float32
    )


def low(array):
    return array.astype(jnp.bfloat16)


def turn(vectors, cosine, sine):
    half = vectors.shape[1] // 2
    lower, upper = vectors[:, :half], vectors[:, half:]
    return jnp.concatenate([lower * cosine - upper * sine, upper * cosine + lower * sine], axis=1)


def remote(source, target, send, recv, device):
    return pltpu.make_async_remote_copy(
        source, target, send, recv, device_id=device, device_id_type=MESH
    )


def rate_of(head, heads, tensor):
    rates = [math.log1p(-(2.0 ** (-5 - order))) for order in range(2 * heads)]
    return jnp.where(tensor == 0, rates[head], rates[heads + head]).astype(jnp.float32)


def upright(row, size):
    diagonal = lax.broadcasted_iota(jnp.int32, (size, size), 0) == lax.broadcasted_iota(
        jnp.int32, (size, size), 1
    )
    return jnp.sum(jnp.where(diagonal, row, 0.0), axis=1, keepdims=True)


def upright_part(row, start, size):
    shape = (size, row.shape[1])
    chosen = lax.broadcasted_iota(jnp.int32, shape, 0) + start == lax.broadcasted_iota(jnp.int32, shape, 1)
    return jnp.sum(jnp.where(chosen, row, 0.0), axis=1, keepdims=True)


GAIN1, GAIN2, GROUP_GAIN, GROUP_BIAS, SEGMENT = range(5)


def greet(devices):
    barrier = pltpu.get_barrier_semaphore()
    for device in devices:
        pl.semaphore_signal(barrier, inc=1, device_id=device, device_id_type=MESH)
    pl.semaphore_wait(barrier, len(devices))


def mlp_part(gate_w, up_w, down_w, h2, cot, tall, rows):
    a = dot(gate_w[tall, :], h2[rows, :], 1, 1)
    b = dot(up_w[tall, :], h2[rows, :], 1, 1)
    dhidden = dot(down_w[tall, :], cot[rows, :], 1, 1)
    square = a * a
    t = jnp.tanh(GELU_A * a * (1.0 + GELU_B * square))
    gelu = 0.5 * a * (1.0 + t)
    slope = 0.5 * (1.0 + t) + 0.5 * a * (1.0 - t * t) * (GELU_A * (1.0 + 3.0 * GELU_B * square))
    dga = low(dhidden * b * slope)
    dup = low(dhidden * gelu)
    more = dot(dga, gate_w[tall, :], 0, 0) + dot(dup, up_w[tall, :], 0, 0)
    return low(gelu * b), dga, dup, more


def forward_kernel(
    chips,
    x_ref,
    rows_ref,
    cos_ref,
    sin_ref,
    wq_hbm,
    wk_hbm,
    wv_hbm,
    wg_hbm,
    wo_ref,
    mg_ref,
    mu_ref,
    md_ref,
    cot_ref,
    h1_out,
    q_out,
    k_out,
    v_out,
    g_out,
    nh_out,
    rstd_out,
    gated_out,
    mid_out,
    dh_out,
    h2_out,
    hid_out,
    grad_mg_out,
    grad_mu_out,
    grad_md_out,
    gath_out,
    weights,
    others,
    cot,
    h1,
    q,
    k,
    v,
    g,
    nh,
    rstd,
    gated,
    acc,
    gsend,
    grecv,
    h2,
    hid,
    da,
    db,
    mid,
    dh_own,
    sums,
    ggain_ref,
    gbias_ref,
    in_sem,
    save_sem,
    out_sem,
    stage_sem,
    mid_sem,
    dh_sem,
    sum_sem,
    xs_sem,
    xr_sem,
    ys_sem,
    yr_sem,
    gs_sem,
    gr_sem,
    cs_sem,
    cr_sem,
):
    index, tensor = lax.axis_index("dp"), lax.axis_index("tensor")
    core = index % 2
    place, _ = ring_place(index // 2, chips)
    nexts = [
        {"dp": ring_chip((place + 1) % chips, chips) * 2 + core},
        {"dp": ring_chip((place + chips - 1) % chips, chips) * 2 + core},
    ]
    sibling, peer = {"dp": index + 1 - 2 * core}, {"tensor": 1 - tensor}
    heads = q.shape[1]
    units, length = v.shape
    block = length // BLOCKS
    third = units // 3
    f32 = jnp.float32

    for number, source in enumerate((wo_ref, mg_ref, mu_ref, md_ref)):
        pltpu.make_async_copy(source, weights.at[number], in_sem.at[number]).start()
    wv_ref, wg_ref = hid, da
    key_width = wq_hbm.shape[1]
    early = [
        pltpu.make_async_copy(wq_hbm, h2.at[:, pl.ds(0, key_width)], in_sem.at[5]),
        pltpu.make_async_copy(wk_hbm, h2.at[:, pl.ds(key_width, key_width)], in_sem.at[6]),
        pltpu.make_async_copy(wv_hbm, wv_ref, in_sem.at[7]),
        pltpu.make_async_copy(wg_hbm, wg_ref, in_sem.at[8]),
    ]
    for copy in early:
        copy.start()
    pltpu.make_async_copy(cot_ref, cot, in_sem.at[4]).start()
    greet([*nexts, sibling, peer])

    rows_slice = units // 2
    half_slice = rows_slice // 2

    def area(w, where, which, half=None):
        start = which * rows_slice + (0 if half is None else half * half_slice)
        size = rows_slice if half is None else half_slice
        return gath_out.at[
            w,
            pl.ds(pl.multiple_of(start, 8), size),
            pl.ds(pl.multiple_of(where * LANE, LANE), LANE),
        ]

    def slice_spot(w):
        return gsend.at[
            BLOCKS - 1,
            pl.ds((w % 2) * rows_slice, rows_slice),
            pl.ds((w // 2) * LANE, LANE),
        ]

    def y_copy(w):
        return remote(slice_spot(w), area(w, place, core), ys_sem.at[w], yr_sem.at[w], peer)

    def hop(w, d, t):
        where = (place - t + chips) % chips if d == 0 else (place + t) % chips
        part = area(w, where, core, d if t == chips // 2 - 1 else None)
        return remote(part, part, gs_sem.at[w, d, t], gr_sem.at[w, d, t], nexts[d])

    def arrived(w, d, t):
        where = (place - t - 1 + chips) % chips if d == 0 else (place + t + 1) % chips
        part = area(w, where, core, d if t == chips // 2 - 1 else None)
        pltpu.make_async_copy(part, part, gr_sem.at[w, d, t]).wait()
        return where

    def share(w, slot, where, half=None):
        part = area(w, where, core, half)
        remote(part, part, cs_sem.at[w, slot], cr_sem.at[w, slot], sibling).start()

    steps = chips // 2

    def begin(w):
        y_copy(w).wait_recv()
        for d in range(2):
            hop(w, d, 0).start()
        share(w, 0, place)

    def pump(w, t):
        for d in range(2):
            where = arrived(w, d, t)
            if t < steps - 1:
                hop(w, d, t + 1).start()
            share(w, 1 + 2 * t + d, where, d if t == steps - 1 else None)

    for number in range(4):
        pltpu.make_async_copy(wo_ref, weights.at[number], in_sem.at[number]).wait()
        slice_spot(number)[...] = weights[
            number,
            pl.ds(pl.multiple_of(core * rows_slice, 16), rows_slice),
            pl.ds(pl.multiple_of(place * LANE, LANE), LANE),
        ].astype(f32)
        y_copy(number).start()

    def exchange(i):
        return remote(gsend.at[i], grecv.at[i], xs_sem.at[i], xr_sem.at[i], peer)

    ahead = lax.broadcasted_iota(jnp.int32, (block, block), 0) - lax.broadcasted_iota(
        jnp.int32, (block, block), 1
    )

    def saves(i):
        slot = i % 2
        rows = pl.ds(pl.multiple_of(i * block, block), block)
        pairs = (
            (h1.at[slot], h1_out.at[rows, :]),
            (q.at[slot], q_out.at[:, rows, :]),
            (g.at[slot], g_out.at[:, rows]),
            (nh.at[slot], nh_out.at[:, rows]),
        )
        return [
            pltpu.make_async_copy(source, target, save_sem.at[number, slot])
            for number, (source, target) in enumerate(pairs)
        ]

    def attention(i, carry):
        rows = pl.ds(pl.multiple_of(i * block, block), block)
        slot = i % 2

        @pl.when(i >= 2)
        def _():
            for copy in saves(i - 2):
                copy.wait()

        xb = x_ref[rows, :].astype(f32)
        r1 = lax.rsqrt(jnp.mean(xb * xb, axis=1, keepdims=True) + EPSILON)
        h1[slot] = low(xb * r1 * rows_ref[GAIN1 : GAIN1 + 1, :])
        cosine, sine = cos_ref[rows, :], sin_ref[rows, :]
        for head in range(heads):
            wide = slice(head * KD, (head + 1) * KD)
            q[slot, head] = low(turn(dot(h1[slot], h2[:, wide], 1, 0), cosine, sine))
            wide = slice(key_width + head * KD, key_width + (head + 1) * KD)
            k[head, rows, :] = low(turn(dot(h1[slot], h2[:, wide], 1, 0), cosine, sine) * KD ** (-0.5))
        v[:, rows] = low(dot(wv_ref[...], h1[slot], 1, 1))

        @pl.when(i == BLOCKS - 1)
        def _():
            for w in range(4):
                y_copy(w).wait_send()

        segc = upright(rows_ref[SEGMENT : SEGMENT + 1, rows], block)
        for head in range(heads):
            tall = slice(head * VD, (head + 1) * VD)
            rate = rate_of(head, heads, tensor)
            acc[...] = jnp.zeros_like(acc)

            def tile(m, carry):
                cols = pl.ds(pl.multiple_of(m * block, block), block)
                s = dot(q[slot, head], k[head, cols, :], 1, 1)
                gap = ahead + (i - m) * block
                seen = (segc == rows_ref[SEGMENT : SEGMENT + 1, cols]) & (gap >= 0)
                s = jnp.where(seen, s * jnp.exp(gap.astype(f32) * rate), 0.0)
                acc[...] += dot(v[tall, cols], low(s), 1, 1)
                return carry

            lax.fori_loop(0, i + 1, tile, 0)
            ret = acc[...]
            centred = ret - jnp.mean(ret, axis=0, keepdims=True)
            scale = lax.rsqrt(jnp.mean(centred * centred, axis=0, keepdims=True) + GROUP_EPSILON)
            nhat = centred * scale
            nh[slot, tall, :] = low(nhat)
            rstd[head : head + 1, rows] = scale
            gate = dot(wg_ref[tall, :], h1[slot], 1, 1)
            g[slot, tall, :] = low(gate)
            gn = nhat * ggain_ref[tall, :] + gbias_ref[tall, :]
            out = low(gate / (1.0 + jnp.exp(-gate)) * gn)
            gated[tall, rows] = out
            gsend[i, tall, :] = out.astype(f32)
        exchange(i).start()
        for copy in saves(i):
            copy.start()

        @pl.when(i == 0)
        def _():
            begin(0)

        @pl.when(i == 1)
        def _():
            pump(0, 0)
            for w in range(1, 4):
                begin(w)

        @pl.when(i == 2)
        def _():
            pump(0, 1)

        return carry

    rstd[...] = jnp.zeros_like(rstd)
    for n in range(3):
        where = slice(n * third, (n + 1) * third)
        ggain_ref[where, :] = upright_part(rows_ref[GROUP_GAIN : GROUP_GAIN + 1, :], n * third, third)
        gbias_ref[where, :] = upright_part(rows_ref[GROUP_BIAS : GROUP_BIAS + 1, :], n * third, third)
    for copy in early:
        copy.wait()
    lax.fori_loop(0, BLOCKS, attention, 0)
    for i in range(BLOCKS - 2, BLOCKS):
        for copy in saves(i):
            copy.wait()
    saved = [(k, k_out), (v, v_out), (rstd, rstd_out), (gated, gated_out)]
    for number, (source, target) in enumerate(saved):
        pltpu.make_async_copy(source, target, out_sem.at[number]).start()

    def cast_ready(w):
        for slot in range(1 + 2 * steps):
            t = (slot - 1) // 2
            d = (slot - 1) % 2
            if slot == 0:
                where = place
            else:
                where = (place - t - 1 + chips) % chips if d == 0 else (place + t + 1) % chips
            part = area(w, where, 1 - core, d if slot > 0 and t == steps - 1 else None)
            pltpu.make_async_copy(part, part, cr_sem.at[w, slot]).wait()

    def stage(number):
        return sums.at[0, pl.ds((number % 2) * third, third), :]

    def cast_in(ws):
        pieces = [(w, n) for w in ws for n in range(3)]

        def piece(number):
            w, n = pieces[number]
            return pltpu.make_async_copy(
                gath_out.at[w, pl.ds(n * third, third), :], stage(number), stage_sem.at[number % 2]
            )

        cast_ready(ws[0])
        piece(0).start()
        for number, (w, n) in enumerate(pieces):
            if number + 1 < len(pieces):
                if pieces[number + 1][1] == 0:
                    cast_ready(pieces[number + 1][0])
                piece(number + 1).start()
            piece(number).wait()
            others[n * third : (n + 1) * third, :] = low(stage(number)[...])

    pump(0, 2)
    pump(0, 3)
    cast_in([0])
    pltpu.make_async_copy(cot_ref, cot, in_sem.at[4]).wait()
    part = units // 2

    def mid_copy(i):
        rows = pl.ds(pl.multiple_of(i * block, block), block)
        return pltpu.make_async_copy(mid.at[i % 2], mid_out.at[rows, :], mid_sem.at[i % 2])

    def dh_copy(i):
        rows = pl.ds(pl.multiple_of(i * block, block), block)
        return pltpu.make_async_copy(dh_own.at[i % 2], dh_out.at[rows, :], dh_sem.at[i % 2])

    def own_half(i):
        rows = pl.ds(pl.multiple_of(i * block, block), block)
        slot = i % 2

        @pl.when(i >= 2)
        def _():
            mid_copy(i - 2).wait()
            dh_copy(i - 2).wait()

        exchange(i).wait_recv()
        mid[slot] = x_ref[rows, :].astype(f32) + (
            dot(gated[:, rows], weights[0], 0, 0) + dot(low(grecv[i]), others[...], 0, 0)
        )
        mid_copy(i).start()
        r2 = lax.rsqrt(jnp.mean(mid[slot] * mid[slot], axis=1, keepdims=True) + EPSILON)
        h2[rows, :] = low(mid[slot] * r2 * rows_ref[GAIN2 : GAIN2 + 1, :])
        for f in range(2):
            tall = slice(f * part, (f + 1) * part)
            hid[tall, rows], da[tall, rows], db[tall, rows], more = mlp_part(
                weights.at[1], weights.at[2], weights.at[3], h2, cot, tall, rows
            )
            dh_own[slot] = more if f == 0 else dh_own[slot] + more
        dh_copy(i).start()

    def first_pass(i, carry):
        for t in range(3):

            @pl.when(i == t)
            def _():
                for w in range(1, 4):
                    pump(w, t)

        own_half(i)
        return carry

    products = ((da, h2, grad_mg_out), (db, h2, grad_mu_out), (hid, cot, grad_md_out))
    before = (BLOCKS - 1) * block
    lax.fori_loop(0, BLOCKS - 1, first_pass, 0)
    for w in range(1, 4):
        pump(w, 3)
    for number, (source, right, _) in enumerate(products):
        for n in range(3):
            where = slice(n * third, (n + 1) * third)
            sums[number, where, :] = dot(source[where, 0:before], right[0:before, :], 1, 0)
    own_half(BLOCKS - 1)
    late = [
        pltpu.make_async_copy(h2, h2_out, out_sem.at[4]),
        pltpu.make_async_copy(hid, hid_out, out_sem.at[5]),
    ]
    for copy in late:
        copy.start()
    for number, (source, right, target) in enumerate(products):
        for n in range(3):
            where = slice(n * third, (n + 1) * third)
            sums[number, where, :] += dot(source[where, before:length], right[before:length, :], 1, 0)
            late.append(
                pltpu.make_async_copy(
                    sums.at[number, pl.ds(n * third, third), :],
                    target.at[pl.ds(n * third, third), :],
                    sum_sem.at[number, n],
                )
            )
            late[-1].start()
    for copy in late:
        copy.wait()
    for w in range(1, 4):
        cast_ready(w)
    for i in range(BLOCKS - 2, BLOCKS):
        mid_copy(i).wait()
        dh_copy(i).wait()
    for number, (source, target) in enumerate(saved):
        pltpu.make_async_copy(source, target, out_sem.at[number]).wait()
    for w in range(4):
        for t in range(steps):
            for d in range(2):
                hop(w, d, t).wait_send()
        for slot in range(1 + 2 * steps):
            last = slot > 0 and (slot - 1) // 2 == steps - 1
            part_ref = area(w, place, core, 0 if last else None)
            pltpu.make_async_copy(part_ref, part_ref, cs_sem.at[w, slot]).wait()
    for i in range(BLOCKS):
        exchange(i).wait_send()


def forward(tokens, vectors, tables, ws, cotangent):
    chips = lax.axis_size("dp") // 2
    length, depth = tokens.shape
    wq, wk, wv, wg, wo, mg, mu, md = ws
    units = wv.shape[0]
    heads = wq.shape[1] // KD
    block = length // BLOCKS
    f32, bf16 = jnp.float32, jnp.bfloat16
    vmem = pl.BlockSpec(memory_space=pltpu.VMEM)
    hbm = pl.BlockSpec(memory_space=pl.ANY)
    dma = lambda *shape: pltpu.SemaphoreType.DMA(shape)
    shape = jax.ShapeDtypeStruct
    tall = (units, length)
    steps = chips // 2
    outs = [
        (shape((length, depth), bf16), hbm),
        (shape((heads, length, KD), bf16), hbm),
        (shape((heads, length, KD), bf16), hbm),
        (shape(tall, bf16), hbm),
        (shape(tall, bf16), hbm),
        (shape(tall, bf16), hbm),
        (shape((8, length), f32), hbm),
        (shape(tall, bf16), hbm),
        (shape((length, depth), f32), hbm),
        (shape((length, depth), f32), hbm),
        (shape((length, depth), bf16), hbm),
        (shape(tall, bf16), hbm),
        (shape((units, depth), f32), hbm),
        (shape((units, depth), f32), hbm),
        (shape((units, depth), f32), hbm),
        (shape((4, units, depth), f32), hbm),
    ]
    scratch = [
        pltpu.VMEM((4, units, depth), bf16),
        pltpu.VMEM((units, depth), bf16),
        pltpu.VMEM((length, depth), bf16),
        pltpu.VMEM((2, block, depth), bf16),
        pltpu.VMEM((2, heads, block, KD), bf16),
        pltpu.VMEM((heads, length, KD), bf16),
        pltpu.VMEM(tall, bf16),
        pltpu.VMEM((2, units, block), bf16),
        pltpu.VMEM((2, units, block), bf16),
        pltpu.VMEM((8, length), f32),
        pltpu.VMEM(tall, bf16),
        pltpu.VMEM((VD, block), f32),
        pltpu.VMEM((BLOCKS, units, block), f32),
        pltpu.VMEM((BLOCKS, units, block), f32),
        pltpu.VMEM((length, depth), bf16),
        pltpu.VMEM(tall, bf16),
        pltpu.VMEM(tall, bf16),
        pltpu.VMEM(tall, bf16),
        pltpu.VMEM((2, block, depth), f32),
        pltpu.VMEM((2, block, depth), f32),
        pltpu.VMEM((3, units, depth), f32),
        pltpu.VMEM((units, 1), f32),
        pltpu.VMEM((units, 1), f32),
        dma(9),
        dma(4, 2),
        dma(6),
        dma(2),
        dma(2),
        dma(2),
        dma(3, 3),
        dma(BLOCKS),
        dma(BLOCKS),
        dma(4),
        dma(4),
        dma(4, 2, steps),
        dma(4, 2, steps),
        dma(4, 1 + 2 * steps),
        dma(4, 1 + 2 * steps),
    ]
    return pl.pallas_call(
        functools.partial(forward_kernel, chips),
        out_shape=tuple(o for o, _ in outs),
        in_specs=[vmem] * 4 + [hbm] * 9,
        out_specs=tuple(s for _, s in outs),
        scratch_shapes=scratch,
        compiler_params=pltpu.CompilerParams(
            collective_id=1, has_side_effects=True, vmem_limit_bytes=VMEM_LIMIT
        ),
        cost_estimate=pl.CostEstimate(
            flops=40 * length * depth * units, bytes_accessed=80 * length * depth, transcendentals=0
        ),
    )(tokens, vectors, *tables, wq, wk, wv, wg, wo, mg, mu, md, cotangent)


def make_tables(length):
    half = KD // 2
    frequency = np.exp(-np.log(10000.0) * np.arange(half) / half)
    angles = np.arange(length)[:, None] * frequency[None, :]
    return jnp.asarray(np.cos(angles), jnp.float32), jnp.asarray(np.sin(angles), jnp.float32)


def pack_rows(arrays, width):
    rows = [jnp.pad(a.astype(jnp.float32), (0, width - a.shape[0])) for a in arrays]
    return jnp.pad(jnp.stack(rows), ((0, 8 - len(rows)), (0, 0)))


class Ring:
    def __init__(self, chips, quarters, own, sib, rcv, own_sem, sbs_sem, sbr_sem, rss_sem, rsr_sem):
        self.chips, self.quarters = chips, quarters
        self.index, self.tensor = lax.axis_index("dp"), lax.axis_index("tensor")
        self.core = self.index % 2
        place, _ = ring_place(self.index // 2, chips)
        self.place = place
        self.nexts = [
            {"dp": ring_chip((place + 1) % chips, chips) * 2 + self.core},
            {"dp": ring_chip((place + chips - 1) % chips, chips) * 2 + self.core},
        ]
        self.virtual = [place, (chips - place) % chips]
        self.sibling = {"dp": self.index + 1 - 2 * self.core}
        self.peer = {"tensor": 1 - self.tensor}
        self.offsets = [sum(quarters[:i]) for i in range(len(quarters))]
        self.own, self.sib, self.rcv = own, sib, rcv
        self.own_sem, self.sbs_sem, self.sbr_sem = own_sem, sbs_sem, sbr_sem
        self.rss_sem, self.rsr_sem = rss_sem, rsr_sem
        self.tokens = [(d, a) for a in range(len(quarters)) for d in range(2)]

    def window(self, which, d, chunk, rows):
        return (
            pl.ds(pl.multiple_of((which * 2 + d) * rows, 8), rows),
            pl.ds(pl.multiple_of(chunk * LANE, LANE), LANE),
        )

    def packed(self, a):
        return pl.ds(self.offsets[a], self.quarters[a])

    def chunk_at(self, d, order):
        return (self.virtual[d] + 2 * self.chips - 1 - order) % self.chips

    def quarter(self, which, d, a):
        rows = self.quarters[a]
        return pl.ds(pl.multiple_of((which * 2 + d) * rows, 8), rows)

    def own_copy(self, grads, d, a):
        return pltpu.make_async_copy(
            grads[a].at[self.quarter(self.core, d, a), :],
            self.own.at[d, self.packed(a), :],
            self.own_sem.at[d, a],
        )

    def sib_copy(self, grads, d, a):
        return remote(
            grads[a].at[self.quarter(1 - self.core, d, a), :],
            self.sib.at[d, self.packed(a), :],
            self.sbs_sem.at[d, a],
            self.sbr_sem.at[d, a],
            self.sibling,
        )

    def load(self, grads):
        for d, a in self.tokens:
            self.own_copy(grads, d, a).start()
            self.sib_copy(grads, d, a).start()

    def columns(self, d, order):
        return pl.ds(pl.multiple_of(self.chunk_at(d, order) * LANE, LANE), LANE)

    def chunk(self, d, a, order):
        return self.own.at[d, self.packed(a), self.columns(d, order)]

    def rs_copy(self, d, a, step):
        return remote(
            self.chunk(d, a, step),
            self.rcv.at[d, step, self.packed(a), :],
            self.rss_sem.at[d, a, step],
            self.rsr_sem.at[d, a, step],
            self.nexts[d],
        )

    def total(self, grads, d, a, step, first=False):
        if first:
            self.own_copy(grads, d, a).wait()
            self.sib_copy(grads, d, a).wait_recv()
        part, where = self.packed(a), self.columns(d, step)
        value = self.own[d, part, where] + self.sib[d, part, where]
        if not first:
            self.rs_copy(d, a, step - 1).wait_recv()
            value = value + self.rcv[d, step - 1, part, :]
        self.own[d, part, where] = value

    def drain_ring(self):
        def ring_step(step, carry):
            for d, a in self.tokens:
                self.rs_copy(d, a, step).wait_send()
            return carry

        lax.fori_loop(0, self.chips - 1, ring_step, 0)

    def drain_pair(self, grads):
        for d, a in self.tokens:
            self.sib_copy(grads, d, a).wait_send()


class Spread:
    def __init__(self, ring, quarters, outs, buffer, ags_sem, agr_sem, cgs_sem, cgr_sem, loc_sem):
        self.ring, self.quarters, self.outs, self.buffer = ring, quarters, outs, buffer
        self.ags_sem, self.agr_sem, self.cgs_sem, self.cgr_sem, self.loc_sem = (
            ags_sem, agr_sem, cgs_sem, cgr_sem, loc_sem,
        )
        self.offsets = [sum(quarters[:i]) for i in range(len(quarters))]
        self.tokens = [(d, a) for a in range(len(quarters)) for d in range(2)]

    def packed(self, a):
        return pl.ds(self.offsets[a], self.quarters[a])

    def part(self, which, d, a, step):
        ring = self.ring
        chunk = (ring.virtual[d] + 2 * ring.chips - step) % ring.chips
        return self.outs[a].at[ring.window(which, d, chunk, self.quarters[a])]

    def slot(self, d, a, step):
        return self.buffer.at[d, step, self.packed(a), :]

    def ring_copy(self, d, a, step, source=None):
        return remote(
            self.slot(d, a, step - 1) if source is None else source,
            self.slot(d, a, step),
            self.ags_sem.at[d, a, step],
            self.agr_sem.at[d, a, step],
            self.ring.nexts[d],
        )

    def pair_copy(self, d, a, step, source=None):
        return remote(
            self.slot(d, a, step - 1) if source is None else source,
            self.part(self.ring.core, d, a, step),
            self.cgs_sem.at[d, a, step],
            self.cgr_sem.at[d, a, step],
            self.ring.sibling,
        )

    def local_copy(self, d, a, step, source=None):
        return pltpu.make_async_copy(
            self.slot(d, a, step - 1) if source is None else source,
            self.part(self.ring.core, d, a, step),
            self.loc_sem.at[d, a, step],
        )

    def place(self, d, a, step, source=None):
        self.pair_copy(d, a, step, source).start()
        self.local_copy(d, a, step, source).start()

    def arrived(self, d, a, step):
        part = self.slot(d, a, step)
        pltpu.make_async_copy(part, part, self.agr_sem.at[d, a, step]).wait()

    def finish(self, step):
        for d, a in self.tokens:
            self.arrived(d, a, step)
            self.place(d, a, step + 1)

    def drain_ring(self):
        def ring_step(step, carry):
            for d, a in self.tokens:
                part = self.slot(d, a, step)
                pltpu.make_async_copy(part, part, self.ags_sem.at[d, a, step]).wait()
            return carry

        lax.fori_loop(0, self.ring.chips - 1, ring_step, 0)

    def drain(self):
        def pair_step(step, carry):
            for d, a in self.tokens:
                part = self.part(self.ring.core, d, a, step)
                pltpu.make_async_copy(part, part, self.cgs_sem.at[d, a, step]).wait()
                pltpu.make_async_copy(part, part, self.cgr_sem.at[d, a, step]).wait()
                pltpu.make_async_copy(part, part, self.loc_sem.at[d, a, step]).wait()
            return carry

        lax.fori_loop(0, self.ring.chips, pair_step, 0)


def backward_kernel(
    chips,
    quarters,
    x_hbm,
    rows_ref,
    cos_ref,
    sin_ref,
    cot_hbm,
    h2_hbm,
    hid_hbm,
    md_hbm,
    mid_hbm,
    dh_hbm,
    gath_hbm,
    wo_hbm,
    g_hbm,
    nh_hbm,
    rstd_hbm,
    q_hbm,
    k_hbm,
    v_hbm,
    wq_hbm,
    wk_hbm,
    wv_hbm,
    wg_hbm,
    h1_hbm,
    gated_hbm,
    grad_mg,
    grad_mu,
    grad_md,
    dmid_out,
    output_out,
    grad_mg_out,
    grad_mu_out,
    grad_md_out,
    part_out,
    grad_qk_out,
    grad_v_out,
    grad_g_out,
    grad_out_out,
    small_out,
    x,
    branch,
    wo,
    g,
    nh,
    rstd,
    q,
    k,
    v,
    wq,
    wk,
    wv,
    wg,
    h1,
    gated,
    acc_gain,
    acc_bias,
    dk,
    dv,
    dq,
    stage,
    fin,
    finished,
    own,
    sib,
    rcv,
    buffer,
    ggain_ref,
    gbias_ref,
    segc_ref,
    in_sem,
    stage_sem,
    column_sem,
    fin_sem,
    dmid_sem,
    output_sem,
    own_sem,
    sbs_sem,
    sbr_sem,
    rss_sem,
    rsr_sem,
    *spread_sems,
):
    ring = Ring(chips, quarters, own, sib, rcv, own_sem, sbs_sem, sbr_sem, rss_sem, rsr_sem)
    grads = (grad_mg, grad_mu, grad_md)
    spread = Spread(ring, quarters, (grad_mg_out, grad_mu_out, grad_md_out), buffer, *spread_sems)
    f32 = jnp.float32
    heads = q.shape[0]
    length = h1.shape[0]
    units = v.shape[0]
    block = length // BLOCKS
    third = units // 3
    cot, h2, hid, md = x, h1, gated, v
    mg_o, mu_o, md_o = wv, wg, wo
    pairs = [
        (cot_hbm, cot), (h2_hbm, h2), (hid_hbm, hid), (md_hbm, md),
        (g_hbm, g), (nh_hbm, nh), (rstd_hbm, rstd), (q_hbm, q), (k_hbm, k), (wq_hbm, wq), (wk_hbm, wk),
        (wo_hbm, wo), (v_hbm, v), (wv_hbm, wv), (wg_hbm, wg), (x_hbm, x), (h1_hbm, h1), (gated_hbm, gated),
    ]
    copies = [pltpu.make_async_copy(a, b, in_sem.at[n]) for n, (a, b) in enumerate(pairs)]
    greet([*ring.nexts, ring.sibling])
    ring.load(grads)

    cast_list = [(w, target, n) for w, target in ((1, mg_o), (2, mu_o), (3, md_o)) for n in range(3)]

    def cast_copy(number):
        w, _, n = cast_list[number]
        return pltpu.make_async_copy(
            gath_hbm.at[w, pl.ds(n * third, third), :], stage.at[number % 2], stage_sem.at[number % 2]
        )

    cast_copy(0).start()
    for copy in copies[:4]:
        copy.start()
    for copy in copies[4:11]:
        copy.start()
    acc_gain[...] = jnp.zeros_like(acc_gain)
    acc_bias[...] = jnp.zeros_like(acc_bias)
    small_out[...] = jnp.zeros_like(small_out)
    for n in range(3):
        where = slice(n * third, (n + 1) * third)
        ggain_ref[where, :] = upright_part(rows_ref[GROUP_GAIN : GROUP_GAIN + 1, :], n * third, third)
        gbias_ref[where, :] = upright_part(rows_ref[GROUP_BIAS : GROUP_BIAS + 1, :], n * third, third)
    for n in range(BLOCKS):
        where = slice(n * block, (n + 1) * block)
        segc_ref[where, :] = upright(rows_ref[SEGMENT : SEGMENT + 1, where], block)
    plan = [(step, a) for step in range(2 * chips - 1) for a in range(len(quarters))]

    def pump(count=1):
        for _ in range(min(count, len(plan))):
            step, a = plan.pop(0)
            for d in range(2):
                if step < chips:
                    ring.total(grads, d, a, step, step == 0)
                if step < chips - 1:
                    ring.rs_copy(d, a, step).start()
                    continue
                turn_step = step - (chips - 1)
                source = ring.chunk(d, a, chips - 1) if turn_step == 0 else None
                if turn_step > 0:
                    spread.arrived(d, a, turn_step - 1)
                if turn_step < chips - 1:
                    spread.ring_copy(d, a, turn_step, source).start()
                spread.place(d, a, turn_step, source)

    fin_rows = [pl.ds(i * block, block) for i in range(BLOCKS)]

    def fin_copy(i, which):
        source = (mid_hbm, dh_hbm)[which]
        return pltpu.make_async_copy(source.at[fin_rows[i], :], fin.at[which], fin_sem.at[which])

    for which in range(2):
        fin_copy(0, which).start()
    for number, (_, target, n) in enumerate(cast_list):
        if number + 1 < len(cast_list):
            cast_copy(number + 1).start()
        cast_copy(number).wait()
        target[n * third : (n + 1) * third, :] = low(stage[number % 2])
        if number % 2 == 0:
            pump()
    for copy in copies[:4]:
        copy.wait()
    dh_oth, out_sum = stage.at[0, pl.ds(0, block), :], stage.at[1, pl.ds(0, block), :]
    half_units = units // 2

    def output_copy(i):
        spot = pl.ds((i % (BLOCKS // 2)) * block, block)
        return pltpu.make_async_copy(finished, output_out.at[spot, :], output_sem)

    def dmid_copy(i):
        return pltpu.make_async_copy(fin.at[1], dmid_out.at[fin_rows[i], :], dmid_sem)

    gain2 = rows_ref[GAIN2 : GAIN2 + 1, :]
    for i in range(BLOCKS):
        rows = fin_rows[i]
        for which in range(2):
            fin_copy(i, which).wait()
        mine = ring.tensor == i // (BLOCKS // 2)
        for f in range(2):
            tall = slice(f * half_units, (f + 1) * half_units)
            hidden, _, _, more = mlp_part(mg_o, mu_o, md_o, h2, cot, tall, rows)
            dh_oth[...] = more if f == 0 else dh_oth[...] + more

            @pl.when(mine)
            def _():
                lift = dot(hidden, md_o[tall, :], 0, 0) + dot(hid[tall, rows], md[tall, :], 0, 0)
                out_sum[...] = lift if f == 0 else out_sum[...] + lift

            pump()

        @pl.when(mine)
        def _():
            if i % (BLOCKS // 2):
                output_copy(i - 1).wait()
            finished[...] = low(fin[0] + out_sum[...])
            output_copy(i).start()

        mid = fin[0]
        r2 = lax.rsqrt(jnp.mean(mid * mid, axis=1, keepdims=True) + EPSILON)
        dh2 = fin[1] + dh_oth[...]
        e = dh2 * gain2
        inner = jnp.mean(e * mid, axis=1, keepdims=True)
        small_out[1:2, :] += jnp.sum(dh2 * mid * r2, axis=0, keepdims=True)
        result = cot[rows, :].astype(f32) + r2 * e - mid * (r2 * r2 * r2 * inner)
        fin[1] = result
        branch[rows, :] = low(result)
        dmid_copy(i).start()
        if i < BLOCKS - 1:
            fin_copy(i + 1, 0).start()
            dmid_copy(i).wait()
            fin_copy(i + 1, 1).start()
        pump()
    for copy in copies[11:]:
        copy.start()
    for copy in copies[4:7]:
        copy.wait()
    copies[11].wait()

    def fold(values):
        return values[:, :LANE] + values[:, LANE:]

    def gate_block(i):
        rows = pl.ds(i * block, block)
        for head in range(heads):
            tall = slice(head * VD, (head + 1) * VD)
            up = dot(wo[tall, :], branch[rows, :], 1, 1)
            gate = g[tall, rows].astype(f32)
            nhat = nh[tall, rows].astype(f32)
            sigmoid = 1.0 / (1.0 + jnp.exp(-gate))
            silu = gate * sigmoid
            dgn = up * silu
            acc_gain[tall, :] += fold(dgn * nhat)
            acc_bias[tall, :] += fold(dgn)
            gain = ggain_ref[tall, :]
            f = dgn * gain
            mean = jnp.mean(f, axis=0, keepdims=True)
            inner = jnp.mean(f * nhat, axis=0, keepdims=True)
            nh[tall, rows] = low((f - mean - nhat * inner) * rstd[head : head + 1, rows])
            gn = nhat * gain + gbias_ref[tall, :]
            g[tall, rows] = low(up * gn * (sigmoid + silu * (1.0 - sigmoid)))
            pump()

    for i in range(BLOCKS):
        gate_block(i)
    for copy in (copies[7], copies[8], copies[12]):
        copy.wait()

    ahead = lax.broadcasted_iota(jnp.int32, (block, block), 0) - lax.broadcasted_iota(
        jnp.int32, (block, block), 1
    )

    def key_block(head, m):
        tall = slice(head * VD, (head + 1) * VD)
        cols = pl.ds(m * block, block)
        rate = rate_of(head, heads, ring.tensor)
        dk[...] = jnp.zeros_like(dk)
        dv[...] = jnp.zeros_like(dv)

        def tile(i, carry):
            rows = pl.ds(pl.multiple_of(i * block, block), block)
            gap = ahead + (i - m) * block
            seen = (segc_ref[rows, :] == rows_ref[SEGMENT : SEGMENT + 1, cols]) & (gap >= 0)
            decay = jnp.where(seen, jnp.exp(gap.astype(f32) * rate), 0.0)
            scores = low(dot(q[head, rows, :], k[head, cols, :], 1, 1) * decay)
            draw = low(dot(nh[tall, rows], v[tall, cols], 0, 0) * decay)
            dv[...] += dot(nh[tall, rows], scores, 1, 0)
            dk[...] += dot(draw, q[head, rows, :], 0, 0)
            more = dot(draw, k[head, cols, :], 1, 0)
            if m == 0:
                dq[rows, :] = more
            else:
                dq[rows, :] += more
            return carry

        if m == 0:
            lax.fori_loop(0, BLOCKS // 2, tile, 0)
            pump()
            lax.fori_loop(BLOCKS // 2, BLOCKS, tile, 0)
        else:
            lax.fori_loop(m, BLOCKS, tile, 0)
        v[tall, cols] = low(dv[...])
        k[head, cols, :] = low(turn(dk[...], cos_ref[cols, :], -sin_ref[cols, :]) * KD ** (-0.5))

    for head in range(heads):
        for m in range(BLOCKS):
            key_block(head, m)
            if m == BLOCKS - 1:
                q[head] = low(turn(dq[...], cos_ref[...], -sin_ref[...]))
            pump()

    for copy in (*copies[9:11], *copies[13:]):
        copy.wait()
    column = dq

    def stage_wait(slot):
        pltpu.make_async_copy(stage.at[slot], stage.at[slot], stage_sem.at[slot]).wait()

    key_parts = [(q, wq), (k, wk)]
    for i in range(BLOCKS):
        slot = i % 2
        rows = pl.ds(i * block, block)
        if i >= 2:
            stage_wait(slot)
        total = None
        for values, weights in key_parts:
            for head in range(heads):
                wide = slice(head * KD, (head + 1) * KD)
                more = dot(values[head, rows, :], weights[:, wide], 1, 1)
                total = more if total is None else total + more
        stage[slot, 0:block, :] = total
        pump()
        stage[slot, 0:block, :] += dot(v[:, rows], wv[...], 0, 0)
        pump()
        stage[slot, 0:block, :] += dot(g[:, rows], wg[...], 0, 0)
        xb = x[rows, :].astype(f32)
        r1 = lax.rsqrt(jnp.mean(xb * xb, axis=1, keepdims=True) + EPSILON)
        small_out[0:1, :] += jnp.sum(stage[slot, 0:block, :] * (xb * r1), axis=0, keepdims=True)
        pltpu.make_async_copy(stage.at[slot], part_out.at[i], stage_sem.at[slot]).start()
        pump()

    count = BLOCKS
    for source, right, target in ((v, h1, grad_v_out), (g, h1, grad_g_out), (gated, branch, grad_out_out)):
        for n in range(3):
            where = pl.ds(n * third, third)
            slot = count % 2
            stage_wait(slot)
            stage[slot] = dot(source[where, :], right[...], 1, 0)
            pltpu.make_async_copy(stage.at[slot], target.at[where, :], stage_sem.at[slot]).start()
            count += 1
            pump()

    for number, (values, head) in enumerate([(q, 0), (q, 1), (k, 0), (k, 1)][: 2 * heads]):
        if number:
            pltpu.make_async_copy(column, column, column_sem).wait()
        column[...] = dot(h1[...], values[head], 0, 0)
        pltpu.make_async_copy(column, grad_qk_out.at[:, pl.ds(number * KD, KD)], column_sem).start()
        pump()
    pump(len(plan))

    ones = jnp.ones((8, LANE), jnp.bfloat16)

    def row_of(acc):
        whole = acc[...]
        high = low(whole)
        return dot(ones, high, 1, 1) + dot(ones, low(whole - high.astype(f32)), 1, 1)

    small_out[2:3, 0:units] = row_of(acc_gain)[0:1, :]
    small_out[3:4, 0:units] = row_of(acc_bias)[0:1, :]

    ring.drain_ring()
    ring.drain_pair(grads)
    spread.drain_ring()
    spread.drain()
    dmid_copy(BLOCKS - 1).wait()
    output_copy(BLOCKS - 1).wait()
    for slot in range(2):
        stage_wait(slot)
    pltpu.make_async_copy(column, column, column_sem).wait()


def backward(tokens, vectors, tables, cotangent, mlp, saved, ws, mlp_grads):
    chips = lax.axis_size("dp") // 2
    length, depth = tokens.shape
    wq, wk, wv, wg, wo, md = ws
    h1, q, k, v, g, nh, rstd, gated = saved
    mid, dh, h2, hid, gathered = mlp
    units = wv.shape[0]
    heads = q.shape[0]
    block = length // BLOCKS
    quarters = tuple(a.shape[0] // 4 for a in mlp_grads)
    rows = sum(quarters)
    count = len(quarters)
    f32, bf16 = jnp.float32, jnp.bfloat16
    vmem = pl.BlockSpec(memory_space=pltpu.VMEM)
    hbm = pl.BlockSpec(memory_space=pl.ANY)
    dma = lambda *shape: pltpu.SemaphoreType.DMA(shape)
    shape = jax.ShapeDtypeStruct
    tall = (units, length)
    stage_rows = max(block, units // 3)
    outs = [
        (shape((length, depth), f32), hbm),
        (shape((length // 2, depth), bf16), hbm),
        (shape((units, depth), f32), hbm),
        (shape((units, depth), f32), hbm),
        (shape((units, depth), f32), hbm),
        (shape((BLOCKS, stage_rows, depth), f32), hbm),
        (shape((depth, 2 * heads * KD), f32), hbm),
        (shape((units, depth), f32), hbm),
        (shape((units, depth), f32), hbm),
        (shape((units, depth), f32), hbm),
        (shape((8, depth), f32), vmem),
    ]
    scratch = [
        pltpu.VMEM((length, depth), bf16),
        pltpu.VMEM((length, depth), bf16),
        pltpu.VMEM((units, depth), bf16),
        pltpu.VMEM(tall, bf16),
        pltpu.VMEM(tall, bf16),
        pltpu.VMEM((8, length), f32),
        pltpu.VMEM((heads, length, KD), bf16),
        pltpu.VMEM((heads, length, KD), bf16),
        pltpu.VMEM(tall, bf16),
        pltpu.VMEM((depth, heads * KD), bf16),
        pltpu.VMEM((depth, heads * KD), bf16),
        pltpu.VMEM((units, depth), bf16),
        pltpu.VMEM((units, depth), bf16),
        pltpu.VMEM((length, depth), bf16),
        pltpu.VMEM(tall, bf16),
        pltpu.VMEM((units, LANE), f32),
        pltpu.VMEM((units, LANE), f32),
        pltpu.VMEM((block, KD), f32),
        pltpu.VMEM((VD, block), f32),
        pltpu.VMEM((length, KD), f32),
        pltpu.VMEM((2, stage_rows, depth), f32),
        pltpu.VMEM((2, block, depth), f32),
        pltpu.VMEM((block, depth), bf16),
        pltpu.VMEM((2, rows, depth), f32),
        pltpu.VMEM((2, rows, depth), f32),
        pltpu.VMEM((2, chips - 1, rows, LANE), f32),
        pltpu.VMEM((2, chips - 1, rows, LANE), f32),
        pltpu.VMEM((units, 1), f32),
        pltpu.VMEM((units, 1), f32),
        pltpu.VMEM((length, 1), f32),
        dma(18),
        dma(2),
        pltpu.SemaphoreType.DMA,
        dma(2),
        pltpu.SemaphoreType.DMA,
        pltpu.SemaphoreType.DMA,
        dma(2, count),
        dma(2, count),
        dma(2, count),
        dma(2, count, chips - 1),
        dma(2, count, chips - 1),
        dma(2, count, chips - 1),
        dma(2, count, chips - 1),
        dma(2, count, chips),
        dma(2, count, chips),
        dma(2, count, chips),
    ]
    return pl.pallas_call(
        functools.partial(backward_kernel, chips, quarters),
        out_shape=tuple(o for o, _ in outs),
        in_specs=[hbm] + [vmem] * 3 + [hbm] * 23,
        out_specs=tuple(s for _, s in outs),
        scratch_shapes=scratch,
        compiler_params=pltpu.CompilerParams(
            collective_id=2, has_side_effects=True, vmem_limit_bytes=VMEM_LIMIT
        ),
        cost_estimate=pl.CostEstimate(
            flops=20 * length * depth * units, bytes_accessed=80 * length * depth, transcendentals=0
        ),
    )(
        tokens, vectors, *tables, cotangent, h2, hid, md, mid, dh, gathered,
        wo, g, nh, rstd, q, k, v, wq, wk, wv, wg, h1, gated, *mlp_grads,
    )


def finish_kernel(
    chips,
    quarters,
    *refs,
):
    count = len(quarters)
    grads = refs[:count]
    part_hbm, small_ref, x_hbm, dmid_hbm, rows_ref = refs[count : count + 5]
    refs = refs[count + 5 :]
    outs = refs[:count]
    tokens_out, small_out = refs[count : count + 2]
    (late_buffer, own, sib, rcv, sacc, sbuf, part, peer, x, dmid, result, in_sem, res_sem, hs_sem, hr_sem, ss_sem, sr_sem) = refs[
        count + 2 : count + 19
    ]
    sems = refs[count + 19 :]
    ring = Ring(chips, quarters, own, sib, rcv, *sems[:5])
    late = Spread(ring, quarters, outs, late_buffer, *sems[5:10])
    bits = (2 * chips).bit_length() - 1
    f32 = jnp.float32
    block = part.shape[1]
    greet(
        [*ring.nexts, ring.peer] + [{"dp": bit_partner(ring.index, bit)} for bit in range(bits)]
    )

    ring.load(grads)

    few = block // (2 * PIECES)
    swaps = 2 * PIECES * BLOCKS

    def h_copy(n):
        i, inside = n // (2 * PIECES), pl.ds(pl.multiple_of((n % (2 * PIECES)) * few, few), few)
        return remote(part_hbm.at[i, inside, :], peer.at[i, inside, :], hs_sem.at[n], hr_sem.at[n], ring.peer)

    def h_step(n, early=False):
        if not early:
            h_copy(n - 2).wait_send()
        h_copy(n).start()

    loads = [pltpu.make_async_copy(x_hbm, x, in_sem.at[0]), pltpu.make_async_copy(dmid_hbm, dmid, in_sem.at[1])]
    for i in range(BLOCKS):
        loads.append(pltpu.make_async_copy(part_hbm.at[i, pl.ds(0, block), :], part.at[i], in_sem.at[2 + i]))

    def s_copy(level):
        target = ring.peer if level == 0 else {"dp": bit_partner(ring.index, level - 1)}
        return remote(sacc.at[level], sbuf.at[level], ss_sem.at[level], sr_sem.at[level], target)

    def s_finish(level):
        s_copy(level).wait()
        got = sbuf[level]
        if level == 0:
            first = lax.broadcasted_iota(jnp.int32, got.shape, 0) == 0
            got = jnp.where(first, got, 0.0)
        sacc[level + 1] = sacc[level] + got

    sacc[0] = small_ref[...]

    def small_step(step):
        for level in range(bits + 2):

            @pl.when(step == level)
            def _():
                if level > 0:
                    s_finish(level - 1)
                if level <= bits:
                    s_copy(level).start()

    first_order = [(ring, a) for a in range(count)]
    second_order = [(late, a) for a in range(count)]

    each = block // PIECES
    pieces = BLOCKS * PIECES

    def token_piece(number):
        i = number // PIECES
        for n in range(2):
            h_copy(2 * number + n).wait_recv()

        @pl.when(number == 0)
        def _():
            for copy in loads:
                copy.wait()

        inside = pl.ds(pl.multiple_of((number % PIECES) * each, each), each)
        rows = pl.ds(pl.multiple_of(number * each, each), each)
        xb = x[rows, :].astype(f32)
        r1 = lax.rsqrt(jnp.mean(xb * xb, axis=1, keepdims=True) + EPSILON)
        e = (part[i, inside, :] + peer[i, inside, :]) * rows_ref[GAIN1 : GAIN1 + 1, :]
        inner = jnp.mean(e * xb, axis=1, keepdims=True)
        result[rows, :] = low(dmid[rows, :] + r1 * e - xb * (r1 * r1 * r1 * inner))

    def when(condition, action):
        if isinstance(condition, bool):
            if condition:
                action()
        else:
            pl.when(condition)(action)

    def beside(turn):
        piece = (turn // 3) * 2 + turn % 3
        late_turn = turn - LAG
        if isinstance(turn, int):
            when(turn % 3 != 2 and piece < swaps, lambda: h_step(piece, piece < 2))
            when(late_turn >= 0 and late_turn % 3 == 0, lambda: token_piece(late_turn // 3))
        else:
            when((turn % 3 != 2) & (piece < swaps), lambda: h_step(piece))
            ready = (late_turn >= 0) & (late_turn % 3 == 0) & (late_turn // 3 < pieces)
            when(ready, lambda: token_piece(late_turn // 3))

    def first_step(step, before):
        for position, (_, a) in enumerate(first_order):
            for d in range(2):
                ring.total(grads, d, a, step, before is None)
                ring.rs_copy(d, a, step).start()
            beside(step * count + position)

    def rs_step(step, carry):
        first_step(step, (first_order, step - 1))

        small_step(step)
        return carry

    first_step(0, None)
    for copy in loads:
        copy.start()
    small_step(0)
    lax.fori_loop(1, chips - 1, rs_step, 0)
    for position, (_, a) in enumerate(second_order):
        for d in range(2):
            ring.total(grads, d, a, chips - 1)
            source = ring.chunk(d, a, chips - 1)
            late.ring_copy(d, a, 0, source).start()
            late.place(d, a, 0, source)
        beside((chips - 1) * count + position)

    def ag_step(step, carry):
        for position, (_, a) in enumerate(second_order):
            for d in range(2):
                late.arrived(d, a, step - 1)
                late.ring_copy(d, a, step).start()
                late.place(d, a, step)
            beside((chips - 1 + step) * count + position)

        return carry

    lax.fori_loop(1, chips - 1, ag_step, 0)
    tokens_copy = pltpu.make_async_copy(result, tokens_out, res_sem)
    tokens_copy.start()
    late.finish(chips - 2)
    small_out[...] = sacc[bits + 1]
    ring.drain_ring()
    late.drain_ring()
    ring.drain_pair(grads)
    late.drain()
    for n in range(swaps - 2, swaps):
        h_copy(n).wait_send()
    tokens_copy.wait()


def finish(grads, part, small, tokens, dmid, vectors):
    chips = lax.axis_size("dp") // 2
    length, depth = tokens.shape
    block = length // BLOCKS
    quarters = tuple(g.shape[0] // 4 for g in grads)
    rows = sum(quarters)
    count = len(quarters)
    bits = (2 * chips).bit_length() - 1
    f32, bf16 = jnp.float32, jnp.bfloat16
    vmem = pl.BlockSpec(memory_space=pltpu.VMEM)
    hbm = pl.BlockSpec(memory_space=pl.ANY)
    dma = lambda *shape: pltpu.SemaphoreType.DMA(shape)
    shape = jax.ShapeDtypeStruct
    outs = [(shape(g.shape, f32), hbm) for g in grads]
    outs += [
        (shape((length, depth), bf16), hbm),
        (shape(small.shape, f32), vmem),
    ]
    scratch = [
        pltpu.VMEM((2, chips - 1, rows, LANE), f32),
        pltpu.VMEM((2, rows, depth), f32),
        pltpu.VMEM((2, rows, depth), f32),
        pltpu.VMEM((2, chips - 1, rows, LANE), f32),
        pltpu.VMEM((bits + 2, *small.shape), f32),
        pltpu.VMEM((bits + 1, *small.shape), f32),
        pltpu.VMEM((BLOCKS, block, depth), f32),
        pltpu.VMEM((BLOCKS, block, depth), f32),
        pltpu.VMEM((length, depth), bf16),
        pltpu.VMEM((length, depth), f32),
        pltpu.VMEM((length, depth), bf16),
        dma(2 + BLOCKS),
        pltpu.SemaphoreType.DMA,
        dma(2 * PIECES * BLOCKS),
        dma(2 * PIECES * BLOCKS),
        dma(bits + 1),
        dma(bits + 1),
        dma(2, count),
        dma(2, count),
        dma(2, count),
        dma(2, count, chips - 1),
        dma(2, count, chips - 1),
    ]
    scratch += [
        dma(2, count, chips - 1),
        dma(2, count, chips - 1),
        dma(2, count, chips),
        dma(2, count, chips),
        dma(2, count, chips),
    ]
    return pl.pallas_call(
        functools.partial(finish_kernel, chips, quarters),
        out_shape=tuple(o for o, _ in outs),
        in_specs=[hbm] * (count + 1) + [vmem] + [hbm] * 2 + [vmem],
        out_specs=tuple(s for _, s in outs),
        scratch_shapes=scratch,
        compiler_params=pltpu.CompilerParams(
            collective_id=3, has_side_effects=True, vmem_limit_bytes=VMEM_LIMIT
        ),
        cost_estimate=pl.CostEstimate(
            flops=20 * rows * depth, bytes_accessed=80 * rows * depth, transcendentals=0
        ),
    )(*grads, part, small, tokens, dmid, vectors)


def deliver_kernel(count, key_width, *refs):
    sources, targets = refs[:count], refs[count : 2 * count + 1]
    buffer, low_buffer, in_sem, out_sem = refs[2 * count + 1 :]
    pieces = []
    for a in range(count):
        parts = DELIVER if sources[a].dtype == jnp.float32 else 1
        rows = sources[a].shape[0] // parts
        for n in range(parts):
            pieces.append((a, pl.ds(n * rows, rows), rows))
    wide = sum(sources[a].dtype == jnp.float32 for a, _, _ in pieces)
    low_start = [sum(r for _, _, r in pieces[wide:n]) for n in range(wide, len(pieces))]

    def spot(number):
        rows = pieces[number][2]
        if number < wide:
            return buffer.at[number, pl.ds(0, rows), :]
        return low_buffer.at[pl.ds(low_start[number - wide], rows), :]

    def load(number):
        a, where, rows = pieces[number]
        return pltpu.make_async_copy(sources[a].at[where, :], spot(number), in_sem.at[number])

    def stores(number):
        a, where, rows = pieces[number]
        if a:
            spots = [(spot(number), targets[a + 1].at[where, :])]
        else:
            spots = [
                (buffer.at[number, pl.ds(0, rows), pl.ds(half * key_width, key_width)], targets[half].at[where, :])
                for half in range(2)
            ]
        return [pltpu.make_async_copy(s, t, out_sem.at[number, n]) for n, (s, t) in enumerate(spots)]

    for number in range(len(pieces)):
        load(number).start()
    for number in range(len(pieces)):
        load(number).wait()
        for copy in stores(number):
            copy.start()
    for number in range(len(pieces)):
        for copy in stores(number):
            copy.wait()


def deliver(arrays, narrow, key_width):
    hbm = pl.BlockSpec(memory_space=pl.ANY)
    every = (*arrays, *narrow)
    shapes = [((arrays[0].shape[0], key_width), jnp.float32)] * 2 + [(a.shape, a.dtype) for a in every[1:]]
    size = sum(a.size for a in arrays)
    wide = DELIVER * len(arrays)
    pieces = wide + len(narrow)
    depth = arrays[0].shape[1]
    rows = max(a.shape[0] for a in arrays) // DELIVER
    return pl.pallas_call(
        functools.partial(deliver_kernel, len(every), key_width),
        out_shape=tuple(jax.ShapeDtypeStruct(s, t) for s, t in shapes),
        in_specs=[hbm] * len(every),
        out_specs=(hbm,) * len(shapes),
        scratch_shapes=[
            pltpu.VMEM((wide, rows, depth), jnp.float32),
            pltpu.VMEM((sum(a.shape[0] for a in narrow), depth), jnp.bfloat16),
            pltpu.SemaphoreType.DMA((pieces,)),
            pltpu.SemaphoreType.DMA((pieces, 2)),
        ],
        compiler_params=pltpu.CompilerParams(vmem_limit_bytes=56 * 1024 * 1024),
        cost_estimate=pl.CostEstimate(flops=0, bytes_accessed=8 * size, transcendentals=0),
    )(*every)

def swap(array):
    return lax.ppermute(array, "tensor", [(0, 1), (1, 0)])


def other_half(arrays, zero):
    dp, index = lax.axis_size("dp"), lax.axis_index("dp")
    rows = arrays[0].shape[0]
    count = len(arrays)
    if dp % count == 0 and rows % (8 * (dp // count)) == 0:
        share = rows * count // dp
        each = dp // count
        inside = (index % each) * share
        own = [lax.dynamic_slice_in_dim(a, inside, share, 0) for a in arrays]
        part = own[0]
        for number in range(1, count):
            part = jnp.where(index // each == number, own[number], part)
    else:
        share = -(-rows * count // (8 * dp)) * 8
        whole = jnp.concatenate(arrays, axis=0)
        whole = jnp.pad(whole, ((0, share * dp - rows * count), (0, 0)))
        part = lax.dynamic_slice_in_dim(whole, index * share, share, 0)
    got = lax.all_gather(swap(part.astype(jnp.float32)), "dp", axis=0, tiled=True)
    got = low(got + zero)
    return [got[number * rows : (number + 1) * rows] for number in range(count)]


def plain_body(
    tokens,
    segment,
    norm1_gain,
    w_query,
    w_key,
    w_value,
    w_gate,
    group_gain,
    group_bias,
    w_out,
    norm2_gain,
    w_mlp_gate,
    w_mlp_up,
    w_mlp_down,
    cotangent,
):
    length, depth = tokens.shape
    heads = w_query.shape[1] // KD
    block = length // BLOCKS
    tensor = lax.axis_index("tensor")
    f32 = jnp.float32
    zero = jnp.minimum(segment[0], 0).astype(f32)
    value_t, gate_t, mg_t, mu_t = w_value.T, w_gate.T, w_mlp_gate.T, w_mlp_up.T
    mg_o, mu_o, md_o, wo_o = other_half([mg_t, mu_t, w_mlp_down, w_out], zero)
    x = tokens.astype(f32)
    gain1 = norm1_gain.astype(f32)
    gain2 = norm2_gain.astype(f32)
    ggain = group_gain.astype(f32)[:, None]
    gbias = group_bias.astype(f32)[:, None]
    r1 = lax.rsqrt(jnp.mean(x * x, axis=1, keepdims=True) + EPSILON)
    h1 = low(x * r1 * gain1)
    half = KD // 2
    frequency = jnp.exp(-jnp.log(10000.0) * jnp.arange(half, dtype=f32) / half)
    angles = jnp.arange(length, dtype=f32)[:, None] * frequency[None, :]
    cosine, sine = jnp.cos(angles), jnp.sin(angles)
    positions = jnp.arange(length, dtype=jnp.int32)
    visible = (positions[:, None] >= positions[None, :]) & (segment[:, None] == segment[None, :])
    offsets = jnp.maximum(positions[:, None] - positions[None, :], 0).astype(f32)

    def decay(head, rows, columns):
        order = (tensor * heads + head).astype(f32)
        rate = jnp.log1p(-jnp.exp2(-5.0 - order))
        return jnp.where(visible[rows, columns], jnp.exp(offsets[rows, columns] * rate), 0.0)

    queries = [[] for _ in range(heads)]
    keys = [[] for _ in range(heads)]
    values = [[] for _ in range(heads)]
    gates = [[] for _ in range(heads)]
    nhats = [[] for _ in range(heads)]
    spreads = [[] for _ in range(heads)]
    gated_blocks, received = [], []
    for number in range(BLOCKS):
        rows = slice(number * block, (number + 1) * block)
        seen = slice(0, (number + 1) * block)
        own = []
        for head in range(heads):
            wide = slice(head * KD, (head + 1) * KD)
            tall = slice(head * VD, (head + 1) * VD)
            q = low(turn(dot(h1[rows], w_query[:, wide], 1, 0), cosine[rows], sine[rows]))
            k = turn(dot(h1[rows], w_key[:, wide], 1, 0), cosine[rows], sine[rows])
            queries[head].append(q)
            keys[head].append(low(k * KD ** (-0.5)))
            values[head].append(low(dot(value_t[tall], h1[rows], 1, 1)))
            g = dot(gate_t[tall], h1[rows], 1, 1)
            gates[head].append(g)
            scores = dot(q, jnp.concatenate(keys[head], axis=0), 1, 1)
            scores = low(scores * decay(head, rows, seen))
            ret = dot(jnp.concatenate(values[head], axis=1), scores, 1, 1)
            centred = ret - jnp.mean(ret, axis=0, keepdims=True)
            scale = lax.rsqrt(jnp.mean(centred * centred, axis=0, keepdims=True) + GROUP_EPSILON)
            nhat = centred * scale
            nhats[head].append(nhat)
            spreads[head].append(scale)
            own.append(low(jax.nn.silu(g) * (nhat * ggain[tall] + gbias[tall])))
        gated_blocks.append(jnp.concatenate(own, axis=0))
        received.append(low(swap(gated_blocks[-1].astype(f32)) + zero))

    mids, h2s, r2s, hidden_own, hidden_oth, das, dbs, dmids = [], [], [], [], [], [], [], []
    norm2_rows = []
    for number in range(BLOCKS):
        rows = slice(number * block, (number + 1) * block)
        mid = x[rows] + (dot(gated_blocks[number], w_out, 0, 0) + dot(received[number], wo_o, 0, 0))
        r2 = lax.rsqrt(jnp.mean(mid * mid, axis=1, keepdims=True) + EPSILON)
        h2 = low(mid * r2 * gain2)
        cot = cotangent[rows]

        def mlp(gate_w, up_w, down_w):
            a, b = dot(gate_w, h2, 1, 1), dot(up_w, h2, 1, 1)
            hidden, pull = jax.vjp(lambda s, t: jax.nn.gelu(s) * t, a, b)
            da, db = pull(dot(down_w, cot, 1, 1))
            da, db = low(da), low(db)
            return low(hidden), da, db, dot(da, gate_w, 0, 0) + dot(db, up_w, 0, 0)

        own_hidden, da, db, part = mlp(mg_t, mu_t, w_mlp_down)
        oth_hidden, _, _, more = mlp(mg_o, mu_o, md_o)
        dh2 = part + more
        e = dh2 * gain2
        dmid = cot.astype(f32) + r2 * e - mid * (r2 * r2 * r2) * jnp.mean(e * mid, axis=1, keepdims=True)
        norm2_rows.append(jnp.sum(dh2 * mid * r2, axis=0))
        for where, value in zip(
            (mids, h2s, hidden_own, hidden_oth, das, dbs, dmids),
            (mid, h2, own_hidden, oth_hidden, da, db, dmid),
        ):
            where.append(value)
    grad_norm2 = sum(norm2_rows)
    mid = jnp.concatenate(mids, axis=0)
    h2 = jnp.concatenate(h2s, axis=0)
    hidden = jnp.concatenate(hidden_own, axis=1)
    hidden_o = jnp.concatenate(hidden_oth, axis=1)
    dmid = jnp.concatenate(dmids, axis=0)
    own_rows = length // lax.axis_size("tensor")
    place = tensor * own_rows
    output = low(
        lax.dynamic_slice_in_dim(mid, place, own_rows, 0)
        + dot(lax.dynamic_slice_in_dim(hidden, place, own_rows, 1), w_mlp_down, 0, 0)
        + dot(lax.dynamic_slice_in_dim(hidden_o, place, own_rows, 1), md_o, 0, 0)
    )
    grad_mg = dot(jnp.concatenate(das, axis=1), h2, 1, 0)
    grad_mu = dot(jnp.concatenate(dbs, axis=1), h2, 1, 0)
    grad_md = dot(hidden, cotangent, 1, 0)

    branch = low(dmid)
    gated = jnp.concatenate(gated_blocks, axis=1)
    grad_out = dot(gated, branch, 1, 0)
    dgated = dot(w_out, branch, 1, 1)
    dqs, dks, dvs, dgs, ggains, gbiases = [], [], [], [], [], []
    everything = slice(0, length)
    for head in range(heads):
        tall = slice(head * VD, (head + 1) * VD)
        g = jnp.concatenate(gates[head], axis=1)
        nhat = jnp.concatenate(nhats[head], axis=1)
        spread = jnp.concatenate(spreads[head], axis=1)
        q = jnp.concatenate(queries[head], axis=0)
        k = jnp.concatenate(keys[head], axis=0)
        v = jnp.concatenate(values[head], axis=1)
        sigmoid = jax.nn.sigmoid(g)
        silu = g * sigmoid
        up = dgated[tall]
        dgn = up * silu
        ggains.append(jnp.sum(dgn * nhat, axis=1))
        gbiases.append(jnp.sum(dgn, axis=1))
        f = dgn * ggain[tall]
        dret = (
            f - jnp.mean(f, axis=0, keepdims=True) - nhat * jnp.mean(f * nhat, axis=0, keepdims=True)
        ) * spread
        dret = low(dret)
        gn = nhat * ggain[tall] + gbias[tall]
        dgs.append(low(up * gn * (sigmoid + silu * (1.0 - sigmoid))))
        table = decay(head, everything, everything)
        scores = low(dot(q, k, 1, 1) * table)
        draw = low(dot(dret, v, 0, 0) * table)
        dvs.append(low(dot(dret, scores, 1, 0)))
        dqs.append(low(turn(dot(draw, k, 1, 0), cosine, -sine)))
        dks.append(low(turn(dot(draw, q, 0, 0), cosine, -sine) * KD ** (-0.5)))
    dv = jnp.concatenate(dvs, axis=0)
    dg = jnp.concatenate(dgs, axis=0)
    dq = jnp.concatenate(dqs, axis=1)
    dk = jnp.concatenate(dks, axis=1)
    partial_in = dot(dq, w_query, 1, 1) + dot(dk, w_key, 1, 1) + dot(dv, value_t, 0, 0) + dot(dg, gate_t, 0, 0)
    grad_norm1 = jnp.sum(partial_in * x * r1, axis=0)
    grad_qk = dot(h1, jnp.concatenate([dq, dk], axis=1), 0, 0)
    grad_v = dot(dv, h1, 1, 0)
    grad_g = dot(dg, h1, 1, 0)

    units = w_value.shape[1]
    small = jnp.stack(
        [
            grad_norm1,
            grad_norm2,
            jnp.pad(jnp.concatenate(ggains), (0, depth - units)),
            jnp.pad(jnp.concatenate(gbiases), (0, depth - units)),
        ]
    )
    small = jnp.pad(small, ((0, 4), (0, 0)))
    grads = lax.psum((grad_qk, grad_v, grad_g, grad_out, grad_mg, grad_mu, grad_md), "dp")
    peer = swap(partial_in)
    small = lax.psum(small.at[0].set(lax.psum(small[0], "tensor")), "dp")
    grad_qk, grad_v, grad_g, grad_out, grad_mg, grad_mu, grad_md = grads
    e1 = (partial_in + peer) * gain1
    grad_tokens = low(dmid + r1 * e1 - x * (r1 * r1 * r1) * jnp.mean(e1 * x, axis=1, keepdims=True))
    key_width = w_query.shape[1]
    return (
        output,
        grad_tokens,
        small[0],
        grad_qk[:, :key_width],
        grad_qk[:, key_width:],
        grad_v.T,
        grad_g.T,
        small[2, :units],
        small[3, :units],
        grad_out,
        small[1],
        grad_mg.T,
        grad_mu.T,
        grad_md,
    )


def body(
    tokens,
    segment,
    norm1_gain,
    w_query,
    w_key,
    w_value,
    w_gate,
    group_gain,
    group_bias,
    w_out,
    norm2_gain,
    w_mlp_gate,
    w_mlp_up,
    w_mlp_down,
    cotangent,
):
    length, depth = tokens.shape
    if depth % (LANE * (lax.axis_size("dp") // 2)):
        return plain_body(
            tokens, segment, norm1_gain, w_query, w_key, w_value, w_gate, group_gain, group_bias, w_out,
            norm2_gain, w_mlp_gate, w_mlp_up, w_mlp_down, cotangent,
        )
    value_t, gate_t, mg_t, mu_t = w_value.T, w_gate.T, w_mlp_gate.T, w_mlp_up.T
    tables = make_tables(length)
    vectors = pack_rows((norm1_gain, norm2_gain, group_gain, group_bias, segment), depth)
    (h1, qs, ks, vs, g, nhat, rstd, gated, mid, dh, h2, hid, grad_mg, grad_mu, grad_md, gathered) = forward(
        tokens,
        vectors,
        tables,
        (w_query, w_key, value_t, gate_t, w_out, mg_t, mu_t, w_mlp_down),
        cotangent,
    )
    (dmid, output, grad_mg, grad_mu, grad_md, part, grad_qk, grad_v, grad_g, grad_out, small) = backward(
        tokens,
        vectors,
        tables,
        cotangent,
        (mid, dh, h2, hid, gathered),
        (h1, qs, ks, vs, g, nhat, rstd, gated),
        (w_query, w_key, value_t, gate_t, w_out, w_mlp_down),
        (grad_mg, grad_mu, grad_md),
    )
    (grad_qk, grad_v, grad_g, grad_out, grad_tokens, small) = finish(
        (grad_qk, grad_v, grad_g, grad_out), part, small, tokens, dmid, vectors
    )
    units = w_value.shape[1]
    grad_q, grad_k, grad_v, grad_g, grad_out, grad_mg, grad_mu, grad_md, output, grad_tokens = deliver(
        (grad_qk, grad_v, grad_g, grad_out, grad_mg, grad_mu, grad_md), (output, grad_tokens), w_query.shape[1]
    )
    return (
        output,
        grad_tokens,
        small[0],
        grad_q,
        grad_k,
        grad_v.T,
        grad_g.T,
        small[2, :units],
        small[3, :units],
        grad_out,
        small[1],
        grad_mg.T,
        grad_mu.T,
        grad_md,
    )


def solution(mesh):
    placed = (
        P("dp", None),
        P("dp"),
        P(),
        P(None, "tensor"),
        P(None, "tensor"),
        P(None, "tensor"),
        P(None, "tensor"),
        P("tensor"),
        P("tensor"),
        P("tensor", None),
        P(),
        P(None, "tensor"),
        P(None, "tensor"),
        P("tensor", None),
        P("dp", None),
    )
    return jax.shard_map(
        body,
        mesh=mesh,
        in_specs=placed,
        out_specs=(
            P(("dp", "tensor"), None),
            P("dp", None),
            P(),
            P(None, "tensor"),
            P(None, "tensor"),
            P(None, "tensor"),
            P(None, "tensor"),
            P("tensor"),
            P("tensor"),
            P("tensor", None),
            P(),
            P(None, "tensor"),
            P(None, "tensor"),
            P("tensor", None),
        ),
        check_vma=False,
    )
```

```python
import functools
import math

import jax
import jax.numpy as jnp
import numpy as np
from jax import lax
from jax.experimental import pallas as pl
from jax.experimental.pallas import tpu as pltpu
from jax.sharding import PartitionSpec as P

KD = 256
VD = 432
LANE = 128
MESH = pl.DeviceIdType.MESH
DELIVER = 4
PIECES = 4
LAG = 8
VMEM_LIMIT = 63 * 1024 * 1024


EPSILON = 1e-06
GROUP_EPSILON = 0.25


def ring_place(chip, chips):
    line = chips // 2
    x = chip % 2
    z = chip // 2
    return z + x * (chips - 1 - 2 * z), line


def ring_chip(place, chips):
    line = chips // 2
    x = place // line
    z = place + x * (chips - 1 - 2 * place)
    return z * 2 + x


def bit_partner(index, bit):
    step = 1 << bit
    return index + (1 - 2 * ((index // step) % 2)) * step


BLOCKS = 4
GELU_A = math.sqrt(2.0 / math.pi)
GELU_B = 0.044715


def dot(left, right, left_dim, right_dim):
    return lax.dot_general(
        left, right, (((left_dim,), (right_dim,)), ((), ())), preferred_element_type=jnp.float32
    )


def low(array):
    return array.astype(jnp.bfloat16)


def turn(vectors, cosine, sine):
    half = vectors.shape[1] // 2
    lower, upper = vectors[:, :half], vectors[:, half:]
    return jnp.concatenate([lower * cosine - upper * sine, upper * cosine + lower * sine], axis=1)


def remote(source, target, send, recv, device):
    return pltpu.make_async_remote_copy(
        source, target, send, recv, device_id=device, device_id_type=MESH
    )


def rate_of(head, heads, tensor):
    rates = [math.log1p(-(2.0 ** (-5 - order))) for order in range(2 * heads)]
    return jnp.where(tensor == 0, rates[head], rates[heads + head]).astype(jnp.float32)


def upright(row, size):
    diagonal = lax.broadcasted_iota(jnp.int32, (size, size), 0) == lax.broadcasted_iota(
        jnp.int32, (size, size), 1
    )
    return jnp.sum(jnp.where(diagonal, row, 0.0), axis=1, keepdims=True)


def upright_part(row, start, size):
    shape = (size, row.shape[1])
    chosen = lax.broadcasted_iota(jnp.int32, shape, 0) + start == lax.broadcasted_iota(jnp.int32, shape, 1)
    return jnp.sum(jnp.where(chosen, row, 0.0), axis=1, keepdims=True)


GAIN1, GAIN2, GROUP_GAIN, GROUP_BIAS, SEGMENT = range(5)


def greet(devices):
    barrier = pltpu.get_barrier_semaphore()
    for device in devices:
        pl.semaphore_signal(barrier, inc=1, device_id=device, device_id_type=MESH)
    pl.semaphore_wait(barrier, len(devices))


def mlp_part(gate_w, up_w, down_w, h2, cot, tall, rows):
    a = dot(gate_w[tall, :], h2[rows, :], 1, 1)
    b = dot(up_w[tall, :], h2[rows, :], 1, 1)
    dhidden = dot(down_w[tall, :], cot[rows, :], 1, 1)
    square = a * a
    t = jnp.tanh(GELU_A * a * (1.0 + GELU_B * square))
    gelu = 0.5 * a * (1.0 + t)
    slope = 0.5 * (1.0 + t) + 0.5 * a * (1.0 - t * t) * (GELU_A * (1.0 + 3.0 * GELU_B * square))
    dga = low(dhidden * b * slope)
    dup = low(dhidden * gelu)
    more = dot(dga, gate_w[tall, :], 0, 0) + dot(dup, up_w[tall, :], 0, 0)
    return low(gelu * b), dga, dup, more


def forward_kernel(
    chips,
    x_ref,
    rows_ref,
    cos_ref,
    sin_ref,
    wq_hbm,
    wk_hbm,
    wv_hbm,
    wg_hbm,
    wo_ref,
    mg_ref,
    mu_ref,
    md_ref,
    cot_ref,
    h1_out,
    q_out,
    k_out,
    v_out,
    g_out,
    nh_out,
    rstd_out,
    gated_out,
    mid_out,
    dh_out,
    h2_out,
    hid_out,
    grad_mg_out,
    grad_mu_out,
    grad_md_out,
    gath_out,
    weights,
    others,
    cot,
    h1,
    q,
    k,
    v,
    g,
    nh,
    rstd,
    gated,
    acc,
    gsend,
    grecv,
    h2,
    hid,
    da,
    db,
    mid,
    dh_own,
    sums,
    ggain_ref,
    gbias_ref,
    in_sem,
    save_sem,
    out_sem,
    stage_sem,
    mid_sem,
    dh_sem,
    sum_sem,
    xs_sem,
    xr_sem,
    ys_sem,
    yr_sem,
    gs_sem,
    gr_sem,
    cs_sem,
    cr_sem,
):
    index, tensor = lax.axis_index("dp"), lax.axis_index("tensor")
    core = index % 2
    place, _ = ring_place(index // 2, chips)
    nexts = [
        {"dp": ring_chip((place + 1) % chips, chips) * 2 + core},
        {"dp": ring_chip((place + chips - 1) % chips, chips) * 2 + core},
    ]
    sibling, peer = {"dp": index + 1 - 2 * core}, {"tensor": 1 - tensor}
    heads = q.shape[1]
    units, length = v.shape
    block = length // BLOCKS
    third = units // 3
    f32 = jnp.float32

    for number, source in enumerate((wo_ref, mg_ref, mu_ref, md_ref)):
        pltpu.make_async_copy(source, weights.at[number], in_sem.at[number]).start()
    wv_ref, wg_ref = hid, da
    key_width = wq_hbm.shape[1]
    early = [
        pltpu.make_async_copy(wq_hbm, h2.at[:, pl.ds(0, key_width)], in_sem.at[5]),
        pltpu.make_async_copy(wk_hbm, h2.at[:, pl.ds(key_width, key_width)], in_sem.at[6]),
        pltpu.make_async_copy(wv_hbm, wv_ref, in_sem.at[7]),
        pltpu.make_async_copy(wg_hbm, wg_ref, in_sem.at[8]),
    ]
    for copy in early:
        copy.start()
    pltpu.make_async_copy(cot_ref, cot, in_sem.at[4]).start()
    greet([*nexts, sibling, peer])

    rows_slice = units // 2
    half_slice = rows_slice // 2

    def area(w, where, which, half=None):
        start = which * rows_slice + (0 if half is None else half * half_slice)
        size = rows_slice if half is None else half_slice
        return gath_out.at[
            w,
            pl.ds(pl.multiple_of(start, 8), size),
            pl.ds(pl.multiple_of(where * LANE, LANE), LANE),
        ]

    def slice_spot(w):
        return gsend.at[
            BLOCKS - 1,
            pl.ds((w % 2) * rows_slice, rows_slice),
            pl.ds((w // 2) * LANE, LANE),
        ]

    def y_copy(w):
        return remote(slice_spot(w), area(w, place, core), ys_sem.at[w], yr_sem.at[w], peer)

    def hop(w, d, t):
        where = (place - t + chips) % chips if d == 0 else (place + t) % chips
        part = area(w, where, core, d if t == chips // 2 - 1 else None)
        return remote(part, part, gs_sem.at[w, d, t], gr_sem.at[w, d, t], nexts[d])

    def arrived(w, d, t):
        where = (place - t - 1 + chips) % chips if d == 0 else (place + t + 1) % chips
        part = area(w, where, core, d if t == chips // 2 - 1 else None)
        pltpu.make_async_copy(part, part, gr_sem.at[w, d, t]).wait()
        return where

    def share(w, slot, where, half=None):
        part = area(w, where, core, half)
        remote(part, part, cs_sem.at[w, slot], cr_sem.at[w, slot], sibling).start()

    steps = chips // 2

    def begin(w):
        y_copy(w).wait_recv()
        for d in range(2):
            hop(w, d, 0).start()
        share(w, 0, place)

    def pump(w, t):
        for d in range(2):
            where = arrived(w, d, t)
            if t < steps - 1:
                hop(w, d, t + 1).start()
            share(w, 1 + 2 * t + d, where, d if t == steps - 1 else None)

    for number in range(4):
        pltpu.make_async_copy(wo_ref, weights.at[number], in_sem.at[number]).wait()
        slice_spot(number)[...] = weights[
            number,
            pl.ds(pl.multiple_of(core * rows_slice, 16), rows_slice),
            pl.ds(pl.multiple_of(place * LANE, LANE), LANE),
        ].astype(f32)
        y_copy(number).start()

    def exchange(i):
        return remote(gsend.at[i], grecv.at[i], xs_sem.at[i], xr_sem.at[i], peer)

    ahead = lax.broadcasted_iota(jnp.int32, (block, block), 0) - lax.broadcasted_iota(
        jnp.int32, (block, block), 1
    )

    def saves(i):
        slot = i % 2
        rows = pl.ds(pl.multiple_of(i * block, block), block)
        pairs = (
            (h1.at[slot], h1_out.at[rows, :]),
            (q.at[slot], q_out.at[:, rows, :]),
            (g.at[slot], g_out.at[:, rows]),
            (nh.at[slot], nh_out.at[:, rows]),
        )
        return [
            pltpu.make_async_copy(source, target, save_sem.at[number, slot])
            for number, (source, target) in enumerate(pairs)
        ]

    def attention(i, carry):
        rows = pl.ds(pl.multiple_of(i * block, block), block)
        slot = i % 2

        @pl.when(i >= 2)
        def _():
            for copy in saves(i - 2):
                copy.wait()

        xb = x_ref[rows, :].astype(f32)
        r1 = lax.rsqrt(jnp.mean(xb * xb, axis=1, keepdims=True) + EPSILON)
        h1[slot] = low(xb * r1 * rows_ref[GAIN1 : GAIN1 + 1, :])
        cosine, sine = cos_ref[rows, :], sin_ref[rows, :]
        for head in range(heads):
            wide = slice(head * KD, (head + 1) * KD)
            q[slot, head] = low(turn(dot(h1[slot], h2[:, wide], 1, 0), cosine, sine))
            wide = slice(key_width + head * KD, key_width + (head + 1) * KD)
            k[head, rows, :] = low(turn(dot(h1[slot], h2[:, wide], 1, 0), cosine, sine) * KD ** (-0.5))
        v[:, rows] = low(dot(wv_ref[...], h1[slot], 1, 1))

        @pl.when(i == BLOCKS - 1)
        def _():
            for w in range(4):
                y_copy(w).wait_send()

        segc = upright(rows_ref[SEGMENT : SEGMENT + 1, rows], block)
        for head in range(heads):
            tall = slice(head * VD, (head + 1) * VD)
            rate = rate_of(head, heads, tensor)
            acc[...] = jnp.zeros_like(acc)

            def tile(m, carry):
                cols = pl.ds(pl.multiple_of(m * block, block), block)
                s = dot(q[slot, head], k[head, cols, :], 1, 1)
                gap = ahead + (i - m) * block
                seen = (segc == rows_ref[SEGMENT : SEGMENT + 1, cols]) & (gap >= 0)
                s = jnp.where(seen, s * jnp.exp(gap.astype(f32) * rate), 0.0)
                acc[...] += dot(v[tall, cols], low(s), 1, 1)
                return carry

            lax.fori_loop(0, i + 1, tile, 0)
            ret = acc[...]
            centred = ret - jnp.mean(ret, axis=0, keepdims=True)
            scale = lax.rsqrt(jnp.mean(centred * centred, axis=0, keepdims=True) + GROUP_EPSILON)
            nhat = centred * scale
            nh[slot, tall, :] = low(nhat)
            rstd[head : head + 1, rows] = scale
            gate = dot(wg_ref[tall, :], h1[slot], 1, 1)
            g[slot, tall, :] = low(gate)
            gn = nhat * ggain_ref[tall, :] + gbias_ref[tall, :]
            out = low(gate / (1.0 + jnp.exp(-gate)) * gn)
            gated[tall, rows] = out
            gsend[i, tall, :] = out.astype(f32)
        exchange(i).start()
        for copy in saves(i):
            copy.start()

        @pl.when(i == 0)
        def _():
            begin(0)

        @pl.when(i == 1)
        def _():
            pump(0, 0)
            for w in range(1, 4):
                begin(w)

        @pl.when(i == 2)
        def _():
            pump(0, 1)

        return carry

    rstd[...] = jnp.zeros_like(rstd)
    for n in range(3):
        where = slice(n * third, (n + 1) * third)
        ggain_ref[where, :] = upright_part(rows_ref[GROUP_GAIN : GROUP_GAIN + 1, :], n * third, third)
        gbias_ref[where, :] = upright_part(rows_ref[GROUP_BIAS : GROUP_BIAS + 1, :], n * third, third)
    for copy in early:
        copy.wait()
    lax.fori_loop(0, BLOCKS, attention, 0)
    for i in range(BLOCKS - 2, BLOCKS):
        for copy in saves(i):
            copy.wait()
    saved = [(k, k_out), (v, v_out), (rstd, rstd_out), (gated, gated_out)]
    for number, (source, target) in enumerate(saved):
        pltpu.make_async_copy(source, target, out_sem.at[number]).start()

    def cast_ready(w):
        for slot in range(1 + 2 * steps):
            t = (slot - 1) // 2
            d = (slot - 1) % 2
            if slot == 0:
                where = place
            else:
                where = (place - t - 1 + chips) % chips if d == 0 else (place + t + 1) % chips
            part = area(w, where, 1 - core, d if slot > 0 and t == steps - 1 else None)
            pltpu.make_async_copy(part, part, cr_sem.at[w, slot]).wait()

    def stage(number):
        return sums.at[0, pl.ds((number % 2) * third, third), :]

    def cast_in(ws):
        pieces = [(w, n) for w in ws for n in range(3)]

        def piece(number):
            w, n = pieces[number]
            return pltpu.make_async_copy(
                gath_out.at[w, pl.ds(n * third, third), :], stage(number), stage_sem.at[number % 2]
            )

        cast_ready(ws[0])
        piece(0).start()
        for number, (w, n) in enumerate(pieces):
            if number + 1 < len(pieces):
                if pieces[number + 1][1] == 0:
                    cast_ready(pieces[number + 1][0])
                piece(number + 1).start()
            piece(number).wait()
            others[n * third : (n + 1) * third, :] = low(stage(number)[...])

    pump(0, 2)
    pump(0, 3)
    cast_in([0])
    pltpu.make_async_copy(cot_ref, cot, in_sem.at[4]).wait()
    part = units // 2

    def mid_copy(i):
        rows = pl.ds(pl.multiple_of(i * block, block), block)
        return pltpu.make_async_copy(mid.at[i % 2], mid_out.at[rows, :], mid_sem.at[i % 2])

    def dh_copy(i):
        rows = pl.ds(pl.multiple_of(i * block, block), block)
        return pltpu.make_async_copy(dh_own.at[i % 2], dh_out.at[rows, :], dh_sem.at[i % 2])

    def own_half(i):
        rows = pl.ds(pl.multiple_of(i * block, block), block)
        slot = i % 2

        @pl.when(i >= 2)
        def _():
            mid_copy(i - 2).wait()
            dh_copy(i - 2).wait()

        exchange(i).wait_recv()
        mid[slot] = x_ref[rows, :].astype(f32) + (
            dot(gated[:, rows], weights[0], 0, 0) + dot(low(grecv[i]), others[...], 0, 0)
        )
        mid_copy(i).start()
        r2 = lax.rsqrt(jnp.mean(mid[slot] * mid[slot], axis=1, keepdims=True) + EPSILON)
        h2[rows, :] = low(mid[slot] * r2 * rows_ref[GAIN2 : GAIN2 + 1, :])
        for f in range(2):
            tall = slice(f * part, (f + 1) * part)
            hid[tall, rows], da[tall, rows], db[tall, rows], more = mlp_part(
                weights.at[1], weights.at[2], weights.at[3], h2, cot, tall, rows
            )
            dh_own[slot] = more if f == 0 else dh_own[slot] + more
        dh_copy(i).start()

    def first_pass(i, carry):
        for t in range(3):

            @pl.when(i == t)
            def _():
                for w in range(1, 4):
                    pump(w, t)

        own_half(i)
        return carry

    products = ((da, h2, grad_mg_out), (db, h2, grad_mu_out), (hid, cot, grad_md_out))
    before = (BLOCKS - 1) * block
    lax.fori_loop(0, BLOCKS - 1, first_pass, 0)
    for w in range(1, 4):
        pump(w, 3)
    for number, (source, right, _) in enumerate(products):
        for n in range(3):
            where = slice(n * third, (n + 1) * third)
            sums[number, where, :] = dot(source[where, 0:before], right[0:before, :], 1, 0)
    own_half(BLOCKS - 1)
    late = [
        pltpu.make_async_copy(h2, h2_out, out_sem.at[4]),
        pltpu.make_async_copy(hid, hid_out, out_sem.at[5]),
    ]
    for copy in late:
        copy.start()
    for number, (source, right, target) in enumerate(products):
        for n in range(3):
            where = slice(n * third, (n + 1) * third)
            sums[number, where, :] += dot(source[where, before:length], right[before:length, :], 1, 0)
            late.append(
                pltpu.make_async_copy(
                    sums.at[number, pl.ds(n * third, third), :],
                    target.at[pl.ds(n * third, third), :],
                    sum_sem.at[number, n],
                )
            )
            late[-1].start()
    for copy in late:
        copy.wait()
    for w in range(1, 4):
        cast_ready(w)
    for i in range(BLOCKS - 2, BLOCKS):
        mid_copy(i).wait()
        dh_copy(i).wait()
    for number, (source, target) in enumerate(saved):
        pltpu.make_async_copy(source, target, out_sem.at[number]).wait()
    for w in range(4):
        for t in range(steps):
            for d in range(2):
                hop(w, d, t).wait_send()
        for slot in range(1 + 2 * steps):
            last = slot > 0 and (slot - 1) // 2 == steps - 1
            part_ref = area(w, place, core, 0 if last else None)
            pltpu.make_async_copy(part_ref, part_ref, cs_sem.at[w, slot]).wait()
    for i in range(BLOCKS):
        exchange(i).wait_send()


def forward(tokens, vectors, tables, ws, cotangent):
    chips = lax.axis_size("dp") // 2
    length, depth = tokens.shape
    wq, wk, wv, wg, wo, mg, mu, md = ws
    units = wv.shape[0]
    heads = wq.shape[1] // KD
    block = length // BLOCKS
    f32, bf16 = jnp.float32, jnp.bfloat16
    vmem = pl.BlockSpec(memory_space=pltpu.VMEM)
    hbm = pl.BlockSpec(memory_space=pl.ANY)
    dma = lambda *shape: pltpu.SemaphoreType.DMA(shape)
    shape = jax.ShapeDtypeStruct
    tall = (units, length)
    steps = chips // 2
    outs = [
        (shape((length, depth), bf16), hbm),
        (shape((heads, length, KD), bf16), hbm),
        (shape((heads, length, KD), bf16), hbm),
        (shape(tall, bf16), hbm),
        (shape(tall, bf16), hbm),
        (shape(tall, bf16), hbm),
        (shape((8, length), f32), hbm),
        (shape(tall, bf16), hbm),
        (shape((length, depth), f32), hbm),
        (shape((length, depth), f32), hbm),
        (shape((length, depth), bf16), hbm),
        (shape(tall, bf16), hbm),
        (shape((units, depth), f32), hbm),
        (shape((units, depth), f32), hbm),
        (shape((units, depth), f32), hbm),
        (shape((4, units, depth), f32), hbm),
    ]
    scratch = [
        pltpu.VMEM((4, units, depth), bf16),
        pltpu.VMEM((units, depth), bf16),
        pltpu.VMEM((length, depth), bf16),
        pltpu.VMEM((2, block, depth), bf16),
        pltpu.VMEM((2, heads, block, KD), bf16),
        pltpu.VMEM((heads, length, KD), bf16),
        pltpu.VMEM(tall, bf16),
        pltpu.VMEM((2, units, block), bf16),
        pltpu.VMEM((2, units, block), bf16),
        pltpu.VMEM((8, length), f32),
        pltpu.VMEM(tall, bf16),
        pltpu.VMEM((VD, block), f32),
        pltpu.VMEM((BLOCKS, units, block), f32),
        pltpu.VMEM((BLOCKS, units, block), f32),
        pltpu.VMEM((length, depth), bf16),
        pltpu.VMEM(tall, bf16),
        pltpu.VMEM(tall, bf16),
        pltpu.VMEM(tall, bf16),
        pltpu.VMEM((2, block, depth), f32),
        pltpu.VMEM((2, block, depth), f32),
        pltpu.VMEM((3, units, depth), f32),
        pltpu.VMEM((units, 1), f32),
        pltpu.VMEM((units, 1), f32),
        dma(9),
        dma(4, 2),
        dma(6),
        dma(2),
        dma(2),
        dma(2),
        dma(3, 3),
        dma(BLOCKS),
        dma(BLOCKS),
        dma(4),
        dma(4),
        dma(4, 2, steps),
        dma(4, 2, steps),
        dma(4, 1 + 2 * steps),
        dma(4, 1 + 2 * steps),
    ]
    return pl.pallas_call(
        functools.partial(forward_kernel, chips),
        out_shape=tuple(o for o, _ in outs),
        in_specs=[vmem] * 4 + [hbm] * 9,
        out_specs=tuple(s for _, s in outs),
        scratch_shapes=scratch,
        compiler_params=pltpu.CompilerParams(
            collective_id=1, has_side_effects=True, vmem_limit_bytes=VMEM_LIMIT
        ),
        cost_estimate=pl.CostEstimate(
            flops=40 * length * depth * units, bytes_accessed=80 * length * depth, transcendentals=0
        ),
    )(tokens, vectors, *tables, wq, wk, wv, wg, wo, mg, mu, md, cotangent)


def make_tables(length):
    half = KD // 2
    frequency = np.exp(-np.log(10000.0) * np.arange(half) / half)
    angles = np.arange(length)[:, None] * frequency[None, :]
    return jnp.asarray(np.cos(angles), jnp.float32), jnp.asarray(np.sin(angles), jnp.float32)


def pack_rows(arrays, width):
    rows = [jnp.pad(a.astype(jnp.float32), (0, width - a.shape[0])) for a in arrays]
    return jnp.pad(jnp.stack(rows), ((0, 8 - len(rows)), (0, 0)))


class Ring:
    def __init__(self, chips, quarters, own, sib, rcv, own_sem, sbs_sem, sbr_sem, rss_sem, rsr_sem):
        self.chips, self.quarters = chips, quarters
        self.index, self.tensor = lax.axis_index("dp"), lax.axis_index("tensor")
        self.core = self.index % 2
        place, _ = ring_place(self.index // 2, chips)
        self.place = place
        self.nexts = [
            {"dp": ring_chip((place + 1) % chips, chips) * 2 + self.core},
            {"dp": ring_chip((place + chips - 1) % chips, chips) * 2 + self.core},
        ]
        self.virtual = [place, (chips - place) % chips]
        self.sibling = {"dp": self.index + 1 - 2 * self.core}
        self.peer = {"tensor": 1 - self.tensor}
        self.offsets = [sum(quarters[:i]) for i in range(len(quarters))]
        self.own, self.sib, self.rcv = own, sib, rcv
        self.own_sem, self.sbs_sem, self.sbr_sem = own_sem, sbs_sem, sbr_sem
        self.rss_sem, self.rsr_sem = rss_sem, rsr_sem
        self.tokens = [(d, a) for a in range(len(quarters)) for d in range(2)]

    def window(self, which, d, chunk, rows):
        return (
            pl.ds(pl.multiple_of((which * 2 + d) * rows, 8), rows),
            pl.ds(pl.multiple_of(chunk * LANE, LANE), LANE),
        )

    def packed(self, a):
        return pl.ds(self.offsets[a], self.quarters[a])

    def chunk_at(self, d, order):
        return (self.virtual[d] + 2 * self.chips - 1 - order) % self.chips

    def quarter(self, which, d, a):
        rows = self.quarters[a]
        return pl.ds(pl.multiple_of((which * 2 + d) * rows, 8), rows)

    def own_copy(self, grads, d, a):
        return pltpu.make_async_copy(
            grads[a].at[self.quarter(self.core, d, a), :],
            self.own.at[d, self.packed(a), :],
            self.own_sem.at[d, a],
        )

    def sib_copy(self, grads, d, a):
        return remote(
            grads[a].at[self.quarter(1 - self.core, d, a), :],
            self.sib.at[d, self.packed(a), :],
            self.sbs_sem.at[d, a],
            self.sbr_sem.at[d, a],
            self.sibling,
        )

    def load(self, grads):
        for d, a in self.tokens:
            self.own_copy(grads, d, a).start()
            self.sib_copy(grads, d, a).start()

    def columns(self, d, order):
        return pl.ds(pl.multiple_of(self.chunk_at(d, order) * LANE, LANE), LANE)

    def chunk(self, d, a, order):
        return self.own.at[d, self.packed(a), self.columns(d, order)]

    def rs_copy(self, d, a, step):
        return remote(
            self.chunk(d, a, step),
            self.rcv.at[d, step, self.packed(a), :],
            self.rss_sem.at[d, a, step],
            self.rsr_sem.at[d, a, step],
            self.nexts[d],
        )

    def total(self, grads, d, a, step, first=False):
        if first:
            self.own_copy(grads, d, a).wait()
            self.sib_copy(grads, d, a).wait_recv()
        part, where = self.packed(a), self.columns(d, step)
        value = self.own[d, part, where] + self.sib[d, part, where]
        if not first:
            self.rs_copy(d, a, step - 1).wait_recv()
            value = value + self.rcv[d, step - 1, part, :]
        self.own[d, part, where] = value

    def drain_ring(self):
        def ring_step(step, carry):
            for d, a in self.tokens:
                self.rs_copy(d, a, step).wait_send()
            return carry

        lax.fori_loop(0, self.chips - 1, ring_step, 0)

    def drain_pair(self, grads):
        for d, a in self.tokens:
            self.sib_copy(grads, d, a).wait_send()


class Spread:
    def __init__(self, ring, quarters, outs, buffer, ags_sem, agr_sem, cgs_sem, cgr_sem, loc_sem):
        self.ring, self.quarters, self.outs, self.buffer = ring, quarters, outs, buffer
        self.ags_sem, self.agr_sem, self.cgs_sem, self.cgr_sem, self.loc_sem = (
            ags_sem, agr_sem, cgs_sem, cgr_sem, loc_sem,
        )
        self.offsets = [sum(quarters[:i]) for i in range(len(quarters))]
        self.tokens = [(d, a) for a in range(len(quarters)) for d in range(2)]

    def packed(self, a):
        return pl.ds(self.offsets[a], self.quarters[a])

    def part(self, which, d, a, step):
        ring = self.ring
        chunk = (ring.virtual[d] + 2 * ring.chips - step) % ring.chips
        return self.outs[a].at[ring.window(which, d, chunk, self.quarters[a])]

    def slot(self, d, a, step):
        return self.buffer.at[d, step, self.packed(a), :]

    def ring_copy(self, d, a, step, source=None):
        return remote(
            self.slot(d, a, step - 1) if source is None else source,
            self.slot(d, a, step),
            self.ags_sem.at[d, a, step],
            self.agr_sem.at[d, a, step],
            self.ring.nexts[d],
        )

    def pair_copy(self, d, a, step, source=None):
        return remote(
            self.slot(d, a, step - 1) if source is None else source,
            self.part(self.ring.core, d, a, step),
            self.cgs_sem.at[d, a, step],
            self.cgr_sem.at[d, a, step],
            self.ring.sibling,
        )

    def local_copy(self, d, a, step, source=None):
        return pltpu.make_async_copy(
            self.slot(d, a, step - 1) if source is None else source,
            self.part(self.ring.core, d, a, step),
            self.loc_sem.at[d, a, step],
        )

    def place(self, d, a, step, source=None):
        self.pair_copy(d, a, step, source).start()
        self.local_copy(d, a, step, source).start()

    def arrived(self, d, a, step):
        part = self.slot(d, a, step)
        pltpu.make_async_copy(part, part, self.agr_sem.at[d, a, step]).wait()

    def finish(self, step):
        for d, a in self.tokens:
            self.arrived(d, a, step)
            self.place(d, a, step + 1)

    def drain_ring(self):
        def ring_step(step, carry):
            for d, a in self.tokens:
                part = self.slot(d, a, step)
                pltpu.make_async_copy(part, part, self.ags_sem.at[d, a, step]).wait()
            return carry

        lax.fori_loop(0, self.ring.chips - 1, ring_step, 0)

    def drain(self):
        def pair_step(step, carry):
            for d, a in self.tokens:
                part = self.part(self.ring.core, d, a, step)
                pltpu.make_async_copy(part, part, self.cgs_sem.at[d, a, step]).wait()
                pltpu.make_async_copy(part, part, self.cgr_sem.at[d, a, step]).wait()
                pltpu.make_async_copy(part, part, self.loc_sem.at[d, a, step]).wait()
            return carry

        lax.fori_loop(0, self.ring.chips, pair_step, 0)


def backward_kernel(
    chips,
    quarters,
    x_hbm,
    rows_ref,
    cos_ref,
    sin_ref,
    cot_hbm,
    h2_hbm,
    hid_hbm,
    md_hbm,
    mid_hbm,
    dh_hbm,
    gath_hbm,
    wo_hbm,
    g_hbm,
    nh_hbm,
    rstd_hbm,
    q_hbm,
    k_hbm,
    v_hbm,
    wq_hbm,
    wk_hbm,
    wv_hbm,
    wg_hbm,
    h1_hbm,
    gated_hbm,
    grad_mg,
    grad_mu,
    grad_md,
    dmid_out,
    output_out,
    grad_mg_out,
    grad_mu_out,
    grad_md_out,
    part_out,
    grad_qk_out,
    grad_v_out,
    grad_g_out,
    grad_out_out,
    small_out,
    x,
    branch,
    wo,
    g,
    nh,
    rstd,
    q,
    k,
    v,
    wq,
    wk,
    wv,
    wg,
    h1,
    gated,
    acc_gain,
    acc_bias,
    dk,
    dv,
    dq,
    stage,
    fin,
    finished,
    own,
    sib,
    rcv,
    buffer,
    ggain_ref,
    gbias_ref,
    segc_ref,
    in_sem,
    stage_sem,
    column_sem,
    fin_sem,
    dmid_sem,
    output_sem,
    own_sem,
    sbs_sem,
    sbr_sem,
    rss_sem,
    rsr_sem,
    *spread_sems,
):
    ring = Ring(chips, quarters, own, sib, rcv, own_sem, sbs_sem, sbr_sem, rss_sem, rsr_sem)
    grads = (grad_mg, grad_mu, grad_md)
    spread = Spread(ring, quarters, (grad_mg_out, grad_mu_out, grad_md_out), buffer, *spread_sems)
    f32 = jnp.float32
    heads = q.shape[0]
    length = h1.shape[0]
    units = v.shape[0]
    block = length // BLOCKS
    third = units // 3
    cot, h2, hid, md = x, h1, gated, v
    mg_o, mu_o, md_o = wv, wg, wo
    pairs = [
        (cot_hbm, cot), (h2_hbm, h2), (hid_hbm, hid), (md_hbm, md),
        (g_hbm, g), (nh_hbm, nh), (rstd_hbm, rstd), (q_hbm, q), (k_hbm, k), (wq_hbm, wq), (wk_hbm, wk),
        (wo_hbm, wo), (v_hbm, v), (wv_hbm, wv), (wg_hbm, wg), (x_hbm, x), (h1_hbm, h1), (gated_hbm, gated),
    ]
    copies = [pltpu.make_async_copy(a, b, in_sem.at[n]) for n, (a, b) in enumerate(pairs)]
    greet([*ring.nexts, ring.sibling])
    ring.load(grads)

    cast_list = [(w, target, n) for w, target in ((1, mg_o), (2, mu_o), (3, md_o)) for n in range(3)]

    def cast_copy(number):
        w, _, n = cast_list[number]
        return pltpu.make_async_copy(
            gath_hbm.at[w, pl.ds(n * third, third), :], stage.at[number % 2], stage_sem.at[number % 2]
        )

    cast_copy(0).start()
    for copy in copies[:4]:
        copy.start()
    for copy in copies[4:11]:
        copy.start()
    acc_gain[...] = jnp.zeros_like(acc_gain)
    acc_bias[...] = jnp.zeros_like(acc_bias)
    small_out[...] = jnp.zeros_like(small_out)
    for n in range(3):
        where = slice(n * third, (n + 1) * third)
        ggain_ref[where, :] = upright_part(rows_ref[GROUP_GAIN : GROUP_GAIN + 1, :], n * third, third)
        gbias_ref[where, :] = upright_part(rows_ref[GROUP_BIAS : GROUP_BIAS + 1, :], n * third, third)
    for n in range(BLOCKS):
        where = slice(n * block, (n + 1) * block)
        segc_ref[where, :] = upright(rows_ref[SEGMENT : SEGMENT + 1, where], block)
    plan = [(step, a) for step in range(2 * chips - 1) for a in range(len(quarters))]

    def pump(count=1):
        for _ in range(min(count, len(plan))):
            step, a = plan.pop(0)
            for d in range(2):
                if step < chips:
                    ring.total(grads, d, a, step, step == 0)
                if step < chips - 1:
                    ring.rs_copy(d, a, step).start()
                    continue
                turn_step = step - (chips - 1)
                source = ring.chunk(d, a, chips - 1) if turn_step == 0 else None
                if turn_step > 0:
                    spread.arrived(d, a, turn_step - 1)
                if turn_step < chips - 1:
                    spread.ring_copy(d, a, turn_step, source).start()
                spread.place(d, a, turn_step, source)

    fin_rows = [pl.ds(i * block, block) for i in range(BLOCKS)]

    def fin_copy(i, which):
        source = (mid_hbm, dh_hbm)[which]
        return pltpu.make_async_copy(source.at[fin_rows[i], :], fin.at[which], fin_sem.at[which])

    for which in range(2):
        fin_copy(0, which).start()
    for number, (_, target, n) in enumerate(cast_list):
        if number + 1 < len(cast_list):
            cast_copy(number + 1).start()
        cast_copy(number).wait()
        target[n * third : (n + 1) * third, :] = low(stage[number % 2])
        if number % 2 == 0:
            pump()
    for copy in copies[:4]:
        copy.wait()
    dh_oth, out_sum = stage.at[0, pl.ds(0, block), :], stage.at[1, pl.ds(0, block), :]
    half_units = units // 2

    def output_copy(i):
        spot = pl.ds((i % (BLOCKS // 2)) * block, block)
        return pltpu.make_async_copy(finished, output_out.at[spot, :], output_sem)

    def dmid_copy(i):
        return pltpu.make_async_copy(fin.at[1], dmid_out.at[fin_rows[i], :], dmid_sem)

    gain2 = rows_ref[GAIN2 : GAIN2 + 1, :]
    for i in range(BLOCKS):
        rows = fin_rows[i]
        for which in range(2):
            fin_copy(i, which).wait()
        mine = ring.tensor == i // (BLOCKS // 2)
        for f in range(2):
            tall = slice(f * half_units, (f + 1) * half_units)
            hidden, _, _, more = mlp_part(mg_o, mu_o, md_o, h2, cot, tall, rows)
            dh_oth[...] = more if f == 0 else dh_oth[...] + more

            @pl.when(mine)
            def _():
                lift = dot(hidden, md_o[tall, :], 0, 0) + dot(hid[tall, rows], md[tall, :], 0, 0)
                out_sum[...] = lift if f == 0 else out_sum[...] + lift

            pump()

        @pl.when(mine)
        def _():
            if i % (BLOCKS // 2):
                output_copy(i - 1).wait()
            finished[...] = low(fin[0] + out_sum[...])
            output_copy(i).start()

        mid = fin[0]
        r2 = lax.rsqrt(jnp.mean(mid * mid, axis=1, keepdims=True) + EPSILON)
        dh2 = fin[1] + dh_oth[...]
        e = dh2 * gain2
        inner = jnp.mean(e * mid, axis=1, keepdims=True)
        small_out[1:2, :] += jnp.sum(dh2 * mid * r2, axis=0, keepdims=True)
        result = cot[rows, :].astype(f32) + r2 * e - mid * (r2 * r2 * r2 * inner)
        fin[1] = result
        branch[rows, :] = low(result)
        dmid_copy(i).start()
        if i < BLOCKS - 1:
            fin_copy(i + 1, 0).start()
            dmid_copy(i).wait()
            fin_copy(i + 1, 1).start()
        pump()
    for copy in copies[11:]:
        copy.start()
    for copy in copies[4:7]:
        copy.wait()
    copies[11].wait()

    def fold(values):
        return values[:, :LANE] + values[:, LANE:]

    def gate_block(i):
        rows = pl.ds(i * block, block)
        for head in range(heads):
            tall = slice(head * VD, (head + 1) * VD)
            up = dot(wo[tall, :], branch[rows, :], 1, 1)
            gate = g[tall, rows].astype(f32)
            nhat = nh[tall, rows].astype(f32)
            sigmoid = 1.0 / (1.0 + jnp.exp(-gate))
            silu = gate * sigmoid
            dgn = up * silu
            acc_gain[tall, :] += fold(dgn * nhat)
            acc_bias[tall, :] += fold(dgn)
            gain = ggain_ref[tall, :]
            f = dgn * gain
            mean = jnp.mean(f, axis=0, keepdims=True)
            inner = jnp.mean(f * nhat, axis=0, keepdims=True)
            nh[tall, rows] = low((f - mean - nhat * inner) * rstd[head : head + 1, rows])
            gn = nhat * gain + gbias_ref[tall, :]
            g[tall, rows] = low(up * gn * (sigmoid + silu * (1.0 - sigmoid)))

    for i in range(BLOCKS):
        gate_block(i)
        pump()
    for copy in (copies[7], copies[8], copies[12]):
        copy.wait()

    ahead = lax.broadcasted_iota(jnp.int32, (block, block), 0) - lax.broadcasted_iota(
        jnp.int32, (block, block), 1
    )

    def key_block(head, m):
        tall = slice(head * VD, (head + 1) * VD)
        cols = pl.ds(m * block, block)
        rate = rate_of(head, heads, ring.tensor)
        dk[...] = jnp.zeros_like(dk)
        dv[...] = jnp.zeros_like(dv)

        def tile(i, carry):
            rows = pl.ds(pl.multiple_of(i * block, block), block)
            gap = ahead + (i - m) * block
            seen = (segc_ref[rows, :] == rows_ref[SEGMENT : SEGMENT + 1, cols]) & (gap >= 0)
            decay = jnp.where(seen, jnp.exp(gap.astype(f32) * rate), 0.0)
            scores = low(dot(q[head, rows, :], k[head, cols, :], 1, 1) * decay)
            draw = low(dot(nh[tall, rows], v[tall, cols], 0, 0) * decay)
            dv[...] += dot(nh[tall, rows], scores, 1, 0)
            dk[...] += dot(draw, q[head, rows, :], 0, 0)
            more = dot(draw, k[head, cols, :], 1, 0)
            if m == 0:
                dq[rows, :] = more
            else:
                dq[rows, :] += more
            return carry

        if m == 0:
            lax.fori_loop(0, BLOCKS // 2, tile, 0)
            pump()
            lax.fori_loop(BLOCKS // 2, BLOCKS, tile, 0)
        else:
            lax.fori_loop(m, BLOCKS, tile, 0)
        v[tall, cols] = low(dv[...])
        k[head, cols, :] = low(turn(dk[...], cos_ref[cols, :], -sin_ref[cols, :]) * KD ** (-0.5))

    for head in range(heads):
        for m in range(BLOCKS):
            key_block(head, m)
            if m == BLOCKS - 1:
                q[head] = low(turn(dq[...], cos_ref[...], -sin_ref[...]))
            pump()

    for copy in (*copies[9:11], *copies[13:]):
        copy.wait()
    column = dq

    def stage_wait(slot):
        pltpu.make_async_copy(stage.at[slot], stage.at[slot], stage_sem.at[slot]).wait()

    key_parts = [(q, wq), (k, wk)]
    for i in range(BLOCKS):
        slot = i % 2
        rows = pl.ds(i * block, block)
        if i >= 2:
            stage_wait(slot)
        total = None
        for values, weights in key_parts:
            for head in range(heads):
                wide = slice(head * KD, (head + 1) * KD)
                more = dot(values[head, rows, :], weights[:, wide], 1, 1)
                total = more if total is None else total + more
        stage[slot, 0:block, :] = total
        stage[slot, 0:block, :] += dot(v[:, rows], wv[...], 0, 0)
        stage[slot, 0:block, :] += dot(g[:, rows], wg[...], 0, 0)
        xb = x[rows, :].astype(f32)
        r1 = lax.rsqrt(jnp.mean(xb * xb, axis=1, keepdims=True) + EPSILON)
        small_out[0:1, :] += jnp.sum(stage[slot, 0:block, :] * (xb * r1), axis=0, keepdims=True)
        pltpu.make_async_copy(stage.at[slot], part_out.at[i], stage_sem.at[slot]).start()
        pump()

    count = BLOCKS
    for source, right, target in ((v, h1, grad_v_out), (g, h1, grad_g_out), (gated, branch, grad_out_out)):
        for n in range(3):
            where = pl.ds(n * third, third)
            slot = count % 2
            stage_wait(slot)
            stage[slot] = dot(source[where, :], right[...], 1, 0)
            pltpu.make_async_copy(stage.at[slot], target.at[where, :], stage_sem.at[slot]).start()
            count += 1
            pump()

    for number, (values, head) in enumerate([(q, 0), (q, 1), (k, 0), (k, 1)][: 2 * heads]):
        if number:
            pltpu.make_async_copy(column, column, column_sem).wait()
        column[...] = dot(h1[...], values[head], 0, 0)
        pltpu.make_async_copy(column, grad_qk_out.at[:, pl.ds(number * KD, KD)], column_sem).start()
        pump()
    pump(len(plan))

    ones = jnp.ones((8, LANE), jnp.bfloat16)

    def row_of(acc):
        whole = acc[...]
        high = low(whole)
        return dot(ones, high, 1, 1) + dot(ones, low(whole - high.astype(f32)), 1, 1)

    small_out[2:3, 0:units] = row_of(acc_gain)[0:1, :]
    small_out[3:4, 0:units] = row_of(acc_bias)[0:1, :]

    ring.drain_ring()
    ring.drain_pair(grads)
    spread.drain_ring()
    spread.drain()
    dmid_copy(BLOCKS - 1).wait()
    output_copy(BLOCKS - 1).wait()
    for slot in range(2):
        stage_wait(slot)
    pltpu.make_async_copy(column, column, column_sem).wait()


def backward(tokens, vectors, tables, cotangent, mlp, saved, ws, mlp_grads):
    chips = lax.axis_size("dp") // 2
    length, depth = tokens.shape
    wq, wk, wv, wg, wo, md = ws
    h1, q, k, v, g, nh, rstd, gated = saved
    mid, dh, h2, hid, gathered = mlp
    units = wv.shape[0]
    heads = q.shape[0]
    block = length // BLOCKS
    quarters = tuple(a.shape[0] // 4 for a in mlp_grads)
    rows = sum(quarters)
    count = len(quarters)
    f32, bf16 = jnp.float32, jnp.bfloat16
    vmem = pl.BlockSpec(memory_space=pltpu.VMEM)
    hbm = pl.BlockSpec(memory_space=pl.ANY)
    dma = lambda *shape: pltpu.SemaphoreType.DMA(shape)
    shape = jax.ShapeDtypeStruct
    tall = (units, length)
    stage_rows = max(block, units // 3)
    outs = [
        (shape((length, depth), f32), hbm),
        (shape((length // 2, depth), bf16), hbm),
        (shape((units, depth), f32), hbm),
        (shape((units, depth), f32), hbm),
        (shape((units, depth), f32), hbm),
        (shape((BLOCKS, stage_rows, depth), f32), hbm),
        (shape((depth, 2 * heads * KD), f32), hbm),
        (shape((units, depth), f32), hbm),
        (shape((units, depth), f32), hbm),
        (shape((units, depth), f32), hbm),
        (shape((8, depth), f32), vmem),
    ]
    scratch = [
        pltpu.VMEM((length, depth), bf16),
        pltpu.VMEM((length, depth), bf16),
        pltpu.VMEM((units, depth), bf16),
        pltpu.VMEM(tall, bf16),
        pltpu.VMEM(tall, bf16),
        pltpu.VMEM((8, length), f32),
        pltpu.VMEM((heads, length, KD), bf16),
        pltpu.VMEM((heads, length, KD), bf16),
        pltpu.VMEM(tall, bf16),
        pltpu.VMEM((depth, heads * KD), bf16),
        pltpu.VMEM((depth, heads * KD), bf16),
        pltpu.VMEM((units, depth), bf16),
        pltpu.VMEM((units, depth), bf16),
        pltpu.VMEM((length, depth), bf16),
        pltpu.VMEM(tall, bf16),
        pltpu.VMEM((units, LANE), f32),
        pltpu.VMEM((units, LANE), f32),
        pltpu.VMEM((block, KD), f32),
        pltpu.VMEM((VD, block), f32),
        pltpu.VMEM((length, KD), f32),
        pltpu.VMEM((2, stage_rows, depth), f32),
        pltpu.VMEM((2, block, depth), f32),
        pltpu.VMEM((block, depth), bf16),
        pltpu.VMEM((2, rows, depth), f32),
        pltpu.VMEM((2, rows, depth), f32),
        pltpu.VMEM((2, chips - 1, rows, LANE), f32),
        pltpu.VMEM((2, chips - 1, rows, LANE), f32),
        pltpu.VMEM((units, 1), f32),
        pltpu.VMEM((units, 1), f32),
        pltpu.VMEM((length, 1), f32),
        dma(18),
        dma(2),
        pltpu.SemaphoreType.DMA,
        dma(2),
        pltpu.SemaphoreType.DMA,
        pltpu.SemaphoreType.DMA,
        dma(2, count),
        dma(2, count),
        dma(2, count),
        dma(2, count, chips - 1),
        dma(2, count, chips - 1),
        dma(2, count, chips - 1),
        dma(2, count, chips - 1),
        dma(2, count, chips),
        dma(2, count, chips),
        dma(2, count, chips),
    ]
    return pl.pallas_call(
        functools.partial(backward_kernel, chips, quarters),
        out_shape=tuple(o for o, _ in outs),
        in_specs=[hbm] + [vmem] * 3 + [hbm] * 23,
        out_specs=tuple(s for _, s in outs),
        scratch_shapes=scratch,
        compiler_params=pltpu.CompilerParams(
            collective_id=2, has_side_effects=True, vmem_limit_bytes=VMEM_LIMIT
        ),
        cost_estimate=pl.CostEstimate(
            flops=20 * length * depth * units, bytes_accessed=80 * length * depth, transcendentals=0
        ),
    )(
        tokens, vectors, *tables, cotangent, h2, hid, md, mid, dh, gathered,
        wo, g, nh, rstd, q, k, v, wq, wk, wv, wg, h1, gated, *mlp_grads,
    )


def finish_kernel(
    chips,
    quarters,
    *refs,
):
    count = len(quarters)
    grads = refs[:count]
    part_hbm, small_ref, x_hbm, dmid_hbm, rows_ref = refs[count : count + 5]
    refs = refs[count + 5 :]
    outs = refs[:count]
    tokens_out, small_out = refs[count : count + 2]
    (late_buffer, own, sib, rcv, sacc, sbuf, part, peer, x, dmid, result, in_sem, res_sem, hs_sem, hr_sem, ss_sem, sr_sem) = refs[
        count + 2 : count + 19
    ]
    sems = refs[count + 19 :]
    ring = Ring(chips, quarters, own, sib, rcv, *sems[:5])
    late = Spread(ring, quarters, outs, late_buffer, *sems[5:10])
    bits = (2 * chips).bit_length() - 1
    f32 = jnp.float32
    block = part.shape[1]
    greet(
        [*ring.nexts, ring.peer] + [{"dp": bit_partner(ring.index, bit)} for bit in range(bits)]
    )

    ring.load(grads)

    few = block // (2 * PIECES)
    swaps = 2 * PIECES * BLOCKS

    def h_copy(n):
        i, inside = n // (2 * PIECES), pl.ds(pl.multiple_of((n % (2 * PIECES)) * few, few), few)
        return remote(part_hbm.at[i, inside, :], peer.at[i, inside, :], hs_sem.at[n], hr_sem.at[n], ring.peer)

    def h_step(n, early=False):
        if not early:
            h_copy(n - 2).wait_send()
        h_copy(n).start()

    loads = [pltpu.make_async_copy(x_hbm, x, in_sem.at[0]), pltpu.make_async_copy(dmid_hbm, dmid, in_sem.at[1])]
    for i in range(BLOCKS):
        loads.append(pltpu.make_async_copy(part_hbm.at[i, pl.ds(0, block), :], part.at[i], in_sem.at[2 + i]))

    def s_copy(level):
        target = ring.peer if level == 0 else {"dp": bit_partner(ring.index, level - 1)}
        return remote(sacc.at[level], sbuf.at[level], ss_sem.at[level], sr_sem.at[level], target)

    def s_finish(level):
        s_copy(level).wait()
        got = sbuf[level]
        if level == 0:
            first = lax.broadcasted_iota(jnp.int32, got.shape, 0) == 0
            got = jnp.where(first, got, 0.0)
        sacc[level + 1] = sacc[level] + got

    sacc[0] = small_ref[...]

    def small_step(step):
        for level in range(bits + 2):

            @pl.when(step == level)
            def _():
                if level > 0:
                    s_finish(level - 1)
                if level <= bits:
                    s_copy(level).start()

    first_order = [(ring, a) for a in range(count)]
    second_order = [(late, a) for a in range(count)]

    each = block // PIECES
    pieces = BLOCKS * PIECES

    def token_piece(number):
        i = number // PIECES
        for n in range(2):
            h_copy(2 * number + n).wait_recv()

        @pl.when(number == 0)
        def _():
            for copy in loads:
                copy.wait()

        inside = pl.ds(pl.multiple_of((number % PIECES) * each, each), each)
        rows = pl.ds(pl.multiple_of(number * each, each), each)
        xb = x[rows, :].astype(f32)
        r1 = lax.rsqrt(jnp.mean(xb * xb, axis=1, keepdims=True) + EPSILON)
        e = (part[i, inside, :] + peer[i, inside, :]) * rows_ref[GAIN1 : GAIN1 + 1, :]
        inner = jnp.mean(e * xb, axis=1, keepdims=True)
        result[rows, :] = low(dmid[rows, :] + r1 * e - xb * (r1 * r1 * r1 * inner))

    def when(condition, action):
        if isinstance(condition, bool):
            if condition:
                action()
        else:
            pl.when(condition)(action)

    def beside(turn):
        piece = (turn // 3) * 2 + turn % 3
        late_turn = turn - LAG
        if isinstance(turn, int):
            when(turn % 3 != 2 and piece < swaps, lambda: h_step(piece, piece < 2))
            when(late_turn >= 0 and late_turn % 3 == 0, lambda: token_piece(late_turn // 3))
        else:
            when((turn % 3 != 2) & (piece < swaps), lambda: h_step(piece))
            ready = (late_turn >= 0) & (late_turn % 3 == 0) & (late_turn // 3 < pieces)
            when(ready, lambda: token_piece(late_turn // 3))

    def first_step(step, before):
        for position, (_, a) in enumerate(first_order):
            for d in range(2):
                ring.total(grads, d, a, step, before is None)
                ring.rs_copy(d, a, step).start()
            beside(step * count + position)

    def rs_step(step, carry):
        first_step(step, (first_order, step - 1))

        small_step(step)
        return carry

    first_step(0, None)
    for copy in loads:
        copy.start()
    small_step(0)
    lax.fori_loop(1, chips - 1, rs_step, 0)
    for position, (_, a) in enumerate(second_order):
        for d in range(2):
            ring.total(grads, d, a, chips - 1)
            source = ring.chunk(d, a, chips - 1)
            late.ring_copy(d, a, 0, source).start()
            late.place(d, a, 0, source)
        beside((chips - 1) * count + position)

    def ag_step(step, carry):
        for position, (_, a) in enumerate(second_order):
            for d in range(2):
                late.arrived(d, a, step - 1)
                late.ring_copy(d, a, step).start()
                late.place(d, a, step)
            beside((chips - 1 + step) * count + position)

        return carry

    lax.fori_loop(1, chips - 1, ag_step, 0)
    tokens_copy = pltpu.make_async_copy(result, tokens_out, res_sem)
    tokens_copy.start()
    late.finish(chips - 2)
    small_out[...] = sacc[bits + 1]
    ring.drain_ring()
    late.drain_ring()
    ring.drain_pair(grads)
    late.drain()
    for n in range(swaps - 2, swaps):
        h_copy(n).wait_send()
    tokens_copy.wait()


def finish(grads, part, small, tokens, dmid, vectors):
    chips = lax.axis_size("dp") // 2
    length, depth = tokens.shape
    block = length // BLOCKS
    quarters = tuple(g.shape[0] // 4 for g in grads)
    rows = sum(quarters)
    count = len(quarters)
    bits = (2 * chips).bit_length() - 1
    f32, bf16 = jnp.float32, jnp.bfloat16
    vmem = pl.BlockSpec(memory_space=pltpu.VMEM)
    hbm = pl.BlockSpec(memory_space=pl.ANY)
    dma = lambda *shape: pltpu.SemaphoreType.DMA(shape)
    shape = jax.ShapeDtypeStruct
    outs = [(shape(g.shape, f32), hbm) for g in grads]
    outs += [
        (shape((length, depth), bf16), hbm),
        (shape(small.shape, f32), vmem),
    ]
    scratch = [
        pltpu.VMEM((2, chips - 1, rows, LANE), f32),
        pltpu.VMEM((2, rows, depth), f32),
        pltpu.VMEM((2, rows, depth), f32),
        pltpu.VMEM((2, chips - 1, rows, LANE), f32),
        pltpu.VMEM((bits + 2, *small.shape), f32),
        pltpu.VMEM((bits + 1, *small.shape), f32),
        pltpu.VMEM((BLOCKS, block, depth), f32),
        pltpu.VMEM((BLOCKS, block, depth), f32),
        pltpu.VMEM((length, depth), bf16),
        pltpu.VMEM((length, depth), f32),
        pltpu.VMEM((length, depth), bf16),
        dma(2 + BLOCKS),
        pltpu.SemaphoreType.DMA,
        dma(2 * PIECES * BLOCKS),
        dma(2 * PIECES * BLOCKS),
        dma(bits + 1),
        dma(bits + 1),
        dma(2, count),
        dma(2, count),
        dma(2, count),
        dma(2, count, chips - 1),
        dma(2, count, chips - 1),
    ]
    scratch += [
        dma(2, count, chips - 1),
        dma(2, count, chips - 1),
        dma(2, count, chips),
        dma(2, count, chips),
        dma(2, count, chips),
    ]
    return pl.pallas_call(
        functools.partial(finish_kernel, chips, quarters),
        out_shape=tuple(o for o, _ in outs),
        in_specs=[hbm] * (count + 1) + [vmem] + [hbm] * 2 + [vmem],
        out_specs=tuple(s for _, s in outs),
        scratch_shapes=scratch,
        compiler_params=pltpu.CompilerParams(
            collective_id=3, has_side_effects=True, vmem_limit_bytes=VMEM_LIMIT
        ),
        cost_estimate=pl.CostEstimate(
            flops=20 * rows * depth, bytes_accessed=80 * rows * depth, transcendentals=0
        ),
    )(*grads, part, small, tokens, dmid, vectors)


def deliver_kernel(count, key_width, *refs):
    sources, targets = refs[:count], refs[count : 2 * count + 1]
    buffer, low_buffer, in_sem, out_sem = refs[2 * count + 1 :]
    pieces = []
    for a in range(count):
        parts = DELIVER if sources[a].dtype == jnp.float32 else 1
        rows = sources[a].shape[0] // parts
        for n in range(parts):
            pieces.append((a, pl.ds(n * rows, rows), rows))
    wide = sum(sources[a].dtype == jnp.float32 for a, _, _ in pieces)
    low_start = [sum(r for _, _, r in pieces[wide:n]) for n in range(wide, len(pieces))]

    def spot(number):
        rows = pieces[number][2]
        if number < wide:
            return buffer.at[number, pl.ds(0, rows), :]
        return low_buffer.at[pl.ds(low_start[number - wide], rows), :]

    def load(number):
        a, where, rows = pieces[number]
        return pltpu.make_async_copy(sources[a].at[where, :], spot(number), in_sem.at[number])

    def stores(number):
        a, where, rows = pieces[number]
        if a:
            spots = [(spot(number), targets[a + 1].at[where, :])]
        else:
            spots = [
                (buffer.at[number, pl.ds(0, rows), pl.ds(half * key_width, key_width)], targets[half].at[where, :])
                for half in range(2)
            ]
        return [pltpu.make_async_copy(s, t, out_sem.at[number, n]) for n, (s, t) in enumerate(spots)]

    for number in range(len(pieces)):
        load(number).start()
    for number in range(len(pieces)):
        load(number).wait()
        for copy in stores(number):
            copy.start()
    for number in range(len(pieces)):
        for copy in stores(number):
            copy.wait()


def deliver(arrays, narrow, key_width):
    hbm = pl.BlockSpec(memory_space=pl.ANY)
    every = (*arrays, *narrow)
    shapes = [((arrays[0].shape[0], key_width), jnp.float32)] * 2 + [(a.shape, a.dtype) for a in every[1:]]
    size = sum(a.size for a in arrays)
    wide = DELIVER * len(arrays)
    pieces = wide + len(narrow)
    depth = arrays[0].shape[1]
    rows = max(a.shape[0] for a in arrays) // DELIVER
    return pl.pallas_call(
        functools.partial(deliver_kernel, len(every), key_width),
        out_shape=tuple(jax.ShapeDtypeStruct(s, t) for s, t in shapes),
        in_specs=[hbm] * len(every),
        out_specs=(hbm,) * len(shapes),
        scratch_shapes=[
            pltpu.VMEM((wide, rows, depth), jnp.float32),
            pltpu.VMEM((sum(a.shape[0] for a in narrow), depth), jnp.bfloat16),
            pltpu.SemaphoreType.DMA((pieces,)),
            pltpu.SemaphoreType.DMA((pieces, 2)),
        ],
        compiler_params=pltpu.CompilerParams(vmem_limit_bytes=56 * 1024 * 1024),
        cost_estimate=pl.CostEstimate(flops=0, bytes_accessed=8 * size, transcendentals=0),
    )(*every)

def swap(array):
    return lax.ppermute(array, "tensor", [(0, 1), (1, 0)])


def other_half(arrays, zero):
    dp, index = lax.axis_size("dp"), lax.axis_index("dp")
    rows = arrays[0].shape[0]
    count = len(arrays)
    if dp % count == 0 and rows % (8 * (dp // count)) == 0:
        share = rows * count // dp
        each = dp // count
        inside = (index % each) * share
        own = [lax.dynamic_slice_in_dim(a, inside, share, 0) for a in arrays]
        part = own[0]
        for number in range(1, count):
            part = jnp.where(index // each == number, own[number], part)
    else:
        share = -(-rows * count // (8 * dp)) * 8
        whole = jnp.concatenate(arrays, axis=0)
        whole = jnp.pad(whole, ((0, share * dp - rows * count), (0, 0)))
        part = lax.dynamic_slice_in_dim(whole, index * share, share, 0)
    got = lax.all_gather(swap(part.astype(jnp.float32)), "dp", axis=0, tiled=True)
    got = low(got + zero)
    return [got[number * rows : (number + 1) * rows] for number in range(count)]


def plain_body(
    tokens,
    segment,
    norm1_gain,
    w_query,
    w_key,
    w_value,
    w_gate,
    group_gain,
    group_bias,
    w_out,
    norm2_gain,
    w_mlp_gate,
    w_mlp_up,
    w_mlp_down,
    cotangent,
):
    length, depth = tokens.shape
    heads = w_query.shape[1] // KD
    block = length // BLOCKS
    tensor = lax.axis_index("tensor")
    f32 = jnp.float32
    zero = jnp.minimum(segment[0], 0).astype(f32)
    value_t, gate_t, mg_t, mu_t = w_value.T, w_gate.T, w_mlp_gate.T, w_mlp_up.T
    mg_o, mu_o, md_o, wo_o = other_half([mg_t, mu_t, w_mlp_down, w_out], zero)
    x = tokens.astype(f32)
    gain1 = norm1_gain.astype(f32)
    gain2 = norm2_gain.astype(f32)
    ggain = group_gain.astype(f32)[:, None]
    gbias = group_bias.astype(f32)[:, None]
    r1 = lax.rsqrt(jnp.mean(x * x, axis=1, keepdims=True) + EPSILON)
    h1 = low(x * r1 * gain1)
    half = KD // 2
    frequency = jnp.exp(-jnp.log(10000.0) * jnp.arange(half, dtype=f32) / half)
    angles = jnp.arange(length, dtype=f32)[:, None] * frequency[None, :]
    cosine, sine = jnp.cos(angles), jnp.sin(angles)
    positions = jnp.arange(length, dtype=jnp.int32)
    visible = (positions[:, None] >= positions[None, :]) & (segment[:, None] == segment[None, :])
    offsets = jnp.maximum(positions[:, None] - positions[None, :], 0).astype(f32)

    def decay(head, rows, columns):
        order = (tensor * heads + head).astype(f32)
        rate = jnp.log1p(-jnp.exp2(-5.0 - order))
        return jnp.where(visible[rows, columns], jnp.exp(offsets[rows, columns] * rate), 0.0)

    queries = [[] for _ in range(heads)]
    keys = [[] for _ in range(heads)]
    values = [[] for _ in range(heads)]
    gates = [[] for _ in range(heads)]
    nhats = [[] for _ in range(heads)]
    spreads = [[] for _ in range(heads)]
    gated_blocks, received = [], []
    for number in range(BLOCKS):
        rows = slice(number * block, (number + 1) * block)
        seen = slice(0, (number + 1) * block)
        own = []
        for head in range(heads):
            wide = slice(head * KD, (head + 1) * KD)
            tall = slice(head * VD, (head + 1) * VD)
            q = low(turn(dot(h1[rows], w_query[:, wide], 1, 0), cosine[rows], sine[rows]))
            k = turn(dot(h1[rows], w_key[:, wide], 1, 0), cosine[rows], sine[rows])
            queries[head].append(q)
            keys[head].append(low(k * KD ** (-0.5)))
            values[head].append(low(dot(value_t[tall], h1[rows], 1, 1)))
            g = dot(gate_t[tall], h1[rows], 1, 1)
            gates[head].append(g)
            scores = dot(q, jnp.concatenate(keys[head], axis=0), 1, 1)
            scores = low(scores * decay(head, rows, seen))
            ret = dot(jnp.concatenate(values[head], axis=1), scores, 1, 1)
            centred = ret - jnp.mean(ret, axis=0, keepdims=True)
            scale = lax.rsqrt(jnp.mean(centred * centred, axis=0, keepdims=True) + GROUP_EPSILON)
            nhat = centred * scale
            nhats[head].append(nhat)
            spreads[head].append(scale)
            own.append(low(jax.nn.silu(g) * (nhat * ggain[tall] + gbias[tall])))
        gated_blocks.append(jnp.concatenate(own, axis=0))
        received.append(low(swap(gated_blocks[-1].astype(f32)) + zero))

    mids, h2s, r2s, hidden_own, hidden_oth, das, dbs, dmids = [], [], [], [], [], [], [], []
    norm2_rows = []
    for number in range(BLOCKS):
        rows = slice(number * block, (number + 1) * block)
        mid = x[rows] + (dot(gated_blocks[number], w_out, 0, 0) + dot(received[number], wo_o, 0, 0))
        r2 = lax.rsqrt(jnp.mean(mid * mid, axis=1, keepdims=True) + EPSILON)
        h2 = low(mid * r2 * gain2)
        cot = cotangent[rows]

        def mlp(gate_w, up_w, down_w):
            a, b = dot(gate_w, h2, 1, 1), dot(up_w, h2, 1, 1)
            hidden, pull = jax.vjp(lambda s, t: jax.nn.gelu(s) * t, a, b)
            da, db = pull(dot(down_w, cot, 1, 1))
            da, db = low(da), low(db)
            return low(hidden), da, db, dot(da, gate_w, 0, 0) + dot(db, up_w, 0, 0)

        own_hidden, da, db, part = mlp(mg_t, mu_t, w_mlp_down)
        oth_hidden, _, _, more = mlp(mg_o, mu_o, md_o)
        dh2 = part + more
        e = dh2 * gain2
        dmid = cot.astype(f32) + r2 * e - mid * (r2 * r2 * r2) * jnp.mean(e * mid, axis=1, keepdims=True)
        norm2_rows.append(jnp.sum(dh2 * mid * r2, axis=0))
        for where, value in zip(
            (mids, h2s, hidden_own, hidden_oth, das, dbs, dmids),
            (mid, h2, own_hidden, oth_hidden, da, db, dmid),
        ):
            where.append(value)
    grad_norm2 = sum(norm2_rows)
    mid = jnp.concatenate(mids, axis=0)
    h2 = jnp.concatenate(h2s, axis=0)
    hidden = jnp.concatenate(hidden_own, axis=1)
    hidden_o = jnp.concatenate(hidden_oth, axis=1)
    dmid = jnp.concatenate(dmids, axis=0)
    own_rows = length // lax.axis_size("tensor")
    place = tensor * own_rows
    output = low(
        lax.dynamic_slice_in_dim(mid, place, own_rows, 0)
        + dot(lax.dynamic_slice_in_dim(hidden, place, own_rows, 1), w_mlp_down, 0, 0)
        + dot(lax.dynamic_slice_in_dim(hidden_o, place, own_rows, 1), md_o, 0, 0)
    )
    grad_mg = dot(jnp.concatenate(das, axis=1), h2, 1, 0)
    grad_mu = dot(jnp.concatenate(dbs, axis=1), h2, 1, 0)
    grad_md = dot(hidden, cotangent, 1, 0)

    branch = low(dmid)
    gated = jnp.concatenate(gated_blocks, axis=1)
    grad_out = dot(gated, branch, 1, 0)
    dgated = dot(w_out, branch, 1, 1)
    dqs, dks, dvs, dgs, ggains, gbiases = [], [], [], [], [], []
    everything = slice(0, length)
    for head in range(heads):
        tall = slice(head * VD, (head + 1) * VD)
        g = jnp.concatenate(gates[head], axis=1)
        nhat = jnp.concatenate(nhats[head], axis=1)
        spread = jnp.concatenate(spreads[head], axis=1)
        q = jnp.concatenate(queries[head], axis=0)
        k = jnp.concatenate(keys[head], axis=0)
        v = jnp.concatenate(values[head], axis=1)
        sigmoid = jax.nn.sigmoid(g)
        silu = g * sigmoid
        up = dgated[tall]
        dgn = up * silu
        ggains.append(jnp.sum(dgn * nhat, axis=1))
        gbiases.append(jnp.sum(dgn, axis=1))
        f = dgn * ggain[tall]
        dret = (
            f - jnp.mean(f, axis=0, keepdims=True) - nhat * jnp.mean(f * nhat, axis=0, keepdims=True)
        ) * spread
        dret = low(dret)
        gn = nhat * ggain[tall] + gbias[tall]
        dgs.append(low(up * gn * (sigmoid + silu * (1.0 - sigmoid))))
        table = decay(head, everything, everything)
        scores = low(dot(q, k, 1, 1) * table)
        draw = low(dot(dret, v, 0, 0) * table)
        dvs.append(low(dot(dret, scores, 1, 0)))
        dqs.append(low(turn(dot(draw, k, 1, 0), cosine, -sine)))
        dks.append(low(turn(dot(draw, q, 0, 0), cosine, -sine) * KD ** (-0.5)))
    dv = jnp.concatenate(dvs, axis=0)
    dg = jnp.concatenate(dgs, axis=0)
    dq = jnp.concatenate(dqs, axis=1)
    dk = jnp.concatenate(dks, axis=1)
    partial_in = dot(dq, w_query, 1, 1) + dot(dk, w_key, 1, 1) + dot(dv, value_t, 0, 0) + dot(dg, gate_t, 0, 0)
    grad_norm1 = jnp.sum(partial_in * x * r1, axis=0)
    grad_qk = dot(h1, jnp.concatenate([dq, dk], axis=1), 0, 0)
    grad_v = dot(dv, h1, 1, 0)
    grad_g = dot(dg, h1, 1, 0)

    units = w_value.shape[1]
    small = jnp.stack(
        [
            grad_norm1,
            grad_norm2,
            jnp.pad(jnp.concatenate(ggains), (0, depth - units)),
            jnp.pad(jnp.concatenate(gbiases), (0, depth - units)),
        ]
    )
    small = jnp.pad(small, ((0, 4), (0, 0)))
    grads = lax.psum((grad_qk, grad_v, grad_g, grad_out, grad_mg, grad_mu, grad_md), "dp")
    peer = swap(partial_in)
    small = lax.psum(small.at[0].set(lax.psum(small[0], "tensor")), "dp")
    grad_qk, grad_v, grad_g, grad_out, grad_mg, grad_mu, grad_md = grads
    e1 = (partial_in + peer) * gain1
    grad_tokens = low(dmid + r1 * e1 - x * (r1 * r1 * r1) * jnp.mean(e1 * x, axis=1, keepdims=True))
    key_width = w_query.shape[1]
    return (
        output,
        grad_tokens,
        small[0],
        grad_qk[:, :key_width],
        grad_qk[:, key_width:],
        grad_v.T,
        grad_g.T,
        small[2, :units],
        small[3, :units],
        grad_out,
        small[1],
        grad_mg.T,
        grad_mu.T,
        grad_md,
    )


def body(
    tokens,
    segment,
    norm1_gain,
    w_query,
    w_key,
    w_value,
    w_gate,
    group_gain,
    group_bias,
    w_out,
    norm2_gain,
    w_mlp_gate,
    w_mlp_up,
    w_mlp_down,
    cotangent,
):
    length, depth = tokens.shape
    if depth % (LANE * (lax.axis_size("dp") // 2)):
        return plain_body(
            tokens, segment, norm1_gain, w_query, w_key, w_value, w_gate, group_gain, group_bias, w_out,
            norm2_gain, w_mlp_gate, w_mlp_up, w_mlp_down, cotangent,
        )
    value_t, gate_t, mg_t, mu_t = w_value.T, w_gate.T, w_mlp_gate.T, w_mlp_up.T
    tables = make_tables(length)
    vectors = pack_rows((norm1_gain, norm2_gain, group_gain, group_bias, segment), depth)
    (h1, qs, ks, vs, g, nhat, rstd, gated, mid, dh, h2, hid, grad_mg, grad_mu, grad_md, gathered) = forward(
        tokens,
        vectors,
        tables,
        (w_query, w_key, value_t, gate_t, w_out, mg_t, mu_t, w_mlp_down),
        cotangent,
    )
    (dmid, output, grad_mg, grad_mu, grad_md, part, grad_qk, grad_v, grad_g, grad_out, small) = backward(
        tokens,
        vectors,
        tables,
        cotangent,
        (mid, dh, h2, hid, gathered),
        (h1, qs, ks, vs, g, nhat, rstd, gated),
        (w_query, w_key, value_t, gate_t, w_out, w_mlp_down),
        (grad_mg, grad_mu, grad_md),
    )
    (grad_qk, grad_v, grad_g, grad_out, grad_tokens, small) = finish(
        (grad_qk, grad_v, grad_g, grad_out), part, small, tokens, dmid, vectors
    )
    units = w_value.shape[1]
    grad_q, grad_k, grad_v, grad_g, grad_out, grad_mg, grad_mu, grad_md, output, grad_tokens = deliver(
        (grad_qk, grad_v, grad_g, grad_out, grad_mg, grad_mu, grad_md), (output, grad_tokens), w_query.shape[1]
    )
    return (
        output,
        grad_tokens,
        small[0],
        grad_q,
        grad_k,
        grad_v.T,
        grad_g.T,
        small[2, :units],
        small[3, :units],
        grad_out,
        small[1],
        grad_mg.T,
        grad_mu.T,
        grad_md,
    )


def solution(mesh):
    placed = (
        P("dp", None),
        P("dp"),
        P(),
        P(None, "tensor"),
        P(None, "tensor"),
        P(None, "tensor"),
        P(None, "tensor"),
        P("tensor"),
        P("tensor"),
        P("tensor", None),
        P(),
        P(None, "tensor"),
        P(None, "tensor"),
        P("tensor", None),
        P("dp", None),
    )
    return jax.shard_map(
        body,
        mesh=mesh,
        in_specs=placed,
        out_specs=(
            P(("dp", "tensor"), None),
            P("dp", None),
            P(),
            P(None, "tensor"),
            P(None, "tensor"),
            P(None, "tensor"),
            P(None, "tensor"),
            P("tensor"),
            P("tensor"),
            P("tensor", None),
            P(),
            P(None, "tensor"),
            P(None, "tensor"),
            P("tensor", None),
        ),
        check_vma=False,
    )
```
